32 devices in a mesh: groups: 2 (over x), heads: 16 (over z, y, core).
Axes of the slice: x: 2, y: 2, z: 4, core: 2. Of those that a mesh axis runs over, the one named last changes fastest.
Arguments:
- prompt_x: bfloat16 [16, 8192, 256], P('groups', 'heads'), parts along dimension 0, may hold values from -6 to 6
- prompt_b: bfloat16 [16, 256, 1024], P('groups'), parts along dimension 0, may hold values from -6 to 6
- prompt_c: bfloat16 [16, 256, 1024], P('groups'), parts along dimension 0, may hold values from -6 to 6
- prompt_dt: bfloat16 [128, 16, 256], P('heads', 'groups'), parts along dimension 1, may hold values from 0 to 2, as said below
- decay_rate: float32 [128], replicated, may hold values from 0.5 to 2
- skip_gain: float32 [128], replicated, may hold values from 0.5 to 1.5
- lengths: int32 [16], P('groups'), parts along dimension 0, may hold values from 64 to 256, as said below
- owner_list: int32 [32, 2], P('groups'), parts along dimension 0, may hold values from 0 to 7, as said below
- page_table: int32 [16, 128], P('groups'), parts along dimension 0, may hold values from 0 to 1023, as said below
- cache_pages: bfloat16 [2048, 16, 256], P(('groups', 'heads')), parts along dimension 0, may hold values from -8 to 8
- row_slot: int32 [64], P('groups'), parts along dimension 0, may hold values from 0 to 1
- step_x: bfloat16 [64, 3, 8192], P(('groups', 'heads')), parts along dimension 0, may hold values from -6 to 6
- step_b: bfloat16 [64, 3, 1024], P(('groups', 'heads')), parts along dimension 0, may hold values from -6 to 6
- step_c: bfloat16 [64, 3, 1024], P(('groups', 'heads')), parts along dimension 0, may hold values from -6 to 6
- step_dt: bfloat16 [64, 3, 128], P(('groups', 'heads')), parts along dimension 0, may hold values from 0 to 2, as said below
- queries: bfloat16 [64, 3, 8192], P(('groups', 'heads')), parts along dimension 0, may hold values from -8 to 8
- fresh_cache: bfloat16 [64, 3, 2048], P(('groups', 'heads')), parts along dimension 0, may hold values from -8 to 8
Outputs:
- prompt_out: bfloat16 [16, 8192, 256], P('groups', 'heads'), parts along dimension 0
- mixer_out: bfloat16 [64, 3, 8192], P(('groups', 'heads')), parts along dimension 0
- attention_out: bfloat16 [64, 3, 8192], P(('groups', 'heads')), parts along dimension 0
The draws below stay inside these ranges and needn't reach their ends.
There are 2 independent parts, one for each index of `groups`. The reference program is written for one: setup_inputs(seed, part) draws one part's arguments, and reference() takes and returns one part's arrays. A program takes and returns all parts, laid end to end along the dimension named above; an argument that names none is the same for every part. Nothing has to cross between parts.
Inputs may be any that keep to these rules, and one draw needn't show every extreme that they name: `lengths`: every prompt holds 64 positions or more; in every draw one prompt holds exactly 256. `owner_list`: each row names 2 different prompts; every prompt is named in some row. `page_table`: every pool row is named by exactly one entry; entry [r, j] lies among the 64 pool rows that start at (j // 8) * 8 * 8. `prompt_dt`: positive. `step_dt`: positive.
All inputs are finite; a program needn't handle non-finite values.
Results may differ from the reference program's by a relative error of at most 0.0047.
Values may be sent and summed in bfloat16 or wider, within the bound.
No kernel may reach another device: no remote copies, remote signals or barrier semaphores. Data moves between devices by JAX's collectives and lax.ppermute only.
A program may use at most 192 MiB of HBM per device.

```python
import math
import jax
import jax.numpy as jnp
from jax import lax

NH = 128
HP = 64
NS = 256
HPG = 32
QH = 64
KVH = 8
HD = 128
PAGE = 16
BLOCK = 128
STEPS = 3
REQ_DEV = 2
PROMPT_COUNT = 8
ROWS_DEV = 2
NGRP = 4
PADDED_LENGTH = 256
PHEADS = 128
PHD = 8
OWNERS = 16
ROWS = 32
SLOTS = 1024


def head_rate(key, fast_share):
    key = jax.random.fold_in(key, 303)
    first, second_pick, third = jax.random.split(key, 3)
    fast = jax.random.bernoulli(first, fast_share, (NH,))
    quick = jnp.exp(jax.random.uniform(second_pick, (NH,), jnp.float32, math.log(1.0 / 50.0), math.log(1.0 / 30.0)))
    slow = jnp.exp(jax.random.uniform(third, (NH,), jnp.float32, math.log(0.3 / PADDED_LENGTH), math.log(2.0 / PADDED_LENGTH)))
    return jnp.where(fast, quick, slow)


def shared_mix(key):
    key = jax.random.fold_in(key, 606)
    return jax.random.normal(key, (ROWS, STEPS, KVH, 1, HD), jnp.float32)


def draw_prompt_dt(key, part):
    share = 0.5
    decay_speed = head_rate(key, share)
    key = jax.random.fold_in(key, 4)
    first, second_pick, third = jax.random.split(key, 3)
    coarse_draw = jnp.exp(jax.random.uniform(first, (NH, PROMPT_COUNT, PADDED_LENGTH), jnp.float32, math.log(0.5), math.log(2.0)))
    spike_amount = jax.random.bernoulli(second_pick, 3.0 / PADDED_LENGTH, (PROMPT_COUNT, PADDED_LENGTH))
    effect_level = jax.random.uniform(third, (PROMPT_COUNT, PADDED_LENGTH), jnp.float32, 0.3, 0.45)
    value_rows = jnp.where(spike_amount[None], effect_level[None], decay_speed[:, None, None] * coarse_draw)
    return value_rows.astype(jnp.bfloat16)


def draw_step_dt(key, part):
    share = 0.5
    decay_speed = head_rate(key, share)
    key = jax.random.fold_in(key, 5)
    coarse_draw = jnp.exp(jax.random.uniform(key, (ROWS, STEPS, NH), jnp.float32, math.log(0.5), math.log(2.0)))
    return (decay_speed[None, None, :] * coarse_draw).astype(jnp.bfloat16)


def draw_lengths(key, part):
    key = jax.random.fold_in(key, 1)
    first, second_pick = jax.random.split(key)
    value_rows = jax.random.randint(first, (PROMPT_COUNT,), PADDED_LENGTH // 4, PADDED_LENGTH + 1)
    longest = jax.random.randint(second_pick, (), 0, PROMPT_COUNT)
    return jnp.where(jnp.arange(PROMPT_COUNT) == longest, PADDED_LENGTH, value_rows).astype(jnp.int32)


def draw_owner_list(key, part):
    key = jax.random.fold_in(key, 2)
    keys = jax.random.split(key, OWNERS + 2)

    def pick_some(single):
        return jax.random.permutation(single, PROMPT_COUNT)[:REQ_DEV]
    picks = jax.vmap(pick_some)(keys[:OWNERS])
    cover = jax.random.permutation(keys[OWNERS], PROMPT_COUNT).reshape(PROMPT_COUNT // REQ_DEV, REQ_DEV)
    picks = picks.at[:PROMPT_COUNT // REQ_DEV].set(cover)
    order = jax.random.permutation(keys[OWNERS + 1], OWNERS)
    return picks[order].astype(jnp.int32)


def draw_page_table(key, part):
    key = jax.random.fold_in(key, 3)
    keys = jax.random.split(key, OWNERS)

    def shuffle(single):
        return jax.random.permutation(single, PROMPT_COUNT * PHD)
    perms = jax.vmap(shuffle)(keys)
    base = jnp.arange(OWNERS, dtype=jnp.int32)[:, None] * (PROMPT_COUNT * PHD)
    table = (perms + base).reshape(OWNERS, PROMPT_COUNT, PHD)
    return jnp.transpose(table, (1, 0, 2)).reshape(PROMPT_COUNT, PHEADS).astype(jnp.int32)


def draw_cache_pages(key, part):
    key = jax.random.fold_in(key, 6)
    first, second_pick = jax.random.split(key)
    shape = (SLOTS, PAGE, HD)
    keys = jax.random.normal(first, shape, jnp.float32)
    value_rows = jax.random.normal(second_pick, shape, jnp.float32)
    both = jnp.concatenate([keys, value_rows], axis=2)
    return jnp.clip(both, -8.0, 8.0).astype(jnp.bfloat16)


def draw_queries(key, part):
    mixing = shared_mix(key)
    key = jax.random.fold_in(key, 7)
    first = jax.random.fold_in(key, 0)
    shape = (ROWS, STEPS, KVH, QH // KVH, HD)
    weight = math.sqrt(math.log(PADDED_LENGTH) / math.sqrt(HD))
    value_rows = jax.random.normal(first, shape, jnp.float32) + weight * mixing
    return jnp.clip(value_rows, -8.0, 8.0).reshape(ROWS, STEPS, QH * HD).astype(jnp.bfloat16)


def draw_fresh_cache(key, part):
    mixing = shared_mix(key)[:, :, :, 0, :]
    key = jax.random.fold_in(key, 8)
    first, second_pick = jax.random.split(key)
    shape = (ROWS, STEPS, KVH, HD)
    weight = math.sqrt(math.log(PADDED_LENGTH) / math.sqrt(HD))
    keys = jax.random.normal(first, shape, jnp.float32) + weight * mixing
    value_rows = jax.random.normal(second_pick, shape, jnp.float32)
    both = jnp.stack([keys, value_rows], axis=2)
    return jnp.clip(both, -8.0, 8.0).reshape(ROWS, STEPS, 2 * KVH * HD).astype(jnp.bfloat16)


def touch_ends(drawn, rng, smallest, high):
    longest = drawn.shape.index(max(drawn.shape))
    spots = []
    for shift in (0, 1):
        where = [jax.random.randint(jax.random.fold_in(rng, axis), (), 0, length) for axis, length in enumerate(drawn.shape)]
        where[longest] = (where[longest] + shift) % drawn.shape[longest]
        spots.append(tuple(where))
    return drawn.at[spots[0]].set(smallest).at[spots[1]].set(high)


def levels(rng, shape, cuts, low, high):
    def one(dim, shards_of):
        draws = jax.random.uniform(jax.random.fold_in(jax.random.fold_in(rng, 6), dim), (shards_of,), jnp.float32, low / len(cuts), high / len(cuts))
        return jnp.repeat(jnp.exp(draws), shape[dim] // shards_of).reshape((-1,) + (1,) * (len(shape) - dim - 1))

    factor_of = one(*cuts[0])
    for cut in cuts[1:]:
        factor_of = factor_of * one(*cut)
    return factor_of


def normal_values(own_key, dims, scale, most, cuts=(), held_as=jnp.bfloat16):
    drawn = jax.random.normal(own_key, dims, jnp.float32) * scale
    if len(cuts) > 0:
        drawn = levels(own_key, dims, cuts, -0.22, 0.18) * drawn
    return jnp.clip(drawn, min=-most, max=most).astype(held_as)


def setup_inputs(seed: int = 0, part: int = 0) -> dict:
    seeds = jax.random.split(jax.random.key(seed), 18)
    part_keys = jax.random.split(jax.random.fold_in(seeds[17], part), 18)
    prompt_x = normal_values(part_keys[0], (PROMPT_COUNT, NH * HP, PADDED_LENGTH), 1.0, 6.0, ((1, 16),))
    prompt_b = normal_values(part_keys[1], (PROMPT_COUNT, PADDED_LENGTH, NGRP * NS), 1.0, 6.0)
    prompt_c = normal_values(part_keys[2], (PROMPT_COUNT, PADDED_LENGTH, NGRP * NS), 1.0, 6.0)
    prompt_dt = draw_prompt_dt(jax.random.fold_in(jax.random.fold_in(seeds[17], part), 71), part)
    decay_rate = jnp.clip(jnp.exp(jax.random.uniform(seeds[4], (NH,), jnp.float32, math.log(0.5), math.log(2.0))), 0.5, 2.0)
    skip_gain = jnp.clip(jax.random.uniform(seeds[5], (NH,), jnp.float32, 0.5, 1.5), 0.5, 1.5)
    lengths = draw_lengths(jax.random.fold_in(jax.random.fold_in(seeds[17], part), 71), part)
    owner_list = draw_owner_list(jax.random.fold_in(jax.random.fold_in(seeds[17], part), 71), part)
    page_table = draw_page_table(jax.random.fold_in(jax.random.fold_in(seeds[17], part), 71), part)
    cache_pages = draw_cache_pages(jax.random.fold_in(jax.random.fold_in(seeds[17], part), 71), part)
    row_slot = touch_ends(jax.random.randint(part_keys[10], (ROWS,), 0, REQ_DEV), jax.random.fold_in(part_keys[10], 1), 0, REQ_DEV - 1).astype(jnp.int32)
    step_x = normal_values(part_keys[11], (ROWS, STEPS, NH * HP), 1.0, 6.0, ((0, 16),))
    step_b = normal_values(part_keys[12], (ROWS, STEPS, NGRP * NS), 1.0, 6.0, ((0, 16),))
    step_c = normal_values(part_keys[13], (ROWS, STEPS, NGRP * NS), 1.0, 6.0, ((0, 16),))
    step_dt = draw_step_dt(jax.random.fold_in(jax.random.fold_in(seeds[17], part), 71), part)
    queries = draw_queries(jax.random.fold_in(jax.random.fold_in(seeds[17], part), 71), part)
    fresh_cache = draw_fresh_cache(jax.random.fold_in(jax.random.fold_in(seeds[17], part), 71), part)
    return dict(prompt_x=prompt_x, prompt_b=prompt_b, prompt_c=prompt_c, prompt_dt=prompt_dt, decay_rate=decay_rate, skip_gain=skip_gain, lengths=lengths, owner_list=owner_list, page_table=page_table, cache_pages=cache_pages, row_slot=row_slot, step_x=step_x, step_b=step_b, step_c=step_c, step_dt=step_dt, queries=queries, fresh_cache=fresh_cache)


precise = lax.Precision.HIGHEST

def prefill_heads(x_block, b_block, c_block, dt_block, decay_speed, skip, valid, block_len):
    prompts, width_all, length = x_block.shape
    group = dt_block.shape[0]
    width = width_all // group
    state_dim = b_block.shape[2] // group
    count = length // block_len
    moved = jnp.where(valid[None], dt_block.astype(jnp.float32), 0.0)
    logdec = -(decay_speed[:, None, None] * moved)
    logdec = logdec.reshape(group, prompts, count, block_len)
    moved = moved.reshape(group, prompts, count, block_len)
    cumul = jnp.cumsum(logdec, axis=3)
    inputs = x_block.astype(jnp.float32).reshape(prompts, group, width, count, block_len)
    entry = b_block.astype(jnp.float32).reshape(prompts, count, block_len, group, state_dim)
    readout = c_block.astype(jnp.float32).reshape(prompts, count, block_len, group, state_dim)
    scores = jnp.einsum('rcihn,rcjhn->hrcij', readout, entry, precision=precise)
    later = lax.broadcasted_iota(jnp.int32, (block_len, block_len), 0)
    earlier = lax.broadcasted_iota(jnp.int32, (block_len, block_len), 1)
    spread = cumul[..., :, None] - cumul[..., None, :]
    decays = jnp.exp(jnp.where(later >= earlier, spread, -jnp.inf))
    mixing = scores * decays * moved[..., None, :]
    inner = jnp.einsum('hrcij,rhpcj->rhpci', mixing, inputs, precision=precise)
    tail = jnp.transpose(jnp.exp(cumul[..., -1:] - cumul) * moved, (1, 0, 2, 3))[:, :, None]
    local = jnp.einsum('rhpcj,rcjhn->crhpn', inputs * tail, entry, precision=precise)
    fades = jnp.transpose(jnp.exp(cumul[..., -1]), (2, 1, 0))

    def advance(carry, piece):
        fade, fresh = piece
        return (carry * fade[:, :, None, None] + fresh, carry)
    start = jnp.zeros((prompts, group, width, state_dim), jnp.float32)
    final, before = lax.scan(advance, start, (fades, local))
    outer = jnp.einsum('rcihn,crhpn->rhpci', readout, before, precision=precise)
    outer = outer * jnp.transpose(jnp.exp(cumul), (1, 0, 2, 3))[:, :, None]
    result = inner + outer + skip[None, :, None, None, None] * inputs
    result = jnp.where(valid.reshape(prompts, 1, 1, count, block_len), result, 0.0)
    return (result.reshape(prompts, width_all, length).astype(jnp.bfloat16), final)

def reference(prompt_x, prompt_b, prompt_c, prompt_dt, decay_rate, skip_gain, lengths, owner_list, page_table, cache_pages, row_slot, step_x, step_b, step_c, step_dt, queries, fresh_cache):
    valid = jnp.arange(PADDED_LENGTH, dtype=jnp.int32)[None, :] < lengths[:, None]
    head_x = jnp.moveaxis(prompt_x.reshape(PROMPT_COUNT, NH, HP, PADDED_LENGTH), 1, 0)
    group_b = jnp.moveaxis(prompt_b.reshape(PROMPT_COUNT, PADDED_LENGTH, NGRP, NS), 2, 0)
    group_c = jnp.moveaxis(prompt_c.reshape(PROMPT_COUNT, PADDED_LENGTH, NGRP, NS), 2, 0)
    head_group = (jnp.arange(NH, dtype=jnp.int32) // HPG).astype(jnp.int32)

    def one_head(item):
        x_one, grp, dt_one, rate_one, skip_one = item
        b_one = lax.dynamic_index_in_dim(group_b, grp, 0, keepdims=False)
        c_one = lax.dynamic_index_in_dim(group_c, grp, 0, keepdims=False)
        return prefill_heads(x_one, b_one, c_one, dt_one[None], rate_one[None], skip_one[None], valid, BLOCK)
    outs, finals = lax.map(one_head, (head_x, head_group, prompt_dt, decay_rate, skip_gain))
    prompt_out = jnp.moveaxis(outs, 0, 1).reshape(PROMPT_COUNT, NH * HP, PADDED_LENGTH)
    prompt_state = jnp.moveaxis(finals[:, :, 0], 0, 1)
    owners = jnp.arange(ROWS, dtype=jnp.int32) // ROWS_DEV
    request = owner_list[owners, row_slot]
    keys_all = jnp.take(cache_pages, page_table.reshape(-1), axis=0).reshape(PROMPT_COUNT, KVH, PADDED_LENGTH, 2 * HD)
    per_group = QH // KVH
    scale = 1.0 / math.sqrt(HD)
    causal = lax.broadcasted_iota(jnp.int32, (STEPS, STEPS), 1) <= lax.broadcasted_iota(jnp.int32, (STEPS, STEPS), 0)

    def one_row(item):
        target, row_x, row_b, row_c, row_dt, row_q, row_fresh = item
        states = lax.dynamic_index_in_dim(prompt_state, target, 0, keepdims=False)
        mixed = []
        for step in range(STEPS):
            moved = row_dt[step].astype(jnp.float32)
            decay = jnp.exp(-(decay_rate * moved))
            inputs = row_x[step].reshape(NH, HP).astype(jnp.float32)
            entry = jnp.take(row_b[step].reshape(NGRP, NS).astype(jnp.float32), head_group, axis=0)
            readout = jnp.take(row_c[step].reshape(NGRP, NS).astype(jnp.float32), head_group, axis=0)
            states = decay[:, None, None] * states + (moved[:, None] * inputs)[:, :, None] * entry[:, None, :]
            value = jnp.einsum('hpn,hn->hp', states, readout, precision=precise) + skip_gain[:, None] * inputs
            mixed.append(value.reshape(NH * HP).astype(jnp.bfloat16))
        block = lax.dynamic_index_in_dim(keys_all, target, 0, keepdims=False).astype(jnp.float32)
        length = lax.dynamic_index_in_dim(lengths, target, 0, keepdims=False)
        query = row_q.astype(jnp.float32).reshape(STEPS, KVH, per_group, HD)
        fresh = row_fresh.astype(jnp.float32).reshape(STEPS, 2, KVH, HD)
        prompt_scores = jnp.einsum('tkgd,kld->tkgl', query, block[..., :HD], precision=precise) * scale
        seen = jnp.arange(PADDED_LENGTH, dtype=jnp.int32) < length
        prompt_scores = jnp.where(seen, prompt_scores, -jnp.inf)
        own_scores = jnp.einsum('tkgd,ukd->tkgu', query, fresh[:, 0], precision=precise) * scale
        own_scores = jnp.where(causal[:, None, None, :], own_scores, -jnp.inf)
        highest = jnp.maximum(lax.optimization_barrier(jnp.max(prompt_scores, axis=-1)), lax.optimization_barrier(jnp.max(own_scores, axis=-1)))
        prompt_exp = jnp.exp(prompt_scores - highest[..., None])
        own_exp = jnp.exp(own_scores - highest[..., None])
        total = lax.optimization_barrier(jnp.sum(prompt_exp, axis=-1)) + lax.optimization_barrier(jnp.sum(own_exp, axis=-1))
        prompt_weight = (prompt_exp / total[..., None]).astype(jnp.bfloat16)
        own_weight = (own_exp / total[..., None]).astype(jnp.bfloat16)
        attended = jnp.einsum('tkgl,kld->tkgd', prompt_weight.astype(jnp.float32), block[..., HD:], precision=precise)
        attended = attended + jnp.einsum('tkgu,ukd->tkgd', own_weight.astype(jnp.float32), fresh[:, 1], precision=precise)
        return (jnp.stack(mixed), attended.astype(jnp.bfloat16).reshape(STEPS, QH * HD))
    mixer_out, attention_out = lax.map(one_row, (request, step_x, step_b, step_c, step_dt, queries, fresh_cache))
    return (prompt_out, mixer_out, attention_out)
```

```python
import functools
import math

import jax
import jax.numpy as jnp
from jax import lax
from jax.experimental import pallas as pl
from jax.experimental.pallas import tpu as pltpu
from jax.sharding import PartitionSpec as P

NS = 256
HP = 64
HPG = 32
KVH = 8
HD = 128
PAGE = 16
LANES = 128
SUB = 8
HALF = 512
LEVELS = (128, 64, 32, 16)
LOG2E = math.log2(math.e)
SCORE = LOG2E / math.sqrt(HD)
NONE = -1e30
FLOOR = -1e29
EARLY = 2
VMEM_LIMIT = 40 * 1024 * 1024

f32 = jnp.float32
bf16 = jnp.bfloat16


def iota(shape, dim):
    return lax.broadcasted_iota(jnp.int32, shape, dim)


def dot_nt(left, right):
    return lax.dot_general(left, right, (((1,), (1,)), ((), ())), preferred_element_type=f32)


def stack_rows(source, held):
    rows, steps = source.shape[0], source.shape[1]
    held[...] = jnp.zeros_like(held)
    for i in range(rows):
        held[i * steps : (i + 1) * steps, :] = source[i].astype(f32)


def pack_kernel(group, ways, q_ref, c_ref, out_ref, q_held, c_held):
    owners = out_ref.shape[0]
    stack_rows(q_ref, q_held)
    stack_rows(c_ref, c_held)
    span = 2 * HALF
    for v in range(KVH):
        both = jnp.concatenate(
            [q_held[:, v * span : v * span + HALF], q_held[:, v * span + HALF : (v + 1) * span]], axis=0
        ).astype(bf16)
        for way in range(ways):
            out_ref[v * ways + way, :, :HALF] = both
    for e in range(c_ref.shape[2] // NS):
        low = c_held[:, e * NS : e * NS + LANES]
        high = c_held[:, e * NS + LANES : (e + 1) * NS]
        both = jnp.concatenate([low, high], axis=0).astype(bf16)
        for d in range(owners):
            if (d * group) // HPG == e:
                out_ref[d, :, HALF:] = both


def head_factors(first, dt_ref, rate_ref, skip_ref, len_ref, levels, w_in, w_out, w_skip, w_tail):
    group, prompts, length = dt_ref.shape
    row = iota((prompts, length), 0)
    lens = jnp.zeros((prompts, length), jnp.int32)
    for r in range(prompts):
        lens = jnp.where(row == r, len_ref[r], lens)
    valid = iota((prompts, length), 1) < lens
    moved = [jnp.where(valid, dt_ref[h].astype(f32), 0.0) for h in range(group)]
    every = jnp.concatenate(moved, axis=0).astype(bf16)
    j = iota((length, length), 0)
    i = iota((length, length), 1)
    rates = [rate_ref[first + h] * LOG2E for h in range(group)]
    if w_tail is not None:
        after = jnp.where(j > i, 1.0, 0.0).astype(bf16)
        total = jnp.dot(every, after, preferred_element_type=f32)
        for h in range(group):
            part = total[h * prompts : (h + 1) * prompts]
            w_tail[:, h, :] = jnp.exp2(-(rates[h] * part)) * moved[h]
    if not levels:
        return
    for h in range(group):
        w_skip[:, h, :] = jnp.where(valid, skip_ref[first + h], 0.0)
    for l, n in enumerate(levels):
        middle = (i // (2 * n)) * (2 * n) + (n - 1)
        signs = (jnp.where(j <= i, 1.0, 0.0) - jnp.where(j <= middle, 1.0, 0.0)).astype(bf16)
        total = jnp.dot(every, signs, preferred_element_type=f32)
        for h in range(group):
            gap = rates[h] * total[h * prompts : (h + 1) * prompts]
            if n == LEVELS[-1]:
                up, down = jnp.exp2(gap), jnp.exp2(-gap)
            else:
                up, down = jnp.exp2(jnp.minimum(gap, 0.0)), jnp.exp2(-jnp.maximum(gap, 0.0))
            w_in[l, :, h, :] = up * moved[h]
            w_out[l, :, h, :] = jnp.where(valid, down, 0.0)


def level_masks(masks):
    length = masks.shape[-1]
    j = iota((length, length), 0)
    i = iota((length, length), 1)
    for l, n in enumerate(LEVELS):
        same = (j // (2 * n)) == (i // (2 * n))
        if n == LEVELS[-1]:
            keep = same & (j <= i)
        else:
            keep = same & ((j % (2 * n)) < n) & ((i % (2 * n)) >= n)
        masks[l] = jnp.where(keep, 1.0, 0.0).astype(bf16)


def prompt_result(r, x_held, b_held, c_held, w_in, w_out, w_skip, masks, out_held):
    width, length = x_held.shape[1], x_held.shape[2]
    group = width // HP
    half = length // 2
    inputs = x_held[r].astype(f32).reshape(group, HP, length)
    scores = dot_nt(b_held[r], c_held[r]).astype(bf16)
    total = inputs * w_skip[r][:, None, :]
    left, right = total[..., :half], total[..., half:]
    for l, n in enumerate(LEVELS):
        if 2 * n == length:
            scaled = (inputs[..., :half] * w_in[l, r][:, None, :half]).astype(bf16).reshape(width, half)
            added = jnp.dot(scaled, scores[:half, half:], preferred_element_type=f32)
            right = right + added.reshape(group, HP, half) * w_out[l, r][:, None, half:]
        else:
            scaled = (inputs * w_in[l, r][:, None, :]).astype(bf16).reshape(width, length)
            added = jnp.dot(scaled, scores * masks[l], preferred_element_type=f32)
            added = added.reshape(group, HP, length) * w_out[l, r][:, None, :]
            left = left + added[..., :half]
            right = right + added[..., half:]
    out_held[r] = jnp.concatenate([left, right], axis=-1).reshape(width, length).astype(bf16)


def state_kernel(
    rate_ref,
    skip_ref,
    len_ref,
    owner_ref,
    table_ref,
    slot_ref,
    dt_ref,
    x_any,
    b_any,
    c_any,
    state_ref,
    tag_ref,
    req_ref,
    out_any,
    x_held,
    b_held,
    c_held,
    out_held,
    w_in,
    w_out,
    w_skip,
    w_tail,
    masks,
    x_sem,
    b_sem,
    c_sem,
    out_sem,
):
    group, prompts, length = dt_ref.shape
    me = lax.axis_index("heads")
    first = me * group
    column = pl.multiple_of((first // HPG) * NS, NS)

    def x_copy(r):
        return pltpu.make_async_copy(x_any.at[r], x_held.at[r], x_sem.at[r])

    def b_copy(r):
        return pltpu.make_async_copy(b_any.at[r, :, pl.ds(column, NS)], b_held.at[r], b_sem.at[r])

    def c_copy(r):
        return pltpu.make_async_copy(c_any.at[r, :, pl.ds(column, NS)], c_held.at[r], c_sem.at[r])

    def out_copy(r):
        return pltpu.make_async_copy(out_held.at[r], out_any.at[r], out_sem.at[r])

    for r in range(prompts):
        x_copy(r).start()
        b_copy(r).start()
    for r in range(EARLY):
        c_copy(r).start()

    head_factors(
        first, dt_ref, rate_ref, skip_ref, len_ref, LEVELS if EARLY else (), w_in, w_out, w_skip, w_tail
    )

    spread = table_ref.shape[1] // owner_ref.shape[0]
    key_page = iota((SUB, LANES), 0) * (LANES // PAGE) + iota((SUB, LANES), 1) // PAGE
    key_offset = iota((SUB, LANES), 1) % PAGE
    tag = jnp.full((SUB, LANES), -1, jnp.int32)
    per_head = table_ref.shape[1] // KVH
    for r in range(prompts):
        for page in range(spread):
            entry = me * spread + page
            row = table_ref[r, entry] - me * (prompts * spread)
            begin = lax.rem(entry, per_head) * PAGE
            inside = (key_page == row) & (key_offset < len_ref[r] - begin)
            tag = jnp.where(inside, r, tag)
    tag_ref[...] = tag

    owners = owner_ref.shape[0]
    rows_dev = slot_ref.shape[0] // owners
    steps = 3
    inner = iota((2 * SUB, LANES), 0) % SUB

    def fill(s, _):
        block = jnp.full((2 * SUB, LANES), -2, jnp.int32)
        for i in range(rows_dev):
            target = owner_ref[s, slot_ref[s * rows_dev + i]]
            block = jnp.where((inner >= i * steps) & (inner < (i + 1) * steps), target, block)
        req_ref[pl.ds(pl.multiple_of(s * 2 * SUB, 2 * SUB), 2 * SUB), :] = block
        return 0

    lax.fori_loop(0, owners, fill, 0)

    def one(r, _):
        x_copy(r).wait()
        b_copy(r).wait()
        width = x_held.shape[1]
        inputs = x_held[r].astype(f32).reshape(group, HP, length)
        scaled = (inputs * w_tail[r][:, None, :]).astype(bf16).reshape(width, length)
        state_ref[r] = jnp.dot(scaled, b_held[r], preferred_element_type=f32).astype(bf16)
        return 0

    lax.fori_loop(0, prompts, one, 0)

    if EARLY:
        level_masks(masks)

        def early(r, _):
            c_copy(r).wait()
            prompt_result(r, x_held, b_held, c_held, w_in, w_out, w_skip, masks, out_held)
            out_copy(r).start()
            return 0

        lax.fori_loop(0, EARLY, early, 0)
        for r in range(EARLY):
            out_copy(r).wait()


def serve_kernel(recv_ref, pages_ref, tag_ref, req_ref, state_ref, out_ref, bias):
    rows = recv_ref.shape[0]
    keys = pages_ref.shape[0]
    prompts, width = state_ref.shape[0], state_ref.shape[1]
    tag = tag_ref[...]
    for b in range(keys // LANES):
        mine = jnp.broadcast_to(tag[b : b + 1, :], (rows, LANES))
        bias[:, b * LANES : (b + 1) * LANES] = jnp.where(req_ref[...] == mine, 0.0, NONE)
    lane = iota((rows, LANES), 1)
    sums = jnp.zeros((rows, LANES), f32)
    for g in range(HALF // HD):
        scores = dot_nt(recv_ref[:, g * HD : (g + 1) * HD], pages_ref[:, :HD]) * SCORE + bias[...]
        highest = jnp.maximum(jnp.max(scores, axis=1, keepdims=True), FLOOR)
        weight = jnp.exp2(scores - highest)
        total = jnp.sum(weight, axis=1, keepdims=True)
        value = jnp.dot(weight.astype(bf16), pages_ref[:, HD:], preferred_element_type=f32)
        some = total > 0.0
        safe = jnp.where(some, total, 1.0)
        out_ref[:, g * HD : (g + 1) * HD] = (value / safe).astype(bf16)
        sums = jnp.where(lane % 4 == g, highest + jnp.log2(safe), sums)
    high = sums.astype(bf16)
    rest = sums - high.astype(f32)
    middle = rest.astype(bf16)
    low = rest - middle.astype(f32)
    third = lane // 4
    pieces = jnp.where(third == 0, high.astype(f32), jnp.where(third == 1, middle.astype(f32), low))
    held = projected_columns(width)
    out_ref[:, HALF + held :] = pieces.astype(bf16)

    blocks = rows // (2 * SUB)
    ahead = recv_ref[:, HALF:].astype(f32).reshape(blocks, 2, SUB, LANES)
    readout = jnp.concatenate([ahead[:, 0], ahead[:, 1]], axis=-1).reshape(blocks * SUB, NS)
    target = req_ref[...].reshape(blocks, 2, SUB, LANES)[:, 0].reshape(blocks * SUB, LANES)
    target = jnp.concatenate([target, target], axis=-1)
    found = jnp.zeros((blocks * SUB, width), f32)
    for r in range(prompts):
        picked = jnp.where(target == r, readout, 0.0).astype(bf16)
        found = found + dot_nt(picked, state_ref[r])
    if width == 2 * held:
        found = found.reshape(blocks, SUB, width)
        both = jnp.stack([found[..., :held], found[..., held:]], axis=1)
    else:
        found = jnp.concatenate([found, jnp.zeros((blocks * SUB, held - width), f32)], axis=-1)
        found = found.reshape(blocks, SUB, held)
        both = jnp.stack([found, found], axis=1)
    out_ref[:, HALF : HALF + held] = both.reshape(rows, held).astype(bf16)


def projected_columns(width):
    return max(LANES, width // 2)


def prompt_kernel(
    rate_ref,
    skip_ref,
    len_ref,
    dt_ref,
    rates_ref,
    skips_ref,
    send_ref,
    fresh_ref,
    sx_ref,
    sb_ref,
    sc_ref,
    sdt_ref,
    x_any,
    b_any,
    c_any,
    after_any,
    early_any,
    out_any,
    own_ref,
    ownsum_ref,
    fade_ref,
    local_ref,
    x_held,
    b_held,
    c_held,
    out_held,
    w_in,
    w_out,
    w_skip,
    masks,
    fresh_held,
    c_rows,
    x_rows,
    x_sem,
    b_sem,
    c_sem,
    out_sem,
):
    group, prompts, length = dt_ref.shape
    me = lax.axis_index("heads")
    first = me * group
    column = pl.multiple_of((first // HPG) * NS, NS)

    def x_copy(r):
        return pltpu.make_async_copy(x_any.at[r], x_held.at[r], x_sem.at[r])

    def b_copy(r):
        return pltpu.make_async_copy(b_any.at[r, :, pl.ds(column, NS)], b_held.at[r], b_sem.at[r])

    def c_copy(r):
        return pltpu.make_async_copy(c_any.at[r, :, pl.ds(column, NS)], c_held.at[r], c_sem.at[r])

    def out_copy(r):
        return pltpu.make_async_copy(out_held.at[r], out_any.at[r], out_sem.at[r])

    for r in range(EARLY, prompts):
        x_copy(r).start()
        b_copy(r).start()
        c_copy(r).start()

    head_factors(first, dt_ref, rate_ref, skip_ref, len_ref, LEVELS, w_in, w_out, w_skip, None)
    level_masks(masks)

    def one(r, _):
        x_copy(r).wait()
        b_copy(r).wait()
        c_copy(r).wait()
        prompt_result(r, x_held, b_held, c_held, w_in, w_out, w_skip, masks, out_held)
        out_copy(r).start()
        return 0

    lax.fori_loop(EARLY, prompts, one, 0)
    own_attention(send_ref, fresh_ref, fresh_held, own_ref, ownsum_ref)
    own_mixer(rates_ref, skips_ref, sx_ref, sb_ref, sc_ref, sdt_ref, c_rows, x_rows, fade_ref, local_ref)
    for r in range(EARLY, prompts):
        out_copy(r).wait()


def own_attention(send_ref, fresh_ref, fresh_held, own_ref, ownsum_ref):
    rows, steps = fresh_ref.shape[0], fresh_ref.shape[1]
    ways = send_ref.shape[0] // KVH
    stack_rows(fresh_ref, fresh_held)
    count = HALF // HD * 2 * SUB
    pair = iota((count, SUB), 0) % SUB
    key = iota((count, SUB), 1)
    seen = (key // steps == pair // steps) & (key <= pair) & (key < rows * steps)
    seen = seen | ((pair >= rows * steps) & (key == 0))
    for v in range(KVH):
        block = send_ref[v * ways]
        query = jnp.concatenate([block[:, g * HD : (g + 1) * HD] for g in range(HALF // HD)], axis=0)
        keys = fresh_held[:, v * HD : (v + 1) * HD].astype(bf16)
        values = fresh_held[:, (KVH + v) * HD : (KVH + v + 1) * HD].astype(bf16)
        scores = jnp.where(seen, dot_nt(query, keys) * SCORE, NONE)
        highest = jnp.max(scores, axis=1, keepdims=True)
        weight = jnp.exp2(scores - highest)
        total = jnp.sum(weight, axis=1, keepdims=True)
        weight = (weight / total).astype(bf16)
        own_ref[v] = jnp.dot(weight, values, preferred_element_type=f32)
        ownsum_ref[v] = jnp.broadcast_to(highest + jnp.log2(total), (count, HD))


def own_mixer(rates_ref, skips_ref, sx_ref, sb_ref, sc_ref, sdt_ref, c_rows, x_rows, fade_ref, local_ref):
    rows, steps, heads = sdt_ref.shape
    stack_rows(sc_ref, c_rows)
    for u in range(steps):
        x_rows[u] = jnp.zeros(x_rows.shape[1:], f32)
        for i in range(rows):
            x_rows[u, i * steps : (i + 1) * steps, :] = jnp.broadcast_to(
                sx_ref[i, u : u + 1, :].astype(f32), (steps, x_rows.shape[2])
            )
    pair = iota((SUB, heads), 0)
    step = pair % steps
    live = pair < rows * steps
    head = iota((SUB, heads), 1)

    def spread_rows(ref, u):
        picked = jnp.broadcast_to(ref[0, u : u + 1, :].astype(f32), (SUB, ref.shape[2]))
        which = iota(picked.shape, 0) // steps
        for i in range(1, rows):
            other = jnp.broadcast_to(ref[i, u : u + 1, :].astype(f32), (SUB, ref.shape[2]))
            picked = jnp.where(which == i, other, picked)
        return picked

    rates = jnp.broadcast_to(rates_ref[...], (SUB, heads)) * LOG2E
    skips = jnp.broadcast_to(skips_ref[...], (SUB, heads))
    moved = [spread_rows(sdt_ref, u) for u in range(steps)]
    kept = [jnp.where(u <= step, moved[u], 0.0) for u in range(steps)]
    parts = [jnp.where(live, jnp.exp2(-(rates * sum(kept))), 0.0)]
    for u in range(steps):
        products = c_rows[...] * spread_rows(sb_ref, u)
        inner = jnp.zeros((SUB, heads), f32)
        for e in range(products.shape[1] // NS):
            found = jnp.sum(products[:, e * NS : (e + 1) * NS], axis=1, keepdims=True)
            inner = jnp.where(head // HPG == e, found, inner)
        gap = jnp.zeros((SUB, heads), f32)
        for t in range(u + 1, steps):
            gap = gap + kept[t]
        weight = jnp.where(u <= step, jnp.exp2(-(rates * gap)) * moved[u] * inner, 0.0)
        weight = weight + jnp.where(u == step, skips, 0.0)
        parts.append(jnp.where(live, weight, 0.0))
    stacked = jnp.concatenate(parts, axis=0)
    high = stacked.astype(bf16)
    low = (stacked - high.astype(f32)).astype(bf16)
    both = jnp.concatenate([high.astype(f32), low.astype(f32)], axis=0)
    count = stacked.shape[0]
    chunk = SUB * HP
    widen = jnp.where(iota((heads, chunk), 0) % SUB == iota((heads, chunk), 1) // HP, 1.0, 0.0).astype(bf16)
    lane = iota(both.shape, 1)
    for d in range(heads // SUB):
        picked = jnp.where(lane // SUB == d, both, 0.0).astype(bf16)
        wide = jnp.dot(picked, widen, preferred_element_type=f32)
        wide = wide[:count] + wide[count:]
        columns = slice(d * chunk, (d + 1) * chunk)
        fade_ref[:, columns] = wide[:SUB]
        value = jnp.zeros((SUB, chunk), f32)
        for u in range(steps):
            value = value + wide[(u + 1) * SUB : (u + 2) * SUB] * x_rows[u, :, columns]
        local_ref[:, columns] = value


def merge_kernel(
    width, back_ref, own_ref, ownsum_ref, fade_ref, local_ref, mixer_ref, attention_ref, mixed, attended
):
    owners = back_ref.shape[0]
    ways = owners // KVH
    held = projected_columns(width)
    rows, steps = mixer_ref.shape[0], mixer_ref.shape[1]
    if width == 2 * held:
        for d in range(owners):
            for half in range(2):
                columns = slice(d * width + half * held, d * width + (half + 1) * held)
                found = back_ref[d, :, HALF : HALF + held].astype(f32)[half * SUB : (half + 1) * SUB]
                mixed[:, columns] = found * fade_ref[:, columns] + local_ref[:, columns]
    else:
        many = LANES // width
        for d in range(0, owners, many):
            found = jnp.concatenate(
                [back_ref[d + n, :, HALF : HALF + held].astype(f32)[:SUB, :width] for n in range(many)], axis=-1
            )
            columns = slice(d * width, (d + many) * width)
            mixed[:, columns] = found * fade_ref[:, columns] + local_ref[:, columns]
    for i in range(rows):
        mixer_ref[i] = mixed[i * steps : (i + 1) * steps, :].astype(bf16)
    for v in range(KVH):
        sums = []
        for way in range(ways):
            pieces = back_ref[v * ways + way, :, HALF + held :].astype(f32)
            sums.append(pieces[:, 0:4] + (pieces[:, 4:8] + pieces[:, 8:12]))
        for g in range(HALF // HD):
            mine = slice(g * 2 * SUB, (g + 1) * 2 * SUB)
            own_sum = ownsum_ref[v, mine, :]
            wide = [jnp.broadcast_to(one[:, g : g + 1], (2 * SUB, HD)) for one in sums]
            highest = functools.reduce(jnp.maximum, wide, own_sum)
            weight = jnp.exp2(own_sum - highest)
            total = weight
            value = weight * own_ref[v, mine, :]
            for way in range(ways):
                weight = jnp.exp2(wide[way] - highest)
                total = total + weight
                value = value + weight * back_ref[v * ways + way, :, g * HD : (g + 1) * HD].astype(f32)
            value = value / total
            start = v * 2 * HALF + g * HD
            attended[:, start : start + HD] = value[:SUB]
            attended[:, start + HALF : start + HALF + HD] = value[SUB:]
    for i in range(rows):
        attention_ref[i] = attended[i * steps : (i + 1) * steps, :].astype(bf16)


def call(kernel, out_shape, in_spaces, out_spaces, scratch, cost, aliases=None):
    def spec(space):
        return pl.BlockSpec(memory_space=space)

    return pl.pallas_call(
        kernel,
        out_shape=out_shape,
        in_specs=[spec(space) for space in in_spaces],
        out_specs=jax.tree.map(spec, out_spaces),
        scratch_shapes=scratch,
        input_output_aliases=aliases or {},
        compiler_params=pltpu.CompilerParams(vmem_limit_bytes=VMEM_LIMIT),
        cost_estimate=pl.CostEstimate(flops=cost[0], bytes_accessed=cost[1], transcendentals=0),
    )


def on_device(
    prompt_x,
    prompt_b,
    prompt_c,
    prompt_dt,
    decay_rate,
    skip_gain,
    lengths,
    owner_list,
    page_table,
    cache_pages,
    row_slot,
    step_x,
    step_b,
    step_c,
    step_dt,
    queries,
    fresh_cache,
):
    owners = lax.axis_size("heads")
    ways = owners // KVH
    group, prompts, length = prompt_dt.shape
    width = prompt_x.shape[1]
    keys = cache_pages.shape[0] * PAGE
    rows, steps = step_x.shape[0], step_x.shape[1]
    held = projected_columns(width)
    all_rows = owners * 2 * SUB
    shape = jax.ShapeDtypeStruct
    smem, vmem, anywhere = pltpu.SMEM, pltpu.VMEM, pl.ANY
    sem = pltpu.SemaphoreType.DMA((prompts,))
    levels = len(LEVELS)

    send = call(
        functools.partial(pack_kernel, group, ways),
        shape((owners, 2 * SUB, HALF + LANES), bf16),
        [vmem, vmem],
        vmem,
        [vmem((SUB, queries.shape[2]), f32), vmem((SUB, step_c.shape[2]), f32)],
        (0, 1 << 19),
    )(queries, step_c)
    recv = lax.all_to_all(send, "heads", split_axis=0, concat_axis=0, tiled=True)

    block = [
        vmem((prompts, width, length), bf16),
        vmem((prompts, length, NS), bf16),
        vmem((prompts, length, NS), bf16),
        vmem((prompts, width, length), bf16),
        vmem((levels, prompts, group, length), f32),
        vmem((levels, prompts, group, length), f32),
        vmem((prompts, group, length), f32),
    ]
    masks = vmem((levels, length, length), bf16)
    work = 2 * width * length * NS
    states, tag, requests, early_out = call(
        state_kernel,
        (
            shape((prompts, width, NS), bf16),
            shape((SUB, LANES), jnp.int32),
            shape((all_rows, LANES), jnp.int32),
            shape(prompt_x.shape, bf16),
        ),
        [smem] * 6 + [vmem] + [anywhere] * 3,
        (vmem, vmem, vmem, anywhere),
        block + [vmem((prompts, group, length), f32), masks, sem, sem, sem, sem],
        (work * (prompts + 5 * EARLY), 6 << 20),
    )(
        decay_rate,
        skip_gain,
        lengths,
        owner_list,
        page_table,
        row_slot,
        prompt_dt,
        prompt_x,
        prompt_b,
        prompt_c,
    )

    back = call(
        serve_kernel,
        shape((all_rows, HALF + held + LANES), bf16),
        [vmem] * 5,
        vmem,
        [vmem((all_rows, keys), f32)],
        (8 * all_rows * keys * HD, 4 << 20),
    )(
        recv.reshape(all_rows, HALF + LANES),
        cache_pages.reshape(keys, 2 * HD),
        tag,
        requests,
        states,
    )
    returned = lax.all_to_all(
        back.reshape(owners, 2 * SUB, back.shape[1]), "heads", split_axis=0, concat_axis=0, tiled=True
    )

    count = HALF // HD * 2 * SUB
    channels = step_x.shape[2]
    prompt_out, own, own_sum, fade, local = call(
        prompt_kernel,
        (
            shape(prompt_x.shape, bf16),
            shape((KVH, count, HD), f32),
            shape((KVH, count, HD), f32),
            shape((SUB, channels), f32),
            shape((SUB, channels), f32),
        ),
        [smem] * 3 + [vmem] * 9 + [anywhere] * 5,
        (anywhere, vmem, vmem, vmem, vmem),
        block
        + [
            masks,
            vmem((SUB, fresh_cache.shape[2]), f32),
            vmem((SUB, step_c.shape[2]), f32),
            vmem((steps, SUB, channels), f32),
            sem,
            sem,
            sem,
            sem,
        ],
        (work * 5 * (prompts - EARLY), 8 << 20),
        {16: 0},
    )(
        decay_rate,
        skip_gain,
        lengths,
        prompt_dt,
        decay_rate.reshape(1, -1),
        skip_gain.reshape(1, -1),
        send,
        fresh_cache,
        step_x,
        step_b,
        step_c,
        step_dt,
        prompt_x,
        prompt_b,
        prompt_c,
        back,
        early_out,
    )

    mixer_out, attention_out = call(
        functools.partial(merge_kernel, width),
        (shape(step_x.shape, bf16), shape(queries.shape, bf16)),
        [vmem] * 5,
        (vmem, vmem),
        [vmem((SUB, channels), f32), vmem((SUB, queries.shape[2]), f32)],
        (0, 2 << 20),
    )(returned, own, own_sum, fade, local)
    return (prompt_out, mixer_out, attention_out)


def solution(mesh):
    in_specs = (
        P("groups", "heads", None),
        P("groups", None, None),
        P("groups", None, None),
        P("heads", "groups", None),
        P(),
        P(),
        P("groups"),
        P("groups", None),
        P("groups", None),
        P(("groups", "heads"), None, None),
        P("groups"),
        P(("groups", "heads"), None, None),
        P(("groups", "heads"), None, None),
        P(("groups", "heads"), None, None),
        P(("groups", "heads"), None, None),
        P(("groups", "heads"), None, None),
        P(("groups", "heads"), None, None),
    )
    out_specs = (
        P("groups", "heads", None),
        P(("groups", "heads"), None, None),
        P(("groups", "heads"), None, None),
    )
    return jax.shard_map(
        on_device, mesh=mesh, in_specs=in_specs, out_specs=out_specs, check_vma=False
    )
```

```python
import functools
import math

import jax
import jax.numpy as jnp
from jax import lax
from jax.experimental import pallas as pl
from jax.experimental.pallas import tpu as pltpu
from jax.sharding import PartitionSpec as P

NS = 256
HP = 64
HPG = 32
KVH = 8
HD = 128
PAGE = 16
LANES = 128
SUB = 8
HALF = 512
LEVELS = (128, 64, 32, 16)
LOG2E = math.log2(math.e)
SCORE = LOG2E / math.sqrt(HD)
NONE = -1e30
FLOOR = -1e29
EARLY = 2
VMEM_LIMIT = 64 * 1024 * 1024

f32 = jnp.float32
bf16 = jnp.bfloat16


def iota(shape, dim):
    return lax.broadcasted_iota(jnp.int32, shape, dim)


def dot_nt(left, right):
    return lax.dot_general(left, right, (((1,), (1,)), ((), ())), preferred_element_type=f32)


def stack_rows(source, held):
    steps, rows = source.shape[0], source.shape[1]
    held[...] = jnp.zeros_like(held)
    for k in range(steps):
        held[k * rows : (k + 1) * rows, :] = source[k].astype(f32)


def fetches(pairs, sems):
    copies = [pltpu.make_async_copy(src, dst, sems.at[n]) for n, (src, dst) in enumerate(pairs)]
    for copy in copies:
        copy.start()
    return copies


def pack_kernel(group, ways, q_any, c_any, out_ref, q_ref, c_ref, q_held, c_held, sems):
    owners = out_ref.shape[0]
    for copy in fetches([(q_any, q_ref), (c_any, c_ref)], sems):
        copy.wait()
    stack_rows(q_ref, q_held)
    stack_rows(c_ref, c_held)
    span = 2 * HALF
    for v in range(KVH):
        both = jnp.concatenate(
            [q_held[:, v * span : v * span + HALF], q_held[:, v * span + HALF : (v + 1) * span]], axis=0
        ).astype(bf16)
        for way in range(ways):
            out_ref[v * ways + way, :, :HALF] = both
    for e in range(c_ref.shape[2] // NS):
        low = c_held[:, e * NS : e * NS + LANES]
        high = c_held[:, e * NS + LANES : (e + 1) * NS]
        both = jnp.concatenate([low, high], axis=0).astype(bf16)
        for d in range(owners):
            if (d * group) // HPG == e:
                out_ref[d, :, HALF:] = both


def head_factors(first, dt_ref, rate_ref, skip_ref, len_ref, levels, w_in, w_out, w_skip, w_tail):
    group, prompts, length = dt_ref.shape
    row = iota((prompts, length), 0)
    lens = jnp.zeros((prompts, length), jnp.int32)
    for r in range(prompts):
        lens = jnp.where(row == r, len_ref[r], lens)
    valid = iota((prompts, length), 1) < lens
    moved = [jnp.where(valid, dt_ref[h].astype(f32), 0.0) for h in range(group)]
    every = jnp.concatenate(moved, axis=0).astype(bf16)
    j = iota((length, length), 0)
    i = iota((length, length), 1)
    rates = [rate_ref[first + h] * LOG2E for h in range(group)]
    if w_tail is not None:
        after = jnp.where(j > i, 1.0, 0.0).astype(bf16)
        total = jnp.dot(every, after, preferred_element_type=f32)
        for h in range(group):
            part = total[h * prompts : (h + 1) * prompts]
            w_tail[:, h, :] = jnp.exp2(-(rates[h] * part)) * moved[h]
    if not levels:
        return
    for h in range(group):
        w_skip[:, h, :] = jnp.where(valid, skip_ref[first + h], 0.0)
    for l, n in enumerate(levels):
        middle = (i // (2 * n)) * (2 * n) + (n - 1)
        signs = (jnp.where(j <= i, 1.0, 0.0) - jnp.where(j <= middle, 1.0, 0.0)).astype(bf16)
        total = jnp.dot(every, signs, preferred_element_type=f32)
        for h in range(group):
            gap = rates[h] * total[h * prompts : (h + 1) * prompts]
            if n == LEVELS[-1]:
                up, down = jnp.exp2(gap), jnp.exp2(-gap)
            else:
                up, down = jnp.exp2(jnp.minimum(gap, 0.0)), jnp.exp2(-jnp.maximum(gap, 0.0))
            w_in[l, :, h, :] = up * moved[h]
            w_out[l, :, h, :] = jnp.where(valid, down, 0.0)


def level_masks(masks):
    length = masks.shape[-1]
    j = iota((length, length), 0)
    i = iota((length, length), 1)
    for l, n in enumerate(LEVELS):
        same = (j // (2 * n)) == (i // (2 * n))
        if n == LEVELS[-1]:
            keep = same & (j <= i)
        else:
            keep = same & ((j % (2 * n)) < n) & ((i % (2 * n)) >= n)
        masks[l] = jnp.where(keep, 1.0, 0.0).astype(bf16)


def prompt_result(r, x_held, b_held, c_held, w_in, w_out, w_skip, masks, out_held):
    width, length = x_held.shape[1], x_held.shape[2]
    group = width // HP
    half = length // 2
    inputs = x_held[r].astype(f32).reshape(group, HP, length)
    scores = dot_nt(b_held[r], c_held[r]).astype(bf16)
    total = inputs * w_skip[r][:, None, :]
    left, right = total[..., :half], total[..., half:]
    for l, n in enumerate(LEVELS):
        if 2 * n == length:
            scaled = (inputs[..., :half] * w_in[l, r][:, None, :half]).astype(bf16).reshape(width, half)
            added = jnp.dot(scaled, scores[:half, half:], preferred_element_type=f32)
            right = right + added.reshape(group, HP, half) * w_out[l, r][:, None, half:]
        else:
            scaled = (inputs * w_in[l, r][:, None, :]).astype(bf16).reshape(width, length)
            added = jnp.dot(scaled, scores * masks[l], preferred_element_type=f32)
            added = added.reshape(group, HP, length) * w_out[l, r][:, None, :]
            left = left + added[..., :half]
            right = right + added[..., half:]
    out_held[r] = jnp.concatenate([left, right], axis=-1).reshape(width, length).astype(bf16)


def state_kernel(
    rate_any,
    skip_any,
    len_any,
    owner_any,
    table_any,
    slot_any,
    dt_any,
    x_any,
    b_any,
    c_any,
    state_any,
    tag_ref,
    req_ref,
    out_any,
    x_held,
    b_held,
    c_held,
    out_held,
    w_in,
    w_out,
    w_skip,
    w_tail,
    masks,
    state_held,
    rate_ref,
    skip_ref,
    len_ref,
    owner_ref,
    table_ref,
    slot_ref,
    dt_ref,
    x_sem,
    b_sem,
    c_sem,
    out_sem,
    state_sem,
    sems,
):
    group, prompts, length = dt_ref.shape
    smalls = fetches(
        [
            (dt_any, dt_ref),
            (rate_any, rate_ref),
            (skip_any, skip_ref),
            (len_any, len_ref),
            (owner_any, owner_ref),
            (table_any, table_ref),
            (slot_any, slot_ref),
        ],
        sems,
    )
    me = lax.axis_index("heads")
    first = me * group
    column = pl.multiple_of((first // HPG) * NS, NS)

    def x_copy(r):
        return pltpu.make_async_copy(x_any.at[r], x_held.at[r], x_sem.at[r])

    def b_copy(r):
        return pltpu.make_async_copy(b_any.at[r, :, pl.ds(column, NS)], b_held.at[r], b_sem.at[r])

    def c_copy(r):
        return pltpu.make_async_copy(c_any.at[r, :, pl.ds(column, NS)], c_held.at[r], c_sem.at[r])

    def out_copy(r):
        return pltpu.make_async_copy(out_held.at[r], out_any.at[r], out_sem.at[r])

    def state_copy(r):
        return pltpu.make_async_copy(state_held.at[r], state_any.at[r], state_sem.at[r])

    for r in range(prompts):
        x_copy(r).start()
        b_copy(r).start()
    for r in range(EARLY):
        c_copy(r).start()
    for copy in smalls:
        copy.wait()

    head_factors(
        first, dt_ref, rate_ref, skip_ref, len_ref, LEVELS if EARLY else (), w_in, w_out, w_skip, w_tail
    )

    spread = table_ref.shape[1] // owner_ref.shape[1]
    key_page = iota((SUB, LANES), 0) * (LANES // PAGE) + iota((SUB, LANES), 1) // PAGE
    key_offset = iota((SUB, LANES), 1) % PAGE
    tag = jnp.full((SUB, LANES), -1, jnp.int32)
    per_head = table_ref.shape[1] // KVH
    for r in range(prompts):
        for page in range(spread):
            entry = me * spread + page
            row = table_ref[r, entry] - me * (prompts * spread)
            begin = lax.rem(entry, per_head) * PAGE
            inside = (key_page == row) & (key_offset < len_ref[r] - begin)
            tag = jnp.where(inside, r, tag)
    tag_ref[...] = tag

    owners = owner_ref.shape[1]
    rows_dev = slot_ref.shape[0] // owners
    inner = iota((2 * SUB, LANES), 0) % SUB

    def fill(s, _):
        block = jnp.full((2 * SUB, LANES), -2, jnp.int32)
        for i in range(rows_dev):
            target = owner_ref[slot_ref[s * rows_dev + i], s]
            block = jnp.where(inner % rows_dev == i, target, block)
        req_ref[pl.ds(pl.multiple_of(s * 2 * SUB, 2 * SUB), 2 * SUB), :] = block
        return 0

    lax.fori_loop(0, owners, fill, 0)

    def one(r, _):
        x_copy(r).wait()
        b_copy(r).wait()
        width = x_held.shape[1]
        inputs = x_held[r].astype(f32).reshape(group, HP, length)
        scaled = (inputs * w_tail[r][:, None, :]).astype(bf16).reshape(width, length)
        state_held[r] = jnp.dot(scaled, b_held[r], preferred_element_type=f32).astype(bf16)
        state_copy(r).start()
        return 0

    lax.fori_loop(0, prompts, one, 0, unroll=2)

    if EARLY:
        level_masks(masks)

        def early(r, _):
            c_copy(r).wait()
            prompt_result(r, x_held, b_held, c_held, w_in, w_out, w_skip, masks, out_held)
            out_copy(r).start()
            return 0

        lax.fori_loop(0, EARLY, early, 0, unroll=2)
        for r in range(EARLY):
            out_copy(r).wait()
    for r in range(prompts):
        state_copy(r).wait()


def serve_kernel(
    recv_any,
    pages_any,
    tag_any,
    req_any,
    state_any,
    out_ref,
    recv_ref,
    pages_ref,
    tag_ref,
    req_ref,
    state_ref,
    bias,
    state_sem,
    sems,
):
    smalls = fetches(
        [(tag_any, tag_ref), (req_any, req_ref), (pages_any, pages_ref), (recv_any, recv_ref)], sems
    )
    states = fetches([(state_any.at[r], state_ref.at[r]) for r in range(state_any.shape[0])], state_sem)
    for copy in smalls:
        copy.wait()
    rows = recv_ref.shape[0]
    keys = pages_ref.shape[0]
    prompts, width = state_ref.shape[0], state_ref.shape[1]
    tag = tag_ref[...]
    for b in range(keys // LANES):
        mine = jnp.broadcast_to(tag[b : b + 1, :], (rows, LANES))
        bias[:, b * LANES : (b + 1) * LANES] = jnp.where(req_ref[...] == mine, 0.0, NONE)
    lane = iota((rows, LANES), 1)
    sums = jnp.zeros((rows, LANES), f32)
    for g in range(HALF // HD):
        scores = dot_nt(recv_ref[:, g * HD : (g + 1) * HD], pages_ref[:, :HD]) * SCORE + bias[...]
        highest = jnp.maximum(jnp.max(scores, axis=1, keepdims=True), FLOOR)
        weight = jnp.exp2(scores - highest)
        total = jnp.sum(weight, axis=1, keepdims=True)
        value = jnp.dot(weight.astype(bf16), pages_ref[:, HD:], preferred_element_type=f32)
        some = total > 0.0
        safe = jnp.where(some, total, 1.0)
        out_ref[:, g * HD : (g + 1) * HD] = (value / safe).astype(bf16)
        sums = jnp.where(lane % 4 == g, highest + jnp.log2(safe), sums)
    high = sums.astype(bf16)
    rest = sums - high.astype(f32)
    middle = rest.astype(bf16)
    low = rest - middle.astype(f32)
    third = lane // 4
    pieces = jnp.where(third == 0, high.astype(f32), jnp.where(third == 1, middle.astype(f32), low))
    held = projected_columns(width)
    out_ref[:, HALF + held :] = pieces.astype(bf16)

    blocks = rows // (2 * SUB)
    ahead = recv_ref[:, HALF:].astype(f32).reshape(blocks, 2, SUB, LANES)
    readout = jnp.concatenate([ahead[:, 0], ahead[:, 1]], axis=-1).reshape(blocks * SUB, NS)
    target = req_ref[...].reshape(blocks, 2, SUB, LANES)[:, 0].reshape(blocks * SUB, LANES)
    target = jnp.concatenate([target, target], axis=-1)
    found = jnp.zeros((blocks * SUB, width), f32)
    for r in range(prompts):
        picked = jnp.where(target == r, readout, 0.0).astype(bf16)
        states[r].wait()
        found = found + dot_nt(picked, state_ref[r])
    if width == 2 * held:
        found = found.reshape(blocks, SUB, width)
        both = jnp.stack([found[..., :held], found[..., held:]], axis=1)
    else:
        found = jnp.concatenate([found, jnp.zeros((blocks * SUB, held - width), f32)], axis=-1)
        found = found.reshape(blocks, SUB, held)
        both = jnp.stack([found, found], axis=1)
    out_ref[:, HALF : HALF + held] = both.reshape(rows, held).astype(bf16)


def projected_columns(width):
    return max(LANES, width // 2)


def prompt_kernel(
    rate_any,
    skip_any,
    len_any,
    dt_any,
    rates_any,
    skips_any,
    send_any,
    fresh_any,
    sx_any,
    sb_any,
    sc_any,
    sdt_any,
    x_any,
    b_any,
    c_any,
    after_any,
    early_any,
    out_any,
    own_ref,
    ownsum_ref,
    fade_ref,
    local_ref,
    x_held,
    b_held,
    c_held,
    out_held,
    w_in,
    w_out,
    w_skip,
    masks,
    fresh_held,
    c_rows,
    x_rows,
    rate_ref,
    skip_ref,
    len_ref,
    dt_ref,
    rates_ref,
    skips_ref,
    send_ref,
    fresh_ref,
    sx_ref,
    sb_ref,
    sc_ref,
    sdt_ref,
    x_sem,
    b_sem,
    c_sem,
    out_sem,
    sems,
):
    group, prompts, length = dt_ref.shape
    smalls = fetches(
        [
            (dt_any, dt_ref),
            (rate_any, rate_ref),
            (skip_any, skip_ref),
            (len_any, len_ref),
            (rates_any, rates_ref),
            (skips_any, skips_ref),
            (send_any, send_ref),
            (fresh_any, fresh_ref),
            (sx_any, sx_ref),
            (sb_any, sb_ref),
            (sc_any, sc_ref),
            (sdt_any, sdt_ref),
        ],
        sems,
    )
    me = lax.axis_index("heads")
    first = me * group
    column = pl.multiple_of((first // HPG) * NS, NS)

    def x_copy(r):
        return pltpu.make_async_copy(x_any.at[r], x_held.at[r], x_sem.at[r])

    def b_copy(r):
        return pltpu.make_async_copy(b_any.at[r, :, pl.ds(column, NS)], b_held.at[r], b_sem.at[r])

    def c_copy(r):
        return pltpu.make_async_copy(c_any.at[r, :, pl.ds(column, NS)], c_held.at[r], c_sem.at[r])

    def out_copy(r):
        return pltpu.make_async_copy(out_held.at[r], out_any.at[r], out_sem.at[r])

    for r in range(EARLY, prompts):
        x_copy(r).start()
        b_copy(r).start()
        c_copy(r).start()
    for copy in smalls:
        copy.wait()

    head_factors(first, dt_ref, rate_ref, skip_ref, len_ref, LEVELS, w_in, w_out, w_skip, None)
    level_masks(masks)

    def one(r, _):
        x_copy(r).wait()
        b_copy(r).wait()
        c_copy(r).wait()
        prompt_result(r, x_held, b_held, c_held, w_in, w_out, w_skip, masks, out_held)
        out_copy(r).start()
        return 0

    lax.fori_loop(EARLY, prompts, one, 0, unroll=2)
    own_attention(send_ref, fresh_ref, fresh_held, own_ref, ownsum_ref)
    own_mixer(rates_ref, skips_ref, sx_ref, sb_ref, sc_ref, sdt_ref, c_rows, x_rows, fade_ref, local_ref)
    for r in range(EARLY, prompts):
        out_copy(r).wait()


def own_attention(send_ref, fresh_ref, fresh_held, own_ref, ownsum_ref):
    steps, rows = fresh_ref.shape[0], fresh_ref.shape[1]
    ways = send_ref.shape[0] // KVH
    stack_rows(fresh_ref, fresh_held)
    count = HALF // HD * 2 * SUB
    pair = iota((count, SUB), 0) % SUB
    key = iota((count, SUB), 1)
    seen = (key % rows == pair % rows) & (key <= pair) & (key < rows * steps)
    seen = seen | ((pair >= rows * steps) & (key == 0))
    for v in range(KVH):
        block = send_ref[v * ways]
        query = jnp.concatenate([block[:, g * HD : (g + 1) * HD] for g in range(HALF // HD)], axis=0)
        keys = fresh_held[:, v * HD : (v + 1) * HD].astype(bf16)
        values = fresh_held[:, (KVH + v) * HD : (KVH + v + 1) * HD].astype(bf16)
        scores = jnp.where(seen, dot_nt(query, keys) * SCORE, NONE)
        highest = jnp.max(scores, axis=1, keepdims=True)
        weight = jnp.exp2(scores - highest)
        total = jnp.sum(weight, axis=1, keepdims=True)
        weight = (weight / total).astype(bf16)
        own_ref[v] = jnp.dot(weight, values, preferred_element_type=f32)
        ownsum_ref[v] = jnp.broadcast_to(highest + jnp.log2(total), (count, HD))


def own_mixer(rates_ref, skips_ref, sx_ref, sb_ref, sc_ref, sdt_ref, c_rows, x_rows, fade_ref, local_ref):
    steps, rows, heads = sdt_ref.shape
    stack_rows(sc_ref, c_rows)
    for u in range(steps):
        given = sx_ref[u].astype(f32)
        for k in range(SUB // rows):
            x_rows[u, k * rows : (k + 1) * rows, :] = given
    pair = iota((SUB, heads), 0)
    step = pair // rows
    live = pair < rows * steps
    head = iota((SUB, heads), 1)

    def spread_rows(ref, u):
        given = ref[u].astype(f32)
        return jnp.concatenate([given] * (SUB // rows), axis=0)

    rates = jnp.broadcast_to(rates_ref[...], (SUB, heads)) * LOG2E
    skips = jnp.broadcast_to(skips_ref[...], (SUB, heads))
    moved = [spread_rows(sdt_ref, u) for u in range(steps)]
    kept = [jnp.where(u <= step, moved[u], 0.0) for u in range(steps)]
    parts = [jnp.where(live, jnp.exp2(-(rates * sum(kept))), 0.0)]
    for u in range(steps):
        products = c_rows[...] * spread_rows(sb_ref, u)
        inner = jnp.zeros((SUB, heads), f32)
        for e in range(products.shape[1] // NS):
            found = jnp.sum(products[:, e * NS : (e + 1) * NS], axis=1, keepdims=True)
            inner = jnp.where(head // HPG == e, found, inner)
        gap = jnp.zeros((SUB, heads), f32)
        for t in range(u + 1, steps):
            gap = gap + kept[t]
        weight = jnp.where(u <= step, jnp.exp2(-(rates * gap)) * moved[u] * inner, 0.0)
        weight = weight + jnp.where(u == step, skips, 0.0)
        parts.append(jnp.where(live, weight, 0.0))
    stacked = jnp.concatenate(parts, axis=0)
    high = stacked.astype(bf16)
    low = (stacked - high.astype(f32)).astype(bf16)
    both = jnp.concatenate([high.astype(f32), low.astype(f32)], axis=0)
    count = stacked.shape[0]
    chunk = SUB * HP
    widen = jnp.where(iota((heads, chunk), 0) % SUB == iota((heads, chunk), 1) // HP, 1.0, 0.0).astype(bf16)
    lane = iota(both.shape, 1)
    for d in range(heads // SUB):
        picked = jnp.where(lane // SUB == d, both, 0.0).astype(bf16)
        wide = jnp.dot(picked, widen, preferred_element_type=f32)
        wide = wide[:count] + wide[count:]
        columns = slice(d * chunk, (d + 1) * chunk)
        fade_ref[:, columns] = wide[:SUB]
        value = jnp.zeros((SUB, chunk), f32)
        for u in range(steps):
            value = value + wide[(u + 1) * SUB : (u + 2) * SUB] * x_rows[u, :, columns]
        local_ref[:, columns] = value


def merge_kernel(
    width,
    back_any,
    own_any,
    ownsum_any,
    fade_any,
    local_any,
    mixer_ref,
    attention_ref,
    back_ref,
    own_ref,
    ownsum_ref,
    fade_ref,
    local_ref,
    mixed,
    attended,
    sems,
):
    copies = fetches(
        [
            (back_any, back_ref),
            (own_any, own_ref),
            (ownsum_any, ownsum_ref),
            (fade_any, fade_ref),
            (local_any, local_ref),
        ],
        sems,
    )
    for copy in copies:
        copy.wait()
    owners = back_ref.shape[0]
    ways = owners // KVH
    held = projected_columns(width)
    steps, rows = mixer_ref.shape[0], mixer_ref.shape[1]
    if width == 2 * held:
        for d in range(owners):
            for half in range(2):
                columns = slice(d * width + half * held, d * width + (half + 1) * held)
                found = back_ref[d, :, HALF : HALF + held].astype(f32)[half * SUB : (half + 1) * SUB]
                mixed[:, columns] = found * fade_ref[:, columns] + local_ref[:, columns]
    else:
        many = LANES // width
        for d in range(0, owners, many):
            found = jnp.concatenate(
                [back_ref[d + n, :, HALF : HALF + held].astype(f32)[:SUB, :width] for n in range(many)], axis=-1
            )
            columns = slice(d * width, (d + many) * width)
            mixed[:, columns] = found * fade_ref[:, columns] + local_ref[:, columns]
    for k in range(steps):
        mixer_ref[k] = mixed[k * rows : (k + 1) * rows, :].astype(bf16)
    for v in range(KVH):
        sums = []
        for way in range(ways):
            pieces = back_ref[v * ways + way, :, HALF + held :].astype(f32)
            sums.append(pieces[:, 0:4] + (pieces[:, 4:8] + pieces[:, 8:12]))
        for g in range(HALF // HD):
            mine = slice(g * 2 * SUB, (g + 1) * 2 * SUB)
            own_sum = ownsum_ref[v, mine, :]
            wide = [jnp.broadcast_to(one[:, g : g + 1], (2 * SUB, HD)) for one in sums]
            highest = functools.reduce(jnp.maximum, wide, own_sum)
            weight = jnp.exp2(own_sum - highest)
            total = weight
            value = weight * own_ref[v, mine, :]
            for way in range(ways):
                weight = jnp.exp2(wide[way] - highest)
                total = total + weight
                value = value + weight * back_ref[v * ways + way, :, g * HD : (g + 1) * HD].astype(f32)
            value = value / total
            start = v * 2 * HALF + g * HD
            attended[:, start : start + HD] = value[:SUB]
            attended[:, start + HALF : start + HALF + HD] = value[SUB:]
    for k in range(steps):
        attention_ref[k] = attended[k * rows : (k + 1) * rows, :].astype(bf16)


def call(kernel, out_shape, in_spaces, out_spaces, scratch, cost, aliases=None):
    def spec(space):
        return pl.BlockSpec(memory_space=space)

    return pl.pallas_call(
        kernel,
        out_shape=out_shape,
        in_specs=[spec(space) for space in in_spaces],
        out_specs=jax.tree.map(spec, out_spaces),
        scratch_shapes=scratch,
        input_output_aliases=aliases or {},
        compiler_params=pltpu.CompilerParams(vmem_limit_bytes=VMEM_LIMIT),
        cost_estimate=pl.CostEstimate(flops=cost[0], bytes_accessed=cost[1], transcendentals=0),
    )


def on_device(
    prompt_x,
    prompt_b,
    prompt_c,
    prompt_dt,
    decay_rate,
    skip_gain,
    lengths,
    owner_list,
    page_table,
    cache_pages,
    row_slot,
    step_x,
    step_b,
    step_c,
    step_dt,
    queries,
    fresh_cache,
):
    owners = lax.axis_size("heads")
    ways = owners // KVH
    group, prompts, length = prompt_dt.shape
    width = prompt_x.shape[1]
    keys = cache_pages.shape[0] * PAGE
    steps = step_x.shape[1]
    held = projected_columns(width)
    all_rows = owners * 2 * SUB
    shape = jax.ShapeDtypeStruct
    smem, vmem, hbm = pltpu.SMEM, pltpu.VMEM, pltpu.HBM
    sem = pltpu.SemaphoreType.DMA((prompts,))
    levels = len(LEVELS)
    step_x, step_b, step_c, step_dt, queries, fresh_cache = (
        jnp.swapaxes(one, 0, 1) for one in (step_x, step_b, step_c, step_dt, queries, fresh_cache)
    )
    owner_list = owner_list.T

    def like(space, array):
        return space(array.shape, array.dtype)

    def sems(count):
        return pltpu.SemaphoreType.DMA((count,))

    send = call(
        functools.partial(pack_kernel, group, ways),
        shape((owners, 2 * SUB, HALF + LANES), bf16),
        [hbm, hbm],
        vmem,
        [
            like(vmem, queries),
            like(vmem, step_c),
            vmem((SUB, queries.shape[2]), f32),
            vmem((SUB, step_c.shape[2]), f32),
            sems(2),
        ],
        (0, 1 << 19),
    )(queries, step_c)
    recv = lax.all_to_all(send, "heads", split_axis=0, concat_axis=0, tiled=True)

    block = [
        vmem((prompts, width, length), bf16),
        vmem((prompts, length, NS), bf16),
        vmem((prompts, length, NS), bf16),
        vmem((prompts, width, length), bf16),
        vmem((levels, prompts, group, length), f32),
        vmem((levels, prompts, group, length), f32),
        vmem((prompts, group, length), f32),
    ]
    masks = vmem((levels, length, length), bf16)
    work = 2 * width * length * NS
    states, tag, requests, early_out = call(
        state_kernel,
        (
            shape((prompts, width, NS), bf16),
            shape((SUB, LANES), jnp.int32),
            shape((all_rows, LANES), jnp.int32),
            shape(prompt_x.shape, bf16),
        ),
        [hbm] * 10,
        (hbm, vmem, vmem, hbm),
        block
        + [vmem((prompts, group, length), f32), masks, vmem((prompts, width, NS), bf16)]
        + [like(smem, one) for one in (decay_rate, skip_gain, lengths, owner_list, page_table, row_slot)]
        + [like(vmem, prompt_dt), sem, sem, sem, sem, sem, sems(7)],
        (work * (prompts + 5 * EARLY), 6 << 20),
    )(
        decay_rate,
        skip_gain,
        lengths,
        owner_list,
        page_table,
        row_slot,
        prompt_dt,
        prompt_x,
        prompt_b,
        prompt_c,
    )

    back = call(
        serve_kernel,
        shape((all_rows, HALF + held + LANES), bf16),
        [hbm] * 5,
        vmem,
        [
            vmem((all_rows, HALF + LANES), bf16),
            vmem((keys, 2 * HD), bf16),
            like(vmem, tag),
            like(vmem, requests),
            like(vmem, states),
            vmem((all_rows, keys), f32),
            sem,
            sems(4),
        ],
        (8 * all_rows * keys * HD, 4 << 20),
    )(
        recv.reshape(all_rows, HALF + LANES),
        cache_pages.reshape(keys, 2 * HD),
        tag,
        requests,
        states,
    )
    returned = lax.all_to_all(
        back.reshape(owners, 2 * SUB, back.shape[1]), "heads", split_axis=0, concat_axis=0, tiled=True
    )

    count = HALF // HD * 2 * SUB
    channels = step_x.shape[2]
    rates, skips = decay_rate.reshape(1, -1), skip_gain.reshape(1, -1)
    prompt_out, own, own_sum, fade, local = call(
        prompt_kernel,
        (
            shape(prompt_x.shape, bf16),
            shape((KVH, count, HD), f32),
            shape((KVH, count, HD), f32),
            shape((SUB, channels), f32),
            shape((SUB, channels), f32),
        ),
        [hbm] * 17,
        (hbm, vmem, vmem, vmem, vmem),
        block
        + [
            masks,
            vmem((SUB, fresh_cache.shape[2]), f32),
            vmem((SUB, step_c.shape[2]), f32),
            vmem((steps, SUB, channels), f32),
            like(smem, decay_rate),
            like(smem, skip_gain),
            like(smem, lengths),
            like(vmem, prompt_dt),
            like(vmem, rates),
            like(vmem, skips),
            like(vmem, send),
            like(vmem, fresh_cache),
            like(vmem, step_x),
            like(vmem, step_b),
            like(vmem, step_c),
            like(vmem, step_dt),
            sem,
            sem,
            sem,
            sem,
            sems(12),
        ],
        (work * 5 * (prompts - EARLY), 8 << 20),
        {16: 0},
    )(
        decay_rate,
        skip_gain,
        lengths,
        prompt_dt,
        rates,
        skips,
        send,
        fresh_cache,
        step_x,
        step_b,
        step_c,
        step_dt,
        prompt_x,
        prompt_b,
        prompt_c,
        back,
        early_out,
    )

    mixer_out, attention_out = call(
        functools.partial(merge_kernel, width),
        (shape(step_x.shape, bf16), shape(queries.shape, bf16)),
        [hbm] * 5,
        (vmem, vmem),
        [like(vmem, one) for one in (returned, own, own_sum, fade, local)]
        + [vmem((SUB, channels), f32), vmem((SUB, queries.shape[2]), f32), sems(5)],
        (0, 2 << 20),
    )(returned, own, own_sum, fade, local)
    return (prompt_out, jnp.swapaxes(mixer_out, 0, 1), jnp.swapaxes(attention_out, 0, 1))


def solution(mesh):
    in_specs = (
        P("groups", "heads", None),
        P("groups", None, None),
        P("groups", None, None),
        P("heads", "groups", None),
        P(),
        P(),
        P("groups"),
        P("groups", None),
        P("groups", None),
        P(("groups", "heads"), None, None),
        P("groups"),
        P(("groups", "heads"), None, None),
        P(("groups", "heads"), None, None),
        P(("groups", "heads"), None, None),
        P(("groups", "heads"), None, None),
        P(("groups", "heads"), None, None),
        P(("groups", "heads"), None, None),
    )
    out_specs = (
        P("groups", "heads", None),
        P(("groups", "heads"), None, None),
        P(("groups", "heads"), None, None),
    )
    return jax.shard_map(
        on_device, mesh=mesh, in_specs=in_specs, out_specs=out_specs, check_vma=False
    )
```

```python
import functools
import math

import jax
import jax.numpy as jnp
from jax import lax
from jax.experimental import pallas as pl
from jax.experimental.pallas import tpu as pltpu
from jax.sharding import PartitionSpec as P

NS = 256
HP = 64
HPG = 32
KVH = 8
HD = 128
PAGE = 16
LANES = 128
SUB = 8
HALF = 512
LEVELS = (128, 64, 32, 16)
LOG2E = math.log2(math.e)
SCORE = LOG2E / math.sqrt(HD)
NONE = -1e30
FLOOR = -1e29
SUMS_ROW = 6
EARLY = 2
VMEM_LIMIT = 64 * 1024 * 1024

f32 = jnp.float32
bf16 = jnp.bfloat16


def iota(shape, dim):
    return lax.broadcasted_iota(jnp.int32, shape, dim)


def dot_nt(left, right):
    return lax.dot_general(left, right, (((1,), (1,)), ((), ())), preferred_element_type=f32)


def stack_rows(source, held):
    steps, rows = source.shape[0], source.shape[1]
    held[...] = jnp.zeros_like(held)
    for k in range(steps):
        held[k * rows : (k + 1) * rows, :] = source[k].astype(f32)


def fetches(pairs, sems):
    copies = [pltpu.make_async_copy(src, dst, sems.at[n]) for n, (src, dst) in enumerate(pairs)]
    for copy in copies:
        copy.start()
    return copies


def pack_kernel(group, ways, q_any, c_any, out_ref, q_ref, c_ref, q_held, c_held, sems):
    owners = out_ref.shape[0] // SUB
    for copy in fetches([(q_any, q_ref), (c_any, c_ref)], sems):
        copy.wait()
    stack_rows(q_ref, q_held)
    stack_rows(c_ref, c_held)
    span = 2 * HALF
    for d in range(0, owners, 2):
        v, e = d // ways, (d * group) // HPG
        low = q_held[:, v * span : v * span + HALF]
        high = q_held[:, v * span + HALF : (v + 1) * span]
        out_ref[d * SUB : (d + 2) * SUB, :HALF] = jnp.concatenate([low, high], axis=0).astype(bf16)
        readout = c_held[:, e * NS : (e + 1) * NS]
        out_ref[d * SUB : (d + 2) * SUB, HALF:] = jnp.concatenate([readout, readout], axis=0).astype(bf16)


def head_factors(first, dt_ref, rate_ref, skip_ref, len_ref, levels, w_in, w_out, w_skip, w_tail):
    group, prompts, length = dt_ref.shape
    row = iota((prompts, length), 0)
    lens = jnp.zeros((prompts, length), jnp.int32)
    for r in range(prompts):
        lens = jnp.where(row == r, len_ref[r], lens)
    valid = iota((prompts, length), 1) < lens
    moved = [jnp.where(valid, dt_ref[h].astype(f32), 0.0) for h in range(group)]
    every = jnp.concatenate(moved, axis=0).astype(bf16)
    j = iota((length, length), 0)
    i = iota((length, length), 1)
    rates = [rate_ref[first + h] * LOG2E for h in range(group)]
    if w_tail is not None:
        after = jnp.where(j > i, 1.0, 0.0).astype(bf16)
        total = jnp.dot(every, after, preferred_element_type=f32)
        for h in range(group):
            part = total[h * prompts : (h + 1) * prompts]
            w_tail[:, h, :] = jnp.exp2(-(rates[h] * part)) * moved[h]
    if not levels:
        return
    for h in range(group):
        w_skip[:, h, :] = jnp.where(valid, skip_ref[first + h], 0.0)
    for l, n in enumerate(levels):
        middle = (i // (2 * n)) * (2 * n) + (n - 1)
        signs = (jnp.where(j <= i, 1.0, 0.0) - jnp.where(j <= middle, 1.0, 0.0)).astype(bf16)
        total = jnp.dot(every, signs, preferred_element_type=f32)
        for h in range(group):
            gap = rates[h] * total[h * prompts : (h + 1) * prompts]
            if n == LEVELS[-1]:
                up, down = jnp.exp2(gap), jnp.exp2(-gap)
            else:
                up, down = jnp.exp2(jnp.minimum(gap, 0.0)), jnp.exp2(-jnp.maximum(gap, 0.0))
            w_in[l, :, h, :] = up * moved[h]
            w_out[l, :, h, :] = jnp.where(valid, down, 0.0)


def level_masks(masks):
    length = masks.shape[-1]
    j = iota((length, length), 0)
    i = iota((length, length), 1)
    for l, n in enumerate(LEVELS):
        same = (j // (2 * n)) == (i // (2 * n))
        if n == LEVELS[-1]:
            keep = same & (j <= i)
        else:
            keep = same & ((j % (2 * n)) < n) & ((i % (2 * n)) >= n)
        masks[l] = jnp.where(keep, 1.0, 0.0).astype(bf16)


def prompt_result(r, x_held, b_held, c_held, w_in, w_out, w_skip, masks, out_held):
    width, length = x_held.shape[1], x_held.shape[2]
    group = width // HP
    half = length // 2
    inputs = x_held[r].astype(f32).reshape(group, HP, length)
    scores = dot_nt(b_held[r], c_held[r]).astype(bf16)
    total = inputs * w_skip[r][:, None, :]
    left, right = total[..., :half], total[..., half:]
    for l, n in enumerate(LEVELS):
        if 2 * n == length:
            scaled = (inputs[..., :half] * w_in[l, r][:, None, :half]).astype(bf16).reshape(width, half)
            added = jnp.dot(scaled, scores[:half, half:], preferred_element_type=f32)
            right = right + added.reshape(group, HP, half) * w_out[l, r][:, None, half:]
        else:
            scaled = (inputs * w_in[l, r][:, None, :]).astype(bf16).reshape(width, length)
            added = jnp.dot(scaled, scores * masks[l], preferred_element_type=f32)
            added = added.reshape(group, HP, length) * w_out[l, r][:, None, :]
            left = left + added[..., :half]
            right = right + added[..., half:]
    out_held[r] = jnp.concatenate([left, right], axis=-1).reshape(width, length).astype(bf16)


def state_kernel(
    rate_any,
    skip_any,
    len_any,
    owner_any,
    table_any,
    slot_any,
    dt_any,
    x_any,
    b_any,
    c_any,
    state_any,
    tag_ref,
    req_ref,
    out_any,
    x_held,
    b_held,
    c_held,
    out_held,
    w_in,
    w_out,
    w_skip,
    w_tail,
    masks,
    state_held,
    rate_ref,
    skip_ref,
    len_ref,
    owner_ref,
    table_ref,
    slot_ref,
    dt_ref,
    x_sem,
    b_sem,
    c_sem,
    out_sem,
    state_sem,
    sems,
):
    group, prompts, length = dt_ref.shape
    smalls = fetches(
        [
            (dt_any, dt_ref),
            (rate_any, rate_ref),
            (skip_any, skip_ref),
            (len_any, len_ref),
            (owner_any, owner_ref),
            (table_any, table_ref),
            (slot_any, slot_ref),
        ],
        sems,
    )
    me = lax.axis_index("heads")
    first = me * group
    column = pl.multiple_of((first // HPG) * NS, NS)

    def x_copy(r):
        return pltpu.make_async_copy(x_any.at[r], x_held.at[r], x_sem.at[r])

    def b_copy(r):
        return pltpu.make_async_copy(b_any.at[r, :, pl.ds(column, NS)], b_held.at[r], b_sem.at[r])

    def c_copy(r):
        return pltpu.make_async_copy(c_any.at[r, :, pl.ds(column, NS)], c_held.at[r], c_sem.at[r])

    def out_copy(r):
        return pltpu.make_async_copy(out_held.at[r], out_any.at[r], out_sem.at[r])

    def state_copy(r):
        return pltpu.make_async_copy(state_held.at[r], state_any.at[r], state_sem.at[r])

    for r in range(prompts):
        x_copy(r).start()
        b_copy(r).start()
    for r in range(EARLY):
        c_copy(r).start()
    for copy in smalls:
        copy.wait()

    head_factors(
        first, dt_ref, rate_ref, skip_ref, len_ref, LEVELS if EARLY else (), w_in, w_out, w_skip, w_tail
    )

    spread = table_ref.shape[1] // owner_ref.shape[1]
    key_page = iota((SUB, LANES), 0) * (LANES // PAGE) + iota((SUB, LANES), 1) // PAGE
    key_offset = iota((SUB, LANES), 1) % PAGE
    per_head = table_ref.shape[1] // KVH
    for n, holder in enumerate((me, me + 1 - 2 * lax.rem(me, 2))):
        tag = jnp.full((SUB, LANES), -1, jnp.int32)
        for r in range(prompts):
            for page in range(spread):
                entry = holder * spread + page
                row = table_ref[r, entry] - holder * (prompts * spread)
                begin = lax.rem(entry, per_head) * PAGE
                inside = (key_page == row) & (key_offset < len_ref[r] - begin)
                tag = jnp.where(inside, r, tag)
        tag_ref[n] = tag

    owners = owner_ref.shape[1]
    rows_dev = slot_ref.shape[0] // owners
    inner = iota((2 * SUB, LANES), 0)

    def fill(s, _):
        block = jnp.full((2 * SUB, LANES), -2, jnp.int32)
        for n in range(2):
            for i in range(rows_dev):
                target = owner_ref[slot_ref[(2 * s + n) * rows_dev + i], 2 * s + n]
                block = jnp.where((inner // SUB == n) & (inner % rows_dev == i), target, block)
        req_ref[pl.ds(pl.multiple_of(s * 2 * SUB, 2 * SUB), 2 * SUB), :] = block
        return 0

    lax.fori_loop(0, owners // 2, fill, 0)

    def one(r, _):
        x_copy(r).wait()
        b_copy(r).wait()
        width = x_held.shape[1]
        inputs = x_held[r].astype(f32).reshape(group, HP, length)
        scaled = (inputs * w_tail[r][:, None, :]).astype(bf16).reshape(width, length)
        state_held[r] = jnp.dot(scaled, b_held[r], preferred_element_type=f32).astype(bf16)
        state_copy(r).start()
        return 0

    lax.fori_loop(0, prompts, one, 0, unroll=2)

    if EARLY:
        level_masks(masks)

        def early(r, _):
            c_copy(r).wait()
            prompt_result(r, x_held, b_held, c_held, w_in, w_out, w_skip, masks, out_held)
            out_copy(r).start()
            return 0

        lax.fori_loop(0, EARLY, early, 0, unroll=2)
        for r in range(EARLY):
            out_copy(r).wait()
    for r in range(prompts):
        state_copy(r).wait()


def serve_kernel(
    recv_any,
    pages_any,
    other_any,
    tag_any,
    req_any,
    state_any,
    out_ref,
    recv_ref,
    pages_ref,
    tag_ref,
    req_ref,
    state_ref,
    bias,
    state_sem,
    sems,
):
    marks = fetches([(tag_any, tag_ref), (req_any, req_ref)], sems.at[pl.ds(0, 2)])
    smalls = fetches(
        [(recv_any, recv_ref), (pages_any, pages_ref.at[0]), (other_any, pages_ref.at[1])],
        sems.at[pl.ds(2, 3)],
    )
    states = fetches([(state_any.at[r], state_ref.at[r]) for r in range(state_any.shape[0])], state_sem)
    for copy in marks:
        copy.wait()
    rows = recv_ref.shape[0]
    holders, keys = pages_ref.shape[0], pages_ref.shape[1]
    prompts, width = state_ref.shape[0], state_ref.shape[1]
    for n in range(holders):
        tag = tag_ref[n]
        for b in range(keys // LANES):
            mine = jnp.broadcast_to(tag[b : b + 1, :], (rows, LANES))
            bias[n, :, b * LANES : (b + 1) * LANES] = jnp.where(req_ref[...] == mine, 0.0, NONE)
    for copy in smalls:
        copy.wait()
    lane = iota((rows, LANES), 1)
    sums = jnp.zeros((rows, LANES), f32)
    values = []
    for g in range(HALF // HD):
        query = recv_ref[:, g * HD : (g + 1) * HD]
        scores = [dot_nt(query, pages_ref[n, :, :HD]) * SCORE + bias[n] for n in range(holders)]
        highest = jnp.full((rows, 1), FLOOR, f32)
        for one in scores:
            highest = jnp.maximum(highest, jnp.max(one, axis=1, keepdims=True))
        total = jnp.zeros((rows, 1), f32)
        value = jnp.zeros((rows, HD), f32)
        for n in range(holders):
            weight = jnp.exp2(scores[n] - highest)
            total = total + jnp.sum(weight, axis=1, keepdims=True)
            value = value + jnp.dot(weight.astype(bf16), pages_ref[n, :, HD:], preferred_element_type=f32)
        some = total > 0.0
        safe = jnp.where(some, total, 1.0)
        values.append(value / safe)
        sums = jnp.where(lane % 4 == g, highest + jnp.log2(safe), sums)
    high = sums.astype(bf16).astype(f32)
    rest = sums - high
    middle = rest.astype(bf16).astype(f32)
    piece = lane % 16 // 4
    pieces = jnp.where(piece == 0, high, jnp.where(piece == 1, middle, rest - middle))
    pair = iota((rows, LANES), 0) % SUB
    pieces = jnp.where((lane // 16 == pair) & (piece < 3), pieces, 0.0)
    packed = jnp.sum(pieces.reshape(rows // SUB, SUB, LANES), axis=1, keepdims=True)
    packed = jnp.broadcast_to(packed, (rows // SUB, SUB, LANES)).reshape(rows, LANES)
    values[0] = jnp.where(pair == SUMS_ROW, packed, values[0])
    for g in range(HALF // HD):
        out_ref[:, g * HD : (g + 1) * HD] = values[g].astype(bf16)

    readout = recv_ref[:, HALF:].astype(f32)
    target = jnp.concatenate([req_ref[...], req_ref[...]], axis=-1)
    found = jnp.zeros((rows, width), f32)
    for r in range(prompts):
        picked = jnp.where(target == r, readout, 0.0).astype(bf16)
        states[r].wait()
        found = found + dot_nt(picked, state_ref[r])
    if width < LANES:
        found = jnp.concatenate([found, jnp.zeros((rows, LANES - width), f32)], axis=-1)
    out_ref[:, HALF:] = found.astype(bf16)


def prompt_kernel(
    rate_any,
    skip_any,
    len_any,
    dt_any,
    rates_any,
    skips_any,
    send_any,
    fresh_any,
    sx_any,
    sb_any,
    sc_any,
    sdt_any,
    x_any,
    b_any,
    c_any,
    after_any,
    early_any,
    out_any,
    own_ref,
    ownsum_ref,
    fade_ref,
    local_ref,
    x_held,
    b_held,
    c_held,
    out_held,
    w_in,
    w_out,
    w_skip,
    masks,
    fresh_held,
    c_rows,
    x_rows,
    rate_ref,
    skip_ref,
    len_ref,
    dt_ref,
    rates_ref,
    skips_ref,
    send_ref,
    fresh_ref,
    sx_ref,
    sb_ref,
    sc_ref,
    sdt_ref,
    x_sem,
    b_sem,
    c_sem,
    out_sem,
    sems,
):
    group, prompts, length = dt_ref.shape
    smalls = fetches(
        [
            (dt_any, dt_ref),
            (rate_any, rate_ref),
            (skip_any, skip_ref),
            (len_any, len_ref),
            (rates_any, rates_ref),
            (skips_any, skips_ref),
            (send_any, send_ref),
            (fresh_any, fresh_ref),
            (sx_any, sx_ref),
            (sb_any, sb_ref),
            (sc_any, sc_ref),
            (sdt_any, sdt_ref),
        ],
        sems,
    )
    me = lax.axis_index("heads")
    first = me * group
    column = pl.multiple_of((first // HPG) * NS, NS)

    def x_copy(r):
        return pltpu.make_async_copy(x_any.at[r], x_held.at[r], x_sem.at[r])

    def b_copy(r):
        return pltpu.make_async_copy(b_any.at[r, :, pl.ds(column, NS)], b_held.at[r], b_sem.at[r])

    def c_copy(r):
        return pltpu.make_async_copy(c_any.at[r, :, pl.ds(column, NS)], c_held.at[r], c_sem.at[r])

    def out_copy(r):
        return pltpu.make_async_copy(out_held.at[r], out_any.at[r], out_sem.at[r])

    for r in range(EARLY, prompts):
        x_copy(r).start()
        b_copy(r).start()
        c_copy(r).start()
    for copy in smalls:
        copy.wait()

    head_factors(first, dt_ref, rate_ref, skip_ref, len_ref, LEVELS, w_in, w_out, w_skip, None)
    level_masks(masks)

    def one(r, _):
        x_copy(r).wait()
        b_copy(r).wait()
        c_copy(r).wait()
        prompt_result(r, x_held, b_held, c_held, w_in, w_out, w_skip, masks, out_held)
        out_copy(r).start()
        return 0

    lax.fori_loop(EARLY, prompts, one, 0, unroll=2)
    own_attention(send_ref, fresh_ref, fresh_held, own_ref, ownsum_ref)
    own_mixer(rates_ref, skips_ref, sx_ref, sb_ref, sc_ref, sdt_ref, c_rows, x_rows, fade_ref, local_ref)
    for r in range(EARLY, prompts):
        out_copy(r).wait()


def own_attention(send_ref, fresh_ref, fresh_held, own_ref, ownsum_ref):
    steps, rows = fresh_ref.shape[0], fresh_ref.shape[1]
    ways = send_ref.shape[0] // SUB // KVH
    stack_rows(fresh_ref, fresh_held)
    count = HALF // HD * 2 * SUB
    pair = iota((count, SUB), 0) % SUB
    key = iota((count, SUB), 1)
    seen = (key % rows == pair % rows) & (key <= pair) & (key < rows * steps)
    seen = seen | ((pair >= rows * steps) & (key == 0))
    for v in range(KVH):
        block = send_ref[v * ways * SUB : (v * ways + 2) * SUB]
        query = jnp.concatenate([block[:, g * HD : (g + 1) * HD] for g in range(HALF // HD)], axis=0)
        keys = fresh_held[:, v * HD : (v + 1) * HD].astype(bf16)
        values = fresh_held[:, (KVH + v) * HD : (KVH + v + 1) * HD].astype(bf16)
        scores = jnp.where(seen, dot_nt(query, keys) * SCORE, NONE)
        highest = jnp.max(scores, axis=1, keepdims=True)
        weight = jnp.exp2(scores - highest)
        total = jnp.sum(weight, axis=1, keepdims=True)
        weight = (weight / total).astype(bf16)
        own_ref[v] = jnp.dot(weight, values, preferred_element_type=f32)
        ownsum_ref[v] = jnp.broadcast_to(highest + jnp.log2(total), (count, HD))


def own_mixer(rates_ref, skips_ref, sx_ref, sb_ref, sc_ref, sdt_ref, c_rows, x_rows, fade_ref, local_ref):
    steps, rows, heads = sdt_ref.shape
    stack_rows(sc_ref, c_rows)
    for u in range(steps):
        given = sx_ref[u].astype(f32)
        for k in range(SUB // rows):
            x_rows[u, k * rows : (k + 1) * rows, :] = given
    pair = iota((SUB, heads), 0)
    step = pair // rows
    live = pair < rows * steps
    head = iota((SUB, heads), 1)

    def spread_rows(ref, u):
        given = ref[u].astype(f32)
        return jnp.concatenate([given] * (SUB // rows), axis=0)

    rates = jnp.broadcast_to(rates_ref[...], (SUB, heads)) * LOG2E
    skips = jnp.broadcast_to(skips_ref[...], (SUB, heads))
    moved = [spread_rows(sdt_ref, u) for u in range(steps)]
    kept = [jnp.where(u <= step, moved[u], 0.0) for u in range(steps)]
    parts = [jnp.where(live, jnp.exp2(-(rates * sum(kept))), 0.0)]
    for u in range(steps):
        products = c_rows[...] * spread_rows(sb_ref, u)
        inner = jnp.zeros((SUB, heads), f32)
        for e in range(products.shape[1] // NS):
            found = jnp.sum(products[:, e * NS : (e + 1) * NS], axis=1, keepdims=True)
            inner = jnp.where(head // HPG == e, found, inner)
        gap = jnp.zeros((SUB, heads), f32)
        for t in range(u + 1, steps):
            gap = gap + kept[t]
        weight = jnp.where(u <= step, jnp.exp2(-(rates * gap)) * moved[u] * inner, 0.0)
        weight = weight + jnp.where(u == step, skips, 0.0)
        parts.append(jnp.where(live, weight, 0.0))
    stacked = jnp.concatenate(parts, axis=0)
    high = stacked.astype(bf16)
    low = (stacked - high.astype(f32)).astype(bf16)
    both = jnp.concatenate([high.astype(f32), low.astype(f32)], axis=0)
    count = stacked.shape[0]
    chunk = SUB * HP
    widen = jnp.where(iota((heads, chunk), 0) % SUB == iota((heads, chunk), 1) // HP, 1.0, 0.0).astype(bf16)
    lane = iota(both.shape, 1)
    for d in range(heads // SUB):
        picked = jnp.where(lane // SUB == d, both, 0.0).astype(bf16)
        wide = jnp.dot(picked, widen, preferred_element_type=f32)
        wide = wide[:count] + wide[count:]
        columns = slice(d * chunk, (d + 1) * chunk)
        fade_ref[:, columns] = wide[:SUB]
        value = jnp.zeros((SUB, chunk), f32)
        for u in range(steps):
            value = value + wide[(u + 1) * SUB : (u + 2) * SUB] * x_rows[u, :, columns]
        local_ref[:, columns] = value


def merge_kernel(
    width,
    back_any,
    own_any,
    ownsum_any,
    fade_any,
    local_any,
    mixer_ref,
    attention_ref,
    back_ref,
    own_ref,
    ownsum_ref,
    fade_ref,
    local_ref,
    mixed,
    attended,
    sems,
):
    copies = fetches(
        [
            (back_any, back_ref),
            (own_any, own_ref),
            (ownsum_any, ownsum_ref),
            (fade_any, fade_ref),
            (local_any, local_ref),
        ],
        sems,
    )
    for copy in copies:
        copy.wait()
    owners = back_ref.shape[0] // SUB
    ways = owners // KVH
    steps, rows = mixer_ref.shape[0], mixer_ref.shape[1]
    for d in range(0, owners, 2):
        found = back_ref[d * SUB : (d + 2) * SUB, HALF : HALF + width].astype(f32)
        found = jnp.concatenate([found[:SUB], found[SUB:]], axis=-1)
        columns = slice(d * width, (d + 2) * width)
        mixed[:, columns] = found * fade_ref[:, columns] + local_ref[:, columns]
    for k in range(steps):
        mixer_ref[k] = mixed[k * rows : (k + 1) * rows, :].astype(bf16)
    lane = iota((2, SUB, LANES), 2)
    mine = (lane // 16 == iota((2, SUB, LANES), 1)) & (lane % 16 < 12)
    for v in range(KVH):
        blocks, pieces = [], []
        for d in range(v * ways, (v + 1) * ways, 2):
            block = back_ref[d * SUB : (d + 2) * SUB, :HALF].astype(f32)
            packed = block[:, :LANES].reshape(2, SUB, LANES)[:, SUMS_ROW : SUMS_ROW + 1, :]
            blocks.append(block)
            pieces.append(jnp.where(mine, jnp.broadcast_to(packed, (2, SUB, LANES)), 0.0))
        for g in range(HALF // HD):
            part = slice(g * 2 * SUB, (g + 1) * 2 * SUB)
            own_sum = ownsum_ref[v, part, :]
            wide = []
            for piece in pieces:
                one = jnp.sum(jnp.where(lane % 4 == g, piece, 0.0), axis=-1, keepdims=True)
                wide.append(jnp.broadcast_to(one, (2, SUB, HD)).reshape(2 * SUB, HD))
            highest = functools.reduce(jnp.maximum, wide, own_sum)
            weight = jnp.exp2(own_sum - highest)
            total = weight
            value = weight * own_ref[v, part, :]
            for one, block in zip(wide, blocks):
                weight = jnp.exp2(one - highest)
                total = total + weight
                value = value + weight * block[:, g * HD : (g + 1) * HD]
            value = value / total
            start = v * 2 * HALF + g * HD
            attended[:, start : start + HD] = value[:SUB]
            attended[:, start + HALF : start + HALF + HD] = value[SUB:]
    for k in range(steps):
        attention_ref[k] = attended[k * rows : (k + 1) * rows, :].astype(bf16)


def call(kernel, out_shape, in_spaces, out_spaces, scratch, cost, aliases=None):
    def spec(space):
        return pl.BlockSpec(memory_space=space)

    return pl.pallas_call(
        kernel,
        out_shape=out_shape,
        in_specs=[spec(space) for space in in_spaces],
        out_specs=jax.tree.map(spec, out_spaces),
        scratch_shapes=scratch,
        input_output_aliases=aliases or {},
        compiler_params=pltpu.CompilerParams(vmem_limit_bytes=VMEM_LIMIT),
        cost_estimate=pl.CostEstimate(flops=cost[0], bytes_accessed=cost[1], transcendentals=0),
    )


def on_device(
    prompt_x,
    prompt_b,
    prompt_c,
    prompt_dt,
    decay_rate,
    skip_gain,
    lengths,
    owner_list,
    page_table,
    cache_pages,
    row_slot,
    step_x,
    step_b,
    step_c,
    step_dt,
    queries,
    fresh_cache,
):
    owners = lax.axis_size("heads")
    ways = owners // KVH
    group, prompts, length = prompt_dt.shape
    width = prompt_x.shape[1]
    keys = cache_pages.shape[0] * PAGE
    steps = step_x.shape[1]
    all_rows = owners * SUB
    shape = jax.ShapeDtypeStruct
    smem, vmem, hbm = pltpu.SMEM, pltpu.VMEM, pltpu.HBM
    sem = pltpu.SemaphoreType.DMA((prompts,))
    levels = len(LEVELS)
    step_x, step_b, step_c, step_dt, queries, fresh_cache = (
        jnp.swapaxes(one, 0, 1) for one in (step_x, step_b, step_c, step_dt, queries, fresh_cache)
    )
    owner_list = owner_list.T

    def like(space, array):
        return space(array.shape, array.dtype)

    def sems(count):
        return pltpu.SemaphoreType.DMA((count,))

    other_pages = lax.ppermute(cache_pages, "heads", [(d, d + 1 - 2 * (d % 2)) for d in range(owners)])
    send = call(
        functools.partial(pack_kernel, group, ways),
        shape((all_rows, HALF + NS), bf16),
        [hbm, hbm],
        vmem,
        [
            like(vmem, queries),
            like(vmem, step_c),
            vmem((SUB, queries.shape[2]), f32),
            vmem((SUB, step_c.shape[2]), f32),
            sems(2),
        ],
        (0, 1 << 19),
    )(queries, step_c)
    recv = lax.all_to_all(send, "heads", split_axis=0, concat_axis=0, tiled=True)

    block = [
        vmem((prompts, width, length), bf16),
        vmem((prompts, length, NS), bf16),
        vmem((prompts, length, NS), bf16),
        vmem((prompts, width, length), bf16),
        vmem((levels, prompts, group, length), f32),
        vmem((levels, prompts, group, length), f32),
        vmem((prompts, group, length), f32),
    ]
    masks = vmem((levels, length, length), bf16)
    work = 2 * width * length * NS
    states, tag, requests, early_out = call(
        state_kernel,
        (
            shape((prompts, width, NS), bf16),
            shape((2, SUB, LANES), jnp.int32),
            shape((all_rows, LANES), jnp.int32),
            shape(prompt_x.shape, bf16),
        ),
        [hbm] * 10,
        (hbm, vmem, vmem, hbm),
        block
        + [vmem((prompts, group, length), f32), masks, vmem((prompts, width, NS), bf16)]
        + [like(smem, one) for one in (decay_rate, skip_gain, lengths, owner_list, page_table, row_slot)]
        + [like(vmem, prompt_dt), sem, sem, sem, sem, sem, sems(7)],
        (work * (prompts + 5 * EARLY), 6 << 20),
    )(
        decay_rate,
        skip_gain,
        lengths,
        owner_list,
        page_table,
        row_slot,
        prompt_dt,
        prompt_x,
        prompt_b,
        prompt_c,
    )

    back = call(
        serve_kernel,
        shape((all_rows, HALF + max(LANES, width)), bf16),
        [hbm] * 6,
        vmem,
        [
            like(vmem, recv),
            vmem((2, keys, 2 * HD), bf16),
            like(vmem, tag),
            like(vmem, requests),
            like(vmem, states),
            vmem((2, all_rows, keys), f32),
            sem,
            sems(5),
        ],
        (8 * all_rows * keys * HD, 4 << 20),
    )(
        recv,
        cache_pages.reshape(keys, 2 * HD),
        other_pages.reshape(keys, 2 * HD),
        tag,
        requests,
        states,
    )
    returned = lax.all_to_all(back, "heads", split_axis=0, concat_axis=0, tiled=True)

    count = HALF // HD * 2 * SUB
    channels = step_x.shape[2]
    rates, skips = decay_rate.reshape(1, -1), skip_gain.reshape(1, -1)
    prompt_out, own, own_sum, fade, local = call(
        prompt_kernel,
        (
            shape(prompt_x.shape, bf16),
            shape((KVH, count, HD), f32),
            shape((KVH, count, HD), f32),
            shape((SUB, channels), f32),
            shape((SUB, channels), f32),
        ),
        [hbm] * 17,
        (hbm, vmem, vmem, vmem, vmem),
        block
        + [
            masks,
            vmem((SUB, fresh_cache.shape[2]), f32),
            vmem((SUB, step_c.shape[2]), f32),
            vmem((steps, SUB, channels), f32),
            like(smem, decay_rate),
            like(smem, skip_gain),
            like(smem, lengths),
            like(vmem, prompt_dt),
            like(vmem, rates),
            like(vmem, skips),
            like(vmem, send),
            like(vmem, fresh_cache),
            like(vmem, step_x),
            like(vmem, step_b),
            like(vmem, step_c),
            like(vmem, step_dt),
            sem,
            sem,
            sem,
            sem,
            sems(12),
        ],
        (work * 5 * (prompts - EARLY), 8 << 20),
        {16: 0},
    )(
        decay_rate,
        skip_gain,
        lengths,
        prompt_dt,
        rates,
        skips,
        send,
        fresh_cache,
        step_x,
        step_b,
        step_c,
        step_dt,
        prompt_x,
        prompt_b,
        prompt_c,
        back,
        early_out,
    )

    mixer_out, attention_out = call(
        functools.partial(merge_kernel, width),
        (shape(step_x.shape, bf16), shape(queries.shape, bf16)),
        [hbm] * 5,
        (vmem, vmem),
        [like(vmem, one) for one in (returned, own, own_sum, fade, local)]
        + [vmem((SUB, channels), f32), vmem((SUB, queries.shape[2]), f32), sems(5)],
        (0, 2 << 20),
    )(returned, own, own_sum, fade, local)
    return (prompt_out, jnp.swapaxes(mixer_out, 0, 1), jnp.swapaxes(attention_out, 0, 1))


def solution(mesh):
    in_specs = (
        P("groups", "heads", None),
        P("groups", None, None),
        P("groups", None, None),
        P("heads", "groups", None),
        P(),
        P(),
        P("groups"),
        P("groups", None),
        P("groups", None),
        P(("groups", "heads"), None, None),
        P("groups"),
        P(("groups", "heads"), None, None),
        P(("groups", "heads"), None, None),
        P(("groups", "heads"), None, None),
        P(("groups", "heads"), None, None),
        P(("groups", "heads"), None, None),
        P(("groups", "heads"), None, None),
    )
    out_specs = (
        P("groups", "heads", None),
        P(("groups", "heads"), None, None),
        P(("groups", "heads"), None, None),
    )
    return jax.shard_map(
        on_device, mesh=mesh, in_specs=in_specs, out_specs=out_specs, check_vma=False
    )
```

```python
import functools
import math

import jax
import jax.numpy as jnp
from jax import lax
from jax.experimental import pallas as pl
from jax.experimental.pallas import tpu as pltpu
from jax.sharding import PartitionSpec as P

NS = 256
HP = 64
HPG = 32
KVH = 8
HD = 128
PAGE = 16
LANES = 128
SUB = 8
HALF = 512
LEVELS = (128, 64, 32, 16)
LOG2E = math.log2(math.e)
SCORE = LOG2E / math.sqrt(HD)
NONE = -1e30
PAIRS = 6
MATCH = 32768.0
EARLY = 2
VMEM_LIMIT = 64 * 1024 * 1024

f32 = jnp.float32
bf16 = jnp.bfloat16


def iota(shape, dim):
    return lax.broadcasted_iota(jnp.int32, shape, dim)


def dot_nt(left, right):
    return lax.dot_general(left, right, (((1,), (1,)), ((), ())), preferred_element_type=f32)


def stack_rows(source, held):
    steps, rows = source.shape[0], source.shape[1]
    held[...] = jnp.zeros_like(held)
    for k in range(steps):
        held[k * rows : (k + 1) * rows, :] = source[k].astype(f32)


def spare(blocks, taken):
    return [(row, b) for row in range(PAIRS, SUB) for b in range(blocks)][taken : taken + PAIRS]


def lift(value, slots):
    row = iota(value.shape[:2] + (LANES,), 1)
    found = jnp.zeros(row.shape, f32)
    for pair, (at, b) in enumerate(slots):
        one = value[:, at : at + 1, b * LANES : (b + 1) * LANES]
        found = jnp.where(row == pair, jnp.broadcast_to(one, row.shape), found)
    return found


def fetches(pairs, sems):
    copies = [pltpu.make_async_copy(src, dst, sems.at[n]) for n, (src, dst) in enumerate(pairs)]
    for copy in copies:
        copy.start()
    return copies


def pack_kernel(group, ways, q_any, c_any, out_ref, q_ref, c_ref, q_held, c_held, rest, sems):
    owners = out_ref.shape[0] // SUB
    for copy in fetches([(q_any, q_ref), (c_any, c_ref)], sems):
        copy.wait()
    stack_rows(q_ref, q_held)
    stack_rows(c_ref, c_held)
    span = 2 * HALF
    slots = spare(HALF // LANES + 1, 0)
    rest[...] = jnp.zeros_like(rest)
    for e in range(c_ref.shape[2] // NS):
        rest[e, :PAIRS, HALF:] = c_held[:PAIRS, e * NS : e * NS + LANES]
        for pair, (row, b) in enumerate(slots):
            rest[e, row : row + 1, b * LANES : (b + 1) * LANES] = c_held[
                pair : pair + 1, e * NS + LANES : (e + 1) * NS
            ]
    real = iota((SUB, HALF), 0) < PAIRS
    for d in range(0, owners, 2):
        v, e = d // ways, (d * group) // HPG
        low = jnp.where(real, q_held[:, v * span : v * span + HALF], rest[e, :, :HALF])
        high = jnp.where(real, q_held[:, v * span + HALF : (v + 1) * span], rest[e, :, :HALF])
        out_ref[d * SUB : (d + 2) * SUB, :HALF] = jnp.concatenate([low, high], axis=0).astype(bf16)
        end = rest[e, :, HALF:]
        out_ref[d * SUB : (d + 2) * SUB, HALF:] = jnp.concatenate([end, end], axis=0).astype(bf16)


def head_factors(first, dt_ref, rate_ref, skip_ref, len_ref, levels, w_in, w_out, w_skip, w_tail):
    group, prompts, length = dt_ref.shape
    row = iota((prompts, length), 0)
    lens = jnp.zeros((prompts, length), jnp.int32)
    for r in range(prompts):
        lens = jnp.where(row == r, len_ref[r], lens)
    valid = iota((prompts, length), 1) < lens
    moved = [jnp.where(valid, dt_ref[h].astype(f32), 0.0) for h in range(group)]
    every = jnp.concatenate(moved, axis=0).astype(bf16)
    j = iota((length, length), 0)
    i = iota((length, length), 1)
    rates = [rate_ref[first + h] * LOG2E for h in range(group)]
    if w_tail is not None:
        after = jnp.where(j > i, 1.0, 0.0).astype(bf16)
        total = jnp.dot(every, after, preferred_element_type=f32)
        for h in range(group):
            part = total[h * prompts : (h + 1) * prompts]
            w_tail[:, h, :] = jnp.exp2(-(rates[h] * part)) * moved[h]
    if not levels:
        return
    for h in range(group):
        w_skip[:, h, :] = jnp.where(valid, skip_ref[first + h], 0.0)
    for l, n in enumerate(levels):
        middle = (i // (2 * n)) * (2 * n) + (n - 1)
        signs = (jnp.where(j <= i, 1.0, 0.0) - jnp.where(j <= middle, 1.0, 0.0)).astype(bf16)
        total = jnp.dot(every, signs, preferred_element_type=f32)
        for h in range(group):
            gap = rates[h] * total[h * prompts : (h + 1) * prompts]
            if n == LEVELS[-1]:
                up, down = jnp.exp2(gap), jnp.exp2(-gap)
            else:
                up, down = jnp.exp2(jnp.minimum(gap, 0.0)), jnp.exp2(-jnp.maximum(gap, 0.0))
            w_in[l, :, h, :] = up * moved[h]
            w_out[l, :, h, :] = jnp.where(valid, down, 0.0)


def level_masks(masks):
    length = masks.shape[-1]
    j = iota((length, length), 0)
    i = iota((length, length), 1)
    for l, n in enumerate(LEVELS):
        same = (j // (2 * n)) == (i // (2 * n))
        if n == LEVELS[-1]:
            keep = same & (j <= i)
        else:
            keep = same & ((j % (2 * n)) < n) & ((i % (2 * n)) >= n)
        masks[l] = jnp.where(keep, 1.0, 0.0).astype(bf16)


def prompt_result(r, x_held, b_held, c_held, w_in, w_out, w_skip, masks, out_held):
    width, length = x_held.shape[1], x_held.shape[2]
    group = width // HP
    half = length // 2
    inputs = x_held[r].astype(f32).reshape(group, HP, length)
    scores = dot_nt(b_held[r], c_held[r]).astype(bf16)
    total = inputs * w_skip[r][:, None, :]
    left, right = total[..., :half], total[..., half:]
    for l, n in enumerate(LEVELS):
        if 2 * n == length:
            scaled = (inputs[..., :half] * w_in[l, r][:, None, :half]).astype(bf16).reshape(width, half)
            added = jnp.dot(scaled, scores[:half, half:], preferred_element_type=f32)
            right = right + added.reshape(group, HP, half) * w_out[l, r][:, None, half:]
        else:
            scaled = (inputs * w_in[l, r][:, None, :]).astype(bf16).reshape(width, length)
            added = jnp.dot(scaled, scores * masks[l], preferred_element_type=f32)
            added = added.reshape(group, HP, length) * w_out[l, r][:, None, :]
            left = left + added[..., :half]
            right = right + added[..., half:]
    out_held[r] = jnp.concatenate([left, right], axis=-1).reshape(width, length).astype(bf16)


def state_kernel(
    rate_any,
    skip_any,
    len_any,
    owner_any,
    table_any,
    slot_any,
    dt_any,
    x_any,
    b_any,
    c_any,
    state_any,
    mark_any,
    hot_ref,
    req_ref,
    out_any,
    x_held,
    b_held,
    c_held,
    out_held,
    w_in,
    w_out,
    w_skip,
    w_tail,
    masks,
    state_held,
    mark_held,
    rate_ref,
    skip_ref,
    len_ref,
    owner_ref,
    table_ref,
    slot_ref,
    dt_ref,
    x_sem,
    b_sem,
    c_sem,
    out_sem,
    state_sem,
    mark_sem,
    sems,
):
    group, prompts, length = dt_ref.shape
    smalls = fetches(
        [
            (dt_any, dt_ref),
            (rate_any, rate_ref),
            (skip_any, skip_ref),
            (len_any, len_ref),
            (owner_any, owner_ref),
            (table_any, table_ref),
            (slot_any, slot_ref),
        ],
        sems,
    )
    me = lax.axis_index("heads")
    first = me * group
    column = pl.multiple_of((first // HPG) * NS, NS)

    def x_copy(r):
        return pltpu.make_async_copy(x_any.at[r], x_held.at[r], x_sem.at[r])

    def b_copy(r):
        return pltpu.make_async_copy(b_any.at[r, :, pl.ds(column, NS)], b_held.at[r], b_sem.at[r])

    def c_copy(r):
        return pltpu.make_async_copy(c_any.at[r, :, pl.ds(column, NS)], c_held.at[r], c_sem.at[r])

    def out_copy(r):
        return pltpu.make_async_copy(out_held.at[r], out_any.at[r], out_sem.at[r])

    def state_copy(r):
        return pltpu.make_async_copy(state_held.at[r], state_any.at[r], state_sem.at[r])

    for r in range(prompts):
        x_copy(r).start()
        b_copy(r).start()
    for r in range(EARLY):
        c_copy(r).start()
    for copy in smalls:
        copy.wait()

    head_factors(
        first, dt_ref, rate_ref, skip_ref, len_ref, LEVELS if EARLY else (), w_in, w_out, w_skip, w_tail
    )

    spread = table_ref.shape[1] // owner_ref.shape[1]
    per_head = table_ref.shape[1] // KVH
    offset, lane = iota((PAGE, LANES), 0), iota((PAGE, LANES), 1)
    for n, holder in enumerate((me, me + 1 - 2 * lax.rem(me, 2))):
        for r in range(prompts):
            for page in range(spread):
                entry = holder * spread + page
                row = table_ref[r, entry] - holder * (prompts * spread)
                begin = lax.rem(entry, per_head) * PAGE
                inside = (lane == r) & (offset < len_ref[r] - begin)
                block = jnp.where(inside, MATCH, 0.0).astype(bf16)
                mark_held[n, pl.ds(pl.multiple_of(row * PAGE, PAGE), PAGE), :] = block
    mark_copy = pltpu.make_async_copy(mark_held, mark_any, mark_sem)
    mark_copy.start()

    owners = owner_ref.shape[1]
    rows_dev = slot_ref.shape[0] // owners
    inner = iota((2 * SUB, LANES), 0)
    lanes = iota((2 * SUB, LANES), 1)

    def fill(s, _):
        block = jnp.full((2 * SUB, LANES), -2, jnp.int32)
        for n in range(2):
            for i in range(rows_dev):
                target = owner_ref[slot_ref[(2 * s + n) * rows_dev + i], 2 * s + n]
                block = jnp.where((inner // SUB == n) & (inner % rows_dev == i), target, block)
        place = pl.ds(pl.multiple_of(s * 2 * SUB, 2 * SUB), 2 * SUB)
        req_ref[place, :] = block
        hot_ref[place, :] = jnp.where(lanes == block, 1.0, 0.0).astype(bf16)
        return 0

    lax.fori_loop(0, owners // 2, fill, 0)

    def one(r, _):
        x_copy(r).wait()
        b_copy(r).wait()
        width = x_held.shape[1]
        inputs = x_held[r].astype(f32).reshape(group, HP, length)
        scaled = (inputs * w_tail[r][:, None, :]).astype(bf16).reshape(width, length)
        state_held[r] = jnp.dot(scaled, b_held[r], preferred_element_type=f32).astype(bf16)
        state_copy(r).start()
        return 0

    lax.fori_loop(0, prompts, one, 0, unroll=2)

    if EARLY:
        level_masks(masks)

        def early(r, _):
            c_copy(r).wait()
            prompt_result(r, x_held, b_held, c_held, w_in, w_out, w_skip, masks, out_held)
            out_copy(r).start()
            return 0

        lax.fori_loop(0, EARLY, early, 0, unroll=2)
        for r in range(EARLY):
            out_copy(r).wait()
    for r in range(prompts):
        state_copy(r).wait()
    mark_copy.wait()


def serve_kernel(
    recv_any,
    pages_any,
    other_any,
    mark_any,
    hot_any,
    req_any,
    state_any,
    out_ref,
    recv_ref,
    key_ref,
    value_ref,
    hot_ref,
    req_ref,
    state_ref,
    query_ref,
    score_ref,
    state_sem,
    sems,
):
    rows = recv_ref.shape[0]
    held = pages_any.shape[0]
    prompts, width = state_ref.shape[0], state_ref.shape[1]
    mine, other = pl.ds(0, held), pl.ds(held, held)
    copies = fetches(
        [
            (recv_any, recv_ref),
            (hot_any, hot_ref),
            (pages_any.at[:, pl.ds(0, HD)], key_ref.at[mine, pl.ds(0, HD)]),
            (other_any.at[:, pl.ds(0, HD)], key_ref.at[other, pl.ds(0, HD)]),
            (mark_any.at[0], key_ref.at[mine, pl.ds(HD, LANES)]),
            (mark_any.at[1], key_ref.at[other, pl.ds(HD, LANES)]),
            (pages_any.at[:, pl.ds(HD, HD)], value_ref.at[mine]),
            (other_any.at[:, pl.ds(HD, HD)], value_ref.at[other]),
            (req_any, req_ref),
        ],
        sems,
    )
    states = fetches([(state_any.at[r], state_ref.at[r]) for r in range(prompts)], state_sem)
    copies[0].wait()
    copies[1].wait()
    heads = HALF // HD
    for g in range(heads):
        query_ref[g * rows : (g + 1) * rows, :HD] = recv_ref[:, g * HD : (g + 1) * HD]
        query_ref[g * rows : (g + 1) * rows, HD:] = hot_ref[...]
    for copy in copies[2:6]:
        copy.wait()
    keys = key_ref.shape[0]
    chunk = min(keys, 2 * NS)
    widest = jnp.full((heads * rows, LANES), NONE, f32)
    for k in range(0, keys, chunk):
        scores = dot_nt(query_ref[...], key_ref[k : k + chunk, :])
        score_ref[:, k : k + chunk] = scores
        for b in range(0, chunk, LANES):
            widest = jnp.maximum(widest, scores[:, b : b + LANES])
    highest = jnp.max(widest, axis=1, keepdims=True)
    for copy in copies[6:]:
        copy.wait()
    total = jnp.zeros((heads * rows, LANES), f32)
    value = jnp.zeros((heads * rows, HD), f32)
    for k in range(0, keys, chunk):
        weight = jnp.exp2((score_ref[:, k : k + chunk] - highest) * SCORE)
        for b in range(0, chunk, LANES):
            total = total + weight[:, b : b + LANES]
        value = value + jnp.dot(weight.astype(bf16), value_ref[k : k + chunk, :], preferred_element_type=f32)
    total = jnp.sum(total, axis=1, keepdims=True)
    value = value / total
    result = jnp.where(highest > 0.5 * MATCH, (highest - MATCH) * SCORE + jnp.log2(total), NONE)
    lane = iota((rows, LANES), 1)
    sums = jnp.zeros((rows, LANES), f32)
    for g in range(heads):
        sums = jnp.where(lane % 4 == g, result[g * rows : (g + 1) * rows], sums)
    high = sums.astype(bf16).astype(f32)
    rest = sums - high
    middle = rest.astype(bf16).astype(f32)
    piece = lane % 16 // 4
    pieces = jnp.where(piece == 0, high, jnp.where(piece == 1, middle, rest - middle))
    pair = iota((rows, LANES), 0) % SUB
    pieces = jnp.where((lane // 16 == pair) & (piece < 3), pieces, 0.0)
    packed = jnp.sum(pieces.reshape(rows // SUB, SUB, LANES), axis=1, keepdims=True)

    given = recv_ref[...].astype(f32).reshape(rows // SUB, SUB, recv_ref.shape[1])
    ending = lift(given, spare(heads + 1, 0))
    readout = jnp.concatenate([given[..., HALF:], ending], axis=-1).reshape(rows, NS)
    target = jnp.concatenate([req_ref[...], req_ref[...]], axis=-1)
    found = jnp.zeros((rows, width), f32)
    for r in range(prompts):
        picked = jnp.where(target == r, readout, 0.0).astype(bf16)
        states[r].wait()
        found = found + dot_nt(picked, state_ref[r])
    if width < LANES:
        found = jnp.concatenate([found, jnp.zeros((rows, LANES - width), f32)], axis=-1)
    blocks = [value[g * rows : (g + 1) * rows] for g in range(heads)]
    blocks += [found[:, b : b + LANES] for b in range(0, found.shape[1], LANES)]
    blocks = [one.reshape(rows // SUB, SUB, LANES) for one in blocks]
    row = iota((rows // SUB, SUB, LANES), 1)
    last = blocks.pop()
    blocks[0] = jnp.where(row == PAIRS, jnp.broadcast_to(packed, row.shape), blocks[0])
    for n, (at, b) in enumerate(spare(len(blocks), 1)):
        one = jnp.broadcast_to(last[:, n : n + 1, :], row.shape)
        blocks[b] = jnp.where(row == at, one, blocks[b])
    for b, one in enumerate(blocks):
        out_ref[:, b * LANES : (b + 1) * LANES] = one.reshape(rows, LANES).astype(bf16)


def prompt_kernel(
    rate_any,
    skip_any,
    len_any,
    dt_any,
    rates_any,
    skips_any,
    send_any,
    fresh_any,
    sx_any,
    sb_any,
    sc_any,
    sdt_any,
    x_any,
    b_any,
    c_any,
    after_any,
    early_any,
    out_any,
    own_ref,
    ownsum_ref,
    fade_ref,
    local_ref,
    x_held,
    b_held,
    c_held,
    out_held,
    w_in,
    w_out,
    w_skip,
    masks,
    fresh_held,
    c_rows,
    x_rows,
    rate_ref,
    skip_ref,
    len_ref,
    dt_ref,
    rates_ref,
    skips_ref,
    send_ref,
    fresh_ref,
    sx_ref,
    sb_ref,
    sc_ref,
    sdt_ref,
    x_sem,
    b_sem,
    c_sem,
    out_sem,
    sems,
):
    group, prompts, length = dt_ref.shape
    smalls = fetches(
        [
            (dt_any, dt_ref),
            (rate_any, rate_ref),
            (skip_any, skip_ref),
            (len_any, len_ref),
            (rates_any, rates_ref),
            (skips_any, skips_ref),
            (send_any, send_ref),
            (fresh_any, fresh_ref),
            (sx_any, sx_ref),
            (sb_any, sb_ref),
            (sc_any, sc_ref),
            (sdt_any, sdt_ref),
        ],
        sems,
    )
    me = lax.axis_index("heads")
    first = me * group
    column = pl.multiple_of((first // HPG) * NS, NS)

    def x_copy(r):
        return pltpu.make_async_copy(x_any.at[r], x_held.at[r], x_sem.at[r])

    def b_copy(r):
        return pltpu.make_async_copy(b_any.at[r, :, pl.ds(column, NS)], b_held.at[r], b_sem.at[r])

    def c_copy(r):
        return pltpu.make_async_copy(c_any.at[r, :, pl.ds(column, NS)], c_held.at[r], c_sem.at[r])

    def out_copy(r):
        return pltpu.make_async_copy(out_held.at[r], out_any.at[r], out_sem.at[r])

    for r in range(EARLY, prompts):
        x_copy(r).start()
        b_copy(r).start()
        c_copy(r).start()
    for copy in smalls:
        copy.wait()

    head_factors(first, dt_ref, rate_ref, skip_ref, len_ref, LEVELS, w_in, w_out, w_skip, None)
    level_masks(masks)

    def one(r, _):
        x_copy(r).wait()
        b_copy(r).wait()
        c_copy(r).wait()
        prompt_result(r, x_held, b_held, c_held, w_in, w_out, w_skip, masks, out_held)
        out_copy(r).start()
        return 0

    lax.fori_loop(EARLY, prompts, one, 0, unroll=2)
    own_attention(send_ref, fresh_ref, fresh_held, own_ref, ownsum_ref)
    own_mixer(rates_ref, skips_ref, sx_ref, sb_ref, sc_ref, sdt_ref, c_rows, x_rows, fade_ref, local_ref)
    for r in range(EARLY, prompts):
        out_copy(r).wait()


def own_attention(send_ref, fresh_ref, fresh_held, own_ref, ownsum_ref):
    steps, rows = fresh_ref.shape[0], fresh_ref.shape[1]
    ways = send_ref.shape[0] // SUB // KVH
    stack_rows(fresh_ref, fresh_held)
    count = HALF // HD * 2 * SUB
    pair = iota((count, SUB), 0) % SUB
    key = iota((count, SUB), 1)
    seen = (key % rows == pair % rows) & (key <= pair) & (key < rows * steps)
    seen = seen | ((pair >= rows * steps) & (key == 0))
    for v in range(KVH):
        block = send_ref[v * ways * SUB : (v * ways + 2) * SUB]
        query = jnp.concatenate([block[:, g * HD : (g + 1) * HD] for g in range(HALF // HD)], axis=0)
        keys = fresh_held[:, v * HD : (v + 1) * HD].astype(bf16)
        values = fresh_held[:, (KVH + v) * HD : (KVH + v + 1) * HD].astype(bf16)
        scores = jnp.where(seen, dot_nt(query, keys) * SCORE, NONE)
        highest = jnp.max(scores, axis=1, keepdims=True)
        weight = jnp.exp2(scores - highest)
        total = jnp.sum(weight, axis=1, keepdims=True)
        weight = (weight / total).astype(bf16)
        own_ref[v] = jnp.dot(weight, values, preferred_element_type=f32)
        ownsum_ref[v] = jnp.broadcast_to(highest + jnp.log2(total), (count, HD))


def own_mixer(rates_ref, skips_ref, sx_ref, sb_ref, sc_ref, sdt_ref, c_rows, x_rows, fade_ref, local_ref):
    steps, rows, heads = sdt_ref.shape
    stack_rows(sc_ref, c_rows)
    for u in range(steps):
        given = sx_ref[u].astype(f32)
        for k in range(SUB // rows):
            x_rows[u, k * rows : (k + 1) * rows, :] = given
    pair = iota((SUB, heads), 0)
    step = pair // rows
    live = pair < rows * steps
    head = iota((SUB, heads), 1)

    def spread_rows(ref, u):
        given = ref[u].astype(f32)
        return jnp.concatenate([given] * (SUB // rows), axis=0)

    rates = jnp.broadcast_to(rates_ref[...], (SUB, heads)) * LOG2E
    skips = jnp.broadcast_to(skips_ref[...], (SUB, heads))
    moved = [spread_rows(sdt_ref, u) for u in range(steps)]
    kept = [jnp.where(u <= step, moved[u], 0.0) for u in range(steps)]
    parts = [jnp.where(live, jnp.exp2(-(rates * sum(kept))), 0.0)]
    for u in range(steps):
        products = c_rows[...] * spread_rows(sb_ref, u)
        inner = jnp.zeros((SUB, heads), f32)
        for e in range(products.shape[1] // NS):
            found = jnp.sum(products[:, e * NS : (e + 1) * NS], axis=1, keepdims=True)
            inner = jnp.where(head // HPG == e, found, inner)
        gap = jnp.zeros((SUB, heads), f32)
        for t in range(u + 1, steps):
            gap = gap + kept[t]
        weight = jnp.where(u <= step, jnp.exp2(-(rates * gap)) * moved[u] * inner, 0.0)
        weight = weight + jnp.where(u == step, skips, 0.0)
        parts.append(jnp.where(live, weight, 0.0))
    stacked = jnp.concatenate(parts, axis=0)
    high = stacked.astype(bf16)
    low = (stacked - high.astype(f32)).astype(bf16)
    both = jnp.concatenate([high.astype(f32), low.astype(f32)], axis=0)
    count = stacked.shape[0]
    chunk = SUB * HP
    widen = jnp.where(iota((heads, chunk), 0) % SUB == iota((heads, chunk), 1) // HP, 1.0, 0.0).astype(bf16)
    lane = iota(both.shape, 1)
    for d in range(heads // SUB):
        picked = jnp.where(lane // SUB == d, both, 0.0).astype(bf16)
        wide = jnp.dot(picked, widen, preferred_element_type=f32)
        wide = wide[:count] + wide[count:]
        columns = slice(d * chunk, (d + 1) * chunk)
        fade_ref[:, columns] = wide[:SUB]
        value = jnp.zeros((SUB, chunk), f32)
        for u in range(steps):
            value = value + wide[(u + 1) * SUB : (u + 2) * SUB] * x_rows[u, :, columns]
        local_ref[:, columns] = value


def merge_kernel(
    width,
    back_any,
    own_any,
    ownsum_any,
    fade_any,
    local_any,
    mixer_ref,
    attention_ref,
    back_ref,
    own_ref,
    ownsum_ref,
    fade_ref,
    local_ref,
    mixed,
    attended,
    sems,
):
    copies = fetches(
        [
            (back_any, back_ref),
            (own_any, own_ref),
            (ownsum_any, ownsum_ref),
            (fade_any, fade_ref),
            (local_any, local_ref),
        ],
        sems,
    )
    for copy in copies:
        copy.wait()
    owners = back_ref.shape[0] // SUB
    ways = owners // KVH
    steps, rows = mixer_ref.shape[0], mixer_ref.shape[1]
    for d in range(0, owners, 2):
        block = back_ref[d * SUB : (d + 2) * SUB, :].astype(f32).reshape(2, SUB, back_ref.shape[1])
        ending = lift(block, spare(back_ref.shape[1] // LANES, 1))
        if back_ref.shape[1] > HALF:
            ending = jnp.concatenate([block[..., HALF:], ending], axis=-1)
        found = ending[..., :width]
        found = jnp.concatenate([found[0], found[1]], axis=-1)
        columns = slice(d * width, (d + 2) * width)
        mixed[:, columns] = found * fade_ref[:, columns] + local_ref[:, columns]
    for k in range(steps):
        mixer_ref[k] = mixed[k * rows : (k + 1) * rows, :].astype(bf16)
    lane = iota((2, SUB, LANES), 2)
    mine = (lane // 16 == iota((2, SUB, LANES), 1)) & (lane % 16 < 12)
    for v in range(KVH):
        blocks, pieces = [], []
        for d in range(v * ways, (v + 1) * ways, 2):
            block = back_ref[d * SUB : (d + 2) * SUB, :HALF].astype(f32)
            packed = block[:, :LANES].reshape(2, SUB, LANES)[:, PAIRS : PAIRS + 1, :]
            blocks.append(block)
            pieces.append(jnp.where(mine, jnp.broadcast_to(packed, (2, SUB, LANES)), 0.0))
        for g in range(HALF // HD):
            part = slice(g * 2 * SUB, (g + 1) * 2 * SUB)
            own_sum = ownsum_ref[v, part, :]
            wide = []
            for piece in pieces:
                one = jnp.sum(jnp.where(lane % 4 == g, piece, 0.0), axis=-1, keepdims=True)
                wide.append(jnp.broadcast_to(one, (2, SUB, HD)).reshape(2 * SUB, HD))
            highest = functools.reduce(jnp.maximum, wide, own_sum)
            weight = jnp.exp2(own_sum - highest)
            total = weight
            value = weight * own_ref[v, part, :]
            for one, block in zip(wide, blocks):
                weight = jnp.exp2(one - highest)
                total = total + weight
                value = value + weight * block[:, g * HD : (g + 1) * HD]
            value = value / total
            start = v * 2 * HALF + g * HD
            attended[:, start : start + HD] = value[:SUB]
            attended[:, start + HALF : start + HALF + HD] = value[SUB:]
    for k in range(steps):
        attention_ref[k] = attended[k * rows : (k + 1) * rows, :].astype(bf16)


def call(kernel, out_shape, in_spaces, out_spaces, scratch, cost, aliases=None):
    def spec(space):
        return pl.BlockSpec(memory_space=space)

    return pl.pallas_call(
        kernel,
        out_shape=out_shape,
        in_specs=[spec(space) for space in in_spaces],
        out_specs=jax.tree.map(spec, out_spaces),
        scratch_shapes=scratch,
        input_output_aliases=aliases or {},
        compiler_params=pltpu.CompilerParams(vmem_limit_bytes=VMEM_LIMIT),
        cost_estimate=pl.CostEstimate(flops=cost[0], bytes_accessed=cost[1], transcendentals=0),
    )


def on_device(
    prompt_x,
    prompt_b,
    prompt_c,
    prompt_dt,
    decay_rate,
    skip_gain,
    lengths,
    owner_list,
    page_table,
    cache_pages,
    row_slot,
    step_x,
    step_b,
    step_c,
    step_dt,
    queries,
    fresh_cache,
):
    owners = lax.axis_size("heads")
    ways = owners // KVH
    group, prompts, length = prompt_dt.shape
    width = prompt_x.shape[1]
    keys = cache_pages.shape[0] * PAGE
    steps = step_x.shape[1]
    all_rows = owners * SUB
    shape = jax.ShapeDtypeStruct
    smem, vmem, hbm = pltpu.SMEM, pltpu.VMEM, pltpu.HBM
    sem = pltpu.SemaphoreType.DMA((prompts,))
    levels = len(LEVELS)
    step_x, step_b, step_c, step_dt, queries, fresh_cache = (
        jnp.swapaxes(one, 0, 1) for one in (step_x, step_b, step_c, step_dt, queries, fresh_cache)
    )
    owner_list = owner_list.T

    def like(space, array):
        return space(array.shape, array.dtype)

    def sems(count):
        return pltpu.SemaphoreType.DMA((count,))

    other_pages = lax.ppermute(cache_pages, "heads", [(d, d + 1 - 2 * (d % 2)) for d in range(owners)])
    send = call(
        functools.partial(pack_kernel, group, ways),
        shape((all_rows, HALF + LANES), bf16),
        [hbm, hbm],
        vmem,
        [
            like(vmem, queries),
            like(vmem, step_c),
            vmem((SUB, queries.shape[2]), f32),
            vmem((SUB, step_c.shape[2]), f32),
            vmem((step_c.shape[2] // NS, SUB, HALF + LANES), f32),
            sems(2),
        ],
        (0, 1 << 19),
    )(queries, step_c)
    recv = lax.all_to_all(send, "heads", split_axis=0, concat_axis=0, tiled=True)

    block = [
        vmem((prompts, width, length), bf16),
        vmem((prompts, length, NS), bf16),
        vmem((prompts, length, NS), bf16),
        vmem((prompts, width, length), bf16),
        vmem((levels, prompts, group, length), f32),
        vmem((levels, prompts, group, length), f32),
        vmem((prompts, group, length), f32),
    ]
    masks = vmem((levels, length, length), bf16)
    work = 2 * width * length * NS
    states, marks, hot, requests, early_out = call(
        state_kernel,
        (
            shape((prompts, width, NS), bf16),
            shape((2, keys, LANES), bf16),
            shape((all_rows, LANES), bf16),
            shape((all_rows, LANES), jnp.int32),
            shape(prompt_x.shape, bf16),
        ),
        [hbm] * 10,
        (hbm, hbm, vmem, vmem, hbm),
        block
        + [vmem((prompts, group, length), f32), masks]
        + [vmem((prompts, width, NS), bf16), vmem((2, keys, LANES), bf16)]
        + [like(smem, one) for one in (decay_rate, skip_gain, lengths, owner_list, page_table, row_slot)]
        + [like(vmem, prompt_dt), sem, sem, sem, sem, sem, pltpu.SemaphoreType.DMA, sems(7)],
        (work * (prompts + 5 * EARLY), 6 << 20),
    )(
        decay_rate,
        skip_gain,
        lengths,
        owner_list,
        page_table,
        row_slot,
        prompt_dt,
        prompt_x,
        prompt_b,
        prompt_c,
    )

    back = call(
        serve_kernel,
        shape((all_rows, HALF + max(LANES, width) - LANES), bf16),
        [hbm] * 7,
        vmem,
        [
            like(vmem, recv),
            vmem((2 * keys, HD + LANES), bf16),
            vmem((2 * keys, HD), bf16),
            like(vmem, hot),
            like(vmem, requests),
            like(vmem, states),
            vmem((HALF // HD * all_rows, HD + LANES), bf16),
            vmem((HALF // HD * all_rows, 2 * keys), f32),
            sem,
            sems(9),
        ],
        (8 * all_rows * keys * HD, 4 << 20),
    )(
        recv,
        cache_pages.reshape(keys, 2 * HD),
        other_pages.reshape(keys, 2 * HD),
        marks,
        hot,
        requests,
        states,
    )
    returned = lax.all_to_all(back, "heads", split_axis=0, concat_axis=0, tiled=True)

    count = HALF // HD * 2 * SUB
    channels = step_x.shape[2]
    rates, skips = decay_rate.reshape(1, -1), skip_gain.reshape(1, -1)
    prompt_out, own, own_sum, fade, local = call(
        prompt_kernel,
        (
            shape(prompt_x.shape, bf16),
            shape((KVH, count, HD), f32),
            shape((KVH, count, HD), f32),
            shape((SUB, channels), f32),
            shape((SUB, channels), f32),
        ),
        [hbm] * 17,
        (hbm, vmem, vmem, vmem, vmem),
        block
        + [
            masks,
            vmem((SUB, fresh_cache.shape[2]), f32),
            vmem((SUB, step_c.shape[2]), f32),
            vmem((steps, SUB, channels), f32),
            like(smem, decay_rate),
            like(smem, skip_gain),
            like(smem, lengths),
            like(vmem, prompt_dt),
            like(vmem, rates),
            like(vmem, skips),
            like(vmem, send),
            like(vmem, fresh_cache),
            like(vmem, step_x),
            like(vmem, step_b),
            like(vmem, step_c),
            like(vmem, step_dt),
            sem,
            sem,
            sem,
            sem,
            sems(12),
        ],
        (work * 5 * (prompts - EARLY), 8 << 20),
        {16: 0},
    )(
        decay_rate,
        skip_gain,
        lengths,
        prompt_dt,
        rates,
        skips,
        send,
        fresh_cache,
        step_x,
        step_b,
        step_c,
        step_dt,
        prompt_x,
        prompt_b,
        prompt_c,
        back,
        early_out,
    )

    mixer_out, attention_out = call(
        functools.partial(merge_kernel, width),
        (shape(step_x.shape, bf16), shape(queries.shape, bf16)),
        [hbm] * 5,
        (vmem, vmem),
        [like(vmem, one) for one in (returned, own, own_sum, fade, local)]
        + [vmem((SUB, channels), f32), vmem((SUB, queries.shape[2]), f32), sems(5)],
        (0, 2 << 20),
    )(returned, own, own_sum, fade, local)
    return (prompt_out, jnp.swapaxes(mixer_out, 0, 1), jnp.swapaxes(attention_out, 0, 1))


def solution(mesh):
    in_specs = (
        P("groups", "heads", None),
        P("groups", None, None),
        P("groups", None, None),
        P("heads", "groups", None),
        P(),
        P(),
        P("groups"),
        P("groups", None),
        P("groups", None),
        P(("groups", "heads"), None, None),
        P("groups"),
        P(("groups", "heads"), None, None),
        P(("groups", "heads"), None, None),
        P(("groups", "heads"), None, None),
        P(("groups", "heads"), None, None),
        P(("groups", "heads"), None, None),
        P(("groups", "heads"), None, None),
    )
    out_specs = (
        P("groups", "heads", None),
        P(("groups", "heads"), None, None),
        P(("groups", "heads"), None, None),
    )
    return jax.shard_map(
        on_device, mesh=mesh, in_specs=in_specs, out_specs=out_specs, check_vma=False
    )
```

```python
import functools
import math

import jax
import jax.numpy as jnp
from jax import lax
from jax.experimental import pallas as pl
from jax.experimental.pallas import tpu as pltpu
from jax.sharding import PartitionSpec as P

NS = 256
HP = 64
HPG = 32
KVH = 8
HD = 128
PAGE = 16
LANES = 128
SUB = 8
HALF = 512
LEVELS = (128, 64, 32, 16)
LOG2E = math.log2(math.e)
SCORE = LOG2E / math.sqrt(HD)
NONE = -1e30
PAIRS = 6
MATCH = 32768.0
EARLY = 2
VMEM_LIMIT = 64 * 1024 * 1024

f32 = jnp.float32
bf16 = jnp.bfloat16


def iota(shape, dim):
    return lax.broadcasted_iota(jnp.int32, shape, dim)


def dot_nt(left, right):
    return lax.dot_general(left, right, (((1,), (1,)), ((), ())), preferred_element_type=f32)


def stack_rows(source, held):
    steps, rows = source.shape[0], source.shape[1]
    held[...] = jnp.zeros_like(held)
    for k in range(steps):
        held[k * rows : (k + 1) * rows, :] = source[k].astype(f32)


def spare(blocks, taken):
    return [(row, b) for row in range(PAIRS, SUB) for b in range(blocks)][taken : taken + PAIRS]


def lift(value, slots):
    row = iota(value.shape[:2] + (LANES,), 1)
    found = jnp.zeros(row.shape, f32)
    for pair, (at, b) in enumerate(slots):
        one = value[:, at : at + 1, b * LANES : (b + 1) * LANES]
        found = jnp.where(row == pair, jnp.broadcast_to(one, row.shape), found)
    return found


def exchange(blocks):
    if len(blocks) == 1:
        return [lax.all_to_all(blocks[0], "heads", split_axis=0, concat_axis=0, tiled=True)]
    count = len(blocks)
    return [blocks[0]] + [
        lax.ppermute(blocks[n], "heads", [(d, (d + n) % count) for d in range(count)]) for n in range(1, count)
    ]


def leave(held, outs):
    if len(outs) == 1:
        return [(held, outs[0])]
    me = lax.axis_index("heads")
    return [(held.at[lax.rem(me + n, len(outs))], out) for n, out in enumerate(outs)]


def arrive(ins, held):
    if len(ins) == 1:
        return [(ins[0], held)]
    me = lax.axis_index("heads")
    count = len(ins)
    return [(one, held.at[lax.rem(me + count - n, count)]) for n, one in enumerate(ins)]


def fetches(pairs, sems):
    copies = [pltpu.make_async_copy(src, dst, sems.at[n]) for n, (src, dst) in enumerate(pairs)]
    for copy in copies:
        copy.start()
    return copies


def pack_kernel(group, ways, q_any, c_any, *refs):
    *outs, held, q_ref, c_ref, q_held, c_held, rest, sems = refs
    owners = held.shape[0]
    for copy in fetches([(q_any, q_ref), (c_any, c_ref)], sems):
        copy.wait()
    stack_rows(q_ref, q_held)
    stack_rows(c_ref, c_held)
    span = 2 * HALF
    slots = spare(HALF // LANES + 1, 0)
    rest[...] = jnp.zeros_like(rest)
    for e in range(c_ref.shape[2] // NS):
        rest[e, :PAIRS, HALF:] = c_held[:PAIRS, e * NS : e * NS + LANES]
        for pair, (row, b) in enumerate(slots):
            rest[e, row : row + 1, b * LANES : (b + 1) * LANES] = c_held[
                pair : pair + 1, e * NS + LANES : (e + 1) * NS
            ]
    real = iota((SUB, HALF), 0) < PAIRS
    for d in range(0, owners, 2):
        v, e = d // ways, (d * group) // HPG
        low = jnp.where(real, q_held[:, v * span : v * span + HALF], rest[e, :, :HALF])
        high = jnp.where(real, q_held[:, v * span + HALF : (v + 1) * span], rest[e, :, :HALF])
        for n, one in enumerate((low, high)):
            held[d + n, :, :HALF] = one.astype(bf16)
            held[d + n, :, HALF:] = rest[e, :, HALF:].astype(bf16)
    for copy in fetches(leave(held, outs), sems):
        copy.wait()


def head_factors(first, dt_ref, rate_ref, skip_ref, len_ref, levels, w_in, w_out, w_skip, w_tail):
    group, prompts, length = dt_ref.shape
    row = iota((prompts, length), 0)
    lens = jnp.zeros((prompts, length), jnp.int32)
    for r in range(prompts):
        lens = jnp.where(row == r, len_ref[r], lens)
    valid = iota((prompts, length), 1) < lens
    moved = [jnp.where(valid, dt_ref[h].astype(f32), 0.0) for h in range(group)]
    every = jnp.concatenate(moved, axis=0).astype(bf16)
    j = iota((length, length), 0)
    i = iota((length, length), 1)
    rates = [rate_ref[first + h] * LOG2E for h in range(group)]
    if w_tail is not None:
        after = jnp.where(j > i, 1.0, 0.0).astype(bf16)
        total = jnp.dot(every, after, preferred_element_type=f32)
        for h in range(group):
            part = total[h * prompts : (h + 1) * prompts]
            w_tail[:, h, :] = jnp.exp2(-(rates[h] * part)) * moved[h]
    if not levels:
        return
    for h in range(group):
        w_skip[:, h, :] = jnp.where(valid, skip_ref[first + h], 0.0)
    for l, n in enumerate(levels):
        middle = (i // (2 * n)) * (2 * n) + (n - 1)
        signs = (jnp.where(j <= i, 1.0, 0.0) - jnp.where(j <= middle, 1.0, 0.0)).astype(bf16)
        total = jnp.dot(every, signs, preferred_element_type=f32)
        for h in range(group):
            gap = rates[h] * total[h * prompts : (h + 1) * prompts]
            if n == LEVELS[-1]:
                up, down = jnp.exp2(gap), jnp.exp2(-gap)
            else:
                up, down = jnp.exp2(jnp.minimum(gap, 0.0)), jnp.exp2(-jnp.maximum(gap, 0.0))
            w_in[l, :, h, :] = up * moved[h]
            w_out[l, :, h, :] = jnp.where(valid, down, 0.0)


def level_masks(masks):
    length = masks.shape[-1]
    j = iota((length, length), 0)
    i = iota((length, length), 1)
    for l, n in enumerate(LEVELS):
        same = (j // (2 * n)) == (i // (2 * n))
        if n == LEVELS[-1]:
            keep = same & (j <= i)
        else:
            keep = same & ((j % (2 * n)) < n) & ((i % (2 * n)) >= n)
        masks[l] = jnp.where(keep, 1.0, 0.0).astype(bf16)


def prompt_result(r, x_held, b_held, c_held, w_in, w_out, w_skip, masks, out_held):
    width, length = x_held.shape[1], x_held.shape[2]
    group = width // HP
    half = length // 2
    inputs = x_held[r].astype(f32).reshape(group, HP, length)
    scores = dot_nt(b_held[r], c_held[r]).astype(bf16)
    total = inputs * w_skip[r][:, None, :]
    left, right = total[..., :half], total[..., half:]
    for l, n in enumerate(LEVELS):
        if 2 * n == length:
            scaled = (inputs[..., :half] * w_in[l, r][:, None, :half]).astype(bf16).reshape(width, half)
            added = jnp.dot(scaled, scores[:half, half:], preferred_element_type=f32)
            right = right + added.reshape(group, HP, half) * w_out[l, r][:, None, half:]
        else:
            scaled = (inputs * w_in[l, r][:, None, :]).astype(bf16).reshape(width, length)
            added = jnp.dot(scaled, scores * masks[l], preferred_element_type=f32)
            added = added.reshape(group, HP, length) * w_out[l, r][:, None, :]
            left = left + added[..., :half]
            right = right + added[..., half:]
    out_held[r] = jnp.concatenate([left, right], axis=-1).reshape(width, length).astype(bf16)


def state_kernel(
    rate_any,
    skip_any,
    len_any,
    owner_any,
    table_any,
    slot_any,
    dt_any,
    x_any,
    b_any,
    c_any,
    state_any,
    mark_any,
    hot_ref,
    req_ref,
    out_any,
    x_held,
    b_held,
    c_held,
    out_held,
    w_in,
    w_out,
    w_skip,
    w_tail,
    masks,
    state_held,
    mark_held,
    rate_ref,
    skip_ref,
    len_ref,
    owner_ref,
    table_ref,
    slot_ref,
    dt_ref,
    x_sem,
    b_sem,
    c_sem,
    out_sem,
    state_sem,
    mark_sem,
    sems,
):
    group, prompts, length = dt_ref.shape
    smalls = fetches(
        [
            (dt_any, dt_ref),
            (rate_any, rate_ref),
            (skip_any, skip_ref),
            (len_any, len_ref),
            (owner_any, owner_ref),
            (table_any, table_ref),
            (slot_any, slot_ref),
        ],
        sems,
    )
    me = lax.axis_index("heads")
    first = me * group
    column = pl.multiple_of((first // HPG) * NS, NS)

    def x_copy(r):
        return pltpu.make_async_copy(x_any.at[r], x_held.at[r], x_sem.at[r])

    def b_copy(r):
        return pltpu.make_async_copy(b_any.at[r, :, pl.ds(column, NS)], b_held.at[r], b_sem.at[r])

    def c_copy(r):
        return pltpu.make_async_copy(c_any.at[r, :, pl.ds(column, NS)], c_held.at[r], c_sem.at[r])

    def out_copy(r):
        return pltpu.make_async_copy(out_held.at[r], out_any.at[r], out_sem.at[r])

    def state_copy(r):
        return pltpu.make_async_copy(state_held.at[r], state_any.at[r], state_sem.at[r])

    for r in range(prompts):
        x_copy(r).start()
        b_copy(r).start()
    for r in range(EARLY):
        c_copy(r).start()
    for copy in smalls:
        copy.wait()

    head_factors(
        first, dt_ref, rate_ref, skip_ref, len_ref, LEVELS if EARLY else (), w_in, w_out, w_skip, w_tail
    )

    spread = table_ref.shape[1] // owner_ref.shape[1]
    per_head = table_ref.shape[1] // KVH
    offset, lane = iota((PAGE, LANES), 0), iota((PAGE, LANES), 1)
    for n, holder in enumerate((me, me + 1 - 2 * lax.rem(me, 2))):
        for r in range(prompts):
            for page in range(spread):
                entry = holder * spread + page
                row = table_ref[r, entry] - holder * (prompts * spread)
                begin = lax.rem(entry, per_head) * PAGE
                inside = (lane == r) & (offset < len_ref[r] - begin)
                block = jnp.where(inside, MATCH, 0.0).astype(bf16)
                mark_held[n, pl.ds(pl.multiple_of(row * PAGE, PAGE), PAGE), :] = block
    mark_copy = pltpu.make_async_copy(mark_held, mark_any, mark_sem)
    mark_copy.start()

    owners = owner_ref.shape[1]
    rows_dev = slot_ref.shape[0] // owners
    inner = iota((2 * SUB, LANES), 0)
    lanes = iota((2 * SUB, LANES), 1)

    def fill(s, _):
        block = jnp.full((2 * SUB, LANES), -2, jnp.int32)
        for n in range(2):
            for i in range(rows_dev):
                target = owner_ref[slot_ref[(2 * s + n) * rows_dev + i], 2 * s + n]
                block = jnp.where((inner // SUB == n) & (inner % rows_dev == i), target, block)
        place = pl.ds(pl.multiple_of(s * 2 * SUB, 2 * SUB), 2 * SUB)
        req_ref[place, :] = block
        hot_ref[place, :] = jnp.where(lanes == block, 1.0, 0.0).astype(bf16)
        return 0

    lax.fori_loop(0, owners // 2, fill, 0)

    def one(r, _):
        x_copy(r).wait()
        b_copy(r).wait()
        width = x_held.shape[1]
        inputs = x_held[r].astype(f32).reshape(group, HP, length)
        scaled = (inputs * w_tail[r][:, None, :]).astype(bf16).reshape(width, length)
        state_held[r] = jnp.dot(scaled, b_held[r], preferred_element_type=f32).astype(bf16)
        state_copy(r).start()
        return 0

    lax.fori_loop(0, prompts, one, 0, unroll=2)

    if EARLY:
        level_masks(masks)

        def early(r, _):
            c_copy(r).wait()
            prompt_result(r, x_held, b_held, c_held, w_in, w_out, w_skip, masks, out_held)
            out_copy(r).start()
            return 0

        lax.fori_loop(0, EARLY, early, 0, unroll=2)
        for r in range(EARLY):
            out_copy(r).wait()
    for r in range(prompts):
        state_copy(r).wait()
    mark_copy.wait()


def serve_kernel(blocks_in, *refs):
    recv_anys, refs = refs[:blocks_in], refs[blocks_in:]
    pages_any, other_any, mark_any, hot_any, req_any, state_any, *refs = refs
    outs, refs = refs[:blocks_in], refs[blocks_in:]
    (
        back_held,
        recv_held,
        key_ref,
        value_ref,
        hot_ref,
        req_ref,
        state_ref,
        query_ref,
        score_ref,
        recv_sem,
        state_sem,
        sems,
    ) = refs
    rows = recv_held.shape[0] * SUB
    held = pages_any.shape[0]
    prompts, width = state_ref.shape[0], state_ref.shape[1]
    mine, other = pl.ds(0, held), pl.ds(held, held)
    received = fetches(arrive(recv_anys, recv_held), recv_sem)
    copies = fetches(
        [
            (hot_any, hot_ref),
            (pages_any.at[:, pl.ds(0, HD)], key_ref.at[mine, pl.ds(0, HD)]),
            (other_any.at[:, pl.ds(0, HD)], key_ref.at[other, pl.ds(0, HD)]),
            (mark_any.at[0], key_ref.at[mine, pl.ds(HD, LANES)]),
            (mark_any.at[1], key_ref.at[other, pl.ds(HD, LANES)]),
            (pages_any.at[:, pl.ds(HD, HD)], value_ref.at[mine]),
            (other_any.at[:, pl.ds(HD, HD)], value_ref.at[other]),
            (req_any, req_ref),
        ],
        sems,
    )
    states = fetches([(state_any.at[r], state_ref.at[r]) for r in range(prompts)], state_sem)
    for copy in received:
        copy.wait()
    copies[0].wait()
    heads = HALF // HD
    given = recv_held[...].astype(f32)
    for g in range(heads):
        one = given[..., g * HD : (g + 1) * HD].reshape(rows, HD)
        query_ref[g * rows : (g + 1) * rows, :HD] = one.astype(bf16)
        query_ref[g * rows : (g + 1) * rows, HD:] = hot_ref[...]
    for copy in copies[1:5]:
        copy.wait()
    keys = key_ref.shape[0]
    chunk = min(keys, 2 * NS)
    widest = jnp.full((heads * rows, LANES), NONE, f32)
    for k in range(0, keys, chunk):
        scores = dot_nt(query_ref[...], key_ref[k : k + chunk, :])
        score_ref[:, k : k + chunk] = scores
        for b in range(0, chunk, LANES):
            widest = jnp.maximum(widest, scores[:, b : b + LANES])
    highest = jnp.max(widest, axis=1, keepdims=True)
    for copy in copies[5:]:
        copy.wait()
    total = jnp.zeros((heads * rows, LANES), f32)
    value = jnp.zeros((heads * rows, HD), f32)
    for k in range(0, keys, chunk):
        weight = jnp.exp2((score_ref[:, k : k + chunk] - highest) * SCORE)
        for b in range(0, chunk, LANES):
            total = total + weight[:, b : b + LANES]
        value = value + jnp.dot(weight.astype(bf16), value_ref[k : k + chunk, :], preferred_element_type=f32)
    total = jnp.sum(total, axis=1, keepdims=True)
    value = value / total
    result = jnp.where(highest > 0.5 * MATCH, (highest - MATCH) * SCORE + jnp.log2(total), NONE)
    lane = iota((rows, LANES), 1)
    sums = jnp.zeros((rows, LANES), f32)
    for g in range(heads):
        sums = jnp.where(lane % 4 == g, result[g * rows : (g + 1) * rows], sums)
    high = sums.astype(bf16).astype(f32)
    rest = sums - high
    middle = rest.astype(bf16).astype(f32)
    piece = lane % 16 // 4
    pieces = jnp.where(piece == 0, high, jnp.where(piece == 1, middle, rest - middle))
    pair = iota((rows, LANES), 0) % SUB
    pieces = jnp.where((lane // 16 == pair) & (piece < 3), pieces, 0.0)
    packed = jnp.sum(pieces.reshape(rows // SUB, SUB, LANES), axis=1, keepdims=True)

    ending = lift(given, spare(heads + 1, 0))
    readout = jnp.concatenate([given[..., HALF:], ending], axis=-1).reshape(rows, NS)
    target = jnp.concatenate([req_ref[...], req_ref[...]], axis=-1)
    found = jnp.zeros((rows, width), f32)
    for r in range(prompts):
        picked = jnp.where(target == r, readout, 0.0).astype(bf16)
        states[r].wait()
        found = found + dot_nt(picked, state_ref[r])
    if width < LANES:
        found = jnp.concatenate([found, jnp.zeros((rows, LANES - width), f32)], axis=-1)
    blocks = [value[g * rows : (g + 1) * rows] for g in range(heads)]
    blocks += [found[:, b : b + LANES] for b in range(0, found.shape[1], LANES)]
    blocks = [one.reshape(rows // SUB, SUB, LANES) for one in blocks]
    row = iota((rows // SUB, SUB, LANES), 1)
    last = blocks.pop()
    blocks[0] = jnp.where(row == PAIRS, jnp.broadcast_to(packed, row.shape), blocks[0])
    for n, (at, b) in enumerate(spare(len(blocks), 1)):
        one = jnp.broadcast_to(last[:, n : n + 1, :], row.shape)
        blocks[b] = jnp.where(row == at, one, blocks[b])
    for b, one in enumerate(blocks):
        back_held[:, :, b * LANES : (b + 1) * LANES] = one.astype(bf16)
    for copy in fetches(leave(back_held, outs), recv_sem):
        copy.wait()


def prompt_kernel(
    rate_any,
    skip_any,
    len_any,
    dt_any,
    rates_any,
    skips_any,
    q_any,
    fresh_any,
    sx_any,
    sb_any,
    sc_any,
    sdt_any,
    x_any,
    b_any,
    c_any,
    after_any,
    early_any,
    out_any,
    own_ref,
    ownsum_ref,
    fade_ref,
    local_ref,
    x_held,
    b_held,
    c_held,
    out_held,
    w_in,
    w_out,
    w_skip,
    masks,
    fresh_held,
    q_held,
    c_rows,
    x_rows,
    rate_ref,
    skip_ref,
    len_ref,
    dt_ref,
    rates_ref,
    skips_ref,
    q_ref,
    fresh_ref,
    sx_ref,
    sb_ref,
    sc_ref,
    sdt_ref,
    x_sem,
    b_sem,
    c_sem,
    out_sem,
    sems,
):
    group, prompts, length = dt_ref.shape
    smalls = fetches(
        [
            (dt_any, dt_ref),
            (rate_any, rate_ref),
            (skip_any, skip_ref),
            (len_any, len_ref),
            (rates_any, rates_ref),
            (skips_any, skips_ref),
            (q_any, q_ref),
            (fresh_any, fresh_ref),
            (sx_any, sx_ref),
            (sb_any, sb_ref),
            (sc_any, sc_ref),
            (sdt_any, sdt_ref),
        ],
        sems,
    )
    me = lax.axis_index("heads")
    first = me * group
    column = pl.multiple_of((first // HPG) * NS, NS)

    def x_copy(r):
        return pltpu.make_async_copy(x_any.at[r], x_held.at[r], x_sem.at[r])

    def b_copy(r):
        return pltpu.make_async_copy(b_any.at[r, :, pl.ds(column, NS)], b_held.at[r], b_sem.at[r])

    def c_copy(r):
        return pltpu.make_async_copy(c_any.at[r, :, pl.ds(column, NS)], c_held.at[r], c_sem.at[r])

    def out_copy(r):
        return pltpu.make_async_copy(out_held.at[r], out_any.at[r], out_sem.at[r])

    for r in range(EARLY, prompts):
        x_copy(r).start()
        b_copy(r).start()
        c_copy(r).start()
    for copy in smalls:
        copy.wait()

    head_factors(first, dt_ref, rate_ref, skip_ref, len_ref, LEVELS, w_in, w_out, w_skip, None)
    level_masks(masks)

    def one(r, _):
        x_copy(r).wait()
        b_copy(r).wait()
        c_copy(r).wait()
        prompt_result(r, x_held, b_held, c_held, w_in, w_out, w_skip, masks, out_held)
        out_copy(r).start()
        return 0

    lax.fori_loop(EARLY, prompts, one, 0, unroll=2)
    own_attention(q_ref, fresh_ref, q_held, fresh_held, own_ref, ownsum_ref)
    own_mixer(rates_ref, skips_ref, sx_ref, sb_ref, sc_ref, sdt_ref, c_rows, x_rows, fade_ref, local_ref)
    for r in range(EARLY, prompts):
        out_copy(r).wait()


def own_attention(q_ref, fresh_ref, q_held, fresh_held, own_ref, ownsum_ref):
    steps, rows = fresh_ref.shape[0], fresh_ref.shape[1]
    stack_rows(q_ref, q_held)
    stack_rows(fresh_ref, fresh_held)
    count = HALF // HD * 2 * SUB
    pair = iota((count, SUB), 0) % SUB
    key = iota((count, SUB), 1)
    seen = (key % rows == pair % rows) & (key <= pair) & (key < rows * steps)
    seen = seen | ((pair >= rows * steps) & (key == 0))
    for v in range(KVH):
        starts = [v * 2 * HALF + half + g for g in range(0, HALF, HD) for half in (0, HALF)]
        query = jnp.concatenate([q_held[:, at : at + HD] for at in starts], axis=0).astype(bf16)
        keys = fresh_held[:, v * HD : (v + 1) * HD].astype(bf16)
        values = fresh_held[:, (KVH + v) * HD : (KVH + v + 1) * HD].astype(bf16)
        scores = jnp.where(seen, dot_nt(query, keys) * SCORE, NONE)
        highest = jnp.max(scores, axis=1, keepdims=True)
        weight = jnp.exp2(scores - highest)
        total = jnp.sum(weight, axis=1, keepdims=True)
        weight = (weight / total).astype(bf16)
        own_ref[v] = jnp.dot(weight, values, preferred_element_type=f32)
        ownsum_ref[v] = jnp.broadcast_to(highest + jnp.log2(total), (count, HD))


def own_mixer(rates_ref, skips_ref, sx_ref, sb_ref, sc_ref, sdt_ref, c_rows, x_rows, fade_ref, local_ref):
    steps, rows, heads = sdt_ref.shape
    stack_rows(sc_ref, c_rows)
    for u in range(steps):
        given = sx_ref[u].astype(f32)
        for k in range(SUB // rows):
            x_rows[u, k * rows : (k + 1) * rows, :] = given
    pair = iota((SUB, heads), 0)
    step = pair // rows
    live = pair < rows * steps
    head = iota((SUB, heads), 1)

    def spread_rows(ref, u):
        given = ref[u].astype(f32)
        return jnp.concatenate([given] * (SUB // rows), axis=0)

    rates = jnp.broadcast_to(rates_ref[...], (SUB, heads)) * LOG2E
    skips = jnp.broadcast_to(skips_ref[...], (SUB, heads))
    moved = [spread_rows(sdt_ref, u) for u in range(steps)]
    kept = [jnp.where(u <= step, moved[u], 0.0) for u in range(steps)]
    parts = [jnp.where(live, jnp.exp2(-(rates * sum(kept))), 0.0)]
    for u in range(steps):
        products = c_rows[...] * spread_rows(sb_ref, u)
        inner = jnp.zeros((SUB, heads), f32)
        for e in range(products.shape[1] // NS):
            found = jnp.sum(products[:, e * NS : (e + 1) * NS], axis=1, keepdims=True)
            inner = jnp.where(head // HPG == e, found, inner)
        gap = jnp.zeros((SUB, heads), f32)
        for t in range(u + 1, steps):
            gap = gap + kept[t]
        weight = jnp.where(u <= step, jnp.exp2(-(rates * gap)) * moved[u] * inner, 0.0)
        weight = weight + jnp.where(u == step, skips, 0.0)
        parts.append(jnp.where(live, weight, 0.0))
    stacked = jnp.concatenate(parts, axis=0)
    high = stacked.astype(bf16)
    low = (stacked - high.astype(f32)).astype(bf16)
    both = jnp.concatenate([high.astype(f32), low.astype(f32)], axis=0)
    count = stacked.shape[0]
    chunk = SUB * HP
    widen = jnp.where(iota((heads, chunk), 0) % SUB == iota((heads, chunk), 1) // HP, 1.0, 0.0).astype(bf16)
    lane = iota(both.shape, 1)
    for d in range(heads // SUB):
        picked = jnp.where(lane // SUB == d, both, 0.0).astype(bf16)
        wide = jnp.dot(picked, widen, preferred_element_type=f32)
        wide = wide[:count] + wide[count:]
        columns = slice(d * chunk, (d + 1) * chunk)
        fade_ref[:, columns] = wide[:SUB]
        value = jnp.zeros((SUB, chunk), f32)
        for u in range(steps):
            value = value + wide[(u + 1) * SUB : (u + 2) * SUB] * x_rows[u, :, columns]
        local_ref[:, columns] = value


def merge_kernel(width, blocks_in, *refs):
    back_anys, refs = refs[:blocks_in], refs[blocks_in:]
    own_any, ownsum_any, fade_any, local_any, mixer_ref, attention_ref, *refs = refs
    back_ref, own_ref, ownsum_ref, fade_ref, local_ref, mixed, attended, back_sem, sems = refs
    copies = fetches(arrive(back_anys, back_ref), back_sem)
    copies += fetches(
        [
            (own_any, own_ref),
            (ownsum_any, ownsum_ref),
            (fade_any, fade_ref),
            (local_any, local_ref),
        ],
        sems,
    )
    for copy in copies:
        copy.wait()
    owners = back_ref.shape[0]
    ways = owners // KVH
    steps, rows = mixer_ref.shape[0], mixer_ref.shape[1]
    for d in range(0, owners, 2):
        block = back_ref[d : d + 2].astype(f32)
        ending = lift(block, spare(back_ref.shape[2] // LANES, 1))
        if back_ref.shape[2] > HALF:
            ending = jnp.concatenate([block[..., HALF:], ending], axis=-1)
        found = ending[..., :width]
        found = jnp.concatenate([found[0], found[1]], axis=-1)
        columns = slice(d * width, (d + 2) * width)
        mixed[:, columns] = found * fade_ref[:, columns] + local_ref[:, columns]
    for k in range(steps):
        mixer_ref[k] = mixed[k * rows : (k + 1) * rows, :].astype(bf16)
    lane = iota((2, SUB, LANES), 2)
    mine = (lane // 16 == iota((2, SUB, LANES), 1)) & (lane % 16 < 12)
    for v in range(KVH):
        blocks, pieces = [], []
        for d in range(v * ways, (v + 1) * ways, 2):
            block = back_ref[d : d + 2, :, :HALF].astype(f32)
            packed = block[:, PAIRS : PAIRS + 1, :LANES]
            blocks.append(block.reshape(2 * SUB, HALF))
            pieces.append(jnp.where(mine, jnp.broadcast_to(packed, (2, SUB, LANES)), 0.0))
        for g in range(HALF // HD):
            part = slice(g * 2 * SUB, (g + 1) * 2 * SUB)
            own_sum = ownsum_ref[v, part, :]
            wide = []
            for piece in pieces:
                one = jnp.sum(jnp.where(lane % 4 == g, piece, 0.0), axis=-1, keepdims=True)
                wide.append(jnp.broadcast_to(one, (2, SUB, HD)).reshape(2 * SUB, HD))
            highest = functools.reduce(jnp.maximum, wide, own_sum)
            weight = jnp.exp2(own_sum - highest)
            total = weight
            value = weight * own_ref[v, part, :]
            for one, block in zip(wide, blocks):
                weight = jnp.exp2(one - highest)
                total = total + weight
                value = value + weight * block[:, g * HD : (g + 1) * HD]
            value = value / total
            start = v * 2 * HALF + g * HD
            attended[:, start : start + HD] = value[:SUB]
            attended[:, start + HALF : start + HALF + HD] = value[SUB:]
    for k in range(steps):
        attention_ref[k] = attended[k * rows : (k + 1) * rows, :].astype(bf16)


def call(kernel, out_shape, in_spaces, out_spaces, scratch, cost, aliases=None):
    def spec(space):
        return pl.BlockSpec(memory_space=space)

    return pl.pallas_call(
        kernel,
        out_shape=out_shape,
        in_specs=[spec(space) for space in in_spaces],
        out_specs=jax.tree.map(spec, out_spaces),
        scratch_shapes=scratch,
        input_output_aliases=aliases or {},
        compiler_params=pltpu.CompilerParams(vmem_limit_bytes=VMEM_LIMIT),
        cost_estimate=pl.CostEstimate(flops=cost[0], bytes_accessed=cost[1], transcendentals=0),
    )


def on_device(
    prompt_x,
    prompt_b,
    prompt_c,
    prompt_dt,
    decay_rate,
    skip_gain,
    lengths,
    owner_list,
    page_table,
    cache_pages,
    row_slot,
    step_x,
    step_b,
    step_c,
    step_dt,
    queries,
    fresh_cache,
):
    owners = lax.axis_size("heads")
    ways = owners // KVH
    group, prompts, length = prompt_dt.shape
    width = prompt_x.shape[1]
    keys = cache_pages.shape[0] * PAGE
    steps = step_x.shape[1]
    all_rows = owners * SUB
    shape = jax.ShapeDtypeStruct
    smem, vmem, hbm = pltpu.SMEM, pltpu.VMEM, pltpu.HBM
    sem = pltpu.SemaphoreType.DMA((prompts,))
    levels = len(LEVELS)
    step_x, step_b, step_c, step_dt, queries, fresh_cache = (
        jnp.swapaxes(one, 0, 1) for one in (step_x, step_b, step_c, step_dt, queries, fresh_cache)
    )
    owner_list = owner_list.T

    def like(space, array):
        return space(array.shape, array.dtype)

    def sems(count):
        return pltpu.SemaphoreType.DMA((count,))

    other_pages = lax.ppermute(cache_pages, "heads", [(d, d + 1 - 2 * (d % 2)) for d in range(owners)])
    parts = owners if owners <= 16 else 1
    piece = (SUB,) if parts > 1 else (owners, SUB)
    moved = sems(max(parts, 2))
    send = call(
        functools.partial(pack_kernel, group, ways),
        (shape(piece + (HALF + LANES,), bf16),) * parts,
        [hbm, hbm],
        (hbm,) * parts,
        [
            vmem((owners, SUB, HALF + LANES), bf16),
            like(vmem, queries),
            like(vmem, step_c),
            vmem((SUB, queries.shape[2]), f32),
            vmem((SUB, step_c.shape[2]), f32),
            vmem((step_c.shape[2] // NS, SUB, HALF + LANES), f32),
            moved,
        ],
        (0, 1 << 19),
    )(queries, step_c)
    recv = exchange(send)

    block = [
        vmem((prompts, width, length), bf16),
        vmem((prompts, length, NS), bf16),
        vmem((prompts, length, NS), bf16),
        vmem((prompts, width, length), bf16),
        vmem((levels, prompts, group, length), f32),
        vmem((levels, prompts, group, length), f32),
        vmem((prompts, group, length), f32),
    ]
    masks = vmem((levels, length, length), bf16)
    work = 2 * width * length * NS
    states, marks, hot, requests, early_out = call(
        state_kernel,
        (
            shape((prompts, width, NS), bf16),
            shape((2, keys, LANES), bf16),
            shape((all_rows, LANES), bf16),
            shape((all_rows, LANES), jnp.int32),
            shape(prompt_x.shape, bf16),
        ),
        [hbm] * 10,
        (hbm, hbm, vmem, vmem, hbm),
        block
        + [vmem((prompts, group, length), f32), masks]
        + [vmem((prompts, width, NS), bf16), vmem((2, keys, LANES), bf16)]
        + [like(smem, one) for one in (decay_rate, skip_gain, lengths, owner_list, page_table, row_slot)]
        + [like(vmem, prompt_dt), sem, sem, sem, sem, sem, pltpu.SemaphoreType.DMA, sems(7)],
        (work * (prompts + 5 * EARLY), 6 << 20),
    )(
        decay_rate,
        skip_gain,
        lengths,
        owner_list,
        page_table,
        row_slot,
        prompt_dt,
        prompt_x,
        prompt_b,
        prompt_c,
    )

    returns = HALF + max(LANES, width) - LANES
    back = call(
        functools.partial(serve_kernel, parts),
        (shape(piece + (returns,), bf16),) * parts,
        [hbm] * (parts + 6),
        (hbm,) * parts,
        [
            vmem((owners, SUB, returns), bf16),
            vmem((owners, SUB, HALF + LANES), bf16),
            vmem((2 * keys, HD + LANES), bf16),
            vmem((2 * keys, HD), bf16),
            like(vmem, hot),
            like(vmem, requests),
            like(vmem, states),
            vmem((HALF // HD * all_rows, HD + LANES), bf16),
            vmem((HALF // HD * all_rows, 2 * keys), f32),
            moved,
            sem,
            sems(8),
        ],
        (8 * all_rows * keys * HD, 4 << 20),
    )(
        *recv,
        cache_pages.reshape(keys, 2 * HD),
        other_pages.reshape(keys, 2 * HD),
        marks,
        hot,
        requests,
        states,
    )
    returned = exchange(back)

    count = HALF // HD * 2 * SUB
    channels = step_x.shape[2]
    rates, skips = decay_rate.reshape(1, -1), skip_gain.reshape(1, -1)
    prompt_out, own, own_sum, fade, local = call(
        prompt_kernel,
        (
            shape(prompt_x.shape, bf16),
            shape((KVH, count, HD), f32),
            shape((KVH, count, HD), f32),
            shape((SUB, channels), f32),
            shape((SUB, channels), f32),
        ),
        [hbm] * 17,
        (hbm, vmem, vmem, vmem, vmem),
        block
        + [
            masks,
            vmem((SUB, fresh_cache.shape[2]), f32),
            vmem((SUB, queries.shape[2]), f32),
            vmem((SUB, step_c.shape[2]), f32),
            vmem((steps, SUB, channels), f32),
            like(smem, decay_rate),
            like(smem, skip_gain),
            like(smem, lengths),
            like(vmem, prompt_dt),
            like(vmem, rates),
            like(vmem, skips),
            like(vmem, queries),
            like(vmem, fresh_cache),
            like(vmem, step_x),
            like(vmem, step_b),
            like(vmem, step_c),
            like(vmem, step_dt),
            sem,
            sem,
            sem,
            sem,
            sems(12),
        ],
        (work * 5 * (prompts - EARLY), 8 << 20),
        {16: 0},
    )(
        decay_rate,
        skip_gain,
        lengths,
        prompt_dt,
        rates,
        skips,
        queries,
        fresh_cache,
        step_x,
        step_b,
        step_c,
        step_dt,
        prompt_x,
        prompt_b,
        prompt_c,
        back[0],
        early_out,
    )

    mixer_out, attention_out = call(
        functools.partial(merge_kernel, width, parts),
        (shape(step_x.shape, bf16), shape(queries.shape, bf16)),
        [hbm] * (parts + 4),
        (vmem, vmem),
        [vmem((owners, SUB, returns), bf16)]
        + [like(vmem, one) for one in (own, own_sum, fade, local)]
        + [vmem((SUB, channels), f32), vmem((SUB, queries.shape[2]), f32), moved, sems(4)],
        (0, 2 << 20),
    )(*returned, own, own_sum, fade, local)
    return (prompt_out, jnp.swapaxes(mixer_out, 0, 1), jnp.swapaxes(attention_out, 0, 1))


def solution(mesh):
    in_specs = (
        P("groups", "heads", None),
        P("groups", None, None),
        P("groups", None, None),
        P("heads", "groups", None),
        P(),
        P(),
        P("groups"),
        P("groups", None),
        P("groups", None),
        P(("groups", "heads"), None, None),
        P("groups"),
        P(("groups", "heads"), None, None),
        P(("groups", "heads"), None, None),
        P(("groups", "heads"), None, None),
        P(("groups", "heads"), None, None),
        P(("groups", "heads"), None, None),
        P(("groups", "heads"), None, None),
    )
    out_specs = (
        P("groups", "heads", None),
        P(("groups", "heads"), None, None),
        P(("groups", "heads"), None, None),
    )
    return jax.shard_map(
        on_device, mesh=mesh, in_specs=in_specs, out_specs=out_specs, check_vma=False
    )
```

```python
import functools
import math

import jax
import jax.numpy as jnp
from jax import lax
from jax.experimental import pallas as pl
from jax.experimental.pallas import tpu as pltpu
from jax.sharding import PartitionSpec as P

NS = 256
HP = 64
HPG = 32
KVH = 8
HD = 128
PAGE = 16
LANES = 128
SUB = 8
HALF = 512
LEVELS = (128, 64, 32, 16)
LOG2E = math.log2(math.e)
SCORE = LOG2E / math.sqrt(HD)
NONE = -1e30
PAIRS = 6
MATCH = 32768.0
AHEAD = 2
EARLY = 2
VMEM_LIMIT = 64 * 1024 * 1024

f32 = jnp.float32
bf16 = jnp.bfloat16


def iota(shape, dim):
    return lax.broadcasted_iota(jnp.int32, shape, dim)


def dot_nt(left, right):
    return lax.dot_general(left, right, (((1,), (1,)), ((), ())), preferred_element_type=f32)


def stack_rows(source, held):
    steps, rows = source.shape[0], source.shape[1]
    held[...] = jnp.zeros_like(held)
    for k in range(steps):
        held[k * rows : (k + 1) * rows, :] = source[k].astype(f32)


def spare(blocks, taken):
    return [(row, b) for row in range(PAIRS, SUB) for b in range(blocks)][taken : taken + PAIRS]


def lift(value, slots):
    row = iota(value.shape[:2] + (LANES,), 1)
    found = jnp.zeros(row.shape, f32)
    for pair, (at, b) in enumerate(slots):
        one = value[:, at : at + 1, b * LANES : (b + 1) * LANES]
        found = jnp.where(row == pair, jnp.broadcast_to(one, row.shape), found)
    return found


def fetches(pairs, sems, first=0):
    copies = [pltpu.make_async_copy(src, dst, sems.at[first + n]) for n, (src, dst) in enumerate(pairs)]
    for copy in copies:
        copy.start()
    return copies


def pack_kernel(group, ways, q_any, c_any, out_ref, q_ref, c_ref, q_held, c_held, rest, sems):
    owners = out_ref.shape[0] // SUB
    for copy in fetches([(q_any, q_ref), (c_any, c_ref)], sems):
        copy.wait()
    stack_rows(q_ref, q_held)
    stack_rows(c_ref, c_held)
    span = 2 * HALF
    slots = spare(HALF // LANES + 1, 0)
    rest[...] = jnp.zeros_like(rest)
    for e in range(c_ref.shape[2] // NS):
        rest[e, :PAIRS, HALF:] = c_held[:PAIRS, e * NS : e * NS + LANES]
        for pair, (row, b) in enumerate(slots):
            rest[e, row : row + 1, b * LANES : (b + 1) * LANES] = c_held[
                pair : pair + 1, e * NS + LANES : (e + 1) * NS
            ]
    real = iota((SUB, HALF), 0) < PAIRS
    for d in range(0, owners, 2):
        v, e = d // ways, (d * group) // HPG
        low = jnp.where(real, q_held[:, v * span : v * span + HALF], rest[e, :, :HALF])
        high = jnp.where(real, q_held[:, v * span + HALF : (v + 1) * span], rest[e, :, :HALF])
        out_ref[d * SUB : (d + 2) * SUB, :HALF] = jnp.concatenate([low, high], axis=0).astype(bf16)
        end = rest[e, :, HALF:]
        out_ref[d * SUB : (d + 2) * SUB, HALF:] = jnp.concatenate([end, end], axis=0).astype(bf16)


def sign_tables(signs, tail):
    length = signs.shape[-1]
    j = iota((length, length), 0)
    i = iota((length, length), 1)
    for l, n in enumerate(LEVELS):
        middle = (i // (2 * n)) * (2 * n) + (n - 1)
        signs[l] = (jnp.where(j <= i, 1.0, 0.0) - jnp.where(j <= middle, 1.0, 0.0)).astype(bf16)
    if tail:
        signs[len(LEVELS)] = jnp.where(j > i, 1.0, 0.0).astype(bf16)


def head_factors(first, dt_ref, rate_ref, skip_ref, len_ref, signs, w_in, w_out, w_skip, w_tail):
    group, prompts, length = dt_ref.shape
    row = iota((prompts, length), 0)
    lens = jnp.zeros((prompts, length), jnp.int32)
    for r in range(prompts):
        lens = jnp.where(row == r, len_ref[r], lens)
    valid = iota((prompts, length), 1) < lens
    moved = [jnp.where(valid, dt_ref[h].astype(f32), 0.0) for h in range(group)]
    every = jnp.concatenate(moved, axis=0).astype(bf16)
    rates = [rate_ref[first + h] * LOG2E for h in range(group)]
    if w_tail is not None:
        total = jnp.dot(every, signs[len(LEVELS)], preferred_element_type=f32)
        for h in range(group):
            part = total[h * prompts : (h + 1) * prompts]
            w_tail[:, h, :] = jnp.exp2(-(rates[h] * part)) * moved[h]
    for h in range(group):
        w_skip[:, h, :] = jnp.where(valid, skip_ref[first + h], 0.0)
    for l, n in enumerate(LEVELS):
        total = jnp.dot(every, signs[l], preferred_element_type=f32)
        for h in range(group):
            gap = rates[h] * total[h * prompts : (h + 1) * prompts]
            if n == LEVELS[-1]:
                up, down = jnp.exp2(gap), jnp.exp2(-gap)
            else:
                up, down = jnp.exp2(jnp.minimum(gap, 0.0)), jnp.exp2(-jnp.maximum(gap, 0.0))
            w_in[l, :, h, :] = up * moved[h]
            w_out[l, :, h, :] = jnp.where(valid, down, 0.0)


def level_masks(masks):
    length = masks.shape[-1]
    j = iota((length, length), 0)
    i = iota((length, length), 1)
    for l, n in enumerate(LEVELS):
        same = (j // (2 * n)) == (i // (2 * n))
        if n == LEVELS[-1]:
            keep = same & (j <= i)
        else:
            keep = same & ((j % (2 * n)) < n) & ((i % (2 * n)) >= n)
        masks[l] = jnp.where(keep, 1.0, 0.0).astype(bf16)


def prompt_result(r, x_held, b_held, c_held, w_in, w_out, w_skip, masks, out_held):
    width, length = x_held.shape[1], x_held.shape[2]
    group = width // HP
    half = length // 2
    inputs = x_held[r].astype(f32).reshape(group, HP, length)
    scores = dot_nt(b_held[r], c_held[r]).astype(bf16)
    total = inputs * w_skip[r][:, None, :]
    left, right = total[..., :half], total[..., half:]
    for l, n in enumerate(LEVELS):
        if 2 * n == length:
            scaled = (inputs[..., :half] * w_in[l, r][:, None, :half]).astype(bf16).reshape(width, half)
            added = jnp.dot(scaled, scores[:half, half:], preferred_element_type=f32)
            right = right + added.reshape(group, HP, half) * w_out[l, r][:, None, half:]
        else:
            scaled = (inputs * w_in[l, r][:, None, :]).astype(bf16).reshape(width, length)
            added = jnp.dot(scaled, scores * masks[l], preferred_element_type=f32)
            added = added.reshape(group, HP, length) * w_out[l, r][:, None, :]
            left = left + added[..., :half]
            right = right + added[..., half:]
    out_held[r] = jnp.concatenate([left, right], axis=-1).reshape(width, length).astype(bf16)


def state_kernel(
    rate_any,
    skip_any,
    len_any,
    owner_any,
    table_any,
    slot_any,
    dt_any,
    x_any,
    b_any,
    c_any,
    state_any,
    mark_any,
    hot_any,
    req_any,
    out_any,
    x_held,
    b_held,
    c_held,
    out_held,
    w_in,
    w_out,
    w_skip,
    masks,
    signs,
    w_tail,
    state_held,
    mark_held,
    hot_held,
    req_held,
    rate_ref,
    skip_ref,
    len_ref,
    owner_ref,
    table_ref,
    slot_ref,
    dt_ref,
    x_sem,
    b_sem,
    c_sem,
    out_sem,
    state_sem,
    sems,
):
    group, prompts, length = dt_ref.shape
    smalls = fetches(
        [
            (dt_any, dt_ref),
            (rate_any, rate_ref),
            (skip_any, skip_ref),
            (len_any, len_ref),
            (owner_any, owner_ref),
            (table_any, table_ref),
            (slot_any, slot_ref),
        ],
        sems,
    )
    me = lax.axis_index("heads")
    first = me * group
    column = pl.multiple_of((first // HPG) * NS, NS)

    def x_copy(r):
        return pltpu.make_async_copy(x_any.at[r], x_held.at[r], x_sem.at[r])

    def b_copy(r):
        return pltpu.make_async_copy(b_any.at[r, :, pl.ds(column, NS)], b_held.at[r], b_sem.at[r])

    def c_copy(r):
        return pltpu.make_async_copy(c_any.at[r, :, pl.ds(column, NS)], c_held.at[r], c_sem.at[r])

    def out_copy(r):
        return pltpu.make_async_copy(out_held.at[r], out_any.at[r], out_sem.at[r])

    def state_copy(r):
        return pltpu.make_async_copy(state_held.at[r], state_any.at[r], state_sem.at[r])

    def ask(r):
        x_copy(r).start()
        b_copy(r).start()

    for r in range(AHEAD):
        ask(r)
    sign_tables(signs, True)
    level_masks(masks)
    for copy in smalls:
        copy.wait()
    head_factors(first, dt_ref, rate_ref, skip_ref, len_ref, signs, w_in, w_out, w_skip, w_tail)

    def one(r, _):
        @pl.when(r + AHEAD < prompts)
        def _():
            ask(r + AHEAD)

        x_copy(r).wait()
        b_copy(r).wait()
        width = x_held.shape[1]
        inputs = x_held[r].astype(f32).reshape(group, HP, length)
        scaled = (inputs * w_tail[r][:, None, :]).astype(bf16).reshape(width, length)
        state_held[r] = jnp.dot(scaled, b_held[r], preferred_element_type=f32).astype(bf16)
        state_copy(r).start()
        return 0

    lax.fori_loop(0, prompts, one, 0, unroll=2)
    for r in range(EARLY):
        c_copy(r).start()

    spread = table_ref.shape[1] // owner_ref.shape[1]
    per_head = table_ref.shape[1] // KVH
    offset, lane = iota((PAGE, LANES), 0), iota((PAGE, LANES), 1)
    for n, holder in enumerate((me, me + 1 - 2 * lax.rem(me, 2))):
        for r in range(prompts):
            for page in range(spread):
                entry = holder * spread + page
                row = table_ref[r, entry] - holder * (prompts * spread)
                begin = lax.rem(entry, per_head) * PAGE
                inside = (lane == r) & (offset < len_ref[r] - begin)
                block = jnp.where(inside, MATCH, 0.0).astype(bf16)
                mark_held[n, pl.ds(pl.multiple_of(row * PAGE, PAGE), PAGE), :] = block

    owners = owner_ref.shape[1]
    rows_dev = slot_ref.shape[0] // owners
    inner = iota((2 * SUB, LANES), 0)
    lanes = iota((2 * SUB, LANES), 1)

    def fill(s, _):
        block = jnp.full((2 * SUB, LANES), -2, jnp.int32)
        for n in range(2):
            for i in range(rows_dev):
                target = owner_ref[slot_ref[(2 * s + n) * rows_dev + i], 2 * s + n]
                block = jnp.where((inner // SUB == n) & (inner % rows_dev == i), target, block)
        place = pl.ds(pl.multiple_of(s * 2 * SUB, 2 * SUB), 2 * SUB)
        req_held[place, :] = block
        hot_held[place, :] = jnp.where(lanes == block, 1.0, 0.0).astype(bf16)
        return 0

    lax.fori_loop(0, owners // 2, fill, 0)
    marks = fetches([(mark_held, mark_any), (hot_held, hot_any), (req_held, req_any)], sems)

    def early(r, _):
        c_copy(r).wait()
        prompt_result(r, x_held, b_held, c_held, w_in, w_out, w_skip, masks, out_held)
        out_copy(r).start()
        return 0

    lax.fori_loop(0, EARLY, early, 0, unroll=2)
    for copy in marks:
        copy.wait()
    for r in range(prompts):
        state_copy(r).wait()
    for r in range(EARLY):
        out_copy(r).wait()


def serve_kernel(
    recv_any,
    pages_any,
    other_any,
    mark_any,
    hot_any,
    req_any,
    state_any,
    out_ref,
    recv_ref,
    key_ref,
    value_ref,
    hot_ref,
    req_ref,
    state_ref,
    query_ref,
    score_ref,
    state_sem,
    sems,
):
    rows = recv_ref.shape[0]
    held = pages_any.shape[0]
    prompts, width = state_ref.shape[0], state_ref.shape[1]
    mine, other = pl.ds(0, held), pl.ds(held, held)
    copies = fetches(
        [
            (recv_any, recv_ref),
            (hot_any, hot_ref),
            (pages_any.at[:, pl.ds(0, HD)], key_ref.at[mine, pl.ds(0, HD)]),
            (other_any.at[:, pl.ds(0, HD)], key_ref.at[other, pl.ds(0, HD)]),
            (mark_any.at[0], key_ref.at[mine, pl.ds(HD, LANES)]),
            (mark_any.at[1], key_ref.at[other, pl.ds(HD, LANES)]),
        ],
        sems,
    )
    copies[0].wait()
    copies[1].wait()
    heads = HALF // HD
    for g in range(heads):
        query_ref[g * rows : (g + 1) * rows, :HD] = recv_ref[:, g * HD : (g + 1) * HD]
        query_ref[g * rows : (g + 1) * rows, HD:] = hot_ref[...]
    for copy in copies[2:]:
        copy.wait()
    copies = fetches(
        [
            (pages_any.at[:, pl.ds(HD, HD)], value_ref.at[mine]),
            (other_any.at[:, pl.ds(HD, HD)], value_ref.at[other]),
            (req_any, req_ref),
        ],
        sems,
        len(copies),
    )
    states = fetches([(state_any.at[r], state_ref.at[r]) for r in range(prompts)], state_sem)
    keys = key_ref.shape[0]
    chunk = min(keys, 2 * NS)
    widest = jnp.full((heads * rows, LANES), NONE, f32)
    for k in range(0, keys, chunk):
        scores = dot_nt(query_ref[...], key_ref[k : k + chunk, :])
        score_ref[:, k : k + chunk] = scores
        for b in range(0, chunk, LANES):
            widest = jnp.maximum(widest, scores[:, b : b + LANES])
    highest = jnp.max(widest, axis=1, keepdims=True)
    for copy in copies:
        copy.wait()
    total = jnp.zeros((heads * rows, LANES), f32)
    value = jnp.zeros((heads * rows, HD), f32)
    for k in range(0, keys, chunk):
        weight = jnp.exp2((score_ref[:, k : k + chunk] - highest) * SCORE)
        for b in range(0, chunk, LANES):
            total = total + weight[:, b : b + LANES]
        value = value + jnp.dot(weight.astype(bf16), value_ref[k : k + chunk, :], preferred_element_type=f32)
    total = jnp.sum(total, axis=1, keepdims=True)
    value = value / total
    result = jnp.where(highest > 0.5 * MATCH, (highest - MATCH) * SCORE + jnp.log2(total), NONE)
    lane = iota((rows, LANES), 1)
    sums = jnp.zeros((rows, LANES), f32)
    for g in range(heads):
        sums = jnp.where(lane % 4 == g, result[g * rows : (g + 1) * rows], sums)
    high = sums.astype(bf16).astype(f32)
    rest = sums - high
    middle = rest.astype(bf16).astype(f32)
    piece = lane % 16 // 4
    pieces = jnp.where(piece == 0, high, jnp.where(piece == 1, middle, rest - middle))
    pair = iota((rows, LANES), 0) % SUB
    pieces = jnp.where((lane // 16 == pair) & (piece < 3), pieces, 0.0)
    packed = jnp.sum(pieces.reshape(rows // SUB, SUB, LANES), axis=1, keepdims=True)

    given = recv_ref[...].astype(f32).reshape(rows // SUB, SUB, recv_ref.shape[1])
    ending = lift(given, spare(heads + 1, 0))
    readout = jnp.concatenate([given[..., HALF:], ending], axis=-1).reshape(rows, NS)
    target = jnp.concatenate([req_ref[...], req_ref[...]], axis=-1)
    found = jnp.zeros((rows, width), f32)
    for r in range(prompts):
        picked = jnp.where(target == r, readout, 0.0).astype(bf16)
        states[r].wait()
        found = found + dot_nt(picked, state_ref[r])
    if width < LANES:
        found = jnp.concatenate([found, jnp.zeros((rows, LANES - width), f32)], axis=-1)
    blocks = [value[g * rows : (g + 1) * rows] for g in range(heads)]
    blocks += [found[:, b : b + LANES] for b in range(0, found.shape[1], LANES)]
    blocks = [one.reshape(rows // SUB, SUB, LANES) for one in blocks]
    row = iota((rows // SUB, SUB, LANES), 1)
    last = blocks.pop()
    blocks[0] = jnp.where(row == PAIRS, jnp.broadcast_to(packed, row.shape), blocks[0])
    for n, (at, b) in enumerate(spare(len(blocks), 1)):
        one = jnp.broadcast_to(last[:, n : n + 1, :], row.shape)
        blocks[b] = jnp.where(row == at, one, blocks[b])
    for b, one in enumerate(blocks):
        out_ref[:, b * LANES : (b + 1) * LANES] = one.reshape(rows, LANES).astype(bf16)


def prompt_kernel(
    rate_any,
    skip_any,
    len_any,
    dt_any,
    rates_any,
    skips_any,
    send_any,
    fresh_any,
    sx_any,
    sb_any,
    sc_any,
    sdt_any,
    x_any,
    b_any,
    c_any,
    after_any,
    early_any,
    out_any,
    own_any,
    ownsum_any,
    fade_any,
    local_any,
    x_held,
    b_held,
    c_held,
    out_held,
    w_in,
    w_out,
    w_skip,
    masks,
    signs,
    own_ref,
    ownsum_ref,
    fade_ref,
    local_ref,
    fresh_held,
    c_rows,
    x_rows,
    rate_ref,
    skip_ref,
    len_ref,
    dt_ref,
    rates_ref,
    skips_ref,
    send_ref,
    fresh_ref,
    sx_ref,
    sb_ref,
    sc_ref,
    sdt_ref,
    x_sem,
    b_sem,
    c_sem,
    out_sem,
    sems,
):
    group, prompts, length = dt_ref.shape
    smalls = fetches(
        [
            (dt_any, dt_ref),
            (rate_any, rate_ref),
            (skip_any, skip_ref),
            (len_any, len_ref),
            (rates_any, rates_ref),
            (skips_any, skips_ref),
            (send_any, send_ref),
            (fresh_any, fresh_ref),
            (sx_any, sx_ref),
            (sb_any, sb_ref),
            (sc_any, sc_ref),
            (sdt_any, sdt_ref),
        ],
        sems,
    )
    me = lax.axis_index("heads")
    first = me * group
    column = pl.multiple_of((first // HPG) * NS, NS)

    def x_copy(r):
        return pltpu.make_async_copy(x_any.at[r], x_held.at[r], x_sem.at[r])

    def b_copy(r):
        return pltpu.make_async_copy(b_any.at[r, :, pl.ds(column, NS)], b_held.at[r], b_sem.at[r])

    def c_copy(r):
        return pltpu.make_async_copy(c_any.at[r, :, pl.ds(column, NS)], c_held.at[r], c_sem.at[r])

    def out_copy(r):
        return pltpu.make_async_copy(out_held.at[r], out_any.at[r], out_sem.at[r])

    def ask(r):
        x_copy(r).start()
        b_copy(r).start()
        c_copy(r).start()

    for r in range(EARLY, min(EARLY + AHEAD, prompts)):
        ask(r)
    sign_tables(signs, False)
    level_masks(masks)
    for copy in smalls:
        copy.wait()
    head_factors(first, dt_ref, rate_ref, skip_ref, len_ref, signs, w_in, w_out, w_skip, None)
    own_attention(send_ref, fresh_ref, fresh_held, own_ref, ownsum_ref)
    own_mixer(rates_ref, skips_ref, sx_ref, sb_ref, sc_ref, sdt_ref, c_rows, x_rows, fade_ref, local_ref)
    outs = fetches(
        [(own_ref, own_any), (ownsum_ref, ownsum_any), (fade_ref, fade_any), (local_ref, local_any)], sems
    )

    def one(r, _):
        @pl.when(r + AHEAD < prompts)
        def _():
            ask(r + AHEAD)

        x_copy(r).wait()
        b_copy(r).wait()
        c_copy(r).wait()
        prompt_result(r, x_held, b_held, c_held, w_in, w_out, w_skip, masks, out_held)
        out_copy(r).start()
        return 0

    lax.fori_loop(EARLY, prompts, one, 0, unroll=2)
    for copy in outs:
        copy.wait()
    for r in range(EARLY, prompts):
        out_copy(r).wait()


def own_attention(send_ref, fresh_ref, fresh_held, own_ref, ownsum_ref):
    steps, rows = fresh_ref.shape[0], fresh_ref.shape[1]
    ways = send_ref.shape[0] // SUB // KVH
    stack_rows(fresh_ref, fresh_held)
    count = HALF // HD * 2 * SUB
    pair = iota((count, SUB), 0) % SUB
    key = iota((count, SUB), 1)
    seen = (key % rows == pair % rows) & (key <= pair) & (key < rows * steps)
    seen = seen | ((pair >= rows * steps) & (key == 0))
    for v in range(KVH):
        block = send_ref[v * ways * SUB : (v * ways + 2) * SUB]
        query = jnp.concatenate([block[:, g * HD : (g + 1) * HD] for g in range(HALF // HD)], axis=0)
        keys = fresh_held[:, v * HD : (v + 1) * HD].astype(bf16)
        values = fresh_held[:, (KVH + v) * HD : (KVH + v + 1) * HD].astype(bf16)
        scores = jnp.where(seen, dot_nt(query, keys) * SCORE, NONE)
        highest = jnp.max(scores, axis=1, keepdims=True)
        weight = jnp.exp2(scores - highest)
        total = jnp.sum(weight, axis=1, keepdims=True)
        weight = (weight / total).astype(bf16)
        own_ref[v] = jnp.dot(weight, values, preferred_element_type=f32)
        ownsum_ref[v] = jnp.broadcast_to(highest + jnp.log2(total), (count, HD))


def own_mixer(rates_ref, skips_ref, sx_ref, sb_ref, sc_ref, sdt_ref, c_rows, x_rows, fade_ref, local_ref):
    steps, rows, heads = sdt_ref.shape
    stack_rows(sc_ref, c_rows)
    for u in range(steps):
        given = sx_ref[u].astype(f32)
        for k in range(SUB // rows):
            x_rows[u, k * rows : (k + 1) * rows, :] = given
    pair = iota((SUB, heads), 0)
    step = pair // rows
    live = pair < rows * steps
    head = iota((SUB, heads), 1)

    def spread_rows(ref, u):
        given = ref[u].astype(f32)
        return jnp.concatenate([given] * (SUB // rows), axis=0)

    rates = jnp.broadcast_to(rates_ref[...], (SUB, heads)) * LOG2E
    skips = jnp.broadcast_to(skips_ref[...], (SUB, heads))
    moved = [spread_rows(sdt_ref, u) for u in range(steps)]
    kept = [jnp.where(u <= step, moved[u], 0.0) for u in range(steps)]
    parts = [jnp.where(live, jnp.exp2(-(rates * sum(kept))), 0.0)]
    for u in range(steps):
        products = c_rows[...] * spread_rows(sb_ref, u)
        inner = jnp.zeros((SUB, heads), f32)
        for e in range(products.shape[1] // NS):
            found = jnp.sum(products[:, e * NS : (e + 1) * NS], axis=1, keepdims=True)
            inner = jnp.where(head // HPG == e, found, inner)
        gap = jnp.zeros((SUB, heads), f32)
        for t in range(u + 1, steps):
            gap = gap + kept[t]
        weight = jnp.where(u <= step, jnp.exp2(-(rates * gap)) * moved[u] * inner, 0.0)
        weight = weight + jnp.where(u == step, skips, 0.0)
        parts.append(jnp.where(live, weight, 0.0))
    stacked = jnp.concatenate(parts, axis=0)
    high = stacked.astype(bf16)
    low = (stacked - high.astype(f32)).astype(bf16)
    both = jnp.concatenate([high.astype(f32), low.astype(f32)], axis=0)
    count = stacked.shape[0]
    chunk = SUB * HP
    widen = jnp.where(iota((heads, chunk), 0) % SUB == iota((heads, chunk), 1) // HP, 1.0, 0.0).astype(bf16)
    lane = iota(both.shape, 1)
    for d in range(heads // SUB):
        picked = jnp.where(lane // SUB == d, both, 0.0).astype(bf16)
        wide = jnp.dot(picked, widen, preferred_element_type=f32)
        wide = wide[:count] + wide[count:]
        columns = slice(d * chunk, (d + 1) * chunk)
        fade_ref[:, columns] = wide[:SUB]
        value = jnp.zeros((SUB, chunk), f32)
        for u in range(steps):
            value = value + wide[(u + 1) * SUB : (u + 2) * SUB] * x_rows[u, :, columns]
        local_ref[:, columns] = value


def merge_kernel(
    width,
    back_any,
    own_any,
    ownsum_any,
    fade_any,
    local_any,
    mixer_any,
    attention_any,
    back_ref,
    own_ref,
    ownsum_ref,
    fade_ref,
    local_ref,
    mixed,
    attended,
    mixer_ref,
    attention_ref,
    sems,
):
    copies = fetches([(back_any, back_ref), (fade_any, fade_ref), (local_any, local_ref)], sems)
    rest = fetches([(own_any, own_ref), (ownsum_any, ownsum_ref)], sems, len(copies))
    for copy in copies:
        copy.wait()
    owners = back_ref.shape[0] // SUB
    ways = owners // KVH
    steps, rows = mixer_ref.shape[0], mixer_ref.shape[1]
    for d in range(0, owners, 2):
        block = back_ref[d * SUB : (d + 2) * SUB, :].astype(f32).reshape(2, SUB, back_ref.shape[1])
        ending = lift(block, spare(back_ref.shape[1] // LANES, 1))
        if back_ref.shape[1] > HALF:
            ending = jnp.concatenate([block[..., HALF:], ending], axis=-1)
        found = ending[..., :width]
        found = jnp.concatenate([found[0], found[1]], axis=-1)
        columns = slice(d * width, (d + 2) * width)
        mixed[:, columns] = found * fade_ref[:, columns] + local_ref[:, columns]
    for k in range(steps):
        mixer_ref[k] = mixed[k * rows : (k + 1) * rows, :].astype(bf16)
    outs = fetches([(mixer_ref, mixer_any)], sems)
    for copy in rest:
        copy.wait()
    lane = iota((2, SUB, LANES), 2)
    mine = (lane // 16 == iota((2, SUB, LANES), 1)) & (lane % 16 < 12)
    for v in range(KVH):
        blocks, pieces = [], []
        for d in range(v * ways, (v + 1) * ways, 2):
            block = back_ref[d * SUB : (d + 2) * SUB, :HALF].astype(f32)
            packed = block[:, :LANES].reshape(2, SUB, LANES)[:, PAIRS : PAIRS + 1, :]
            blocks.append(block)
            pieces.append(jnp.where(mine, jnp.broadcast_to(packed, (2, SUB, LANES)), 0.0))
        for g in range(HALF // HD):
            part = slice(g * 2 * SUB, (g + 1) * 2 * SUB)
            own_sum = ownsum_ref[v, part, :]
            wide = []
            for piece in pieces:
                one = jnp.sum(jnp.where(lane % 4 == g, piece, 0.0), axis=-1, keepdims=True)
                wide.append(jnp.broadcast_to(one, (2, SUB, HD)).reshape(2 * SUB, HD))
            highest = functools.reduce(jnp.maximum, wide, own_sum)
            weight = jnp.exp2(own_sum - highest)
            total = weight
            value = weight * own_ref[v, part, :]
            for one, block in zip(wide, blocks):
                weight = jnp.exp2(one - highest)
                total = total + weight
                value = value + weight * block[:, g * HD : (g + 1) * HD]
            value = value / total
            start = v * 2 * HALF + g * HD
            attended[:, start : start + HD] = value[:SUB]
            attended[:, start + HALF : start + HALF + HD] = value[SUB:]
    for k in range(steps):
        attention_ref[k] = attended[k * rows : (k + 1) * rows, :].astype(bf16)
    outs += fetches([(attention_ref, attention_any)], sems, 1)
    for copy in outs:
        copy.wait()


def call(kernel, out_shape, in_spaces, out_spaces, scratch, cost, aliases=None):
    def spec(space):
        return pl.BlockSpec(memory_space=space)

    return pl.pallas_call(
        kernel,
        out_shape=out_shape,
        in_specs=[spec(space) for space in in_spaces],
        out_specs=jax.tree.map(spec, out_spaces),
        scratch_shapes=scratch,
        input_output_aliases=aliases or {},
        compiler_params=pltpu.CompilerParams(vmem_limit_bytes=VMEM_LIMIT),
        cost_estimate=pl.CostEstimate(flops=cost[0], bytes_accessed=cost[1], transcendentals=0),
    )


def on_device(
    prompt_x,
    prompt_b,
    prompt_c,
    prompt_dt,
    decay_rate,
    skip_gain,
    lengths,
    owner_list,
    page_table,
    cache_pages,
    row_slot,
    step_x,
    step_b,
    step_c,
    step_dt,
    queries,
    fresh_cache,
):
    owners = lax.axis_size("heads")
    ways = owners // KVH
    group, prompts, length = prompt_dt.shape
    width = prompt_x.shape[1]
    keys = cache_pages.shape[0] * PAGE
    steps = step_x.shape[1]
    all_rows = owners * SUB
    shape = jax.ShapeDtypeStruct
    smem, vmem, hbm = pltpu.SMEM, pltpu.VMEM, pltpu.HBM
    sem = pltpu.SemaphoreType.DMA((prompts,))
    levels = len(LEVELS)
    step_x, step_b, step_c, step_dt, queries, fresh_cache = (
        jnp.swapaxes(one, 0, 1) for one in (step_x, step_b, step_c, step_dt, queries, fresh_cache)
    )
    owner_list = owner_list.T

    def like(space, array):
        return space(array.shape, array.dtype)

    def sems(count):
        return pltpu.SemaphoreType.DMA((count,))

    other_pages = lax.ppermute(cache_pages, "heads", [(d, d + 1 - 2 * (d % 2)) for d in range(owners)])
    send = call(
        functools.partial(pack_kernel, group, ways),
        shape((all_rows, HALF + LANES), bf16),
        [hbm, hbm],
        vmem,
        [
            like(vmem, queries),
            like(vmem, step_c),
            vmem((SUB, queries.shape[2]), f32),
            vmem((SUB, step_c.shape[2]), f32),
            vmem((step_c.shape[2] // NS, SUB, HALF + LANES), f32),
            sems(2),
        ],
        (0, 1 << 19),
    )(queries, step_c)
    recv = lax.all_to_all(send, "heads", split_axis=0, concat_axis=0, tiled=True)

    block = [
        vmem((prompts, width, length), bf16),
        vmem((prompts, length, NS), bf16),
        vmem((prompts, length, NS), bf16),
        vmem((prompts, width, length), bf16),
        vmem((levels, prompts, group, length), f32),
        vmem((levels, prompts, group, length), f32),
        vmem((prompts, group, length), f32),
    ]
    tables = [vmem((levels, length, length), bf16), vmem((levels + 1, length, length), bf16)]
    work = 2 * width * length * NS
    states, marks, hot, requests, early_out = call(
        state_kernel,
        (
            shape((prompts, width, NS), bf16),
            shape((2, keys, LANES), bf16),
            shape((all_rows, LANES), bf16),
            shape((all_rows, LANES), jnp.int32),
            shape(prompt_x.shape, bf16),
        ),
        [hbm] * 10,
        (hbm,) * 5,
        block
        + tables
        + [vmem((prompts, group, length), f32), vmem((prompts, width, NS), bf16)]
        + [vmem((2, keys, LANES), bf16), vmem((all_rows, LANES), bf16), vmem((all_rows, LANES), jnp.int32)]
        + [like(smem, one) for one in (decay_rate, skip_gain, lengths, owner_list, page_table, row_slot)]
        + [like(vmem, prompt_dt), sem, sem, sem, sem, sem, sems(7)],
        (work * (prompts + 5 * EARLY), 6 << 20),
    )(
        decay_rate,
        skip_gain,
        lengths,
        owner_list,
        page_table,
        row_slot,
        prompt_dt,
        prompt_x,
        prompt_b,
        prompt_c,
    )

    back = call(
        serve_kernel,
        shape((all_rows, HALF + max(LANES, width) - LANES), bf16),
        [hbm] * 7,
        vmem,
        [
            like(vmem, recv),
            vmem((2 * keys, HD + LANES), bf16),
            vmem((2 * keys, HD), bf16),
            like(vmem, hot),
            like(vmem, requests),
            like(vmem, states),
            vmem((HALF // HD * all_rows, HD + LANES), bf16),
            vmem((HALF // HD * all_rows, 2 * keys), f32),
            sem,
            sems(9),
        ],
        (8 * all_rows * keys * HD, 4 << 20),
    )(
        recv,
        cache_pages.reshape(keys, 2 * HD),
        other_pages.reshape(keys, 2 * HD),
        marks,
        hot,
        requests,
        states,
    )
    returned = lax.all_to_all(back, "heads", split_axis=0, concat_axis=0, tiled=True)

    count = HALF // HD * 2 * SUB
    channels = step_x.shape[2]
    rates, skips = decay_rate.reshape(1, -1), skip_gain.reshape(1, -1)
    prompt_out, own, own_sum, fade, local = call(
        prompt_kernel,
        (
            shape(prompt_x.shape, bf16),
            shape((KVH, count, HD), f32),
            shape((KVH, count, HD), f32),
            shape((SUB, channels), f32),
            shape((SUB, channels), f32),
        ),
        [hbm] * 17,
        (hbm,) * 5,
        block
        + tables
        + [
            vmem((KVH, count, HD), f32),
            vmem((KVH, count, HD), f32),
            vmem((SUB, channels), f32),
            vmem((SUB, channels), f32),
            vmem((SUB, fresh_cache.shape[2]), f32),
            vmem((SUB, step_c.shape[2]), f32),
            vmem((steps, SUB, channels), f32),
            like(smem, decay_rate),
            like(smem, skip_gain),
            like(smem, lengths),
            like(vmem, prompt_dt),
            like(vmem, rates),
            like(vmem, skips),
            like(vmem, send),
            like(vmem, fresh_cache),
            like(vmem, step_x),
            like(vmem, step_b),
            like(vmem, step_c),
            like(vmem, step_dt),
            sem,
            sem,
            sem,
            sem,
            sems(12),
        ],
        (work * 5 * (prompts - EARLY), 8 << 20),
        {16: 0},
    )(
        decay_rate,
        skip_gain,
        lengths,
        prompt_dt,
        rates,
        skips,
        send,
        fresh_cache,
        step_x,
        step_b,
        step_c,
        step_dt,
        prompt_x,
        prompt_b,
        prompt_c,
        back,
        early_out,
    )

    mixer_out, attention_out = call(
        functools.partial(merge_kernel, width),
        (shape(step_x.shape, bf16), shape(queries.shape, bf16)),
        [hbm] * 5,
        (hbm, hbm),
        [like(vmem, one) for one in (returned, own, own_sum, fade, local)]
        + [vmem((SUB, channels), f32), vmem((SUB, queries.shape[2]), f32)]
        + [like(vmem, step_x), like(vmem, queries), sems(5)],
        (0, 2 << 20),
    )(returned, own, own_sum, fade, local)
    return (prompt_out, jnp.swapaxes(mixer_out, 0, 1), jnp.swapaxes(attention_out, 0, 1))


def solution(mesh):
    in_specs = (
        P("groups", "heads", None),
        P("groups", None, None),
        P("groups", None, None),
        P("heads", "groups", None),
        P(),
        P(),
        P("groups"),
        P("groups", None),
        P("groups", None),
        P(("groups", "heads"), None, None),
        P("groups"),
        P(("groups", "heads"), None, None),
        P(("groups", "heads"), None, None),
        P(("groups", "heads"), None, None),
        P(("groups", "heads"), None, None),
        P(("groups", "heads"), None, None),
        P(("groups", "heads"), None, None),
    )
    out_specs = (
        P("groups", "heads", None),
        P(("groups", "heads"), None, None),
        P(("groups", "heads"), None, None),
    )
    return jax.shard_map(
        on_device, mesh=mesh, in_specs=in_specs, out_specs=out_specs, check_vma=False
    )
```

```python
import functools
import math

import jax
import jax.numpy as jnp
from jax import lax
from jax.experimental import pallas as pl
from jax.experimental.pallas import tpu as pltpu
from jax.sharding import PartitionSpec as P

NS = 256
HP = 64
HPG = 32
KVH = 8
HD = 128
PAGE = 16
LANES = 128
SUB = 8
HALF = 512
LEVELS = (128, 64, 32, 16)
LOG2E = math.log2(math.e)
SCORE = LOG2E / math.sqrt(HD)
NONE = -1e30
PAIRS = 6
MATCH = 32768.0
AHEAD = 2
EARLY = 2
VMEM_LIMIT = 64 * 1024 * 1024

f32 = jnp.float32
bf16 = jnp.bfloat16


def iota(shape, dim):
    return lax.broadcasted_iota(jnp.int32, shape, dim)


def dot_nt(left, right):
    return lax.dot_general(left, right, (((1,), (1,)), ((), ())), preferred_element_type=f32)


def stack_rows(source, held):
    steps, rows = source.shape[0], source.shape[1]
    held[...] = jnp.zeros_like(held)
    for k in range(steps):
        held[k * rows : (k + 1) * rows, :] = source[k].astype(f32)


def spare(blocks, taken):
    return [(row, b) for row in range(PAIRS, SUB) for b in range(blocks)][taken : taken + PAIRS]


def lift(value, slots):
    row = iota(value.shape[:2] + (LANES,), 1)
    found = jnp.zeros(row.shape, f32)
    for pair, (at, b) in enumerate(slots):
        one = value[:, at : at + 1, b * LANES : (b + 1) * LANES]
        found = jnp.where(row == pair, jnp.broadcast_to(one, row.shape), found)
    return found


def fetches(pairs, sems, first=0):
    copies = [pltpu.make_async_copy(src, dst, sems.at[first + n]) for n, (src, dst) in enumerate(pairs)]
    for copy in copies:
        copy.start()
    return copies


def pack_kernel(
    group, ways, q_any, q_other, c_any, c_other, out_any, out_held, q_ref, c_ref, q_held, c_held, rest, sems
):
    chips = out_held.shape[0] // (2 * SUB)
    core = lax.rem(lax.axis_index("heads"), 2)
    copies = fetches(
        [(c_any, c_ref.at[0]), (c_other, c_ref.at[1]), (q_any, q_ref.at[0]), (q_other, q_ref.at[1])], sems
    )
    slots = spare(HALF // LANES + 1, 0)
    rest[...] = jnp.zeros_like(rest)
    for n in range(2):
        copies[n].wait()
        stack_rows(c_ref.at[n], c_held.at[n])
        for e in range(c_ref.shape[3] // NS):
            rest[n, e, :PAIRS, HALF:] = c_held[n, :PAIRS, e * NS : e * NS + LANES]
            for pair, (row, b) in enumerate(slots):
                rest[n, e, row : row + 1, b * LANES : (b + 1) * LANES] = c_held[
                    n, pair : pair + 1, e * NS + LANES : (e + 1) * NS
                ]
    real = iota((SUB, HALF), 0) < PAIRS
    for n in range(2):
        copies[2 + n].wait()
        stack_rows(q_ref.at[n], q_held.at[n])
    for chip in range(chips):
        v, e = 2 * chip // ways, (2 * chip * group) // HPG
        begin = pl.multiple_of(v * 2 * HALF + core * HALF, HALF)
        blocks = [jnp.where(real, q_held[n, :, pl.ds(begin, HALF)], rest[n, e, :, :HALF]) for n in range(2)]
        ends = [rest[n, e, :, HALF:] for n in range(2)]
        place = slice(chip * 2 * SUB, (chip + 1) * 2 * SUB)
        for columns, (mine, other) in ((slice(0, HALF), blocks), (slice(HALF, HALF + LANES), ends)):
            low = jnp.where(core == 0, mine, other)
            high = jnp.where(core == 0, other, mine)
            out_held[place, columns] = jnp.concatenate([low, high], axis=0).astype(bf16)
    for copy in fetches([(out_held, out_any)], sems):
        copy.wait()


def sign_tables(signs, tail):
    length = signs.shape[-1]
    j = iota((length, length), 0)
    i = iota((length, length), 1)
    for l, n in enumerate(LEVELS):
        middle = (i // (2 * n)) * (2 * n) + (n - 1)
        signs[l] = (jnp.where(j <= i, 1.0, 0.0) - jnp.where(j <= middle, 1.0, 0.0)).astype(bf16)
    if tail:
        signs[len(LEVELS)] = jnp.where(j > i, 1.0, 0.0).astype(bf16)


def head_factors(first, dt_ref, rate_ref, skip_ref, len_ref, signs, w_in, w_out, w_skip, w_tail):
    group, prompts, length = dt_ref.shape
    row = iota((prompts, length), 0)
    lens = jnp.zeros((prompts, length), jnp.int32)
    for r in range(prompts):
        lens = jnp.where(row == r, len_ref[r], lens)
    valid = iota((prompts, length), 1) < lens
    moved = [jnp.where(valid, dt_ref[h].astype(f32), 0.0) for h in range(group)]
    every = jnp.concatenate(moved, axis=0).astype(bf16)
    rates = [rate_ref[first + h] * LOG2E for h in range(group)]
    if w_tail is not None:
        total = jnp.dot(every, signs[len(LEVELS)], preferred_element_type=f32)
        for h in range(group):
            part = total[h * prompts : (h + 1) * prompts]
            w_tail[:, h, :] = jnp.exp2(-(rates[h] * part)) * moved[h]
    for h in range(group):
        w_skip[:, h, :] = jnp.where(valid, skip_ref[first + h], 0.0)
    for l, n in enumerate(LEVELS):
        total = jnp.dot(every, signs[l], preferred_element_type=f32)
        for h in range(group):
            gap = rates[h] * total[h * prompts : (h + 1) * prompts]
            if n == LEVELS[-1]:
                up, down = jnp.exp2(gap), jnp.exp2(-gap)
            else:
                up, down = jnp.exp2(jnp.minimum(gap, 0.0)), jnp.exp2(-jnp.maximum(gap, 0.0))
            w_in[l, :, h, :] = up * moved[h]
            w_out[l, :, h, :] = jnp.where(valid, down, 0.0)


def level_masks(masks):
    length = masks.shape[-1]
    j = iota((length, length), 0)
    i = iota((length, length), 1)
    for l, n in enumerate(LEVELS):
        same = (j // (2 * n)) == (i // (2 * n))
        if n == LEVELS[-1]:
            keep = same & (j <= i)
        else:
            keep = same & ((j % (2 * n)) < n) & ((i % (2 * n)) >= n)
        masks[l] = jnp.where(keep, 1.0, 0.0).astype(bf16)


def prompt_result(r, x_held, b_held, c_held, w_in, w_out, w_skip, masks, out_held):
    width, length = x_held.shape[1], x_held.shape[2]
    group = width // HP
    half = length // 2
    inputs = x_held[r].astype(f32).reshape(group, HP, length)
    scores = dot_nt(b_held[r], c_held[r]).astype(bf16)
    total = inputs * w_skip[r][:, None, :]
    left, right = total[..., :half], total[..., half:]
    for l, n in enumerate(LEVELS):
        if 2 * n == length:
            scaled = (inputs[..., :half] * w_in[l, r][:, None, :half]).astype(bf16).reshape(width, half)
            added = jnp.dot(scaled, scores[:half, half:], preferred_element_type=f32)
            right = right + added.reshape(group, HP, half) * w_out[l, r][:, None, half:]
        else:
            scaled = (inputs * w_in[l, r][:, None, :]).astype(bf16).reshape(width, length)
            added = jnp.dot(scaled, scores * masks[l], preferred_element_type=f32)
            added = added.reshape(group, HP, length) * w_out[l, r][:, None, :]
            left = left + added[..., :half]
            right = right + added[..., half:]
    out_held[r] = jnp.concatenate([left, right], axis=-1).reshape(width, length).astype(bf16)


def state_kernel(
    rate_any,
    skip_any,
    len_any,
    owner_any,
    table_any,
    slot_any,
    dt_any,
    x_any,
    b_any,
    c_any,
    state_any,
    mark_any,
    hot_any,
    req_any,
    out_any,
    x_held,
    b_held,
    c_held,
    out_held,
    w_in,
    w_out,
    w_skip,
    masks,
    signs,
    w_tail,
    state_held,
    mark_held,
    hot_held,
    req_held,
    rate_ref,
    skip_ref,
    len_ref,
    owner_ref,
    table_ref,
    slot_ref,
    dt_ref,
    x_sem,
    b_sem,
    c_sem,
    out_sem,
    state_sem,
    sems,
):
    group, prompts, length = dt_ref.shape
    smalls = fetches(
        [
            (dt_any, dt_ref),
            (rate_any, rate_ref),
            (skip_any, skip_ref),
            (len_any, len_ref),
            (owner_any, owner_ref),
            (table_any, table_ref),
            (slot_any, slot_ref),
        ],
        sems,
    )
    me = lax.axis_index("heads")
    first = me * group
    column = pl.multiple_of((first // HPG) * NS, NS)

    def x_copy(r):
        return pltpu.make_async_copy(x_any.at[r], x_held.at[r], x_sem.at[r])

    def b_copy(r):
        return pltpu.make_async_copy(b_any.at[r, :, pl.ds(column, NS)], b_held.at[r], b_sem.at[r])

    def c_copy(r):
        return pltpu.make_async_copy(c_any.at[r, :, pl.ds(column, NS)], c_held.at[r], c_sem.at[r])

    def out_copy(r):
        return pltpu.make_async_copy(out_held.at[r], out_any.at[r], out_sem.at[r])

    def state_copy(r):
        return pltpu.make_async_copy(state_held.at[r], state_any.at[r], state_sem.at[r])

    def ask(r):
        x_copy(r).start()
        b_copy(r).start()

    for r in range(prompts):
        ask(r)
    sign_tables(signs, True)
    level_masks(masks)
    for copy in smalls:
        copy.wait()
    head_factors(first, dt_ref, rate_ref, skip_ref, len_ref, signs, w_in, w_out, w_skip, w_tail)

    def one(r, _):
        x_copy(r).wait()
        b_copy(r).wait()
        width = x_held.shape[1]
        inputs = x_held[r].astype(f32).reshape(group, HP, length)
        scaled = (inputs * w_tail[r][:, None, :]).astype(bf16).reshape(width, length)
        state_held[r] = jnp.dot(scaled, b_held[r], preferred_element_type=f32).astype(bf16)
        state_copy(r).start()
        return 0

    lax.fori_loop(0, prompts, one, 0, unroll=2)
    for r in range(EARLY):
        c_copy(r).start()

    spread = table_ref.shape[1] // owner_ref.shape[1]
    per_head = table_ref.shape[1] // KVH
    offset, lane = iota((PAGE, LANES), 0), iota((PAGE, LANES), 1)
    for n, holder in enumerate((me, me + 1 - 2 * lax.rem(me, 2))):
        for r in range(prompts):
            for page in range(spread):
                entry = holder * spread + page
                row = table_ref[r, entry] - holder * (prompts * spread)
                begin = lax.rem(entry, per_head) * PAGE
                inside = (lane == r) & (offset < len_ref[r] - begin)
                block = jnp.where(inside, MATCH, 0.0).astype(bf16)
                mark_held[n, pl.ds(pl.multiple_of(row * PAGE, PAGE), PAGE), :] = block

    owners = owner_ref.shape[1]
    rows_dev = slot_ref.shape[0] // owners
    inner = iota((2 * SUB, LANES), 0)
    lanes = iota((2 * SUB, LANES), 1)

    def fill(s, _):
        block = jnp.full((2 * SUB, LANES), -2, jnp.int32)
        for n in range(2):
            for i in range(rows_dev):
                target = owner_ref[slot_ref[(2 * s + n) * rows_dev + i], 2 * s + n]
                block = jnp.where((inner // SUB == n) & (inner % rows_dev == i), target, block)
        place = pl.ds(pl.multiple_of(s * 2 * SUB, 2 * SUB), 2 * SUB)
        req_held[place, :] = block
        hot_held[place, :] = jnp.where(lanes == block, 1.0, 0.0).astype(bf16)
        return 0

    lax.fori_loop(0, owners // 2, fill, 0)
    marks = fetches([(mark_held, mark_any), (hot_held, hot_any), (req_held, req_any)], sems)

    def early(r, _):
        c_copy(r).wait()
        prompt_result(r, x_held, b_held, c_held, w_in, w_out, w_skip, masks, out_held)
        out_copy(r).start()
        return 0

    lax.fori_loop(0, EARLY, early, 0, unroll=2)
    for copy in marks:
        copy.wait()
    for r in range(prompts):
        state_copy(r).wait()
    for r in range(EARLY):
        out_copy(r).wait()


def serve_kernel(
    recv_any,
    pages_any,
    other_any,
    mark_any,
    hot_any,
    req_any,
    state_any,
    out_ref,
    recv_ref,
    key_ref,
    value_ref,
    hot_ref,
    req_ref,
    state_ref,
    query_ref,
    score_ref,
    state_sem,
    sems,
):
    rows = recv_ref.shape[0]
    held = pages_any.shape[0]
    prompts, width = state_ref.shape[0], state_ref.shape[1]
    mine, other = pl.ds(0, held), pl.ds(held, held)
    copies = fetches(
        [
            (recv_any, recv_ref),
            (hot_any, hot_ref),
            (pages_any.at[:, pl.ds(0, HD)], key_ref.at[mine, pl.ds(0, HD)]),
            (other_any.at[:, pl.ds(0, HD)], key_ref.at[other, pl.ds(0, HD)]),
            (mark_any.at[0], key_ref.at[mine, pl.ds(HD, LANES)]),
            (mark_any.at[1], key_ref.at[other, pl.ds(HD, LANES)]),
            (pages_any.at[:, pl.ds(HD, HD)], value_ref.at[mine]),
            (other_any.at[:, pl.ds(HD, HD)], value_ref.at[other]),
            (req_any, req_ref),
        ],
        sems,
    )
    states = fetches([(state_any.at[r], state_ref.at[r]) for r in range(prompts)], state_sem)
    copies[0].wait()
    copies[1].wait()
    heads = HALF // HD
    for g in range(heads):
        query_ref[g * rows : (g + 1) * rows, :HD] = recv_ref[:, g * HD : (g + 1) * HD]
        query_ref[g * rows : (g + 1) * rows, HD:] = hot_ref[...]
    for copy in copies[2:6]:
        copy.wait()
    keys = key_ref.shape[0]
    chunk = min(keys, 2 * NS)
    widest = jnp.full((heads * rows, LANES), NONE, f32)
    for k in range(0, keys, chunk):
        scores = dot_nt(query_ref[...], key_ref[k : k + chunk, :])
        score_ref[:, k : k + chunk] = scores
        for b in range(0, chunk, LANES):
            widest = jnp.maximum(widest, scores[:, b : b + LANES])
    highest = jnp.max(widest, axis=1, keepdims=True)
    for copy in copies[6:]:
        copy.wait()
    total = jnp.zeros((heads * rows, LANES), f32)
    value = jnp.zeros((heads * rows, HD), f32)
    for k in range(0, keys, chunk):
        weight = jnp.exp2((score_ref[:, k : k + chunk] - highest) * SCORE)
        for b in range(0, chunk, LANES):
            total = total + weight[:, b : b + LANES]
        value = value + jnp.dot(weight.astype(bf16), value_ref[k : k + chunk, :], preferred_element_type=f32)
    total = jnp.sum(total, axis=1, keepdims=True)
    value = value / total
    result = jnp.where(highest > 0.5 * MATCH, (highest - MATCH) * SCORE + jnp.log2(total), NONE)
    lane = iota((rows, LANES), 1)
    sums = jnp.zeros((rows, LANES), f32)
    for g in range(heads):
        sums = jnp.where(lane % 4 == g, result[g * rows : (g + 1) * rows], sums)
    high = sums.astype(bf16).astype(f32)
    rest = sums - high
    middle = rest.astype(bf16).astype(f32)
    piece = lane % 16 // 4
    pieces = jnp.where(piece == 0, high, jnp.where(piece == 1, middle, rest - middle))
    pair = iota((rows, LANES), 0) % SUB
    pieces = jnp.where((lane // 16 == pair) & (piece < 3), pieces, 0.0)
    packed = jnp.sum(pieces.reshape(rows // SUB, SUB, LANES), axis=1, keepdims=True)

    given = recv_ref[...].astype(f32).reshape(rows // SUB, SUB, recv_ref.shape[1])
    ending = lift(given, spare(heads + 1, 0))
    readout = jnp.concatenate([given[..., HALF:], ending], axis=-1).reshape(rows, NS)
    target = jnp.concatenate([req_ref[...], req_ref[...]], axis=-1)
    found = jnp.zeros((rows, width), f32)
    for r in range(prompts):
        picked = jnp.where(target == r, readout, 0.0).astype(bf16)
        states[r].wait()
        found = found + dot_nt(picked, state_ref[r])
    if width < LANES:
        found = jnp.concatenate([found, jnp.zeros((rows, LANES - width), f32)], axis=-1)
    blocks = [value[g * rows : (g + 1) * rows] for g in range(heads)]
    blocks += [found[:, b : b + LANES] for b in range(0, found.shape[1], LANES)]
    blocks = [one.reshape(rows // SUB, SUB, LANES) for one in blocks]
    row = iota((rows // SUB, SUB, LANES), 1)
    last = blocks.pop()
    blocks[0] = jnp.where(row == PAIRS, jnp.broadcast_to(packed, row.shape), blocks[0])
    for n, (at, b) in enumerate(spare(len(blocks), 1)):
        one = jnp.broadcast_to(last[:, n : n + 1, :], row.shape)
        blocks[b] = jnp.where(row == at, one, blocks[b])
    for b, one in enumerate(blocks):
        out_ref[:, b * LANES : (b + 1) * LANES] = one.reshape(rows, LANES).astype(bf16)


def prompt_kernel(
    rate_any,
    skip_any,
    len_any,
    dt_any,
    rates_any,
    skips_any,
    q_any,
    fresh_any,
    sx_any,
    sb_any,
    sc_any,
    sdt_any,
    x_any,
    b_any,
    c_any,
    after_any,
    early_any,
    out_any,
    own_any,
    ownsum_any,
    fade_any,
    local_any,
    x_held,
    b_held,
    c_held,
    out_held,
    w_in,
    w_out,
    w_skip,
    masks,
    signs,
    own_ref,
    ownsum_ref,
    fade_ref,
    local_ref,
    fresh_held,
    q_held,
    c_rows,
    x_rows,
    rate_ref,
    skip_ref,
    len_ref,
    dt_ref,
    rates_ref,
    skips_ref,
    q_ref,
    fresh_ref,
    sx_ref,
    sb_ref,
    sc_ref,
    sdt_ref,
    x_sem,
    b_sem,
    c_sem,
    out_sem,
    sems,
):
    group, prompts, length = dt_ref.shape
    smalls = fetches(
        [
            (dt_any, dt_ref),
            (rate_any, rate_ref),
            (skip_any, skip_ref),
            (len_any, len_ref),
            (rates_any, rates_ref),
            (skips_any, skips_ref),
            (q_any, q_ref),
            (fresh_any, fresh_ref),
            (sx_any, sx_ref),
            (sb_any, sb_ref),
            (sc_any, sc_ref),
            (sdt_any, sdt_ref),
        ],
        sems,
    )
    me = lax.axis_index("heads")
    first = me * group
    column = pl.multiple_of((first // HPG) * NS, NS)

    def x_copy(r):
        return pltpu.make_async_copy(x_any.at[r], x_held.at[r], x_sem.at[r])

    def b_copy(r):
        return pltpu.make_async_copy(b_any.at[r, :, pl.ds(column, NS)], b_held.at[r], b_sem.at[r])

    def c_copy(r):
        return pltpu.make_async_copy(c_any.at[r, :, pl.ds(column, NS)], c_held.at[r], c_sem.at[r])

    def out_copy(r):
        return pltpu.make_async_copy(out_held.at[r], out_any.at[r], out_sem.at[r])

    def ask(r):
        x_copy(r).start()
        b_copy(r).start()
        c_copy(r).start()

    for r in range(EARLY, min(EARLY + AHEAD, prompts)):
        ask(r)
    sign_tables(signs, False)
    level_masks(masks)
    for copy in smalls:
        copy.wait()
    head_factors(first, dt_ref, rate_ref, skip_ref, len_ref, signs, w_in, w_out, w_skip, None)
    own_attention(q_ref, fresh_ref, q_held, fresh_held, own_ref, ownsum_ref)
    own_mixer(rates_ref, skips_ref, sx_ref, sb_ref, sc_ref, sdt_ref, c_rows, x_rows, fade_ref, local_ref)
    outs = fetches(
        [(own_ref, own_any), (ownsum_ref, ownsum_any), (fade_ref, fade_any), (local_ref, local_any)], sems
    )

    def one(r, _):
        @pl.when(r + AHEAD < prompts)
        def _():
            ask(r + AHEAD)

        x_copy(r).wait()
        b_copy(r).wait()
        c_copy(r).wait()
        prompt_result(r, x_held, b_held, c_held, w_in, w_out, w_skip, masks, out_held)
        out_copy(r).start()
        return 0

    lax.fori_loop(EARLY, prompts, one, 0, unroll=2)
    for copy in outs:
        copy.wait()
    for r in range(EARLY, prompts):
        out_copy(r).wait()


def own_attention(q_ref, fresh_ref, q_held, fresh_held, own_ref, ownsum_ref):
    steps, rows = fresh_ref.shape[0], fresh_ref.shape[1]
    stack_rows(q_ref, q_held)
    stack_rows(fresh_ref, fresh_held)
    count = HALF // HD * 2 * SUB
    pair = iota((count, SUB), 0) % SUB
    key = iota((count, SUB), 1)
    seen = (key % rows == pair % rows) & (key <= pair) & (key < rows * steps)
    seen = seen | ((pair >= rows * steps) & (key == 0))
    for v in range(KVH):
        starts = [v * 2 * HALF + half + g for g in range(0, HALF, HD) for half in (0, HALF)]
        query = jnp.concatenate([q_held[:, at : at + HD] for at in starts], axis=0).astype(bf16)
        keys = fresh_held[:, v * HD : (v + 1) * HD].astype(bf16)
        values = fresh_held[:, (KVH + v) * HD : (KVH + v + 1) * HD].astype(bf16)
        scores = jnp.where(seen, dot_nt(query, keys) * SCORE, NONE)
        highest = jnp.max(scores, axis=1, keepdims=True)
        weight = jnp.exp2(scores - highest)
        total = jnp.sum(weight, axis=1, keepdims=True)
        weight = (weight / total).astype(bf16)
        own_ref[v] = jnp.dot(weight, values, preferred_element_type=f32)
        ownsum_ref[v] = jnp.broadcast_to(highest + jnp.log2(total), (count, HD))


def own_mixer(rates_ref, skips_ref, sx_ref, sb_ref, sc_ref, sdt_ref, c_rows, x_rows, fade_ref, local_ref):
    steps, rows, heads = sdt_ref.shape
    stack_rows(sc_ref, c_rows)
    for u in range(steps):
        given = sx_ref[u].astype(f32)
        for k in range(SUB // rows):
            x_rows[u, k * rows : (k + 1) * rows, :] = given
    pair = iota((SUB, heads), 0)
    step = pair // rows
    live = pair < rows * steps
    head = iota((SUB, heads), 1)

    def spread_rows(ref, u):
        given = ref[u].astype(f32)
        return jnp.concatenate([given] * (SUB // rows), axis=0)

    rates = jnp.broadcast_to(rates_ref[...], (SUB, heads)) * LOG2E
    skips = jnp.broadcast_to(skips_ref[...], (SUB, heads))
    moved = [spread_rows(sdt_ref, u) for u in range(steps)]
    kept = [jnp.where(u <= step, moved[u], 0.0) for u in range(steps)]
    parts = [jnp.where(live, jnp.exp2(-(rates * sum(kept))), 0.0)]
    for u in range(steps):
        products = c_rows[...] * spread_rows(sb_ref, u)
        inner = jnp.zeros((SUB, heads), f32)
        for e in range(products.shape[1] // NS):
            found = jnp.sum(products[:, e * NS : (e + 1) * NS], axis=1, keepdims=True)
            inner = jnp.where(head // HPG == e, found, inner)
        gap = jnp.zeros((SUB, heads), f32)
        for t in range(u + 1, steps):
            gap = gap + kept[t]
        weight = jnp.where(u <= step, jnp.exp2(-(rates * gap)) * moved[u] * inner, 0.0)
        weight = weight + jnp.where(u == step, skips, 0.0)
        parts.append(jnp.where(live, weight, 0.0))
    stacked = jnp.concatenate(parts, axis=0)
    high = stacked.astype(bf16)
    low = (stacked - high.astype(f32)).astype(bf16)
    both = jnp.concatenate([high.astype(f32), low.astype(f32)], axis=0)
    count = stacked.shape[0]
    chunk = SUB * HP
    widen = jnp.where(iota((heads, chunk), 0) % SUB == iota((heads, chunk), 1) // HP, 1.0, 0.0).astype(bf16)
    lane = iota(both.shape, 1)
    for d in range(heads // SUB):
        picked = jnp.where(lane // SUB == d, both, 0.0).astype(bf16)
        wide = jnp.dot(picked, widen, preferred_element_type=f32)
        wide = wide[:count] + wide[count:]
        columns = slice(d * chunk, (d + 1) * chunk)
        fade_ref[:, columns] = wide[:SUB]
        value = jnp.zeros((SUB, chunk), f32)
        for u in range(steps):
            value = value + wide[(u + 1) * SUB : (u + 2) * SUB] * x_rows[u, :, columns]
        local_ref[:, columns] = value


def merge_kernel(
    width,
    back_any,
    own_any,
    ownsum_any,
    fade_any,
    local_any,
    mixer_any,
    attention_any,
    back_ref,
    own_ref,
    ownsum_ref,
    fade_ref,
    local_ref,
    mixed,
    attended,
    mixer_ref,
    attention_ref,
    sems,
):
    copies = fetches([(back_any, back_ref), (fade_any, fade_ref), (local_any, local_ref)], sems)
    rest = fetches([(own_any, own_ref), (ownsum_any, ownsum_ref)], sems, len(copies))
    for copy in copies:
        copy.wait()
    owners = back_ref.shape[0] // SUB
    ways = owners // KVH
    steps, rows = mixer_ref.shape[0], mixer_ref.shape[1]
    for d in range(0, owners, 2):
        block = back_ref[d * SUB : (d + 2) * SUB, :].astype(f32).reshape(2, SUB, back_ref.shape[1])
        ending = lift(block, spare(back_ref.shape[1] // LANES, 1))
        if back_ref.shape[1] > HALF:
            ending = jnp.concatenate([block[..., HALF:], ending], axis=-1)
        found = ending[..., :width]
        found = jnp.concatenate([found[0], found[1]], axis=-1)
        columns = slice(d * width, (d + 2) * width)
        mixed[:, columns] = found * fade_ref[:, columns] + local_ref[:, columns]
    for k in range(steps):
        mixer_ref[k] = mixed[k * rows : (k + 1) * rows, :].astype(bf16)
    outs = fetches([(mixer_ref, mixer_any)], sems)
    for copy in rest:
        copy.wait()
    lane = iota((2, SUB, LANES), 2)
    mine = (lane // 16 == iota((2, SUB, LANES), 1)) & (lane % 16 < 12)
    for v in range(KVH):
        blocks, pieces = [], []
        for d in range(v * ways, (v + 1) * ways, 2):
            block = back_ref[d * SUB : (d + 2) * SUB, :HALF].astype(f32)
            packed = block[:, :LANES].reshape(2, SUB, LANES)[:, PAIRS : PAIRS + 1, :]
            blocks.append(block)
            pieces.append(jnp.where(mine, jnp.broadcast_to(packed, (2, SUB, LANES)), 0.0))
        for g in range(HALF // HD):
            part = slice(g * 2 * SUB, (g + 1) * 2 * SUB)
            own_sum = ownsum_ref[v, part, :]
            wide = []
            for piece in pieces:
                one = jnp.sum(jnp.where(lane % 4 == g, piece, 0.0), axis=-1, keepdims=True)
                wide.append(jnp.broadcast_to(one, (2, SUB, HD)).reshape(2 * SUB, HD))
            highest = functools.reduce(jnp.maximum, wide, own_sum)
            weight = jnp.exp2(own_sum - highest)
            total = weight
            value = weight * own_ref[v, part, :]
            for one, block in zip(wide, blocks):
                weight = jnp.exp2(one - highest)
                total = total + weight
                value = value + weight * block[:, g * HD : (g + 1) * HD]
            value = value / total
            start = v * 2 * HALF + g * HD
            attended[:, start : start + HD] = value[:SUB]
            attended[:, start + HALF : start + HALF + HD] = value[SUB:]
    for k in range(steps):
        attention_ref[k] = attended[k * rows : (k + 1) * rows, :].astype(bf16)
    outs += fetches([(attention_ref, attention_any)], sems, 1)
    for copy in outs:
        copy.wait()


def call(kernel, out_shape, in_spaces, out_spaces, scratch, cost, aliases=None):
    def spec(space):
        return pl.BlockSpec(memory_space=space)

    return pl.pallas_call(
        kernel,
        out_shape=out_shape,
        in_specs=[spec(space) for space in in_spaces],
        out_specs=jax.tree.map(spec, out_spaces),
        scratch_shapes=scratch,
        input_output_aliases=aliases or {},
        compiler_params=pltpu.CompilerParams(vmem_limit_bytes=VMEM_LIMIT),
        cost_estimate=pl.CostEstimate(flops=cost[0], bytes_accessed=cost[1], transcendentals=0),
    )


def on_device(
    prompt_x,
    prompt_b,
    prompt_c,
    prompt_dt,
    decay_rate,
    skip_gain,
    lengths,
    owner_list,
    page_table,
    cache_pages,
    row_slot,
    step_x,
    step_b,
    step_c,
    step_dt,
    queries,
    fresh_cache,
):
    owners = lax.axis_size("heads")
    ways = owners // KVH
    group, prompts, length = prompt_dt.shape
    width = prompt_x.shape[1]
    keys = cache_pages.shape[0] * PAGE
    steps = step_x.shape[1]
    all_rows = owners * SUB
    shape = jax.ShapeDtypeStruct
    smem, vmem, hbm = pltpu.SMEM, pltpu.VMEM, pltpu.HBM
    sem = pltpu.SemaphoreType.DMA((prompts,))
    levels = len(LEVELS)
    step_x, step_b, step_c, step_dt, queries, fresh_cache = (
        jnp.swapaxes(one, 0, 1) for one in (step_x, step_b, step_c, step_dt, queries, fresh_cache)
    )
    owner_list = owner_list.T

    def like(space, array):
        return space(array.shape, array.dtype)

    def sems(count):
        return pltpu.SemaphoreType.DMA((count,))

    across = [(d, d + 1 - 2 * (d % 2)) for d in range(owners)]
    same_core = [list(range(n, owners, 2)) for n in range(2)]
    other_queries = lax.ppermute(queries, "heads", across)
    other_c = lax.ppermute(step_c, "heads", across)
    other_pages = lax.ppermute(cache_pages, "heads", across)
    send = call(
        functools.partial(pack_kernel, group, ways),
        shape((all_rows, HALF + LANES), bf16),
        [hbm] * 4,
        hbm,
        [
            vmem((all_rows, HALF + LANES), bf16),
            vmem((2,) + queries.shape, bf16),
            vmem((2,) + step_c.shape, bf16),
            vmem((2, SUB, queries.shape[2]), f32),
            vmem((2, SUB, step_c.shape[2]), f32),
            vmem((2, step_c.shape[2] // NS, SUB, HALF + LANES), f32),
            sems(4),
        ],
        (0, 1 << 19),
    )(queries, other_queries, step_c, other_c)
    recv = lax.all_to_all(
        send, "heads", split_axis=0, concat_axis=0, tiled=True, axis_index_groups=same_core
    )

    block = [
        vmem((prompts, width, length), bf16),
        vmem((prompts, length, NS), bf16),
        vmem((prompts, length, NS), bf16),
        vmem((prompts, width, length), bf16),
        vmem((levels, prompts, group, length), f32),
        vmem((levels, prompts, group, length), f32),
        vmem((prompts, group, length), f32),
    ]
    tables = [vmem((levels, length, length), bf16), vmem((levels + 1, length, length), bf16)]
    work = 2 * width * length * NS
    states, marks, hot, requests, early_out = call(
        state_kernel,
        (
            shape((prompts, width, NS), bf16),
            shape((2, keys, LANES), bf16),
            shape((all_rows, LANES), bf16),
            shape((all_rows, LANES), jnp.int32),
            shape(prompt_x.shape, bf16),
        ),
        [hbm] * 10,
        (hbm,) * 5,
        block
        + tables
        + [vmem((prompts, group, length), f32), vmem((prompts, width, NS), bf16)]
        + [vmem((2, keys, LANES), bf16), vmem((all_rows, LANES), bf16), vmem((all_rows, LANES), jnp.int32)]
        + [like(smem, one) for one in (decay_rate, skip_gain, lengths, owner_list, page_table, row_slot)]
        + [like(vmem, prompt_dt), sem, sem, sem, sem, sem, sems(7)],
        (work * (prompts + 5 * EARLY), 6 << 20),
    )(
        decay_rate,
        skip_gain,
        lengths,
        owner_list,
        page_table,
        row_slot,
        prompt_dt,
        prompt_x,
        prompt_b,
        prompt_c,
    )

    back = call(
        serve_kernel,
        shape((all_rows, HALF + max(LANES, width) - LANES), bf16),
        [hbm] * 7,
        vmem,
        [
            like(vmem, recv),
            vmem((2 * keys, HD + LANES), bf16),
            vmem((2 * keys, HD), bf16),
            like(vmem, hot),
            like(vmem, requests),
            like(vmem, states),
            vmem((HALF // HD * all_rows, HD + LANES), bf16),
            vmem((HALF // HD * all_rows, 2 * keys), f32),
            sem,
            sems(9),
        ],
        (8 * all_rows * keys * HD, 4 << 20),
    )(
        recv,
        cache_pages.reshape(keys, 2 * HD),
        other_pages.reshape(keys, 2 * HD),
        marks,
        hot,
        requests,
        states,
    )
    returned = lax.all_to_all(back, "heads", split_axis=0, concat_axis=0, tiled=True)

    count = HALF // HD * 2 * SUB
    channels = step_x.shape[2]
    rates, skips = decay_rate.reshape(1, -1), skip_gain.reshape(1, -1)
    prompt_out, own, own_sum, fade, local = call(
        prompt_kernel,
        (
            shape(prompt_x.shape, bf16),
            shape((KVH, count, HD), f32),
            shape((KVH, count, HD), f32),
            shape((SUB, channels), f32),
            shape((SUB, channels), f32),
        ),
        [hbm] * 17,
        (hbm,) * 5,
        block
        + tables
        + [
            vmem((KVH, count, HD), f32),
            vmem((KVH, count, HD), f32),
            vmem((SUB, channels), f32),
            vmem((SUB, channels), f32),
            vmem((SUB, fresh_cache.shape[2]), f32),
            vmem((SUB, queries.shape[2]), f32),
            vmem((SUB, step_c.shape[2]), f32),
            vmem((steps, SUB, channels), f32),
            like(smem, decay_rate),
            like(smem, skip_gain),
            like(smem, lengths),
            like(vmem, prompt_dt),
            like(vmem, rates),
            like(vmem, skips),
            like(vmem, queries),
            like(vmem, fresh_cache),
            like(vmem, step_x),
            like(vmem, step_b),
            like(vmem, step_c),
            like(vmem, step_dt),
            sem,
            sem,
            sem,
            sem,
            sems(12),
        ],
        (work * 5 * (prompts - EARLY), 8 << 20),
        {16: 0},
    )(
        decay_rate,
        skip_gain,
        lengths,
        prompt_dt,
        rates,
        skips,
        queries,
        fresh_cache,
        step_x,
        step_b,
        step_c,
        step_dt,
        prompt_x,
        prompt_b,
        prompt_c,
        back,
        early_out,
    )

    mixer_out, attention_out = call(
        functools.partial(merge_kernel, width),
        (shape(step_x.shape, bf16), shape(queries.shape, bf16)),
        [hbm] * 5,
        (hbm, hbm),
        [like(vmem, one) for one in (returned, own, own_sum, fade, local)]
        + [vmem((SUB, channels), f32), vmem((SUB, queries.shape[2]), f32)]
        + [like(vmem, step_x), like(vmem, queries), sems(5)],
        (0, 2 << 20),
    )(returned, own, own_sum, fade, local)
    return (prompt_out, jnp.swapaxes(mixer_out, 0, 1), jnp.swapaxes(attention_out, 0, 1))


def solution(mesh):
    in_specs = (
        P("groups", "heads", None),
        P("groups", None, None),
        P("groups", None, None),
        P("heads", "groups", None),
        P(),
        P(),
        P("groups"),
        P("groups", None),
        P("groups", None),
        P(("groups", "heads"), None, None),
        P("groups"),
        P(("groups", "heads"), None, None),
        P(("groups", "heads"), None, None),
        P(("groups", "heads"), None, None),
        P(("groups", "heads"), None, None),
        P(("groups", "heads"), None, None),
        P(("groups", "heads"), None, None),
    )
    out_specs = (
        P("groups", "heads", None),
        P(("groups", "heads"), None, None),
        P(("groups", "heads"), None, None),
    )
    return jax.shard_map(
        on_device, mesh=mesh, in_specs=in_specs, out_specs=out_specs, check_vma=False
    )
```

```python
import functools
import math

import jax
import jax.numpy as jnp
from jax import lax
from jax.experimental import pallas as pl
from jax.experimental.pallas import tpu as pltpu
from jax.sharding import PartitionSpec as P

NS = 256
HP = 64
HPG = 32
KVH = 8
HD = 128
PAGE = 16
PAGES = 16
LANES = 128
SUB = 8
HALF = 512
LEVELS = (128, 64, 32, 16)
LOG2E = math.log2(math.e)
SCORE = LOG2E / math.sqrt(HD)
NONE = -1e30
FLOOR = -1e29
PAIRS = 6
LENGTH_BITS = 10
AHEAD = 2
EARLY = 2
VMEM_LIMIT = 64 * 1024 * 1024

f32 = jnp.float32
bf16 = jnp.bfloat16


def iota(shape, dim):
    return lax.broadcasted_iota(jnp.int32, shape, dim)


def dot_nt(left, right):
    return lax.dot_general(left, right, (((1,), (1,)), ((), ())), preferred_element_type=f32)


def stack_rows(source, held):
    steps, rows = source.shape[0], source.shape[1]
    held[...] = jnp.zeros_like(held)
    for k in range(steps):
        held[k * rows : (k + 1) * rows, :] = source[k].astype(f32)


def spare(blocks, taken):
    return [(row, b) for row in range(PAIRS, SUB) for b in range(blocks)][taken : taken + PAIRS]


def lift(value, slots):
    row = iota(value.shape[:2] + (LANES,), 1)
    found = jnp.zeros(row.shape, f32)
    for pair, (at, b) in enumerate(slots):
        one = value[:, at : at + 1, b * LANES : (b + 1) * LANES]
        found = jnp.where(row == pair, jnp.broadcast_to(one, row.shape), found)
    return found


def fetches(pairs, sems, first=0):
    copies = [pltpu.make_async_copy(src, dst, sems.at[first + n]) for n, (src, dst) in enumerate(pairs)]
    for copy in copies:
        copy.start()
    return copies


def pack_kernel(group, ways, q_any, c_any, out_ref, q_ref, c_ref, q_held, c_held, rest, sems):
    owners = out_ref.shape[0] // SUB
    for copy in fetches([(q_any, q_ref), (c_any, c_ref)], sems):
        copy.wait()
    stack_rows(q_ref, q_held)
    stack_rows(c_ref, c_held)
    span = 2 * HALF
    slots = spare(HALF // LANES + 1, 0)
    rest[...] = jnp.zeros_like(rest)
    for e in range(c_ref.shape[2] // NS):
        rest[e, :PAIRS, HALF:] = c_held[:PAIRS, e * NS : e * NS + LANES]
        for pair, (row, b) in enumerate(slots):
            rest[e, row : row + 1, b * LANES : (b + 1) * LANES] = c_held[
                pair : pair + 1, e * NS + LANES : (e + 1) * NS
            ]
    real = iota((SUB, HALF), 0) < PAIRS
    for d in range(0, owners, 2):
        v, e = d // ways, (d * group) // HPG
        low = jnp.where(real, q_held[:, v * span : v * span + HALF], rest[e, :, :HALF])
        high = jnp.where(real, q_held[:, v * span + HALF : (v + 1) * span], rest[e, :, :HALF])
        out_ref[d * SUB : (d + 2) * SUB, :HALF] = jnp.concatenate([low, high], axis=0).astype(bf16)
        end = rest[e, :, HALF:]
        out_ref[d * SUB : (d + 2) * SUB, HALF:] = jnp.concatenate([end, end], axis=0).astype(bf16)


def sign_tables(signs, tail):
    length = signs.shape[-1]
    j = iota((length, length), 0)
    i = iota((length, length), 1)
    for l, n in enumerate(LEVELS):
        middle = (i // (2 * n)) * (2 * n) + (n - 1)
        signs[l] = (jnp.where(j <= i, 1.0, 0.0) - jnp.where(j <= middle, 1.0, 0.0)).astype(bf16)
    if tail:
        signs[len(LEVELS)] = jnp.where(j > i, 1.0, 0.0).astype(bf16)


def head_factors(first, dt_ref, rate_ref, skip_ref, len_ref, signs, w_in, w_out, w_skip, w_tail):
    group, prompts, length = dt_ref.shape
    row = iota((prompts, length), 0)
    lens = jnp.zeros((prompts, length), jnp.int32)
    for r in range(prompts):
        lens = jnp.where(row == r, len_ref[r], lens)
    valid = iota((prompts, length), 1) < lens
    moved = [jnp.where(valid, dt_ref[h].astype(f32), 0.0) for h in range(group)]
    every = jnp.concatenate(moved, axis=0).astype(bf16)
    rates = [rate_ref[first + h] * LOG2E for h in range(group)]
    if w_tail is not None:
        total = jnp.dot(every, signs[len(LEVELS)], preferred_element_type=f32)
        for h in range(group):
            part = total[h * prompts : (h + 1) * prompts]
            w_tail[:, h, :] = jnp.exp2(-(rates[h] * part)) * moved[h]
    for h in range(group):
        w_skip[:, h, :] = jnp.where(valid, skip_ref[first + h], 0.0)
    for l, n in enumerate(LEVELS):
        total = jnp.dot(every, signs[l], preferred_element_type=f32)
        for h in range(group):
            gap = rates[h] * total[h * prompts : (h + 1) * prompts]
            if n == LEVELS[-1]:
                up, down = jnp.exp2(gap), jnp.exp2(-gap)
            else:
                up, down = jnp.exp2(jnp.minimum(gap, 0.0)), jnp.exp2(-jnp.maximum(gap, 0.0))
            w_in[l, :, h, :] = up * moved[h]
            w_out[l, :, h, :] = jnp.where(valid, down, 0.0)


def level_masks(masks):
    length = masks.shape[-1]
    j = iota((length, length), 0)
    i = iota((length, length), 1)
    for l, n in enumerate(LEVELS):
        same = (j // (2 * n)) == (i // (2 * n))
        if n == LEVELS[-1]:
            keep = same & (j <= i)
        else:
            keep = same & ((j % (2 * n)) < n) & ((i % (2 * n)) >= n)
        masks[l] = jnp.where(keep, 1.0, 0.0).astype(bf16)


def prompt_result(r, x_held, b_held, c_held, w_in, w_out, w_skip, masks, out_held):
    width, length = x_held.shape[1], x_held.shape[2]
    group = width // HP
    half = length // 2
    inputs = x_held[r].astype(f32).reshape(group, HP, length)
    scores = dot_nt(b_held[r], c_held[r]).astype(bf16)
    total = inputs * w_skip[r][:, None, :]
    left, right = total[..., :half], total[..., half:]
    for l, n in enumerate(LEVELS):
        if 2 * n == length:
            scaled = (inputs[..., :half] * w_in[l, r][:, None, :half]).astype(bf16).reshape(width, half)
            added = jnp.dot(scaled, scores[:half, half:], preferred_element_type=f32)
            right = right + added.reshape(group, HP, half) * w_out[l, r][:, None, half:]
        else:
            scaled = (inputs * w_in[l, r][:, None, :]).astype(bf16).reshape(width, length)
            added = jnp.dot(scaled, scores * masks[l], preferred_element_type=f32)
            added = added.reshape(group, HP, length) * w_out[l, r][:, None, :]
            left = left + added[..., :half]
            right = right + added[..., half:]
    out_held[r] = jnp.concatenate([left, right], axis=-1).reshape(width, length).astype(bf16)


def state_kernel(
    rate_any,
    skip_any,
    len_any,
    owner_any,
    table_any,
    slot_any,
    dt_any,
    x_any,
    b_any,
    c_any,
    pages_any,
    other_any,
    state_any,
    key_any,
    value_any,
    code_any,
    out_any,
    x_held,
    b_held,
    c_held,
    out_held,
    w_in,
    w_out,
    w_skip,
    masks,
    signs,
    w_tail,
    state_held,
    pages_held,
    key_held,
    value_held,
    code_held,
    rate_ref,
    skip_ref,
    len_ref,
    owner_ref,
    table_ref,
    slot_ref,
    dt_ref,
    x_sem,
    b_sem,
    c_sem,
    out_sem,
    state_sem,
    sems,
):
    group, prompts, length = dt_ref.shape
    smalls = fetches(
        [
            (dt_any, dt_ref),
            (rate_any, rate_ref),
            (skip_any, skip_ref),
            (len_any, len_ref),
            (owner_any, owner_ref),
            (table_any, table_ref),
            (slot_any, slot_ref),
        ],
        sems,
    )
    me = lax.axis_index("heads")
    core = lax.rem(me, 2)
    first = me * group
    column = pl.multiple_of((first // HPG) * NS, NS)

    def x_copy(r):
        return pltpu.make_async_copy(x_any.at[r], x_held.at[r], x_sem.at[r])

    def b_copy(r):
        return pltpu.make_async_copy(b_any.at[r, :, pl.ds(column, NS)], b_held.at[r], b_sem.at[r])

    def c_copy(r):
        return pltpu.make_async_copy(c_any.at[r, :, pl.ds(column, NS)], c_held.at[r], c_sem.at[r])

    def out_copy(r):
        return pltpu.make_async_copy(out_held.at[r], out_any.at[r], out_sem.at[r])

    def state_copy(r):
        return pltpu.make_async_copy(state_held.at[r], state_any.at[r], state_sem.at[r])

    def ask(r):
        x_copy(r).start()
        b_copy(r).start()

    pages = fetches([(pages_any, pages_held.at[core]), (other_any, pages_held.at[1 - core])], sems, len(smalls))
    for r in range(prompts):
        ask(r)
    sign_tables(signs, True)
    level_masks(masks)
    for copy in smalls:
        copy.wait()
    head_factors(first, dt_ref, rate_ref, skip_ref, len_ref, signs, w_in, w_out, w_skip, w_tail)

    def one(r, _):
        x_copy(r).wait()
        b_copy(r).wait()
        width = x_held.shape[1]
        inputs = x_held[r].astype(f32).reshape(group, HP, length)
        scaled = (inputs * w_tail[r][:, None, :]).astype(bf16).reshape(width, length)
        state_held[r] = jnp.dot(scaled, b_held[r], preferred_element_type=f32).astype(bf16)
        state_copy(r).start()
        return 0

    lax.fori_loop(0, prompts, one, 0, unroll=2)
    for r in range(EARLY):
        c_copy(r).start()

    spread = table_ref.shape[1] // owner_ref.shape[1]
    for copy in pages:
        copy.wait()
    for n in range(2):
        for r in range(prompts):
            for page in range(spread):
                holder = me - core + n
                row = table_ref[r, holder * spread + page] - holder * (prompts * spread)
                block = pages_held[n, row]
                place = pl.ds((n * spread + page) * PAGE, PAGE)
                columns = pl.ds(r % 2 * HD, HD)
                key_held[r // 2, place, columns] = block[:, :HD]
                value_held[r // 2, place, columns] = block[:, HD:]

    owners = owner_ref.shape[1]
    rows_dev = slot_ref.shape[0] // owners
    inner = iota((2 * SUB, LANES), 0)

    def fill(s, _):
        block = jnp.zeros((2 * SUB, LANES), jnp.int32)
        for n in range(2):
            for i in range(rows_dev):
                target = owner_ref[slot_ref[(2 * s + n) * rows_dev + i], 2 * s + n]
                code = target * (1 << LENGTH_BITS) + len_ref[target]
                block = jnp.where((inner // SUB == n) & (inner % rows_dev == i), code, block)
        place = pl.ds(pl.multiple_of(s * 2 * SUB, 2 * SUB), 2 * SUB)
        code_held[place, :] = block
        return 0

    lax.fori_loop(0, owners // 2, fill, 0)
    marks = fetches([(key_held, key_any), (value_held, value_any), (code_held, code_any)], sems)

    def early(r, _):
        c_copy(r).wait()
        prompt_result(r, x_held, b_held, c_held, w_in, w_out, w_skip, masks, out_held)
        out_copy(r).start()
        return 0

    lax.fori_loop(0, EARLY, early, 0, unroll=2)
    for copy in marks:
        copy.wait()
    for r in range(prompts):
        state_copy(r).wait()
    for r in range(EARLY):
        out_copy(r).wait()


def serve_kernel(
    recv_any,
    key_any,
    value_any,
    code_any,
    state_any,
    out_ref,
    recv_ref,
    key_ref,
    value_ref,
    code_ref,
    state_ref,
    query_ref,
    state_sem,
    sems,
):
    rows = recv_ref.shape[0]
    prompts, width = state_ref.shape[0], state_ref.shape[1]
    copies = fetches(
        [(recv_any, recv_ref), (code_any, code_ref), (key_any, key_ref), (value_any, value_ref)], sems
    )
    states = fetches([(state_any.at[r], state_ref.at[r]) for r in range(prompts)], state_sem)
    heads = HALF // HD
    keys = key_ref.shape[1]
    chips = keys // PAGE
    begin = lax.rem(lax.axis_index("heads") // 2 * chips, PAGES) * PAGE
    copies[0].wait()
    copies[1].wait()
    code = code_ref[...]
    target = code >> LENGTH_BITS
    lengths = code & ((1 << LENGTH_BITS) - 1)
    for r in range(prompts):
        for g in range(heads):
            query = recv_ref[:, g * HD : (g + 1) * HD].astype(f32)
            query_ref[r // 2, g * rows : (g + 1) * rows, r % 2 * HD : (r % 2 + 1) * HD] = jnp.where(
                target == r, query, 0.0
            ).astype(bf16)
    copies[2].wait()
    scores = jnp.zeros((heads * rows, keys), f32)
    for pair in range(prompts // 2):
        scores = scores + dot_nt(query_ref[pair], key_ref[pair])
    seen = jnp.concatenate([lengths[:, :1]] * heads, axis=0) > iota((heads * rows, keys), 1) + begin
    scores = jnp.where(seen, scores * SCORE, NONE)
    highest = jnp.maximum(jnp.max(scores, axis=1, keepdims=True), FLOOR)
    weight = jnp.exp2(scores - highest)
    total = jnp.sum(weight, axis=1, keepdims=True)
    some = total > 0.0
    safe = jnp.where(some, total, 1.0)
    result = jnp.where(some, highest + jnp.log2(safe), NONE)
    weight = weight.astype(bf16)
    copies[3].wait()
    targets = jnp.concatenate([target] * heads, axis=0)
    value = jnp.zeros((heads * rows, HD), f32)
    for pair in range(prompts // 2):
        both = jnp.dot(weight, value_ref[pair], preferred_element_type=f32)
        for n in range(2):
            value = jnp.where(targets == 2 * pair + n, both[:, n * HD : (n + 1) * HD], value)
    value = value / safe
    lane = iota((rows, LANES), 1)
    sums = jnp.zeros((rows, LANES), f32)
    for g in range(heads):
        sums = jnp.where(lane % 4 == g, result[g * rows : (g + 1) * rows], sums)
    high = sums.astype(bf16).astype(f32)
    rest = sums - high
    middle = rest.astype(bf16).astype(f32)
    piece = lane % 16 // 4
    pieces = jnp.where(piece == 0, high, jnp.where(piece == 1, middle, rest - middle))
    pair = iota((rows, LANES), 0) % SUB
    pieces = jnp.where((lane // 16 == pair) & (piece < 3), pieces, 0.0)
    packed = jnp.sum(pieces.reshape(rows // SUB, SUB, LANES), axis=1, keepdims=True)

    given = recv_ref[...].astype(f32).reshape(rows // SUB, SUB, recv_ref.shape[1])
    ending = lift(given, spare(heads + 1, 0))
    readout = jnp.concatenate([given[..., HALF:], ending], axis=-1).reshape(rows, NS)
    target = jnp.concatenate([target, target], axis=-1)
    found = jnp.zeros((rows, width), f32)
    for r in range(prompts):
        picked = jnp.where(target == r, readout, 0.0).astype(bf16)
        states[r].wait()
        found = found + dot_nt(picked, state_ref[r])
    if width < LANES:
        found = jnp.concatenate([found, jnp.zeros((rows, LANES - width), f32)], axis=-1)
    blocks = [value[g * rows : (g + 1) * rows] for g in range(heads)]
    blocks += [found[:, b : b + LANES] for b in range(0, found.shape[1], LANES)]
    blocks = [one.reshape(rows // SUB, SUB, LANES) for one in blocks]
    row = iota((rows // SUB, SUB, LANES), 1)
    last = blocks.pop()
    blocks[0] = jnp.where(row == PAIRS, jnp.broadcast_to(packed, row.shape), blocks[0])
    for n, (at, b) in enumerate(spare(len(blocks), 1)):
        one = jnp.broadcast_to(last[:, n : n + 1, :], row.shape)
        blocks[b] = jnp.where(row == at, one, blocks[b])
    for b, one in enumerate(blocks):
        out_ref[:, b * LANES : (b + 1) * LANES] = one.reshape(rows, LANES).astype(bf16)


def prompt_kernel(
    rate_any,
    skip_any,
    len_any,
    dt_any,
    rates_any,
    skips_any,
    send_any,
    fresh_any,
    sx_any,
    sb_any,
    sc_any,
    sdt_any,
    x_any,
    b_any,
    c_any,
    after_any,
    early_any,
    out_any,
    own_any,
    ownsum_any,
    fade_any,
    local_any,
    x_held,
    b_held,
    c_held,
    out_held,
    w_in,
    w_out,
    w_skip,
    masks,
    signs,
    own_ref,
    ownsum_ref,
    fade_ref,
    local_ref,
    fresh_held,
    c_rows,
    x_rows,
    rate_ref,
    skip_ref,
    len_ref,
    dt_ref,
    rates_ref,
    skips_ref,
    send_ref,
    fresh_ref,
    sx_ref,
    sb_ref,
    sc_ref,
    sdt_ref,
    x_sem,
    b_sem,
    c_sem,
    out_sem,
    sems,
):
    group, prompts, length = dt_ref.shape
    smalls = fetches(
        [
            (dt_any, dt_ref),
            (rate_any, rate_ref),
            (skip_any, skip_ref),
            (len_any, len_ref),
            (rates_any, rates_ref),
            (skips_any, skips_ref),
            (send_any, send_ref),
            (fresh_any, fresh_ref),
            (sx_any, sx_ref),
            (sb_any, sb_ref),
            (sc_any, sc_ref),
            (sdt_any, sdt_ref),
        ],
        sems,
    )
    me = lax.axis_index("heads")
    first = me * group
    column = pl.multiple_of((first // HPG) * NS, NS)

    def x_copy(r):
        return pltpu.make_async_copy(x_any.at[r], x_held.at[r], x_sem.at[r])

    def b_copy(r):
        return pltpu.make_async_copy(b_any.at[r, :, pl.ds(column, NS)], b_held.at[r], b_sem.at[r])

    def c_copy(r):
        return pltpu.make_async_copy(c_any.at[r, :, pl.ds(column, NS)], c_held.at[r], c_sem.at[r])

    def out_copy(r):
        return pltpu.make_async_copy(out_held.at[r], out_any.at[r], out_sem.at[r])

    def ask(r):
        x_copy(r).start()
        b_copy(r).start()
        c_copy(r).start()

    for r in range(EARLY, min(EARLY + AHEAD, prompts)):
        ask(r)
    sign_tables(signs, False)
    level_masks(masks)
    for copy in smalls:
        copy.wait()
    head_factors(first, dt_ref, rate_ref, skip_ref, len_ref, signs, w_in, w_out, w_skip, None)
    own_attention(send_ref, fresh_ref, fresh_held, own_ref, ownsum_ref)
    own_mixer(rates_ref, skips_ref, sx_ref, sb_ref, sc_ref, sdt_ref, c_rows, x_rows, fade_ref, local_ref)
    outs = fetches(
        [(own_ref, own_any), (ownsum_ref, ownsum_any), (fade_ref, fade_any), (local_ref, local_any)], sems
    )

    def one(r, _):
        @pl.when(r + AHEAD < prompts)
        def _():
            ask(r + AHEAD)

        x_copy(r).wait()
        b_copy(r).wait()
        c_copy(r).wait()
        prompt_result(r, x_held, b_held, c_held, w_in, w_out, w_skip, masks, out_held)
        out_copy(r).start()
        return 0

    lax.fori_loop(EARLY, prompts, one, 0, unroll=2)
    for copy in outs:
        copy.wait()
    for r in range(EARLY, prompts):
        out_copy(r).wait()


def own_attention(send_ref, fresh_ref, fresh_held, own_ref, ownsum_ref):
    steps, rows = fresh_ref.shape[0], fresh_ref.shape[1]
    ways = send_ref.shape[0] // SUB // KVH
    stack_rows(fresh_ref, fresh_held)
    count = HALF // HD * 2 * SUB
    pair = iota((count, SUB), 0) % SUB
    key = iota((count, SUB), 1)
    seen = (key % rows == pair % rows) & (key <= pair) & (key < rows * steps)
    seen = seen | ((pair >= rows * steps) & (key == 0))
    for v in range(KVH):
        block = send_ref[v * ways * SUB : (v * ways + 2) * SUB]
        query = jnp.concatenate([block[:, g * HD : (g + 1) * HD] for g in range(HALF // HD)], axis=0)
        keys = fresh_held[:, v * HD : (v + 1) * HD].astype(bf16)
        values = fresh_held[:, (KVH + v) * HD : (KVH + v + 1) * HD].astype(bf16)
        scores = jnp.where(seen, dot_nt(query, keys) * SCORE, NONE)
        highest = jnp.max(scores, axis=1, keepdims=True)
        weight = jnp.exp2(scores - highest)
        total = jnp.sum(weight, axis=1, keepdims=True)
        weight = (weight / total).astype(bf16)
        own_ref[v] = jnp.dot(weight, values, preferred_element_type=f32)
        ownsum_ref[v] = jnp.broadcast_to(highest + jnp.log2(total), (count, HD))


def own_mixer(rates_ref, skips_ref, sx_ref, sb_ref, sc_ref, sdt_ref, c_rows, x_rows, fade_ref, local_ref):
    steps, rows, heads = sdt_ref.shape
    stack_rows(sc_ref, c_rows)
    for u in range(steps):
        given = sx_ref[u].astype(f32)
        for k in range(SUB // rows):
            x_rows[u, k * rows : (k + 1) * rows, :] = given
    pair = iota((SUB, heads), 0)
    step = pair // rows
    live = pair < rows * steps
    head = iota((SUB, heads), 1)

    def spread_rows(ref, u):
        given = ref[u].astype(f32)
        return jnp.concatenate([given] * (SUB // rows), axis=0)

    rates = jnp.broadcast_to(rates_ref[...], (SUB, heads)) * LOG2E
    skips = jnp.broadcast_to(skips_ref[...], (SUB, heads))
    moved = [spread_rows(sdt_ref, u) for u in range(steps)]
    kept = [jnp.where(u <= step, moved[u], 0.0) for u in range(steps)]
    parts = [jnp.where(live, jnp.exp2(-(rates * sum(kept))), 0.0)]
    for u in range(steps):
        products = c_rows[...] * spread_rows(sb_ref, u)
        inner = jnp.zeros((SUB, heads), f32)
        for e in range(products.shape[1] // NS):
            found = jnp.sum(products[:, e * NS : (e + 1) * NS], axis=1, keepdims=True)
            inner = jnp.where(head // HPG == e, found, inner)
        gap = jnp.zeros((SUB, heads), f32)
        for t in range(u + 1, steps):
            gap = gap + kept[t]
        weight = jnp.where(u <= step, jnp.exp2(-(rates * gap)) * moved[u] * inner, 0.0)
        weight = weight + jnp.where(u == step, skips, 0.0)
        parts.append(jnp.where(live, weight, 0.0))
    stacked = jnp.concatenate(parts, axis=0)
    high = stacked.astype(bf16)
    low = (stacked - high.astype(f32)).astype(bf16)
    both = jnp.concatenate([high.astype(f32), low.astype(f32)], axis=0)
    count = stacked.shape[0]
    chunk = SUB * HP
    widen = jnp.where(iota((heads, chunk), 0) % SUB == iota((heads, chunk), 1) // HP, 1.0, 0.0).astype(bf16)
    lane = iota(both.shape, 1)
    for d in range(heads // SUB):
        picked = jnp.where(lane // SUB == d, both, 0.0).astype(bf16)
        wide = jnp.dot(picked, widen, preferred_element_type=f32)
        wide = wide[:count] + wide[count:]
        columns = slice(d * chunk, (d + 1) * chunk)
        fade_ref[:, columns] = wide[:SUB]
        value = jnp.zeros((SUB, chunk), f32)
        for u in range(steps):
            value = value + wide[(u + 1) * SUB : (u + 2) * SUB] * x_rows[u, :, columns]
        local_ref[:, columns] = value


def merge_kernel(
    width,
    back_any,
    own_any,
    ownsum_any,
    fade_any,
    local_any,
    mixer_any,
    attention_any,
    back_ref,
    own_ref,
    ownsum_ref,
    fade_ref,
    local_ref,
    mixed,
    attended,
    mixer_ref,
    attention_ref,
    sems,
):
    copies = fetches([(back_any, back_ref), (fade_any, fade_ref), (local_any, local_ref)], sems)
    rest = fetches([(own_any, own_ref), (ownsum_any, ownsum_ref)], sems, len(copies))
    for copy in copies:
        copy.wait()
    owners = back_ref.shape[0] // SUB
    ways = owners // KVH
    steps, rows = mixer_ref.shape[0], mixer_ref.shape[1]
    for d in range(0, owners, 2):
        block = back_ref[d * SUB : (d + 2) * SUB, :].astype(f32).reshape(2, SUB, back_ref.shape[1])
        ending = lift(block, spare(back_ref.shape[1] // LANES, 1))
        if back_ref.shape[1] > HALF:
            ending = jnp.concatenate([block[..., HALF:], ending], axis=-1)
        found = ending[..., :width]
        found = jnp.concatenate([found[0], found[1]], axis=-1)
        columns = slice(d * width, (d + 2) * width)
        mixed[:, columns] = found * fade_ref[:, columns] + local_ref[:, columns]
    for k in range(steps):
        mixer_ref[k] = mixed[k * rows : (k + 1) * rows, :].astype(bf16)
    outs = fetches([(mixer_ref, mixer_any)], sems)
    for copy in rest:
        copy.wait()
    lane = iota((2, SUB, LANES), 2)
    mine = (lane // 16 == iota((2, SUB, LANES), 1)) & (lane % 16 < 12)
    for v in range(KVH):
        blocks, pieces = [], []
        for d in range(v * ways, (v + 1) * ways, 2):
            block = back_ref[d * SUB : (d + 2) * SUB, :HALF].astype(f32)
            packed = block[:, :LANES].reshape(2, SUB, LANES)[:, PAIRS : PAIRS + 1, :]
            blocks.append(block)
            pieces.append(jnp.where(mine, jnp.broadcast_to(packed, (2, SUB, LANES)), 0.0))
        for g in range(HALF // HD):
            part = slice(g * 2 * SUB, (g + 1) * 2 * SUB)
            own_sum = ownsum_ref[v, part, :]
            wide = []
            for piece in pieces:
                one = jnp.sum(jnp.where(lane % 4 == g, piece, 0.0), axis=-1, keepdims=True)
                wide.append(jnp.broadcast_to(one, (2, SUB, HD)).reshape(2 * SUB, HD))
            highest = functools.reduce(jnp.maximum, wide, own_sum)
            weight = jnp.exp2(own_sum - highest)
            total = weight
            value = weight * own_ref[v, part, :]
            for one, block in zip(wide, blocks):
                weight = jnp.exp2(one - highest)
                total = total + weight
                value = value + weight * block[:, g * HD : (g + 1) * HD]
            value = value / total
            start = v * 2 * HALF + g * HD
            attended[:, start : start + HD] = value[:SUB]
            attended[:, start + HALF : start + HALF + HD] = value[SUB:]
    for k in range(steps):
        attention_ref[k] = attended[k * rows : (k + 1) * rows, :].astype(bf16)
    outs += fetches([(attention_ref, attention_any)], sems, 1)
    for copy in outs:
        copy.wait()


def call(kernel, out_shape, in_spaces, out_spaces, scratch, cost, aliases=None):
    def spec(space):
        return pl.BlockSpec(memory_space=space)

    return pl.pallas_call(
        kernel,
        out_shape=out_shape,
        in_specs=[spec(space) for space in in_spaces],
        out_specs=jax.tree.map(spec, out_spaces),
        scratch_shapes=scratch,
        input_output_aliases=aliases or {},
        compiler_params=pltpu.CompilerParams(vmem_limit_bytes=VMEM_LIMIT),
        cost_estimate=pl.CostEstimate(flops=cost[0], bytes_accessed=cost[1], transcendentals=0),
    )


def on_device(
    prompt_x,
    prompt_b,
    prompt_c,
    prompt_dt,
    decay_rate,
    skip_gain,
    lengths,
    owner_list,
    page_table,
    cache_pages,
    row_slot,
    step_x,
    step_b,
    step_c,
    step_dt,
    queries,
    fresh_cache,
):
    owners = lax.axis_size("heads")
    ways = owners // KVH
    group, prompts, length = prompt_dt.shape
    width = prompt_x.shape[1]
    keys = cache_pages.shape[0] * PAGE
    span = 2 * keys // prompts
    steps = step_x.shape[1]
    all_rows = owners * SUB
    shape = jax.ShapeDtypeStruct
    smem, vmem, hbm = pltpu.SMEM, pltpu.VMEM, pltpu.HBM
    sem = pltpu.SemaphoreType.DMA((prompts,))
    levels = len(LEVELS)
    step_x, step_b, step_c, step_dt, queries, fresh_cache = (
        jnp.swapaxes(one, 0, 1) for one in (step_x, step_b, step_c, step_dt, queries, fresh_cache)
    )
    owner_list = owner_list.T

    def like(space, array):
        return space(array.shape, array.dtype)

    def sems(count):
        return pltpu.SemaphoreType.DMA((count,))

    other_pages = lax.ppermute(cache_pages, "heads", [(d, d + 1 - 2 * (d % 2)) for d in range(owners)])
    send = call(
        functools.partial(pack_kernel, group, ways),
        shape((all_rows, HALF + LANES), bf16),
        [hbm, hbm],
        vmem,
        [
            like(vmem, queries),
            like(vmem, step_c),
            vmem((SUB, queries.shape[2]), f32),
            vmem((SUB, step_c.shape[2]), f32),
            vmem((step_c.shape[2] // NS, SUB, HALF + LANES), f32),
            sems(2),
        ],
        (0, 1 << 19),
    )(queries, step_c)
    recv = lax.all_to_all(send, "heads", split_axis=0, concat_axis=0, tiled=True)

    block = [
        vmem((prompts, width, length), bf16),
        vmem((prompts, length, NS), bf16),
        vmem((prompts, length, NS), bf16),
        vmem((prompts, width, length), bf16),
        vmem((levels, prompts, group, length), f32),
        vmem((levels, prompts, group, length), f32),
        vmem((prompts, group, length), f32),
    ]
    tables = [vmem((levels, length, length), bf16), vmem((levels + 1, length, length), bf16)]
    work = 2 * width * length * NS
    states, sorted_keys, sorted_values, codes, early_out = call(
        state_kernel,
        (
            shape((prompts, width, NS), bf16),
            shape((prompts // 2, span, 2 * HD), bf16),
            shape((prompts // 2, span, 2 * HD), bf16),
            shape((all_rows, LANES), jnp.int32),
            shape(prompt_x.shape, bf16),
        ),
        [hbm] * 12,
        (hbm,) * 5,
        block
        + tables
        + [vmem((prompts, group, length), f32), vmem((prompts, width, NS), bf16)]
        + [vmem((2,) + cache_pages.shape, bf16)]
        + [vmem((prompts // 2, span, 2 * HD), bf16)] * 2
        + [vmem((all_rows, LANES), jnp.int32)]
        + [like(smem, one) for one in (decay_rate, skip_gain, lengths, owner_list, page_table, row_slot)]
        + [like(vmem, prompt_dt), sem, sem, sem, sem, sem, sems(9)],
        (work * (prompts + 5 * EARLY), 6 << 20),
    )(
        decay_rate,
        skip_gain,
        lengths,
        owner_list,
        page_table,
        row_slot,
        prompt_dt,
        prompt_x,
        prompt_b,
        prompt_c,
        cache_pages,
        other_pages,
    )

    back = call(
        serve_kernel,
        shape((all_rows, HALF + max(LANES, width) - LANES), bf16),
        [hbm] * 5,
        vmem,
        [like(vmem, one) for one in (recv, sorted_keys, sorted_values, codes, states)]
        + [vmem((prompts // 2, HALF // HD * all_rows, 2 * HD), bf16), sem, sems(4)],
        (8 * all_rows * keys * HD, 4 << 20),
    )(recv, sorted_keys, sorted_values, codes, states)
    returned = lax.all_to_all(back, "heads", split_axis=0, concat_axis=0, tiled=True)

    count = HALF // HD * 2 * SUB
    channels = step_x.shape[2]
    rates, skips = decay_rate.reshape(1, -1), skip_gain.reshape(1, -1)
    prompt_out, own, own_sum, fade, local = call(
        prompt_kernel,
        (
            shape(prompt_x.shape, bf16),
            shape((KVH, count, HD), f32),
            shape((KVH, count, HD), f32),
            shape((SUB, channels), f32),
            shape((SUB, channels), f32),
        ),
        [hbm] * 17,
        (hbm,) * 5,
        block
        + tables
        + [
            vmem((KVH, count, HD), f32),
            vmem((KVH, count, HD), f32),
            vmem((SUB, channels), f32),
            vmem((SUB, channels), f32),
            vmem((SUB, fresh_cache.shape[2]), f32),
            vmem((SUB, step_c.shape[2]), f32),
            vmem((steps, SUB, channels), f32),
            like(smem, decay_rate),
            like(smem, skip_gain),
            like(smem, lengths),
            like(vmem, prompt_dt),
            like(vmem, rates),
            like(vmem, skips),
            like(vmem, send),
            like(vmem, fresh_cache),
            like(vmem, step_x),
            like(vmem, step_b),
            like(vmem, step_c),
            like(vmem, step_dt),
            sem,
            sem,
            sem,
            sem,
            sems(12),
        ],
        (work * 5 * (prompts - EARLY), 8 << 20),
        {16: 0},
    )(
        decay_rate,
        skip_gain,
        lengths,
        prompt_dt,
        rates,
        skips,
        send,
        fresh_cache,
        step_x,
        step_b,
        step_c,
        step_dt,
        prompt_x,
        prompt_b,
        prompt_c,
        back,
        early_out,
    )

    mixer_out, attention_out = call(
        functools.partial(merge_kernel, width),
        (shape(step_x.shape, bf16), shape(queries.shape, bf16)),
        [hbm] * 5,
        (hbm, hbm),
        [like(vmem, one) for one in (returned, own, own_sum, fade, local)]
        + [vmem((SUB, channels), f32), vmem((SUB, queries.shape[2]), f32)]
        + [like(vmem, step_x), like(vmem, queries), sems(5)],
        (0, 2 << 20),
    )(returned, own, own_sum, fade, local)
    return (prompt_out, jnp.swapaxes(mixer_out, 0, 1), jnp.swapaxes(attention_out, 0, 1))


def solution(mesh):
    in_specs = (
        P("groups", "heads", None),
        P("groups", None, None),
        P("groups", None, None),
        P("heads", "groups", None),
        P(),
        P(),
        P("groups"),
        P("groups", None),
        P("groups", None),
        P(("groups", "heads"), None, None),
        P("groups"),
        P(("groups", "heads"), None, None),
        P(("groups", "heads"), None, None),
        P(("groups", "heads"), None, None),
        P(("groups", "heads"), None, None),
        P(("groups", "heads"), None, None),
        P(("groups", "heads"), None, None),
    )
    out_specs = (
        P("groups", "heads", None),
        P(("groups", "heads"), None, None),
        P(("groups", "heads"), None, None),
    )
    return jax.shard_map(
        on_device, mesh=mesh, in_specs=in_specs, out_specs=out_specs, check_vma=False
    )
```

```python
import functools
import math

import jax
import jax.numpy as jnp
from jax import lax
from jax.experimental import pallas as pl
from jax.experimental.pallas import tpu as pltpu
from jax.sharding import PartitionSpec as P

NS = 256
HP = 64
HPG = 32
KVH = 8
HD = 128
PAGE = 16
PAGES = 16
LANES = 128
SUB = 8
HALF = 512
LEVELS = (128, 64, 32, 16)
LOG2E = math.log2(math.e)
SCORE = LOG2E / math.sqrt(HD)
NONE = -1e30
FLOOR = -1e29
PAIRS = 6
LENGTH_BITS = 10
AHEAD = 2
EARLY = 2
VMEM_LIMIT = 64 * 1024 * 1024

f32 = jnp.float32
bf16 = jnp.bfloat16


def iota(shape, dim):
    return lax.broadcasted_iota(jnp.int32, shape, dim)


def exchange_order(owners):
    bits = (owners - 1).bit_length()
    return [int(format(owners - 1 - rank, f"0{bits}b")[::-1], 2) for rank in range(owners)]


def dot_nt(left, right):
    return lax.dot_general(left, right, (((1,), (1,)), ((), ())), preferred_element_type=f32)


def stack_rows(source, held):
    steps, rows = source.shape[0], source.shape[1]
    held[...] = jnp.zeros_like(held)
    for k in range(steps):
        held[k * rows : (k + 1) * rows, :] = source[k].astype(f32)


def spare(blocks, taken):
    return [(row, b) for row in range(PAIRS, SUB) for b in range(blocks)][taken : taken + PAIRS]


def lift(value, slots):
    row = iota(value.shape[:2] + (LANES,), 1)
    found = jnp.zeros(row.shape, f32)
    for pair, (at, b) in enumerate(slots):
        one = value[:, at : at + 1, b * LANES : (b + 1) * LANES]
        found = jnp.where(row == pair, jnp.broadcast_to(one, row.shape), found)
    return found


def fetches(pairs, sems, first=0):
    copies = [pltpu.make_async_copy(src, dst, sems.at[first + n]) for n, (src, dst) in enumerate(pairs)]
    for copy in copies:
        copy.start()
    return copies


def pack_kernel(group, ways, q_any, c_any, out_ref, q_ref, c_ref, q_held, c_held, rest, sems):
    owners = out_ref.shape[0] // SUB
    for copy in fetches([(q_any, q_ref), (c_any, c_ref)], sems):
        copy.wait()
    stack_rows(q_ref, q_held)
    stack_rows(c_ref, c_held)
    span = 2 * HALF
    slots = spare(HALF // LANES + 1, 0)
    rest[...] = jnp.zeros_like(rest)
    for e in range(c_ref.shape[2] // NS):
        rest[e, :PAIRS, HALF:] = c_held[:PAIRS, e * NS : e * NS + LANES]
        for pair, (row, b) in enumerate(slots):
            rest[e, row : row + 1, b * LANES : (b + 1) * LANES] = c_held[
                pair : pair + 1, e * NS + LANES : (e + 1) * NS
            ]
    real = iota((SUB, HALF), 0) < PAIRS
    order = exchange_order(owners)
    for rank in range(0, owners, 2):
        blocks, ends = [], []
        for d in order[rank : rank + 2]:
            begin, e = d // ways * span + d % 2 * HALF, (d * group) // HPG
            blocks.append(jnp.where(real, q_held[:, begin : begin + HALF], rest[e, :, :HALF]))
            ends.append(rest[e, :, HALF:])
        place = slice(rank * SUB, (rank + 2) * SUB)
        out_ref[place, :HALF] = jnp.concatenate(blocks, axis=0).astype(bf16)
        out_ref[place, HALF:] = jnp.concatenate(ends, axis=0).astype(bf16)


def sign_tables(signs, tail):
    length = signs.shape[-1]
    j = iota((length, length), 0)
    i = iota((length, length), 1)
    for l, n in enumerate(LEVELS):
        middle = (i // (2 * n)) * (2 * n) + (n - 1)
        signs[l] = (jnp.where(j <= i, 1.0, 0.0) - jnp.where(j <= middle, 1.0, 0.0)).astype(bf16)
    if tail:
        signs[len(LEVELS)] = jnp.where(j > i, 1.0, 0.0).astype(bf16)


def head_factors(first, dt_ref, rate_ref, skip_ref, len_ref, signs, w_in, w_out, w_skip, w_tail):
    group, prompts, length = dt_ref.shape
    row = iota((prompts, length), 0)
    lens = jnp.zeros((prompts, length), jnp.int32)
    for r in range(prompts):
        lens = jnp.where(row == r, len_ref[r], lens)
    valid = iota((prompts, length), 1) < lens
    moved = [jnp.where(valid, dt_ref[h].astype(f32), 0.0) for h in range(group)]
    every = jnp.concatenate(moved, axis=0).astype(bf16)
    rates = [rate_ref[first + h] * LOG2E for h in range(group)]
    if w_tail is not None:
        total = jnp.dot(every, signs[len(LEVELS)], preferred_element_type=f32)
        for h in range(group):
            part = total[h * prompts : (h + 1) * prompts]
            w_tail[:, h, :] = jnp.exp2(-(rates[h] * part)) * moved[h]
    for h in range(group):
        w_skip[:, h, :] = jnp.where(valid, skip_ref[first + h], 0.0)
    for l, n in enumerate(LEVELS):
        total = jnp.dot(every, signs[l], preferred_element_type=f32)
        for h in range(group):
            gap = rates[h] * total[h * prompts : (h + 1) * prompts]
            if n == LEVELS[-1]:
                up, down = jnp.exp2(gap), jnp.exp2(-gap)
            else:
                up, down = jnp.exp2(jnp.minimum(gap, 0.0)), jnp.exp2(-jnp.maximum(gap, 0.0))
            w_in[l, :, h, :] = up * moved[h]
            w_out[l, :, h, :] = jnp.where(valid, down, 0.0)


def level_masks(masks):
    length = masks.shape[-1]
    j = iota((length, length), 0)
    i = iota((length, length), 1)
    for l, n in enumerate(LEVELS):
        same = (j // (2 * n)) == (i // (2 * n))
        if n == LEVELS[-1]:
            keep = same & (j <= i)
        else:
            keep = same & ((j % (2 * n)) < n) & ((i % (2 * n)) >= n)
        masks[l] = jnp.where(keep, 1.0, 0.0).astype(bf16)


def prompt_result(r, x_held, b_held, c_held, w_in, w_out, w_skip, masks, out_held):
    width, length = x_held.shape[1], x_held.shape[2]
    group = width // HP
    half = length // 2
    inputs = x_held[r].astype(f32).reshape(group, HP, length)
    scores = dot_nt(b_held[r], c_held[r]).astype(bf16)
    total = inputs * w_skip[r][:, None, :]
    left, right = total[..., :half], total[..., half:]
    for l, n in enumerate(LEVELS):
        if 2 * n == length:
            scaled = (inputs[..., :half] * w_in[l, r][:, None, :half]).astype(bf16).reshape(width, half)
            added = jnp.dot(scaled, scores[:half, half:], preferred_element_type=f32)
            right = right + added.reshape(group, HP, half) * w_out[l, r][:, None, half:]
        else:
            scaled = (inputs * w_in[l, r][:, None, :]).astype(bf16).reshape(width, length)
            added = jnp.dot(scaled, scores * masks[l], preferred_element_type=f32)
            added = added.reshape(group, HP, length) * w_out[l, r][:, None, :]
            left = left + added[..., :half]
            right = right + added[..., half:]
    out_held[r] = jnp.concatenate([left, right], axis=-1).reshape(width, length).astype(bf16)


def state_kernel(
    rate_any,
    skip_any,
    len_any,
    owner_any,
    table_any,
    slot_any,
    dt_any,
    x_any,
    b_any,
    c_any,
    pages_any,
    other_any,
    state_any,
    key_any,
    value_any,
    code_any,
    out_any,
    x_held,
    b_held,
    c_held,
    out_held,
    w_in,
    w_out,
    w_skip,
    masks,
    signs,
    w_tail,
    state_held,
    pages_held,
    key_held,
    value_held,
    code_held,
    rate_ref,
    skip_ref,
    len_ref,
    owner_ref,
    table_ref,
    slot_ref,
    dt_ref,
    x_sem,
    b_sem,
    c_sem,
    out_sem,
    state_sem,
    sems,
):
    group, prompts, length = dt_ref.shape
    smalls = fetches(
        [
            (dt_any, dt_ref),
            (rate_any, rate_ref),
            (skip_any, skip_ref),
            (len_any, len_ref),
            (owner_any, owner_ref),
            (table_any, table_ref),
            (slot_any, slot_ref),
        ],
        sems,
    )
    me = lax.axis_index("heads")
    core = lax.rem(me, 2)
    first = me * group
    column = pl.multiple_of((first // HPG) * NS, NS)

    def x_copy(r):
        return pltpu.make_async_copy(x_any.at[r], x_held.at[r], x_sem.at[r])

    def b_copy(r):
        return pltpu.make_async_copy(b_any.at[r, :, pl.ds(column, NS)], b_held.at[r], b_sem.at[r])

    def c_copy(r):
        return pltpu.make_async_copy(c_any.at[r, :, pl.ds(column, NS)], c_held.at[r], c_sem.at[r])

    def out_copy(r):
        return pltpu.make_async_copy(out_held.at[r], out_any.at[r], out_sem.at[r])

    def state_copy(r):
        return pltpu.make_async_copy(state_held.at[r], state_any.at[r], state_sem.at[r])

    def ask(r):
        x_copy(r).start()
        b_copy(r).start()

    pages = fetches([(pages_any, pages_held.at[core]), (other_any, pages_held.at[1 - core])], sems, len(smalls))
    for r in range(prompts):
        ask(r)
    sign_tables(signs, True)
    level_masks(masks)
    for copy in smalls:
        copy.wait()
    head_factors(first, dt_ref, rate_ref, skip_ref, len_ref, signs, w_in, w_out, w_skip, w_tail)

    def one(r, _):
        x_copy(r).wait()
        b_copy(r).wait()
        width = x_held.shape[1]
        inputs = x_held[r].astype(f32).reshape(group, HP, length)
        scaled = (inputs * w_tail[r][:, None, :]).astype(bf16).reshape(width, length)
        state_held[r] = jnp.dot(scaled, b_held[r], preferred_element_type=f32).astype(bf16)
        state_copy(r).start()
        return 0

    lax.fori_loop(0, prompts, one, 0, unroll=2)
    for r in range(EARLY):
        c_copy(r).start()

    spread = table_ref.shape[1] // owner_ref.shape[1]
    for copy in pages:
        copy.wait()
    for n in range(2):
        for r in range(prompts):
            for page in range(spread):
                holder = me - core + n
                row = table_ref[r, holder * spread + page] - holder * (prompts * spread)
                block = pages_held[n, row]
                place = pl.ds((n * spread + page) * PAGE, PAGE)
                columns = pl.ds(r % 2 * HD, HD)
                key_held[r // 2, place, columns] = block[:, :HD]
                value_held[r // 2, place, columns] = block[:, HD:]

    owners = owner_ref.shape[1]
    rows_dev = slot_ref.shape[0] // owners
    inner = iota((2 * SUB, LANES), 0)

    order = exchange_order(owners)
    for rank in range(0, owners, 2):
        block = jnp.zeros((2 * SUB, LANES), jnp.int32)
        for n in range(2):
            s = order[rank + n]
            for i in range(rows_dev):
                target = owner_ref[slot_ref[s * rows_dev + i], s]
                code = target * (1 << LENGTH_BITS) + len_ref[target]
                block = jnp.where((inner // SUB == n) & (inner % rows_dev == i), code, block)
        code_held[rank * SUB : (rank + 2) * SUB, :] = block
    marks = fetches([(key_held, key_any), (value_held, value_any), (code_held, code_any)], sems)

    def early(r, _):
        c_copy(r).wait()
        prompt_result(r, x_held, b_held, c_held, w_in, w_out, w_skip, masks, out_held)
        out_copy(r).start()
        return 0

    lax.fori_loop(0, EARLY, early, 0, unroll=2)
    for copy in marks:
        copy.wait()
    for r in range(prompts):
        state_copy(r).wait()
    for r in range(EARLY):
        out_copy(r).wait()


def serve_kernel(
    recv_any,
    key_any,
    value_any,
    code_any,
    state_any,
    out_ref,
    recv_ref,
    key_ref,
    value_ref,
    code_ref,
    state_ref,
    query_ref,
    state_sem,
    sems,
):
    rows = recv_ref.shape[0]
    prompts, width = state_ref.shape[0], state_ref.shape[1]
    copies = fetches(
        [(recv_any, recv_ref), (code_any, code_ref), (key_any, key_ref), (value_any, value_ref)], sems
    )
    states = fetches([(state_any.at[r], state_ref.at[r]) for r in range(prompts)], state_sem)
    heads = HALF // HD
    keys = key_ref.shape[1]
    chips = keys // PAGE
    begin = lax.rem(lax.axis_index("heads") // 2 * chips, PAGES) * PAGE
    copies[0].wait()
    copies[1].wait()
    code = code_ref[...]
    target = code >> LENGTH_BITS
    lengths = code & ((1 << LENGTH_BITS) - 1)
    for r in range(prompts):
        for g in range(heads):
            query = recv_ref[:, g * HD : (g + 1) * HD].astype(f32)
            query_ref[r // 2, g * rows : (g + 1) * rows, r % 2 * HD : (r % 2 + 1) * HD] = jnp.where(
                target == r, query, 0.0
            ).astype(bf16)
    copies[2].wait()
    scores = jnp.zeros((heads * rows, keys), f32)
    for pair in range(prompts // 2):
        scores = scores + dot_nt(query_ref[pair], key_ref[pair])
    seen = jnp.concatenate([lengths[:, :1]] * heads, axis=0) > iota((heads * rows, keys), 1) + begin
    scores = jnp.where(seen, scores * SCORE, NONE)
    highest = jnp.maximum(jnp.max(scores, axis=1, keepdims=True), FLOOR)
    weight = jnp.exp2(scores - highest)
    total = jnp.sum(weight, axis=1, keepdims=True)
    some = total > 0.0
    safe = jnp.where(some, total, 1.0)
    result = jnp.where(some, highest + jnp.log2(safe), NONE)
    weight = weight.astype(bf16)
    copies[3].wait()
    targets = jnp.concatenate([target] * heads, axis=0)
    value = jnp.zeros((heads * rows, HD), f32)
    for pair in range(prompts // 2):
        both = jnp.dot(weight, value_ref[pair], preferred_element_type=f32)
        for n in range(2):
            value = jnp.where(targets == 2 * pair + n, both[:, n * HD : (n + 1) * HD], value)
    value = value / safe
    lane = iota((rows, LANES), 1)
    sums = jnp.zeros((rows, LANES), f32)
    for g in range(heads):
        sums = jnp.where(lane % 4 == g, result[g * rows : (g + 1) * rows], sums)
    high = sums.astype(bf16).astype(f32)
    rest = sums - high
    middle = rest.astype(bf16).astype(f32)
    piece = lane % 16 // 4
    pieces = jnp.where(piece == 0, high, jnp.where(piece == 1, middle, rest - middle))
    pair = iota((rows, LANES), 0) % SUB
    pieces = jnp.where((lane // 16 == pair) & (piece < 3), pieces, 0.0)
    packed = jnp.sum(pieces.reshape(rows // SUB, SUB, LANES), axis=1, keepdims=True)

    given = recv_ref[...].astype(f32).reshape(rows // SUB, SUB, recv_ref.shape[1])
    ending = lift(given, spare(heads + 1, 0))
    readout = jnp.concatenate([given[..., HALF:], ending], axis=-1).reshape(rows, NS)
    target = jnp.concatenate([target, target], axis=-1)
    found = jnp.zeros((rows, width), f32)
    for r in range(prompts):
        picked = jnp.where(target == r, readout, 0.0).astype(bf16)
        states[r].wait()
        found = found + dot_nt(picked, state_ref[r])
    if width < LANES:
        found = jnp.concatenate([found, jnp.zeros((rows, LANES - width), f32)], axis=-1)
    blocks = [value[g * rows : (g + 1) * rows] for g in range(heads)]
    blocks += [found[:, b : b + LANES] for b in range(0, found.shape[1], LANES)]
    blocks = [one.reshape(rows // SUB, SUB, LANES) for one in blocks]
    row = iota((rows // SUB, SUB, LANES), 1)
    last = blocks.pop()
    blocks[0] = jnp.where(row == PAIRS, jnp.broadcast_to(packed, row.shape), blocks[0])
    for n, (at, b) in enumerate(spare(len(blocks), 1)):
        one = jnp.broadcast_to(last[:, n : n + 1, :], row.shape)
        blocks[b] = jnp.where(row == at, one, blocks[b])
    for b, one in enumerate(blocks):
        out_ref[:, b * LANES : (b + 1) * LANES] = one.reshape(rows, LANES).astype(bf16)


def prompt_kernel(
    rate_any,
    skip_any,
    len_any,
    dt_any,
    rates_any,
    skips_any,
    send_any,
    fresh_any,
    sx_any,
    sb_any,
    sc_any,
    sdt_any,
    x_any,
    b_any,
    c_any,
    after_any,
    early_any,
    out_any,
    own_any,
    ownsum_any,
    fade_any,
    local_any,
    x_held,
    b_held,
    c_held,
    out_held,
    w_in,
    w_out,
    w_skip,
    masks,
    signs,
    own_ref,
    ownsum_ref,
    fade_ref,
    local_ref,
    fresh_held,
    c_rows,
    x_rows,
    rate_ref,
    skip_ref,
    len_ref,
    dt_ref,
    rates_ref,
    skips_ref,
    send_ref,
    fresh_ref,
    sx_ref,
    sb_ref,
    sc_ref,
    sdt_ref,
    x_sem,
    b_sem,
    c_sem,
    out_sem,
    sems,
):
    group, prompts, length = dt_ref.shape
    smalls = fetches(
        [
            (dt_any, dt_ref),
            (rate_any, rate_ref),
            (skip_any, skip_ref),
            (len_any, len_ref),
            (rates_any, rates_ref),
            (skips_any, skips_ref),
            (send_any, send_ref),
            (fresh_any, fresh_ref),
            (sx_any, sx_ref),
            (sb_any, sb_ref),
            (sc_any, sc_ref),
            (sdt_any, sdt_ref),
        ],
        sems,
    )
    me = lax.axis_index("heads")
    first = me * group
    column = pl.multiple_of((first // HPG) * NS, NS)

    def x_copy(r):
        return pltpu.make_async_copy(x_any.at[r], x_held.at[r], x_sem.at[r])

    def b_copy(r):
        return pltpu.make_async_copy(b_any.at[r, :, pl.ds(column, NS)], b_held.at[r], b_sem.at[r])

    def c_copy(r):
        return pltpu.make_async_copy(c_any.at[r, :, pl.ds(column, NS)], c_held.at[r], c_sem.at[r])

    def out_copy(r):
        return pltpu.make_async_copy(out_held.at[r], out_any.at[r], out_sem.at[r])

    def ask(r):
        x_copy(r).start()
        b_copy(r).start()
        c_copy(r).start()

    for r in range(EARLY, min(EARLY + AHEAD, prompts)):
        ask(r)
    sign_tables(signs, False)
    level_masks(masks)
    for copy in smalls:
        copy.wait()
    head_factors(first, dt_ref, rate_ref, skip_ref, len_ref, signs, w_in, w_out, w_skip, None)
    own_attention(send_ref, fresh_ref, fresh_held, own_ref, ownsum_ref)
    own_mixer(rates_ref, skips_ref, sx_ref, sb_ref, sc_ref, sdt_ref, c_rows, x_rows, fade_ref, local_ref)
    outs = fetches(
        [(own_ref, own_any), (ownsum_ref, ownsum_any), (fade_ref, fade_any), (local_ref, local_any)], sems
    )

    def one(r, _):
        @pl.when(r + AHEAD < prompts)
        def _():
            ask(r + AHEAD)

        x_copy(r).wait()
        b_copy(r).wait()
        c_copy(r).wait()
        prompt_result(r, x_held, b_held, c_held, w_in, w_out, w_skip, masks, out_held)
        out_copy(r).start()
        return 0

    lax.fori_loop(EARLY, prompts, one, 0, unroll=2)
    for copy in outs:
        copy.wait()
    for r in range(EARLY, prompts):
        out_copy(r).wait()


def own_attention(send_ref, fresh_ref, fresh_held, own_ref, ownsum_ref):
    steps, rows = fresh_ref.shape[0], fresh_ref.shape[1]
    owners = send_ref.shape[0]
    order = exchange_order(owners)
    ways = owners // KVH
    stack_rows(fresh_ref, fresh_held)
    count = HALF // HD * 2 * SUB
    pair = iota((count, SUB), 0) % SUB
    key = iota((count, SUB), 1)
    seen = (key % rows == pair % rows) & (key <= pair) & (key < rows * steps)
    seen = seen | ((pair >= rows * steps) & (key == 0))
    for v in range(KVH):
        halves = [send_ref[order.index(v * ways + n), :, :HALF].astype(f32) for n in range(2)]
        parts = [half[:, g * HD : (g + 1) * HD] for g in range(HALF // HD) for half in halves]
        query = jnp.concatenate(parts, axis=0).astype(bf16)
        keys = fresh_held[:, v * HD : (v + 1) * HD].astype(bf16)
        values = fresh_held[:, (KVH + v) * HD : (KVH + v + 1) * HD].astype(bf16)
        scores = jnp.where(seen, dot_nt(query, keys) * SCORE, NONE)
        highest = jnp.max(scores, axis=1, keepdims=True)
        weight = jnp.exp2(scores - highest)
        total = jnp.sum(weight, axis=1, keepdims=True)
        weight = (weight / total).astype(bf16)
        own_ref[v] = jnp.dot(weight, values, preferred_element_type=f32)
        ownsum_ref[v] = jnp.broadcast_to(highest + jnp.log2(total), (count, HD))


def own_mixer(rates_ref, skips_ref, sx_ref, sb_ref, sc_ref, sdt_ref, c_rows, x_rows, fade_ref, local_ref):
    steps, rows, heads = sdt_ref.shape
    stack_rows(sc_ref, c_rows)
    for u in range(steps):
        given = sx_ref[u].astype(f32)
        for k in range(SUB // rows):
            x_rows[u, k * rows : (k + 1) * rows, :] = given
    pair = iota((SUB, heads), 0)
    step = pair // rows
    live = pair < rows * steps
    head = iota((SUB, heads), 1)

    def spread_rows(ref, u):
        given = ref[u].astype(f32)
        return jnp.concatenate([given] * (SUB // rows), axis=0)

    rates = jnp.broadcast_to(rates_ref[...], (SUB, heads)) * LOG2E
    skips = jnp.broadcast_to(skips_ref[...], (SUB, heads))
    moved = [spread_rows(sdt_ref, u) for u in range(steps)]
    kept = [jnp.where(u <= step, moved[u], 0.0) for u in range(steps)]
    parts = [jnp.where(live, jnp.exp2(-(rates * sum(kept))), 0.0)]
    for u in range(steps):
        products = c_rows[...] * spread_rows(sb_ref, u)
        inner = jnp.zeros((SUB, heads), f32)
        for e in range(products.shape[1] // NS):
            found = jnp.sum(products[:, e * NS : (e + 1) * NS], axis=1, keepdims=True)
            inner = jnp.where(head // HPG == e, found, inner)
        gap = jnp.zeros((SUB, heads), f32)
        for t in range(u + 1, steps):
            gap = gap + kept[t]
        weight = jnp.where(u <= step, jnp.exp2(-(rates * gap)) * moved[u] * inner, 0.0)
        weight = weight + jnp.where(u == step, skips, 0.0)
        parts.append(jnp.where(live, weight, 0.0))
    stacked = jnp.concatenate(parts, axis=0)
    high = stacked.astype(bf16)
    low = (stacked - high.astype(f32)).astype(bf16)
    both = jnp.concatenate([high.astype(f32), low.astype(f32)], axis=0)
    count = stacked.shape[0]
    chunk = SUB * HP
    widen = jnp.where(iota((heads, chunk), 0) % SUB == iota((heads, chunk), 1) // HP, 1.0, 0.0).astype(bf16)
    lane = iota(both.shape, 1)
    for d in range(heads // SUB):
        picked = jnp.where(lane // SUB == d, both, 0.0).astype(bf16)
        wide = jnp.dot(picked, widen, preferred_element_type=f32)
        wide = wide[:count] + wide[count:]
        columns = slice(d * chunk, (d + 1) * chunk)
        fade_ref[:, columns] = wide[:SUB]
        value = jnp.zeros((SUB, chunk), f32)
        for u in range(steps):
            value = value + wide[(u + 1) * SUB : (u + 2) * SUB] * x_rows[u, :, columns]
        local_ref[:, columns] = value


def merge_kernel(
    width,
    back_any,
    own_any,
    ownsum_any,
    fade_any,
    local_any,
    mixer_any,
    attention_any,
    back_ref,
    own_ref,
    ownsum_ref,
    fade_ref,
    local_ref,
    mixed,
    attended,
    mixer_ref,
    attention_ref,
    sems,
):
    copies = fetches([(back_any, back_ref), (fade_any, fade_ref), (local_any, local_ref)], sems)
    rest = fetches([(own_any, own_ref), (ownsum_any, ownsum_ref)], sems, len(copies))
    for copy in copies:
        copy.wait()
    owners = back_ref.shape[0]
    ways = owners // KVH
    order = exchange_order(owners)
    steps, rows = mixer_ref.shape[0], mixer_ref.shape[1]
    for d in range(0, owners, 2):
        block = jnp.stack([back_ref[order.index(d + n)].astype(f32) for n in range(2)])
        ending = lift(block, spare(back_ref.shape[2] // LANES, 1))
        if back_ref.shape[2] > HALF:
            ending = jnp.concatenate([block[..., HALF:], ending], axis=-1)
        found = ending[..., :width]
        found = jnp.concatenate([found[0], found[1]], axis=-1)
        columns = slice(d * width, (d + 2) * width)
        mixed[:, columns] = found * fade_ref[:, columns] + local_ref[:, columns]
    for k in range(steps):
        mixer_ref[k] = mixed[k * rows : (k + 1) * rows, :].astype(bf16)
    outs = fetches([(mixer_ref, mixer_any)], sems)
    for copy in rest:
        copy.wait()
    lane = iota((2, SUB, LANES), 2)
    mine = (lane // 16 == iota((2, SUB, LANES), 1)) & (lane % 16 < 12)
    for v in range(KVH):
        blocks, pieces = [], []
        for d in range(v * ways, (v + 1) * ways, 2):
            block = jnp.stack([back_ref[order.index(d + n), :, :HALF].astype(f32) for n in range(2)])
            packed = block[:, PAIRS : PAIRS + 1, :LANES]
            blocks.append(block.reshape(2 * SUB, HALF))
            pieces.append(jnp.where(mine, jnp.broadcast_to(packed, (2, SUB, LANES)), 0.0))
        for g in range(HALF // HD):
            part = slice(g * 2 * SUB, (g + 1) * 2 * SUB)
            own_sum = ownsum_ref[v, part, :]
            wide = []
            for piece in pieces:
                one = jnp.sum(jnp.where(lane % 4 == g, piece, 0.0), axis=-1, keepdims=True)
                wide.append(jnp.broadcast_to(one, (2, SUB, HD)).reshape(2 * SUB, HD))
            highest = functools.reduce(jnp.maximum, wide, own_sum)
            weight = jnp.exp2(own_sum - highest)
            total = weight
            value = weight * own_ref[v, part, :]
            for one, block in zip(wide, blocks):
                weight = jnp.exp2(one - highest)
                total = total + weight
                value = value + weight * block[:, g * HD : (g + 1) * HD]
            value = value / total
            start = v * 2 * HALF + g * HD
            attended[:, start : start + HD] = value[:SUB]
            attended[:, start + HALF : start + HALF + HD] = value[SUB:]
    for k in range(steps):
        attention_ref[k] = attended[k * rows : (k + 1) * rows, :].astype(bf16)
    outs += fetches([(attention_ref, attention_any)], sems, 1)
    for copy in outs:
        copy.wait()


def call(kernel, out_shape, in_spaces, out_spaces, scratch, cost, aliases=None):
    def spec(space):
        return pl.BlockSpec(memory_space=space)

    return pl.pallas_call(
        kernel,
        out_shape=out_shape,
        in_specs=[spec(space) for space in in_spaces],
        out_specs=jax.tree.map(spec, out_spaces),
        scratch_shapes=scratch,
        input_output_aliases=aliases or {},
        compiler_params=pltpu.CompilerParams(vmem_limit_bytes=VMEM_LIMIT),
        cost_estimate=pl.CostEstimate(flops=cost[0], bytes_accessed=cost[1], transcendentals=0),
    )


def on_device(
    prompt_x,
    prompt_b,
    prompt_c,
    prompt_dt,
    decay_rate,
    skip_gain,
    lengths,
    owner_list,
    page_table,
    cache_pages,
    row_slot,
    step_x,
    step_b,
    step_c,
    step_dt,
    queries,
    fresh_cache,
):
    owners = lax.axis_size("heads")
    ways = owners // KVH
    group, prompts, length = prompt_dt.shape
    width = prompt_x.shape[1]
    keys = cache_pages.shape[0] * PAGE
    span = 2 * keys // prompts
    steps = step_x.shape[1]
    all_rows = owners * SUB
    shape = jax.ShapeDtypeStruct
    smem, vmem, hbm = pltpu.SMEM, pltpu.VMEM, pltpu.HBM
    sem = pltpu.SemaphoreType.DMA((prompts,))
    levels = len(LEVELS)
    step_x, step_b, step_c, step_dt, queries, fresh_cache = (
        jnp.swapaxes(one, 0, 1) for one in (step_x, step_b, step_c, step_dt, queries, fresh_cache)
    )
    owner_list = owner_list.T

    def like(space, array):
        return space(array.shape, array.dtype)

    def sems(count):
        return pltpu.SemaphoreType.DMA((count,))

    other_pages = lax.ppermute(cache_pages, "heads", [(d, d + 1 - 2 * (d % 2)) for d in range(owners)])
    send = call(
        functools.partial(pack_kernel, group, ways),
        shape((all_rows, HALF + LANES), bf16),
        [hbm, hbm],
        vmem,
        [
            like(vmem, queries),
            like(vmem, step_c),
            vmem((SUB, queries.shape[2]), f32),
            vmem((SUB, step_c.shape[2]), f32),
            vmem((step_c.shape[2] // NS, SUB, HALF + LANES), f32),
            sems(2),
        ],
        (0, 1 << 19),
    )(queries, step_c)
    order = [exchange_order(owners)]
    recv = lax.all_to_all(
        send, "heads", split_axis=0, concat_axis=0, tiled=True, axis_index_groups=order
    )

    block = [
        vmem((prompts, width, length), bf16),
        vmem((prompts, length, NS), bf16),
        vmem((prompts, length, NS), bf16),
        vmem((prompts, width, length), bf16),
        vmem((levels, prompts, group, length), f32),
        vmem((levels, prompts, group, length), f32),
        vmem((prompts, group, length), f32),
    ]
    tables = [vmem((levels, length, length), bf16), vmem((levels + 1, length, length), bf16)]
    work = 2 * width * length * NS
    states, sorted_keys, sorted_values, codes, early_out = call(
        state_kernel,
        (
            shape((prompts, width, NS), bf16),
            shape((prompts // 2, span, 2 * HD), bf16),
            shape((prompts // 2, span, 2 * HD), bf16),
            shape((all_rows, LANES), jnp.int32),
            shape(prompt_x.shape, bf16),
        ),
        [hbm] * 12,
        (hbm,) * 5,
        block
        + tables
        + [vmem((prompts, group, length), f32), vmem((prompts, width, NS), bf16)]
        + [vmem((2,) + cache_pages.shape, bf16)]
        + [vmem((prompts // 2, span, 2 * HD), bf16)] * 2
        + [vmem((all_rows, LANES), jnp.int32)]
        + [like(smem, one) for one in (decay_rate, skip_gain, lengths, owner_list, page_table, row_slot)]
        + [like(vmem, prompt_dt), sem, sem, sem, sem, sem, sems(9)],
        (work * (prompts + 5 * EARLY), 6 << 20),
    )(
        decay_rate,
        skip_gain,
        lengths,
        owner_list,
        page_table,
        row_slot,
        prompt_dt,
        prompt_x,
        prompt_b,
        prompt_c,
        cache_pages,
        other_pages,
    )

    back = call(
        serve_kernel,
        shape((all_rows, HALF + max(LANES, width) - LANES), bf16),
        [hbm] * 5,
        vmem,
        [like(vmem, one) for one in (recv, sorted_keys, sorted_values, codes, states)]
        + [vmem((prompts // 2, HALF // HD * all_rows, 2 * HD), bf16), sem, sems(4)],
        (8 * all_rows * keys * HD, 4 << 20),
    )(recv, sorted_keys, sorted_values, codes, states)
    returned = lax.all_to_all(
        back, "heads", split_axis=0, concat_axis=0, tiled=True, axis_index_groups=order
    ).reshape(owners, SUB, back.shape[1])

    count = HALF // HD * 2 * SUB
    channels = step_x.shape[2]
    rates, skips = decay_rate.reshape(1, -1), skip_gain.reshape(1, -1)
    prompt_out, own, own_sum, fade, local = call(
        prompt_kernel,
        (
            shape(prompt_x.shape, bf16),
            shape((KVH, count, HD), f32),
            shape((KVH, count, HD), f32),
            shape((SUB, channels), f32),
            shape((SUB, channels), f32),
        ),
        [hbm] * 17,
        (hbm,) * 5,
        block
        + tables
        + [
            vmem((KVH, count, HD), f32),
            vmem((KVH, count, HD), f32),
            vmem((SUB, channels), f32),
            vmem((SUB, channels), f32),
            vmem((SUB, fresh_cache.shape[2]), f32),
            vmem((SUB, step_c.shape[2]), f32),
            vmem((steps, SUB, channels), f32),
            like(smem, decay_rate),
            like(smem, skip_gain),
            like(smem, lengths),
            like(vmem, prompt_dt),
            like(vmem, rates),
            like(vmem, skips),
            vmem((owners, SUB, HALF + LANES), bf16),
            like(vmem, fresh_cache),
            like(vmem, step_x),
            like(vmem, step_b),
            like(vmem, step_c),
            like(vmem, step_dt),
            sem,
            sem,
            sem,
            sem,
            sems(12),
        ],
        (work * 5 * (prompts - EARLY), 8 << 20),
        {16: 0},
    )(
        decay_rate,
        skip_gain,
        lengths,
        prompt_dt,
        rates,
        skips,
        send.reshape(owners, SUB, HALF + LANES),
        fresh_cache,
        step_x,
        step_b,
        step_c,
        step_dt,
        prompt_x,
        prompt_b,
        prompt_c,
        back,
        early_out,
    )

    mixer_out, attention_out = call(
        functools.partial(merge_kernel, width),
        (shape(step_x.shape, bf16), shape(queries.shape, bf16)),
        [hbm] * 5,
        (hbm, hbm),
        [like(vmem, one) for one in (returned, own, own_sum, fade, local)]
        + [vmem((SUB, channels), f32), vmem((SUB, queries.shape[2]), f32)]
        + [like(vmem, step_x), like(vmem, queries), sems(5)],
        (0, 2 << 20),
    )(returned, own, own_sum, fade, local)
    return (prompt_out, jnp.swapaxes(mixer_out, 0, 1), jnp.swapaxes(attention_out, 0, 1))


def solution(mesh):
    in_specs = (
        P("groups", "heads", None),
        P("groups", None, None),
        P("groups", None, None),
        P("heads", "groups", None),
        P(),
        P(),
        P("groups"),
        P("groups", None),
        P("groups", None),
        P(("groups", "heads"), None, None),
        P("groups"),
        P(("groups", "heads"), None, None),
        P(("groups", "heads"), None, None),
        P(("groups", "heads"), None, None),
        P(("groups", "heads"), None, None),
        P(("groups", "heads"), None, None),
        P(("groups", "heads"), None, None),
    )
    out_specs = (
        P("groups", "heads", None),
        P(("groups", "heads"), None, None),
        P(("groups", "heads"), None, None),
    )
    return jax.shard_map(
        on_device, mesh=mesh, in_specs=in_specs, out_specs=out_specs, check_vma=False
    )
```

```python
import functools
import math

import jax
import jax.numpy as jnp
from jax import lax
from jax.experimental import pallas as pl
from jax.experimental.pallas import tpu as pltpu
from jax.sharding import PartitionSpec as P

NS = 256
HP = 64
HPG = 32
KVH = 8
HD = 128
PAGE = 16
PAGES = 16
LANES = 128
SUB = 8
HALF = 512
LEVELS = (128, 64, 32, 16)
LOG2E = math.log2(math.e)
SCORE = LOG2E / math.sqrt(HD)
NONE = -1e30
FLOOR = -1e29
PAIRS = 6
LENGTH_BITS = 10
AHEAD = 2
EARLY = 2
VMEM_LIMIT = 64 * 1024 * 1024

f32 = jnp.float32
bf16 = jnp.bfloat16


def iota(shape, dim):
    return lax.broadcasted_iota(jnp.int32, shape, dim)


def exchange_order(owners):
    middle = owners // 4
    return [middle] + [d for d in range(owners) if d != middle]


def dot_nt(left, right):
    return lax.dot_general(left, right, (((1,), (1,)), ((), ())), preferred_element_type=f32)


def stack_rows(source, held):
    steps, rows = source.shape[0], source.shape[1]
    held[...] = jnp.zeros_like(held)
    for k in range(steps):
        held[k * rows : (k + 1) * rows, :] = source[k].astype(f32)


def spare(blocks, taken):
    return [(row, b) for row in range(PAIRS, SUB) for b in range(blocks)][taken : taken + PAIRS]


def lift(value, slots):
    row = iota(value.shape[:2] + (LANES,), 1)
    found = jnp.zeros(row.shape, f32)
    for pair, (at, b) in enumerate(slots):
        one = value[:, at : at + 1, b * LANES : (b + 1) * LANES]
        found = jnp.where(row == pair, jnp.broadcast_to(one, row.shape), found)
    return found


def fetches(pairs, sems, first=0):
    copies = [pltpu.make_async_copy(src, dst, sems.at[first + n]) for n, (src, dst) in enumerate(pairs)]
    for copy in copies:
        copy.start()
    return copies


def pack_kernel(group, ways, q_any, c_any, out_ref, q_ref, c_ref, q_held, c_held, rest, sems):
    owners = out_ref.shape[0] // SUB
    for copy in fetches([(q_any, q_ref), (c_any, c_ref)], sems):
        copy.wait()
    stack_rows(q_ref, q_held)
    stack_rows(c_ref, c_held)
    span = 2 * HALF
    slots = spare(HALF // LANES + 1, 0)
    rest[...] = jnp.zeros_like(rest)
    for e in range(c_ref.shape[2] // NS):
        rest[e, :PAIRS, HALF:] = c_held[:PAIRS, e * NS : e * NS + LANES]
        for pair, (row, b) in enumerate(slots):
            rest[e, row : row + 1, b * LANES : (b + 1) * LANES] = c_held[
                pair : pair + 1, e * NS + LANES : (e + 1) * NS
            ]
    real = iota((SUB, HALF), 0) < PAIRS
    order = exchange_order(owners)
    for rank in range(0, owners, 2):
        blocks, ends = [], []
        for d in order[rank : rank + 2]:
            begin, e = d // ways * span + d % 2 * HALF, (d * group) // HPG
            blocks.append(jnp.where(real, q_held[:, begin : begin + HALF], rest[e, :, :HALF]))
            ends.append(rest[e, :, HALF:])
        place = slice(rank * SUB, (rank + 2) * SUB)
        out_ref[place, :HALF] = jnp.concatenate(blocks, axis=0).astype(bf16)
        out_ref[place, HALF:] = jnp.concatenate(ends, axis=0).astype(bf16)


def sign_tables(signs, tail):
    length = signs.shape[-1]
    j = iota((length, length), 0)
    i = iota((length, length), 1)
    for l, n in enumerate(LEVELS):
        middle = (i // (2 * n)) * (2 * n) + (n - 1)
        signs[l] = (jnp.where(j <= i, 1.0, 0.0) - jnp.where(j <= middle, 1.0, 0.0)).astype(bf16)
    if tail:
        signs[len(LEVELS)] = jnp.where(j > i, 1.0, 0.0).astype(bf16)


def head_factors(first, dt_ref, rate_ref, skip_ref, len_ref, signs, w_in, w_out, w_skip, w_tail):
    group, prompts, length = dt_ref.shape
    row = iota((prompts, length), 0)
    lens = jnp.zeros((prompts, length), jnp.int32)
    for r in range(prompts):
        lens = jnp.where(row == r, len_ref[r], lens)
    valid = iota((prompts, length), 1) < lens
    moved = [jnp.where(valid, dt_ref[h].astype(f32), 0.0) for h in range(group)]
    every = jnp.concatenate(moved, axis=0).astype(bf16)
    rates = [rate_ref[first + h] * LOG2E for h in range(group)]
    if w_tail is not None:
        total = jnp.dot(every, signs[len(LEVELS)], preferred_element_type=f32)
        for h in range(group):
            part = total[h * prompts : (h + 1) * prompts]
            w_tail[:, h, :] = jnp.exp2(-(rates[h] * part)) * moved[h]
    for h in range(group):
        w_skip[:, h, :] = jnp.where(valid, skip_ref[first + h], 0.0)
    for l, n in enumerate(LEVELS):
        total = jnp.dot(every, signs[l], preferred_element_type=f32)
        for h in range(group):
            gap = rates[h] * total[h * prompts : (h + 1) * prompts]
            if n == LEVELS[-1]:
                up, down = jnp.exp2(gap), jnp.exp2(-gap)
            else:
                up, down = jnp.exp2(jnp.minimum(gap, 0.0)), jnp.exp2(-jnp.maximum(gap, 0.0))
            w_in[l, :, h, :] = up * moved[h]
            w_out[l, :, h, :] = jnp.where(valid, down, 0.0)


def level_masks(masks):
    length = masks.shape[-1]
    j = iota((length, length), 0)
    i = iota((length, length), 1)
    for l, n in enumerate(LEVELS):
        same = (j // (2 * n)) == (i // (2 * n))
        if n == LEVELS[-1]:
            keep = same & (j <= i)
        else:
            keep = same & ((j % (2 * n)) < n) & ((i % (2 * n)) >= n)
        masks[l] = jnp.where(keep, 1.0, 0.0).astype(bf16)


def prompt_result(r, x_held, b_held, c_held, w_in, w_out, w_skip, masks, out_held):
    width, length = x_held.shape[1], x_held.shape[2]
    group = width // HP
    half = length // 2
    inputs = x_held[r].astype(f32).reshape(group, HP, length)
    scores = dot_nt(b_held[r], c_held[r]).astype(bf16)
    total = inputs * w_skip[r][:, None, :]
    left, right = total[..., :half], total[..., half:]
    for l, n in enumerate(LEVELS):
        if 2 * n == length:
            scaled = (inputs[..., :half] * w_in[l, r][:, None, :half]).astype(bf16).reshape(width, half)
            added = jnp.dot(scaled, scores[:half, half:], preferred_element_type=f32)
            right = right + added.reshape(group, HP, half) * w_out[l, r][:, None, half:]
        else:
            scaled = (inputs * w_in[l, r][:, None, :]).astype(bf16).reshape(width, length)
            added = jnp.dot(scaled, scores * masks[l], preferred_element_type=f32)
            added = added.reshape(group, HP, length) * w_out[l, r][:, None, :]
            left = left + added[..., :half]
            right = right + added[..., half:]
    out_held[r] = jnp.concatenate([left, right], axis=-1).reshape(width, length).astype(bf16)


def state_kernel(
    rate_any,
    skip_any,
    len_any,
    owner_any,
    table_any,
    slot_any,
    dt_any,
    x_any,
    b_any,
    c_any,
    pages_any,
    other_any,
    state_any,
    key_any,
    value_any,
    code_any,
    out_any,
    x_held,
    b_held,
    c_held,
    out_held,
    w_in,
    w_out,
    w_skip,
    masks,
    signs,
    w_tail,
    state_held,
    pages_held,
    key_held,
    value_held,
    code_held,
    rate_ref,
    skip_ref,
    len_ref,
    owner_ref,
    table_ref,
    slot_ref,
    dt_ref,
    x_sem,
    b_sem,
    c_sem,
    out_sem,
    state_sem,
    sems,
):
    group, prompts, length = dt_ref.shape
    smalls = fetches(
        [
            (dt_any, dt_ref),
            (rate_any, rate_ref),
            (skip_any, skip_ref),
            (len_any, len_ref),
            (owner_any, owner_ref),
            (table_any, table_ref),
            (slot_any, slot_ref),
        ],
        sems,
    )
    me = lax.axis_index("heads")
    core = lax.rem(me, 2)
    first = me * group
    column = pl.multiple_of((first // HPG) * NS, NS)

    def x_copy(r):
        return pltpu.make_async_copy(x_any.at[r], x_held.at[r], x_sem.at[r])

    def b_copy(r):
        return pltpu.make_async_copy(b_any.at[r, :, pl.ds(column, NS)], b_held.at[r], b_sem.at[r])

    def c_copy(r):
        return pltpu.make_async_copy(c_any.at[r, :, pl.ds(column, NS)], c_held.at[r], c_sem.at[r])

    def out_copy(r):
        return pltpu.make_async_copy(out_held.at[r], out_any.at[r], out_sem.at[r])

    def state_copy(r):
        return pltpu.make_async_copy(state_held.at[r], state_any.at[r], state_sem.at[r])

    def ask(r):
        x_copy(r).start()
        b_copy(r).start()

    pages = fetches([(pages_any, pages_held.at[core]), (other_any, pages_held.at[1 - core])], sems, len(smalls))
    for r in range(prompts):
        ask(r)
    sign_tables(signs, True)
    level_masks(masks)
    for copy in smalls:
        copy.wait()
    head_factors(first, dt_ref, rate_ref, skip_ref, len_ref, signs, w_in, w_out, w_skip, w_tail)

    def one(r, _):
        x_copy(r).wait()
        b_copy(r).wait()
        width = x_held.shape[1]
        inputs = x_held[r].astype(f32).reshape(group, HP, length)
        scaled = (inputs * w_tail[r][:, None, :]).astype(bf16).reshape(width, length)
        state_held[r] = jnp.dot(scaled, b_held[r], preferred_element_type=f32).astype(bf16)
        state_copy(r).start()
        return 0

    lax.fori_loop(0, prompts, one, 0, unroll=2)
    for r in range(EARLY):
        c_copy(r).start()

    spread = table_ref.shape[1] // owner_ref.shape[1]
    for copy in pages:
        copy.wait()
    for n in range(2):
        for r in range(prompts):
            for page in range(spread):
                holder = me - core + n
                row = table_ref[r, holder * spread + page] - holder * (prompts * spread)
                block = pages_held[n, row]
                place = pl.ds((n * spread + page) * PAGE, PAGE)
                columns = pl.ds(r % 2 * HD, HD)
                key_held[r // 2, place, columns] = block[:, :HD]
                value_held[r // 2, place, columns] = block[:, HD:]

    owners = owner_ref.shape[1]
    rows_dev = slot_ref.shape[0] // owners
    inner = iota((2 * SUB, LANES), 0)

    order = exchange_order(owners)
    for rank in range(0, owners, 2):
        block = jnp.zeros((2 * SUB, LANES), jnp.int32)
        for n in range(2):
            s = order[rank + n]
            for i in range(rows_dev):
                target = owner_ref[slot_ref[s * rows_dev + i], s]
                code = target * (1 << LENGTH_BITS) + len_ref[target]
                block = jnp.where((inner // SUB == n) & (inner % rows_dev == i), code, block)
        code_held[rank * SUB : (rank + 2) * SUB, :] = block
    marks = fetches([(key_held, key_any), (value_held, value_any), (code_held, code_any)], sems)

    def early(r, _):
        c_copy(r).wait()
        prompt_result(r, x_held, b_held, c_held, w_in, w_out, w_skip, masks, out_held)
        out_copy(r).start()
        return 0

    lax.fori_loop(0, EARLY, early, 0, unroll=2)
    for copy in marks:
        copy.wait()
    for r in range(prompts):
        state_copy(r).wait()
    for r in range(EARLY):
        out_copy(r).wait()


def serve_kernel(
    recv_any,
    key_any,
    value_any,
    code_any,
    state_any,
    out_ref,
    recv_ref,
    key_ref,
    value_ref,
    code_ref,
    state_ref,
    query_ref,
    state_sem,
    sems,
):
    rows = recv_ref.shape[0]
    prompts, width = state_ref.shape[0], state_ref.shape[1]
    copies = fetches(
        [(recv_any, recv_ref), (code_any, code_ref), (key_any, key_ref), (value_any, value_ref)], sems
    )
    states = fetches([(state_any.at[r], state_ref.at[r]) for r in range(prompts)], state_sem)
    heads = HALF // HD
    keys = key_ref.shape[1]
    chips = keys // PAGE
    begin = lax.rem(lax.axis_index("heads") // 2 * chips, PAGES) * PAGE
    copies[0].wait()
    copies[1].wait()
    code = code_ref[...]
    target = code >> LENGTH_BITS
    lengths = code & ((1 << LENGTH_BITS) - 1)
    for r in range(prompts):
        for g in range(heads):
            query = recv_ref[:, g * HD : (g + 1) * HD].astype(f32)
            query_ref[r // 2, g * rows : (g + 1) * rows, r % 2 * HD : (r % 2 + 1) * HD] = jnp.where(
                target == r, query, 0.0
            ).astype(bf16)
    copies[2].wait()
    scores = jnp.zeros((heads * rows, keys), f32)
    for pair in range(prompts // 2):
        scores = scores + dot_nt(query_ref[pair], key_ref[pair])
    seen = jnp.concatenate([lengths[:, :1]] * heads, axis=0) > iota((heads * rows, keys), 1) + begin
    scores = jnp.where(seen, scores * SCORE, NONE)
    highest = jnp.maximum(jnp.max(scores, axis=1, keepdims=True), FLOOR)
    weight = jnp.exp2(scores - highest)
    total = jnp.sum(weight, axis=1, keepdims=True)
    some = total > 0.0
    safe = jnp.where(some, total, 1.0)
    result = jnp.where(some, highest + jnp.log2(safe), NONE)
    weight = weight.astype(bf16)
    copies[3].wait()
    targets = jnp.concatenate([target] * heads, axis=0)
    value = jnp.zeros((heads * rows, HD), f32)
    for pair in range(prompts // 2):
        both = jnp.dot(weight, value_ref[pair], preferred_element_type=f32)
        for n in range(2):
            value = jnp.where(targets == 2 * pair + n, both[:, n * HD : (n + 1) * HD], value)
    value = value / safe
    lane = iota((rows, LANES), 1)
    sums = jnp.zeros((rows, LANES), f32)
    for g in range(heads):
        sums = jnp.where(lane % 4 == g, result[g * rows : (g + 1) * rows], sums)
    high = sums.astype(bf16).astype(f32)
    rest = sums - high
    middle = rest.astype(bf16).astype(f32)
    piece = lane % 16 // 4
    pieces = jnp.where(piece == 0, high, jnp.where(piece == 1, middle, rest - middle))
    pair = iota((rows, LANES), 0) % SUB
    pieces = jnp.where((lane // 16 == pair) & (piece < 3), pieces, 0.0)
    packed = jnp.sum(pieces.reshape(rows // SUB, SUB, LANES), axis=1, keepdims=True)

    given = recv_ref[...].astype(f32).reshape(rows // SUB, SUB, recv_ref.shape[1])
    ending = lift(given, spare(heads + 1, 0))
    readout = jnp.concatenate([given[..., HALF:], ending], axis=-1).reshape(rows, NS)
    target = jnp.concatenate([target, target], axis=-1)
    found = jnp.zeros((rows, width), f32)
    for r in range(prompts):
        picked = jnp.where(target == r, readout, 0.0).astype(bf16)
        states[r].wait()
        found = found + dot_nt(picked, state_ref[r])
    if width < LANES:
        found = jnp.concatenate([found, jnp.zeros((rows, LANES - width), f32)], axis=-1)
    blocks = [value[g * rows : (g + 1) * rows] for g in range(heads)]
    blocks += [found[:, b : b + LANES] for b in range(0, found.shape[1], LANES)]
    blocks = [one.reshape(rows // SUB, SUB, LANES) for one in blocks]
    row = iota((rows // SUB, SUB, LANES), 1)
    last = blocks.pop()
    blocks[0] = jnp.where(row == PAIRS, jnp.broadcast_to(packed, row.shape), blocks[0])
    for n, (at, b) in enumerate(spare(len(blocks), 1)):
        one = jnp.broadcast_to(last[:, n : n + 1, :], row.shape)
        blocks[b] = jnp.where(row == at, one, blocks[b])
    for b, one in enumerate(blocks):
        out_ref[:, b * LANES : (b + 1) * LANES] = one.reshape(rows, LANES).astype(bf16)


def prompt_kernel(
    rate_any,
    skip_any,
    len_any,
    dt_any,
    rates_any,
    skips_any,
    send_any,
    fresh_any,
    sx_any,
    sb_any,
    sc_any,
    sdt_any,
    x_any,
    b_any,
    c_any,
    after_any,
    early_any,
    out_any,
    own_any,
    ownsum_any,
    fade_any,
    local_any,
    x_held,
    b_held,
    c_held,
    out_held,
    w_in,
    w_out,
    w_skip,
    masks,
    signs,
    own_ref,
    ownsum_ref,
    fade_ref,
    local_ref,
    fresh_held,
    c_rows,
    x_rows,
    rate_ref,
    skip_ref,
    len_ref,
    dt_ref,
    rates_ref,
    skips_ref,
    send_ref,
    fresh_ref,
    sx_ref,
    sb_ref,
    sc_ref,
    sdt_ref,
    x_sem,
    b_sem,
    c_sem,
    out_sem,
    sems,
):
    group, prompts, length = dt_ref.shape
    smalls = fetches(
        [
            (dt_any, dt_ref),
            (rate_any, rate_ref),
            (skip_any, skip_ref),
            (len_any, len_ref),
            (rates_any, rates_ref),
            (skips_any, skips_ref),
            (send_any, send_ref),
            (fresh_any, fresh_ref),
            (sx_any, sx_ref),
            (sb_any, sb_ref),
            (sc_any, sc_ref),
            (sdt_any, sdt_ref),
        ],
        sems,
    )
    me = lax.axis_index("heads")
    first = me * group
    column = pl.multiple_of((first // HPG) * NS, NS)

    def x_copy(r):
        return pltpu.make_async_copy(x_any.at[r], x_held.at[r], x_sem.at[r])

    def b_copy(r):
        return pltpu.make_async_copy(b_any.at[r, :, pl.ds(column, NS)], b_held.at[r], b_sem.at[r])

    def c_copy(r):
        return pltpu.make_async_copy(c_any.at[r, :, pl.ds(column, NS)], c_held.at[r], c_sem.at[r])

    def out_copy(r):
        return pltpu.make_async_copy(out_held.at[r], out_any.at[r], out_sem.at[r])

    def ask(r):
        x_copy(r).start()
        b_copy(r).start()
        c_copy(r).start()

    for r in range(EARLY, min(EARLY + AHEAD, prompts)):
        ask(r)
    sign_tables(signs, False)
    level_masks(masks)
    for copy in smalls:
        copy.wait()
    head_factors(first, dt_ref, rate_ref, skip_ref, len_ref, signs, w_in, w_out, w_skip, None)
    own_attention(send_ref, fresh_ref, fresh_held, own_ref, ownsum_ref)
    own_mixer(rates_ref, skips_ref, sx_ref, sb_ref, sc_ref, sdt_ref, c_rows, x_rows, fade_ref, local_ref)
    outs = fetches(
        [(own_ref, own_any), (ownsum_ref, ownsum_any), (fade_ref, fade_any), (local_ref, local_any)], sems
    )

    def one(r, _):
        @pl.when(r + AHEAD < prompts)
        def _():
            ask(r + AHEAD)

        x_copy(r).wait()
        b_copy(r).wait()
        c_copy(r).wait()
        prompt_result(r, x_held, b_held, c_held, w_in, w_out, w_skip, masks, out_held)
        out_copy(r).start()
        return 0

    lax.fori_loop(EARLY, prompts, one, 0, unroll=2)
    for copy in outs:
        copy.wait()
    for r in range(EARLY, prompts):
        out_copy(r).wait()


def own_attention(send_ref, fresh_ref, fresh_held, own_ref, ownsum_ref):
    steps, rows = fresh_ref.shape[0], fresh_ref.shape[1]
    owners = send_ref.shape[0]
    order = exchange_order(owners)
    ways = owners // KVH
    stack_rows(fresh_ref, fresh_held)
    count = HALF // HD * 2 * SUB
    pair = iota((count, SUB), 0) % SUB
    key = iota((count, SUB), 1)
    seen = (key % rows == pair % rows) & (key <= pair) & (key < rows * steps)
    seen = seen | ((pair >= rows * steps) & (key == 0))
    for v in range(KVH):
        halves = [send_ref[order.index(v * ways + n), :, :HALF].astype(f32) for n in range(2)]
        parts = [half[:, g * HD : (g + 1) * HD] for g in range(HALF // HD) for half in halves]
        query = jnp.concatenate(parts, axis=0).astype(bf16)
        keys = fresh_held[:, v * HD : (v + 1) * HD].astype(bf16)
        values = fresh_held[:, (KVH + v) * HD : (KVH + v + 1) * HD].astype(bf16)
        scores = jnp.where(seen, dot_nt(query, keys) * SCORE, NONE)
        highest = jnp.max(scores, axis=1, keepdims=True)
        weight = jnp.exp2(scores - highest)
        total = jnp.sum(weight, axis=1, keepdims=True)
        weight = (weight / total).astype(bf16)
        own_ref[v] = jnp.dot(weight, values, preferred_element_type=f32)
        ownsum_ref[v] = jnp.broadcast_to(highest + jnp.log2(total), (count, HD))


def own_mixer(rates_ref, skips_ref, sx_ref, sb_ref, sc_ref, sdt_ref, c_rows, x_rows, fade_ref, local_ref):
    steps, rows, heads = sdt_ref.shape
    stack_rows(sc_ref, c_rows)
    for u in range(steps):
        given = sx_ref[u].astype(f32)
        for k in range(SUB // rows):
            x_rows[u, k * rows : (k + 1) * rows, :] = given
    pair = iota((SUB, heads), 0)
    step = pair // rows
    live = pair < rows * steps
    head = iota((SUB, heads), 1)

    def spread_rows(ref, u):
        given = ref[u].astype(f32)
        return jnp.concatenate([given] * (SUB // rows), axis=0)

    rates = jnp.broadcast_to(rates_ref[...], (SUB, heads)) * LOG2E
    skips = jnp.broadcast_to(skips_ref[...], (SUB, heads))
    moved = [spread_rows(sdt_ref, u) for u in range(steps)]
    kept = [jnp.where(u <= step, moved[u], 0.0) for u in range(steps)]
    parts = [jnp.where(live, jnp.exp2(-(rates * sum(kept))), 0.0)]
    for u in range(steps):
        products = c_rows[...] * spread_rows(sb_ref, u)
        inner = jnp.zeros((SUB, heads), f32)
        for e in range(products.shape[1] // NS):
            found = jnp.sum(products[:, e * NS : (e + 1) * NS], axis=1, keepdims=True)
            inner = jnp.where(head // HPG == e, found, inner)
        gap = jnp.zeros((SUB, heads), f32)
        for t in range(u + 1, steps):
            gap = gap + kept[t]
        weight = jnp.where(u <= step, jnp.exp2(-(rates * gap)) * moved[u] * inner, 0.0)
        weight = weight + jnp.where(u == step, skips, 0.0)
        parts.append(jnp.where(live, weight, 0.0))
    stacked = jnp.concatenate(parts, axis=0)
    high = stacked.astype(bf16)
    low = (stacked - high.astype(f32)).astype(bf16)
    both = jnp.concatenate([high.astype(f32), low.astype(f32)], axis=0)
    count = stacked.shape[0]
    chunk = SUB * HP
    widen = jnp.where(iota((heads, chunk), 0) % SUB == iota((heads, chunk), 1) // HP, 1.0, 0.0).astype(bf16)
    lane = iota(both.shape, 1)
    for d in range(heads // SUB):
        picked = jnp.where(lane // SUB == d, both, 0.0).astype(bf16)
        wide = jnp.dot(picked, widen, preferred_element_type=f32)
        wide = wide[:count] + wide[count:]
        columns = slice(d * chunk, (d + 1) * chunk)
        fade_ref[:, columns] = wide[:SUB]
        value = jnp.zeros((SUB, chunk), f32)
        for u in range(steps):
            value = value + wide[(u + 1) * SUB : (u + 2) * SUB] * x_rows[u, :, columns]
        local_ref[:, columns] = value


def merge_kernel(
    width,
    back_any,
    own_any,
    ownsum_any,
    fade_any,
    local_any,
    mixer_any,
    attention_any,
    back_ref,
    own_ref,
    ownsum_ref,
    fade_ref,
    local_ref,
    mixed,
    attended,
    mixer_ref,
    attention_ref,
    sems,
):
    copies = fetches([(back_any, back_ref), (fade_any, fade_ref), (local_any, local_ref)], sems)
    rest = fetches([(own_any, own_ref), (ownsum_any, ownsum_ref)], sems, len(copies))
    for copy in copies:
        copy.wait()
    owners = back_ref.shape[0]
    ways = owners // KVH
    order = exchange_order(owners)
    steps, rows = mixer_ref.shape[0], mixer_ref.shape[1]
    for d in range(0, owners, 2):
        block = jnp.stack([back_ref[order.index(d + n)].astype(f32) for n in range(2)])
        ending = lift(block, spare(back_ref.shape[2] // LANES, 1))
        if back_ref.shape[2] > HALF:
            ending = jnp.concatenate([block[..., HALF:], ending], axis=-1)
        found = ending[..., :width]
        found = jnp.concatenate([found[0], found[1]], axis=-1)
        columns = slice(d * width, (d + 2) * width)
        mixed[:, columns] = found * fade_ref[:, columns] + local_ref[:, columns]
    for k in range(steps):
        mixer_ref[k] = mixed[k * rows : (k + 1) * rows, :].astype(bf16)
    outs = fetches([(mixer_ref, mixer_any)], sems)
    for copy in rest:
        copy.wait()
    lane = iota((2, SUB, LANES), 2)
    mine = (lane // 16 == iota((2, SUB, LANES), 1)) & (lane % 16 < 12)
    for v in range(KVH):
        blocks, pieces = [], []
        for d in range(v * ways, (v + 1) * ways, 2):
            block = jnp.stack([back_ref[order.index(d + n), :, :HALF].astype(f32) for n in range(2)])
            packed = block[:, PAIRS : PAIRS + 1, :LANES]
            blocks.append(block.reshape(2 * SUB, HALF))
            pieces.append(jnp.where(mine, jnp.broadcast_to(packed, (2, SUB, LANES)), 0.0))
        for g in range(HALF // HD):
            part = slice(g * 2 * SUB, (g + 1) * 2 * SUB)
            own_sum = ownsum_ref[v, part, :]
            wide = []
            for piece in pieces:
                one = jnp.sum(jnp.where(lane % 4 == g, piece, 0.0), axis=-1, keepdims=True)
                wide.append(jnp.broadcast_to(one, (2, SUB, HD)).reshape(2 * SUB, HD))
            highest = functools.reduce(jnp.maximum, wide, own_sum)
            weight = jnp.exp2(own_sum - highest)
            total = weight
            value = weight * own_ref[v, part, :]
            for one, block in zip(wide, blocks):
                weight = jnp.exp2(one - highest)
                total = total + weight
                value = value + weight * block[:, g * HD : (g + 1) * HD]
            value = value / total
            start = v * 2 * HALF + g * HD
            attended[:, start : start + HD] = value[:SUB]
            attended[:, start + HALF : start + HALF + HD] = value[SUB:]
    for k in range(steps):
        attention_ref[k] = attended[k * rows : (k + 1) * rows, :].astype(bf16)
    outs += fetches([(attention_ref, attention_any)], sems, 1)
    for copy in outs:
        copy.wait()


def call(kernel, out_shape, in_spaces, out_spaces, scratch, cost, aliases=None):
    def spec(space):
        return pl.BlockSpec(memory_space=space)

    return pl.pallas_call(
        kernel,
        out_shape=out_shape,
        in_specs=[spec(space) for space in in_spaces],
        out_specs=jax.tree.map(spec, out_spaces),
        scratch_shapes=scratch,
        input_output_aliases=aliases or {},
        compiler_params=pltpu.CompilerParams(vmem_limit_bytes=VMEM_LIMIT),
        cost_estimate=pl.CostEstimate(flops=cost[0], bytes_accessed=cost[1], transcendentals=0),
    )


def on_device(
    prompt_x,
    prompt_b,
    prompt_c,
    prompt_dt,
    decay_rate,
    skip_gain,
    lengths,
    owner_list,
    page_table,
    cache_pages,
    row_slot,
    step_x,
    step_b,
    step_c,
    step_dt,
    queries,
    fresh_cache,
):
    owners = lax.axis_size("heads")
    ways = owners // KVH
    group, prompts, length = prompt_dt.shape
    width = prompt_x.shape[1]
    keys = cache_pages.shape[0] * PAGE
    span = 2 * keys // prompts
    steps = step_x.shape[1]
    all_rows = owners * SUB
    shape = jax.ShapeDtypeStruct
    smem, vmem, hbm = pltpu.SMEM, pltpu.VMEM, pltpu.HBM
    sem = pltpu.SemaphoreType.DMA((prompts,))
    levels = len(LEVELS)
    step_x, step_b, step_c, step_dt, queries, fresh_cache = (
        jnp.swapaxes(one, 0, 1) for one in (step_x, step_b, step_c, step_dt, queries, fresh_cache)
    )
    owner_list = owner_list.T

    def like(space, array):
        return space(array.shape, array.dtype)

    def sems(count):
        return pltpu.SemaphoreType.DMA((count,))

    other_pages = lax.ppermute(cache_pages, "heads", [(d, d + 1 - 2 * (d % 2)) for d in range(owners)])
    send = call(
        functools.partial(pack_kernel, group, ways),
        shape((all_rows, HALF + LANES), bf16),
        [hbm, hbm],
        vmem,
        [
            like(vmem, queries),
            like(vmem, step_c),
            vmem((SUB, queries.shape[2]), f32),
            vmem((SUB, step_c.shape[2]), f32),
            vmem((step_c.shape[2] // NS, SUB, HALF + LANES), f32),
            sems(2),
        ],
        (0, 1 << 19),
    )(queries, step_c)
    order = [exchange_order(owners)]
    recv = lax.all_to_all(
        send, "heads", split_axis=0, concat_axis=0, tiled=True, axis_index_groups=order
    )

    block = [
        vmem((prompts, width, length), bf16),
        vmem((prompts, length, NS), bf16),
        vmem((prompts, length, NS), bf16),
        vmem((prompts, width, length), bf16),
        vmem((levels, prompts, group, length), f32),
        vmem((levels, prompts, group, length), f32),
        vmem((prompts, group, length), f32),
    ]
    tables = [vmem((levels, length, length), bf16), vmem((levels + 1, length, length), bf16)]
    work = 2 * width * length * NS
    states, sorted_keys, sorted_values, codes, early_out = call(
        state_kernel,
        (
            shape((prompts, width, NS), bf16),
            shape((prompts // 2, span, 2 * HD), bf16),
            shape((prompts // 2, span, 2 * HD), bf16),
            shape((all_rows, LANES), jnp.int32),
            shape(prompt_x.shape, bf16),
        ),
        [hbm] * 12,
        (hbm,) * 5,
        block
        + tables
        + [vmem((prompts, group, length), f32), vmem((prompts, width, NS), bf16)]
        + [vmem((2,) + cache_pages.shape, bf16)]
        + [vmem((prompts // 2, span, 2 * HD), bf16)] * 2
        + [vmem((all_rows, LANES), jnp.int32)]
        + [like(smem, one) for one in (decay_rate, skip_gain, lengths, owner_list, page_table, row_slot)]
        + [like(vmem, prompt_dt), sem, sem, sem, sem, sem, sems(9)],
        (work * (prompts + 5 * EARLY), 6 << 20),
    )(
        decay_rate,
        skip_gain,
        lengths,
        owner_list,
        page_table,
        row_slot,
        prompt_dt,
        prompt_x,
        prompt_b,
        prompt_c,
        cache_pages,
        other_pages,
    )

    back = call(
        serve_kernel,
        shape((all_rows, HALF + max(LANES, width) - LANES), bf16),
        [hbm] * 5,
        vmem,
        [like(vmem, one) for one in (recv, sorted_keys, sorted_values, codes, states)]
        + [vmem((prompts // 2, HALF // HD * all_rows, 2 * HD), bf16), sem, sems(4)],
        (8 * all_rows * keys * HD, 4 << 20),
    )(recv, sorted_keys, sorted_values, codes, states)
    returned = lax.all_to_all(
        back, "heads", split_axis=0, concat_axis=0, tiled=True, axis_index_groups=order
    ).reshape(owners, SUB, back.shape[1])

    count = HALF // HD * 2 * SUB
    channels = step_x.shape[2]
    rates, skips = decay_rate.reshape(1, -1), skip_gain.reshape(1, -1)
    prompt_out, own, own_sum, fade, local = call(
        prompt_kernel,
        (
            shape(prompt_x.shape, bf16),
            shape((KVH, count, HD), f32),
            shape((KVH, count, HD), f32),
            shape((SUB, channels), f32),
            shape((SUB, channels), f32),
        ),
        [hbm] * 17,
        (hbm,) * 5,
        block
        + tables
        + [
            vmem((KVH, count, HD), f32),
            vmem((KVH, count, HD), f32),
            vmem((SUB, channels), f32),
            vmem((SUB, channels), f32),
            vmem((SUB, fresh_cache.shape[2]), f32),
            vmem((SUB, step_c.shape[2]), f32),
            vmem((steps, SUB, channels), f32),
            like(smem, decay_rate),
            like(smem, skip_gain),
            like(smem, lengths),
            like(vmem, prompt_dt),
            like(vmem, rates),
            like(vmem, skips),
            vmem((owners, SUB, HALF + LANES), bf16),
            like(vmem, fresh_cache),
            like(vmem, step_x),
            like(vmem, step_b),
            like(vmem, step_c),
            like(vmem, step_dt),
            sem,
            sem,
            sem,
            sem,
            sems(12),
        ],
        (work * 5 * (prompts - EARLY), 8 << 20),
        {16: 0},
    )(
        decay_rate,
        skip_gain,
        lengths,
        prompt_dt,
        rates,
        skips,
        send.reshape(owners, SUB, HALF + LANES),
        fresh_cache,
        step_x,
        step_b,
        step_c,
        step_dt,
        prompt_x,
        prompt_b,
        prompt_c,
        back,
        early_out,
    )

    mixer_out, attention_out = call(
        functools.partial(merge_kernel, width),
        (shape(step_x.shape, bf16), shape(queries.shape, bf16)),
        [hbm] * 5,
        (hbm, hbm),
        [like(vmem, one) for one in (returned, own, own_sum, fade, local)]
        + [vmem((SUB, channels), f32), vmem((SUB, queries.shape[2]), f32)]
        + [like(vmem, step_x), like(vmem, queries), sems(5)],
        (0, 2 << 20),
    )(returned, own, own_sum, fade, local)
    return (prompt_out, jnp.swapaxes(mixer_out, 0, 1), jnp.swapaxes(attention_out, 0, 1))


def solution(mesh):
    in_specs = (
        P("groups", "heads", None),
        P("groups", None, None),
        P("groups", None, None),
        P("heads", "groups", None),
        P(),
        P(),
        P("groups"),
        P("groups", None),
        P("groups", None),
        P(("groups", "heads"), None, None),
        P("groups"),
        P(("groups", "heads"), None, None),
        P(("groups", "heads"), None, None),
        P(("groups", "heads"), None, None),
        P(("groups", "heads"), None, None),
        P(("groups", "heads"), None, None),
        P(("groups", "heads"), None, None),
    )
    out_specs = (
        P("groups", "heads", None),
        P(("groups", "heads"), None, None),
        P(("groups", "heads"), None, None),
    )
    return jax.shard_map(
        on_device, mesh=mesh, in_specs=in_specs, out_specs=out_specs, check_vma=False
    )
```

```python
import functools
import math

import jax
import jax.numpy as jnp
from jax import lax
from jax.experimental import pallas as pl
from jax.experimental.pallas import tpu as pltpu
from jax.sharding import PartitionSpec as P

NS = 256
HP = 64
HPG = 32
KVH = 8
HD = 128
PAGE = 16
PAGES = 16
LANES = 128
SUB = 8
HALF = 512
LEVELS = (128, 64, 32, 16)
LOG2E = math.log2(math.e)
SCORE = LOG2E / math.sqrt(HD)
NONE = -1e30
FLOOR = -1e29
PAIRS = 6
LENGTH_BITS = 10
AHEAD = 2
EARLY = 2
VMEM_LIMIT = 64 * 1024 * 1024

f32 = jnp.float32
bf16 = jnp.bfloat16


def iota(shape, dim):
    return lax.broadcasted_iota(jnp.int32, shape, dim)


def exchange_order(owners):
    middle = owners // 4
    return [middle] + [d for d in range(owners) if d != middle]


def dot_nt(left, right):
    return lax.dot_general(left, right, (((1,), (1,)), ((), ())), preferred_element_type=f32)


def stack_rows(source, held):
    steps, rows = source.shape[0], source.shape[1]
    held[...] = jnp.zeros_like(held)
    for k in range(steps):
        held[k * rows : (k + 1) * rows, :] = source[k].astype(f32)


def spare(blocks, taken):
    return [(row, b) for row in range(PAIRS, SUB) for b in range(blocks)][taken : taken + PAIRS]


def lift(value, slots):
    row = iota(value.shape[:2] + (LANES,), 1)
    found = jnp.zeros(row.shape, f32)
    for pair, (at, b) in enumerate(slots):
        one = value[:, at : at + 1, b * LANES : (b + 1) * LANES]
        found = jnp.where(row == pair, jnp.broadcast_to(one, row.shape), found)
    return found


def fetches(pairs, sems, first=0):
    copies = [pltpu.make_async_copy(src, dst, sems.at[first + n]) for n, (src, dst) in enumerate(pairs)]
    for copy in copies:
        copy.start()
    return copies


def pack_kernel(group, ways, q_any, c_any, out_ref, q_ref, c_ref, q_held, c_held, rest, sems):
    owners = out_ref.shape[0] // SUB
    for copy in fetches([(q_any, q_ref), (c_any, c_ref)], sems):
        copy.wait()
    stack_rows(q_ref, q_held)
    stack_rows(c_ref, c_held)
    span = 2 * HALF
    slots = spare(HALF // LANES + 1, 0)
    rest[...] = jnp.zeros_like(rest)
    for e in range(c_ref.shape[2] // NS):
        rest[e, :PAIRS, HALF:] = c_held[:PAIRS, e * NS : e * NS + LANES]
        for pair, (row, b) in enumerate(slots):
            rest[e, row : row + 1, b * LANES : (b + 1) * LANES] = c_held[
                pair : pair + 1, e * NS + LANES : (e + 1) * NS
            ]
    real = iota((SUB, HALF), 0) < PAIRS
    order = exchange_order(owners)
    for rank in range(0, owners, 2):
        blocks, ends = [], []
        for d in order[rank : rank + 2]:
            begin, e = d // ways * span + d % 2 * HALF, (d * group) // HPG
            blocks.append(jnp.where(real, q_held[:, begin : begin + HALF], rest[e, :, :HALF]))
            ends.append(rest[e, :, HALF:])
        place = slice(rank * SUB, (rank + 2) * SUB)
        out_ref[place, :HALF] = jnp.concatenate(blocks, axis=0).astype(bf16)
        out_ref[place, HALF:] = jnp.concatenate(ends, axis=0).astype(bf16)


def sign_tables(signs, tail):
    length = signs.shape[-1]
    j = iota((length, length), 0)
    i = iota((length, length), 1)
    for l, n in enumerate(LEVELS):
        middle = (i // (2 * n)) * (2 * n) + (n - 1)
        signs[l] = (jnp.where(j <= i, 1.0, 0.0) - jnp.where(j <= middle, 1.0, 0.0)).astype(bf16)
    if tail:
        signs[len(LEVELS)] = jnp.where(j > i, 1.0, 0.0).astype(bf16)


def head_factors(first, dt_ref, rate_ref, skip_ref, len_ref, signs, w_in, w_out, w_skip, w_tail):
    group, prompts, length = dt_ref.shape
    row = iota((prompts, length), 0)
    lens = jnp.zeros((prompts, length), jnp.int32)
    for r in range(prompts):
        lens = jnp.where(row == r, len_ref[r], lens)
    valid = iota((prompts, length), 1) < lens
    moved = [jnp.where(valid, dt_ref[h].astype(f32), 0.0) for h in range(group)]
    every = jnp.concatenate(moved, axis=0).astype(bf16)
    rates = [rate_ref[first + h] * LOG2E for h in range(group)]
    if w_tail is not None:
        total = jnp.dot(every, signs[len(LEVELS)], preferred_element_type=f32)
        for h in range(group):
            part = total[h * prompts : (h + 1) * prompts]
            w_tail[:, h, :] = jnp.exp2(-(rates[h] * part)) * moved[h]
    for h in range(group):
        w_skip[:, h, :] = jnp.where(valid, skip_ref[first + h], 0.0)
    for l, n in enumerate(LEVELS):
        total = jnp.dot(every, signs[l], preferred_element_type=f32)
        for h in range(group):
            gap = rates[h] * total[h * prompts : (h + 1) * prompts]
            if n == LEVELS[-1]:
                up, down = jnp.exp2(gap), jnp.exp2(-gap)
            else:
                up, down = jnp.exp2(jnp.minimum(gap, 0.0)), jnp.exp2(-jnp.maximum(gap, 0.0))
            w_in[l, :, h, :] = up * moved[h]
            w_out[l, :, h, :] = jnp.where(valid, down, 0.0)


def level_masks(masks):
    length = masks.shape[-1]
    j = iota((length, length), 0)
    i = iota((length, length), 1)
    for l, n in enumerate(LEVELS):
        same = (j // (2 * n)) == (i // (2 * n))
        if n == LEVELS[-1]:
            keep = same & (j <= i)
        else:
            keep = same & ((j % (2 * n)) < n) & ((i % (2 * n)) >= n)
        masks[l] = jnp.where(keep, 1.0, 0.0).astype(bf16)


def prompt_result(r, x_held, b_held, c_held, w_in, w_out, w_skip, masks, out_held):
    width, length = x_held.shape[1], x_held.shape[2]
    group = width // HP
    half = length // 2
    inputs = x_held[r].astype(f32).reshape(group, HP, length)
    scores = dot_nt(b_held[r], c_held[r]).astype(bf16)
    total = inputs * w_skip[r][:, None, :]
    left, right = total[..., :half], total[..., half:]
    for l, n in enumerate(LEVELS):
        if 2 * n == length:
            scaled = (inputs[..., :half] * w_in[l, r][:, None, :half]).astype(bf16).reshape(width, half)
            added = jnp.dot(scaled, scores[:half, half:], preferred_element_type=f32)
            right = right + added.reshape(group, HP, half) * w_out[l, r][:, None, half:]
        else:
            scaled = (inputs * w_in[l, r][:, None, :]).astype(bf16).reshape(width, length)
            added = jnp.dot(scaled, scores * masks[l], preferred_element_type=f32)
            added = added.reshape(group, HP, length) * w_out[l, r][:, None, :]
            left = left + added[..., :half]
            right = right + added[..., half:]
    out_held[r] = jnp.concatenate([left, right], axis=-1).reshape(width, length).astype(bf16)


def state_kernel(
    rate_any,
    skip_any,
    len_any,
    owner_any,
    table_any,
    slot_any,
    dt_any,
    x_any,
    b_any,
    c_any,
    pages_any,
    other_any,
    state_any,
    key_any,
    value_any,
    code_any,
    out_any,
    x_held,
    b_held,
    c_held,
    out_held,
    w_in,
    w_out,
    w_skip,
    masks,
    signs,
    w_tail,
    state_held,
    pages_held,
    key_held,
    value_held,
    code_held,
    rate_ref,
    skip_ref,
    len_ref,
    owner_ref,
    table_ref,
    slot_ref,
    dt_ref,
    x_sem,
    b_sem,
    c_sem,
    out_sem,
    state_sem,
    sems,
):
    group, prompts, length = dt_ref.shape
    smalls = fetches(
        [
            (dt_any, dt_ref),
            (rate_any, rate_ref),
            (skip_any, skip_ref),
            (len_any, len_ref),
            (owner_any, owner_ref),
            (table_any, table_ref),
            (slot_any, slot_ref),
        ],
        sems,
    )
    me = lax.axis_index("heads")
    core = lax.rem(me, 2)
    first = me * group
    column = pl.multiple_of((first // HPG) * NS, NS)

    def x_copy(r):
        return pltpu.make_async_copy(x_any.at[r], x_held.at[r], x_sem.at[r])

    def b_copy(r):
        return pltpu.make_async_copy(b_any.at[r, :, pl.ds(column, NS)], b_held.at[r], b_sem.at[r])

    def c_copy(r):
        return pltpu.make_async_copy(c_any.at[r, :, pl.ds(column, NS)], c_held.at[r], c_sem.at[r])

    def out_copy(r):
        return pltpu.make_async_copy(out_held.at[r], out_any.at[r], out_sem.at[r])

    def state_copy(r):
        return pltpu.make_async_copy(state_held.at[r], state_any.at[r], state_sem.at[r])

    def ask(r):
        x_copy(r).start()
        b_copy(r).start()

    pages = fetches([(pages_any, pages_held.at[core]), (other_any, pages_held.at[1 - core])], sems, len(smalls))
    for r in range(prompts):
        ask(r)
    sign_tables(signs, True)
    level_masks(masks)
    for copy in smalls:
        copy.wait()
    head_factors(first, dt_ref, rate_ref, skip_ref, len_ref, signs, w_in, w_out, w_skip, w_tail)

    def one(r, _):
        x_copy(r).wait()
        b_copy(r).wait()
        width = x_held.shape[1]
        inputs = x_held[r].astype(f32).reshape(group, HP, length)
        scaled = (inputs * w_tail[r][:, None, :]).astype(bf16).reshape(width, length)
        state_held[r] = jnp.dot(scaled, b_held[r], preferred_element_type=f32).astype(bf16)
        state_copy(r).start()
        return 0

    lax.fori_loop(0, prompts, one, 0, unroll=2)
    for r in range(EARLY):
        c_copy(r).start()

    spread = table_ref.shape[1] // owner_ref.shape[1]
    for copy in pages:
        copy.wait()
    for n in range(2):
        for r in range(prompts):
            for page in range(spread):
                holder = me - core + n
                row = table_ref[r, holder * spread + page] - holder * (prompts * spread)
                block = pages_held[n, row]
                place = pl.ds((n * spread + page) * PAGE, PAGE)
                columns = pl.ds(r % 2 * HD, HD)
                key_held[r // 2, place, columns] = block[:, :HD]
                value_held[r // 2, place, columns] = block[:, HD:]

    owners = owner_ref.shape[1]
    rows_dev = slot_ref.shape[0] // owners
    inner = iota((2 * SUB, LANES), 0)

    order = exchange_order(owners)
    for rank in range(0, owners, 2):
        block = jnp.zeros((2 * SUB, LANES), jnp.int32)
        for n in range(2):
            s = order[rank + n]
            for i in range(rows_dev):
                target = owner_ref[slot_ref[s * rows_dev + i], s]
                code = target * (1 << LENGTH_BITS) + len_ref[target]
                block = jnp.where((inner // SUB == n) & (inner % rows_dev == i), code, block)
        code_held[rank * SUB : (rank + 2) * SUB, :] = block
    marks = fetches([(key_held, key_any), (value_held, value_any), (code_held, code_any)], sems)

    def early(r, _):
        c_copy(r).wait()
        prompt_result(r, x_held, b_held, c_held, w_in, w_out, w_skip, masks, out_held)
        out_copy(r).start()
        return 0

    lax.fori_loop(0, EARLY, early, 0, unroll=2)
    for copy in marks:
        copy.wait()
    for r in range(prompts):
        state_copy(r).wait()
    for r in range(EARLY):
        out_copy(r).wait()


def serve_kernel(
    recv_any,
    key_any,
    value_any,
    code_any,
    state_any,
    out_ref,
    recv_ref,
    key_ref,
    value_ref,
    code_ref,
    state_ref,
    query_ref,
    state_sem,
    sems,
):
    rows = recv_ref.shape[0]
    prompts, width = state_ref.shape[0], state_ref.shape[1]
    copies = fetches(
        [(recv_any, recv_ref), (code_any, code_ref), (key_any, key_ref), (value_any, value_ref)], sems
    )
    states = fetches([(state_any.at[r], state_ref.at[r]) for r in range(prompts)], state_sem)
    heads = HALF // HD
    keys = key_ref.shape[1]
    chips = keys // PAGE
    begin = lax.rem(lax.axis_index("heads") // 2 * chips, PAGES) * PAGE
    copies[0].wait()
    copies[1].wait()
    code = code_ref[...]
    target = code >> LENGTH_BITS
    lengths = code & ((1 << LENGTH_BITS) - 1)
    for r in range(prompts):
        for g in range(heads):
            query = recv_ref[:, g * HD : (g + 1) * HD].astype(f32)
            query_ref[r // 2, g * rows : (g + 1) * rows, r % 2 * HD : (r % 2 + 1) * HD] = jnp.where(
                target == r, query, 0.0
            ).astype(bf16)
    copies[2].wait()
    scores = jnp.zeros((heads * rows, keys), f32)
    for pair in range(prompts // 2):
        scores = scores + dot_nt(query_ref[pair], key_ref[pair])
    copies[3].wait()
    for copy in states:
        copy.wait()
    seen = jnp.concatenate([lengths[:, :1]] * heads, axis=0) > iota((heads * rows, keys), 1) + begin
    scores = jnp.where(seen, scores * SCORE, NONE)
    highest = jnp.maximum(jnp.max(scores, axis=1, keepdims=True), FLOOR)
    weight = jnp.exp2(scores - highest)
    total = jnp.sum(weight, axis=1, keepdims=True)
    some = total > 0.0
    safe = jnp.where(some, total, 1.0)
    result = jnp.where(some, highest + jnp.log2(safe), NONE)
    weight = weight.astype(bf16)
    targets = jnp.concatenate([target] * heads, axis=0)
    value = jnp.zeros((heads * rows, HD), f32)
    for pair in range(prompts // 2):
        both = jnp.dot(weight, value_ref[pair], preferred_element_type=f32)
        for n in range(2):
            value = jnp.where(targets == 2 * pair + n, both[:, n * HD : (n + 1) * HD], value)
    value = value / safe
    lane = iota((rows, LANES), 1)
    sums = jnp.zeros((rows, LANES), f32)
    for g in range(heads):
        sums = jnp.where(lane % 4 == g, result[g * rows : (g + 1) * rows], sums)
    high = sums.astype(bf16).astype(f32)
    rest = sums - high
    middle = rest.astype(bf16).astype(f32)
    piece = lane % 16 // 4
    pieces = jnp.where(piece == 0, high, jnp.where(piece == 1, middle, rest - middle))
    pair = iota((rows, LANES), 0) % SUB
    pieces = jnp.where((lane // 16 == pair) & (piece < 3), pieces, 0.0)
    packed = jnp.sum(pieces.reshape(rows // SUB, SUB, LANES), axis=1, keepdims=True)

    given = recv_ref[...].astype(f32).reshape(rows // SUB, SUB, recv_ref.shape[1])
    ending = lift(given, spare(heads + 1, 0))
    readout = jnp.concatenate([given[..., HALF:], ending], axis=-1).reshape(rows, NS)
    target = jnp.concatenate([target, target], axis=-1)
    found = jnp.zeros((rows, width), f32)
    for r in range(prompts):
        picked = jnp.where(target == r, readout, 0.0).astype(bf16)
        found = found + dot_nt(picked, state_ref[r])
    if width < LANES:
        found = jnp.concatenate([found, jnp.zeros((rows, LANES - width), f32)], axis=-1)
    blocks = [value[g * rows : (g + 1) * rows] for g in range(heads)]
    blocks += [found[:, b : b + LANES] for b in range(0, found.shape[1], LANES)]
    blocks = [one.reshape(rows // SUB, SUB, LANES) for one in blocks]
    row = iota((rows // SUB, SUB, LANES), 1)
    last = blocks.pop()
    blocks[0] = jnp.where(row == PAIRS, jnp.broadcast_to(packed, row.shape), blocks[0])
    for n, (at, b) in enumerate(spare(len(blocks), 1)):
        one = jnp.broadcast_to(last[:, n : n + 1, :], row.shape)
        blocks[b] = jnp.where(row == at, one, blocks[b])
    for b, one in enumerate(blocks):
        out_ref[:, b * LANES : (b + 1) * LANES] = one.reshape(rows, LANES).astype(bf16)


def prompt_kernel(
    rate_any,
    skip_any,
    len_any,
    dt_any,
    rates_any,
    skips_any,
    send_any,
    fresh_any,
    sx_any,
    sb_any,
    sc_any,
    sdt_any,
    x_any,
    b_any,
    c_any,
    after_any,
    early_any,
    out_any,
    own_any,
    ownsum_any,
    fade_any,
    local_any,
    x_held,
    b_held,
    c_held,
    out_held,
    w_in,
    w_out,
    w_skip,
    masks,
    signs,
    own_ref,
    ownsum_ref,
    fade_ref,
    local_ref,
    fresh_held,
    c_rows,
    x_rows,
    rate_ref,
    skip_ref,
    len_ref,
    dt_ref,
    rates_ref,
    skips_ref,
    send_ref,
    fresh_ref,
    sx_ref,
    sb_ref,
    sc_ref,
    sdt_ref,
    x_sem,
    b_sem,
    c_sem,
    out_sem,
    sems,
):
    group, prompts, length = dt_ref.shape
    smalls = fetches(
        [
            (dt_any, dt_ref),
            (rate_any, rate_ref),
            (skip_any, skip_ref),
            (len_any, len_ref),
            (rates_any, rates_ref),
            (skips_any, skips_ref),
            (send_any, send_ref),
            (fresh_any, fresh_ref),
            (sx_any, sx_ref),
            (sb_any, sb_ref),
            (sc_any, sc_ref),
            (sdt_any, sdt_ref),
        ],
        sems,
    )
    me = lax.axis_index("heads")
    first = me * group
    column = pl.multiple_of((first // HPG) * NS, NS)

    def x_copy(r):
        return pltpu.make_async_copy(x_any.at[r], x_held.at[r], x_sem.at[r])

    def b_copy(r):
        return pltpu.make_async_copy(b_any.at[r, :, pl.ds(column, NS)], b_held.at[r], b_sem.at[r])

    def c_copy(r):
        return pltpu.make_async_copy(c_any.at[r, :, pl.ds(column, NS)], c_held.at[r], c_sem.at[r])

    def out_copy(r):
        return pltpu.make_async_copy(out_held.at[r], out_any.at[r], out_sem.at[r])

    def ask(r):
        x_copy(r).start()
        b_copy(r).start()
        c_copy(r).start()

    for r in range(EARLY, min(EARLY + AHEAD, prompts)):
        ask(r)
    sign_tables(signs, False)
    level_masks(masks)
    for copy in smalls:
        copy.wait()
    head_factors(first, dt_ref, rate_ref, skip_ref, len_ref, signs, w_in, w_out, w_skip, None)
    own_attention(send_ref, fresh_ref, fresh_held, own_ref, ownsum_ref)
    own_mixer(rates_ref, skips_ref, sx_ref, sb_ref, sc_ref, sdt_ref, c_rows, x_rows, fade_ref, local_ref)
    outs = fetches(
        [(own_ref, own_any), (ownsum_ref, ownsum_any), (fade_ref, fade_any), (local_ref, local_any)], sems
    )

    def one(r, _):
        @pl.when(r + AHEAD < prompts)
        def _():
            ask(r + AHEAD)

        x_copy(r).wait()
        b_copy(r).wait()
        c_copy(r).wait()
        prompt_result(r, x_held, b_held, c_held, w_in, w_out, w_skip, masks, out_held)
        out_copy(r).start()
        return 0

    lax.fori_loop(EARLY, prompts, one, 0, unroll=2)
    for copy in outs:
        copy.wait()
    for r in range(EARLY, prompts):
        out_copy(r).wait()


def own_attention(send_ref, fresh_ref, fresh_held, own_ref, ownsum_ref):
    steps, rows = fresh_ref.shape[0], fresh_ref.shape[1]
    owners = send_ref.shape[0]
    order = exchange_order(owners)
    ways = owners // KVH
    stack_rows(fresh_ref, fresh_held)
    count = HALF // HD * 2 * SUB
    pair = iota((count, SUB), 0) % SUB
    key = iota((count, SUB), 1)
    seen = (key % rows == pair % rows) & (key <= pair) & (key < rows * steps)
    seen = seen | ((pair >= rows * steps) & (key == 0))
    for v in range(KVH):
        halves = [send_ref[order.index(v * ways + n), :, :HALF].astype(f32) for n in range(2)]
        parts = [half[:, g * HD : (g + 1) * HD] for g in range(HALF // HD) for half in halves]
        query = jnp.concatenate(parts, axis=0).astype(bf16)
        keys = fresh_held[:, v * HD : (v + 1) * HD].astype(bf16)
        values = fresh_held[:, (KVH + v) * HD : (KVH + v + 1) * HD].astype(bf16)
        scores = jnp.where(seen, dot_nt(query, keys) * SCORE, NONE)
        highest = jnp.max(scores, axis=1, keepdims=True)
        weight = jnp.exp2(scores - highest)
        total = jnp.sum(weight, axis=1, keepdims=True)
        weight = (weight / total).astype(bf16)
        own_ref[v] = jnp.dot(weight, values, preferred_element_type=f32)
        ownsum_ref[v] = jnp.broadcast_to(highest + jnp.log2(total), (count, HD))


def own_mixer(rates_ref, skips_ref, sx_ref, sb_ref, sc_ref, sdt_ref, c_rows, x_rows, fade_ref, local_ref):
    steps, rows, heads = sdt_ref.shape
    stack_rows(sc_ref, c_rows)
    for u in range(steps):
        given = sx_ref[u].astype(f32)
        for k in range(SUB // rows):
            x_rows[u, k * rows : (k + 1) * rows, :] = given
    pair = iota((SUB, heads), 0)
    step = pair // rows
    live = pair < rows * steps
    head = iota((SUB, heads), 1)

    def spread_rows(ref, u):
        given = ref[u].astype(f32)
        return jnp.concatenate([given] * (SUB // rows), axis=0)

    rates = jnp.broadcast_to(rates_ref[...], (SUB, heads)) * LOG2E
    skips = jnp.broadcast_to(skips_ref[...], (SUB, heads))
    moved = [spread_rows(sdt_ref, u) for u in range(steps)]
    kept = [jnp.where(u <= step, moved[u], 0.0) for u in range(steps)]
    parts = [jnp.where(live, jnp.exp2(-(rates * sum(kept))), 0.0)]
    for u in range(steps):
        products = c_rows[...] * spread_rows(sb_ref, u)
        inner = jnp.zeros((SUB, heads), f32)
        for e in range(products.shape[1] // NS):
            found = jnp.sum(products[:, e * NS : (e + 1) * NS], axis=1, keepdims=True)
            inner = jnp.where(head // HPG == e, found, inner)
        gap = jnp.zeros((SUB, heads), f32)
        for t in range(u + 1, steps):
            gap = gap + kept[t]
        weight = jnp.where(u <= step, jnp.exp2(-(rates * gap)) * moved[u] * inner, 0.0)
        weight = weight + jnp.where(u == step, skips, 0.0)
        parts.append(jnp.where(live, weight, 0.0))
    stacked = jnp.concatenate(parts, axis=0)
    high = stacked.astype(bf16)
    low = (stacked - high.astype(f32)).astype(bf16)
    both = jnp.concatenate([high.astype(f32), low.astype(f32)], axis=0)
    count = stacked.shape[0]
    chunk = SUB * HP
    widen = jnp.where(iota((heads, chunk), 0) % SUB == iota((heads, chunk), 1) // HP, 1.0, 0.0).astype(bf16)
    lane = iota(both.shape, 1)
    for d in range(heads // SUB):
        picked = jnp.where(lane // SUB == d, both, 0.0).astype(bf16)
        wide = jnp.dot(picked, widen, preferred_element_type=f32)
        wide = wide[:count] + wide[count:]
        columns = slice(d * chunk, (d + 1) * chunk)
        fade_ref[:, columns] = wide[:SUB]
        value = jnp.zeros((SUB, chunk), f32)
        for u in range(steps):
            value = value + wide[(u + 1) * SUB : (u + 2) * SUB] * x_rows[u, :, columns]
        local_ref[:, columns] = value


def merge_kernel(
    width,
    back_any,
    own_any,
    ownsum_any,
    fade_any,
    local_any,
    mixer_any,
    attention_any,
    back_ref,
    own_ref,
    ownsum_ref,
    fade_ref,
    local_ref,
    mixed,
    attended,
    mixer_ref,
    attention_ref,
    sems,
):
    copies = fetches([(back_any, back_ref), (fade_any, fade_ref), (local_any, local_ref)], sems)
    rest = fetches([(own_any, own_ref), (ownsum_any, ownsum_ref)], sems, len(copies))
    for copy in copies:
        copy.wait()
    owners = back_ref.shape[0]
    ways = owners // KVH
    order = exchange_order(owners)
    steps, rows = mixer_ref.shape[0], mixer_ref.shape[1]
    for d in range(0, owners, 2):
        block = jnp.stack([back_ref[order.index(d + n)].astype(f32) for n in range(2)])
        ending = lift(block, spare(back_ref.shape[2] // LANES, 1))
        if back_ref.shape[2] > HALF:
            ending = jnp.concatenate([block[..., HALF:], ending], axis=-1)
        found = ending[..., :width]
        found = jnp.concatenate([found[0], found[1]], axis=-1)
        columns = slice(d * width, (d + 2) * width)
        mixed[:, columns] = found * fade_ref[:, columns] + local_ref[:, columns]
    for k in range(steps):
        mixer_ref[k] = mixed[k * rows : (k + 1) * rows, :].astype(bf16)
    outs = fetches([(mixer_ref, mixer_any)], sems)
    for copy in rest:
        copy.wait()
    lane = iota((2, SUB, LANES), 2)
    mine = (lane // 16 == iota((2, SUB, LANES), 1)) & (lane % 16 < 12)
    for v in range(KVH):
        blocks, pieces = [], []
        for d in range(v * ways, (v + 1) * ways, 2):
            block = jnp.stack([back_ref[order.index(d + n), :, :HALF].astype(f32) for n in range(2)])
            packed = block[:, PAIRS : PAIRS + 1, :LANES]
            blocks.append(block.reshape(2 * SUB, HALF))
            pieces.append(jnp.where(mine, jnp.broadcast_to(packed, (2, SUB, LANES)), 0.0))
        for g in range(HALF // HD):
            part = slice(g * 2 * SUB, (g + 1) * 2 * SUB)
            own_sum = ownsum_ref[v, part, :]
            wide = []
            for piece in pieces:
                one = jnp.sum(jnp.where(lane % 4 == g, piece, 0.0), axis=-1, keepdims=True)
                wide.append(jnp.broadcast_to(one, (2, SUB, HD)).reshape(2 * SUB, HD))
            highest = functools.reduce(jnp.maximum, wide, own_sum)
            weight = jnp.exp2(own_sum - highest)
            total = weight
            value = weight * own_ref[v, part, :]
            for one, block in zip(wide, blocks):
                weight = jnp.exp2(one - highest)
                total = total + weight
                value = value + weight * block[:, g * HD : (g + 1) * HD]
            value = value / total
            start = v * 2 * HALF + g * HD
            attended[:, start : start + HD] = value[:SUB]
            attended[:, start + HALF : start + HALF + HD] = value[SUB:]
    for k in range(steps):
        attention_ref[k] = attended[k * rows : (k + 1) * rows, :].astype(bf16)
    outs += fetches([(attention_ref, attention_any)], sems, 1)
    for copy in outs:
        copy.wait()


def call(kernel, out_shape, in_spaces, out_spaces, scratch, cost, aliases=None):
    def spec(space):
        return pl.BlockSpec(memory_space=space)

    return pl.pallas_call(
        kernel,
        out_shape=out_shape,
        in_specs=[spec(space) for space in in_spaces],
        out_specs=jax.tree.map(spec, out_spaces),
        scratch_shapes=scratch,
        input_output_aliases=aliases or {},
        compiler_params=pltpu.CompilerParams(vmem_limit_bytes=VMEM_LIMIT),
        cost_estimate=pl.CostEstimate(flops=cost[0], bytes_accessed=cost[1], transcendentals=0),
    )


def on_device(
    prompt_x,
    prompt_b,
    prompt_c,
    prompt_dt,
    decay_rate,
    skip_gain,
    lengths,
    owner_list,
    page_table,
    cache_pages,
    row_slot,
    step_x,
    step_b,
    step_c,
    step_dt,
    queries,
    fresh_cache,
):
    owners = lax.axis_size("heads")
    ways = owners // KVH
    group, prompts, length = prompt_dt.shape
    width = prompt_x.shape[1]
    keys = cache_pages.shape[0] * PAGE
    span = 2 * keys // prompts
    steps = step_x.shape[1]
    all_rows = owners * SUB
    shape = jax.ShapeDtypeStruct
    smem, vmem, hbm = pltpu.SMEM, pltpu.VMEM, pltpu.HBM
    sem = pltpu.SemaphoreType.DMA((prompts,))
    levels = len(LEVELS)
    step_x, step_b, step_c, step_dt, queries, fresh_cache = (
        jnp.swapaxes(one, 0, 1) for one in (step_x, step_b, step_c, step_dt, queries, fresh_cache)
    )
    owner_list = owner_list.T

    def like(space, array):
        return space(array.shape, array.dtype)

    def sems(count):
        return pltpu.SemaphoreType.DMA((count,))

    other_pages = lax.ppermute(cache_pages, "heads", [(d, d + 1 - 2 * (d % 2)) for d in range(owners)])
    send = call(
        functools.partial(pack_kernel, group, ways),
        shape((all_rows, HALF + LANES), bf16),
        [hbm, hbm],
        vmem,
        [
            like(vmem, queries),
            like(vmem, step_c),
            vmem((SUB, queries.shape[2]), f32),
            vmem((SUB, step_c.shape[2]), f32),
            vmem((step_c.shape[2] // NS, SUB, HALF + LANES), f32),
            sems(2),
        ],
        (0, 1 << 19),
    )(queries, step_c)
    order = [exchange_order(owners)]
    recv = lax.all_to_all(
        send, "heads", split_axis=0, concat_axis=0, tiled=True, axis_index_groups=order
    )

    block = [
        vmem((prompts, width, length), bf16),
        vmem((prompts, length, NS), bf16),
        vmem((prompts, length, NS), bf16),
        vmem((prompts, width, length), bf16),
        vmem((levels, prompts, group, length), f32),
        vmem((levels, prompts, group, length), f32),
        vmem((prompts, group, length), f32),
    ]
    tables = [vmem((levels, length, length), bf16), vmem((levels + 1, length, length), bf16)]
    work = 2 * width * length * NS
    states, sorted_keys, sorted_values, codes, early_out = call(
        state_kernel,
        (
            shape((prompts, width, NS), bf16),
            shape((prompts // 2, span, 2 * HD), bf16),
            shape((prompts // 2, span, 2 * HD), bf16),
            shape((all_rows, LANES), jnp.int32),
            shape(prompt_x.shape, bf16),
        ),
        [hbm] * 12,
        (hbm,) * 5,
        block
        + tables
        + [vmem((prompts, group, length), f32), vmem((prompts, width, NS), bf16)]
        + [vmem((2,) + cache_pages.shape, bf16)]
        + [vmem((prompts // 2, span, 2 * HD), bf16)] * 2
        + [vmem((all_rows, LANES), jnp.int32)]
        + [like(smem, one) for one in (decay_rate, skip_gain, lengths, owner_list, page_table, row_slot)]
        + [like(vmem, prompt_dt), sem, sem, sem, sem, sem, sems(9)],
        (work * (prompts + 5 * EARLY), 6 << 20),
    )(
        decay_rate,
        skip_gain,
        lengths,
        owner_list,
        page_table,
        row_slot,
        prompt_dt,
        prompt_x,
        prompt_b,
        prompt_c,
        cache_pages,
        other_pages,
    )

    back = call(
        serve_kernel,
        shape((all_rows, HALF + max(LANES, width) - LANES), bf16),
        [hbm] * 5,
        vmem,
        [like(vmem, one) for one in (recv, sorted_keys, sorted_values, codes, states)]
        + [vmem((prompts // 2, HALF // HD * all_rows, 2 * HD), bf16), sem, sems(4)],
        (8 * all_rows * keys * HD, 4 << 20),
    )(recv, sorted_keys, sorted_values, codes, states)
    returned = lax.all_to_all(
        back, "heads", split_axis=0, concat_axis=0, tiled=True, axis_index_groups=order
    ).reshape(owners, SUB, back.shape[1])

    count = HALF // HD * 2 * SUB
    channels = step_x.shape[2]
    rates, skips = decay_rate.reshape(1, -1), skip_gain.reshape(1, -1)
    prompt_out, own, own_sum, fade, local = call(
        prompt_kernel,
        (
            shape(prompt_x.shape, bf16),
            shape((KVH, count, HD), f32),
            shape((KVH, count, HD), f32),
            shape((SUB, channels), f32),
            shape((SUB, channels), f32),
        ),
        [hbm] * 17,
        (hbm,) * 5,
        block
        + tables
        + [
            vmem((KVH, count, HD), f32),
            vmem((KVH, count, HD), f32),
            vmem((SUB, channels), f32),
            vmem((SUB, channels), f32),
            vmem((SUB, fresh_cache.shape[2]), f32),
            vmem((SUB, step_c.shape[2]), f32),
            vmem((steps, SUB, channels), f32),
            like(smem, decay_rate),
            like(smem, skip_gain),
            like(smem, lengths),
            like(vmem, prompt_dt),
            like(vmem, rates),
            like(vmem, skips),
            vmem((owners, SUB, HALF + LANES), bf16),
            like(vmem, fresh_cache),
            like(vmem, step_x),
            like(vmem, step_b),
            like(vmem, step_c),
            like(vmem, step_dt),
            sem,
            sem,
            sem,
            sem,
            sems(12),
        ],
        (work * 5 * (prompts - EARLY), 8 << 20),
        {16: 0},
    )(
        decay_rate,
        skip_gain,
        lengths,
        prompt_dt,
        rates,
        skips,
        send.reshape(owners, SUB, HALF + LANES),
        fresh_cache,
        step_x,
        step_b,
        step_c,
        step_dt,
        prompt_x,
        prompt_b,
        prompt_c,
        back,
        early_out,
    )

    mixer_out, attention_out = call(
        functools.partial(merge_kernel, width),
        (shape(step_x.shape, bf16), shape(queries.shape, bf16)),
        [hbm] * 5,
        (hbm, hbm),
        [like(vmem, one) for one in (returned, own, own_sum, fade, local)]
        + [vmem((SUB, channels), f32), vmem((SUB, queries.shape[2]), f32)]
        + [like(vmem, step_x), like(vmem, queries), sems(5)],
        (0, 2 << 20),
    )(returned, own, own_sum, fade, local)
    return (prompt_out, jnp.swapaxes(mixer_out, 0, 1), jnp.swapaxes(attention_out, 0, 1))


def solution(mesh):
    in_specs = (
        P("groups", "heads", None),
        P("groups", None, None),
        P("groups", None, None),
        P("heads", "groups", None),
        P(),
        P(),
        P("groups"),
        P("groups", None),
        P("groups", None),
        P(("groups", "heads"), None, None),
        P("groups"),
        P(("groups", "heads"), None, None),
        P(("groups", "heads"), None, None),
        P(("groups", "heads"), None, None),
        P(("groups", "heads"), None, None),
        P(("groups", "heads"), None, None),
        P(("groups", "heads"), None, None),
    )
    out_specs = (
        P("groups", "heads", None),
        P(("groups", "heads"), None, None),
        P(("groups", "heads"), None, None),
    )
    return jax.shard_map(
        on_device, mesh=mesh, in_specs=in_specs, out_specs=out_specs, check_vma=False
    )
```

```python
import functools
import math

import jax
import jax.numpy as jnp
from jax import lax
from jax.experimental import pallas as pl
from jax.experimental.pallas import tpu as pltpu
from jax.sharding import PartitionSpec as P

NS = 256
HP = 64
HPG = 32
KVH = 8
HD = 128
PAGE = 16
PAGES = 16
LANES = 128
SUB = 8
HALF = 512
LEVELS = (128, 64, 32, 16)
LOG2E = math.log2(math.e)
SCORE = LOG2E / math.sqrt(HD)
NONE = -1e30
FLOOR = -1e29
PAIRS = 6
LENGTH_BITS = 10
AHEAD = 2
EARLY = 2
VMEM_LIMIT = 64 * 1024 * 1024

f32 = jnp.float32
bf16 = jnp.bfloat16


def iota(shape, dim):
    return lax.broadcasted_iota(jnp.int32, shape, dim)


def exchange_order(owners):
    middle = owners // 4
    return [middle] + [d for d in reversed(range(owners)) if d != middle]


def dot_nt(left, right):
    return lax.dot_general(left, right, (((1,), (1,)), ((), ())), preferred_element_type=f32)


def stack_rows(source, held):
    steps, rows = source.shape[0], source.shape[1]
    held[...] = jnp.zeros_like(held)
    for k in range(steps):
        held[k * rows : (k + 1) * rows, :] = source[k].astype(f32)


def spare(blocks, taken):
    return [(row, b) for row in range(PAIRS, SUB) for b in range(blocks)][taken : taken + PAIRS]


def lift(value, slots):
    row = iota(value.shape[:2] + (LANES,), 1)
    found = jnp.zeros(row.shape, f32)
    for pair, (at, b) in enumerate(slots):
        one = value[:, at : at + 1, b * LANES : (b + 1) * LANES]
        found = jnp.where(row == pair, jnp.broadcast_to(one, row.shape), found)
    return found


def fetches(pairs, sems, first=0):
    copies = [pltpu.make_async_copy(src, dst, sems.at[first + n]) for n, (src, dst) in enumerate(pairs)]
    for copy in copies:
        copy.start()
    return copies


def pack_kernel(group, ways, q_any, c_any, out_ref, q_ref, c_ref, q_held, c_held, rest, sems):
    owners = out_ref.shape[0] // SUB
    for copy in fetches([(q_any, q_ref), (c_any, c_ref)], sems):
        copy.wait()
    stack_rows(q_ref, q_held)
    stack_rows(c_ref, c_held)
    span = 2 * HALF
    slots = spare(HALF // LANES + 1, 0)
    rest[...] = jnp.zeros_like(rest)
    for e in range(c_ref.shape[2] // NS):
        rest[e, :PAIRS, HALF:] = c_held[:PAIRS, e * NS : e * NS + LANES]
        for pair, (row, b) in enumerate(slots):
            rest[e, row : row + 1, b * LANES : (b + 1) * LANES] = c_held[
                pair : pair + 1, e * NS + LANES : (e + 1) * NS
            ]
    real = iota((SUB, HALF), 0) < PAIRS
    order = exchange_order(owners)
    for rank in range(0, owners, 2):
        blocks, ends = [], []
        for d in order[rank : rank + 2]:
            begin, e = d // ways * span + d % 2 * HALF, (d * group) // HPG
            blocks.append(jnp.where(real, q_held[:, begin : begin + HALF], rest[e, :, :HALF]))
            ends.append(rest[e, :, HALF:])
        place = slice(rank * SUB, (rank + 2) * SUB)
        out_ref[place, :HALF] = jnp.concatenate(blocks, axis=0).astype(bf16)
        out_ref[place, HALF:] = jnp.concatenate(ends, axis=0).astype(bf16)


def sign_tables(signs, tail):
    length = signs.shape[-1]
    j = iota((length, length), 0)
    i = iota((length, length), 1)
    for l, n in enumerate(LEVELS):
        middle = (i // (2 * n)) * (2 * n) + (n - 1)
        signs[l] = (jnp.where(j <= i, 1.0, 0.0) - jnp.where(j <= middle, 1.0, 0.0)).astype(bf16)
    if tail:
        signs[len(LEVELS)] = jnp.where(j > i, 1.0, 0.0).astype(bf16)


def head_factors(first, dt_ref, rate_ref, skip_ref, len_ref, signs, w_in, w_out, w_skip, w_tail):
    group, prompts, length = dt_ref.shape
    row = iota((prompts, length), 0)
    lens = jnp.zeros((prompts, length), jnp.int32)
    for r in range(prompts):
        lens = jnp.where(row == r, len_ref[r], lens)
    valid = iota((prompts, length), 1) < lens
    moved = [jnp.where(valid, dt_ref[h].astype(f32), 0.0) for h in range(group)]
    every = jnp.concatenate(moved, axis=0).astype(bf16)
    rates = [rate_ref[first + h] * LOG2E for h in range(group)]
    if w_tail is not None:
        total = jnp.dot(every, signs[len(LEVELS)], preferred_element_type=f32)
        for h in range(group):
            part = total[h * prompts : (h + 1) * prompts]
            w_tail[:, h, :] = jnp.exp2(-(rates[h] * part)) * moved[h]
    for h in range(group):
        w_skip[:, h, :] = jnp.where(valid, skip_ref[first + h], 0.0)
    for l, n in enumerate(LEVELS):
        total = jnp.dot(every, signs[l], preferred_element_type=f32)
        for h in range(group):
            gap = rates[h] * total[h * prompts : (h + 1) * prompts]
            if n == LEVELS[-1]:
                up, down = jnp.exp2(gap), jnp.exp2(-gap)
            else:
                up, down = jnp.exp2(jnp.minimum(gap, 0.0)), jnp.exp2(-jnp.maximum(gap, 0.0))
            w_in[l, :, h, :] = up * moved[h]
            w_out[l, :, h, :] = jnp.where(valid, down, 0.0)


def level_masks(masks):
    length = masks.shape[-1]
    j = iota((length, length), 0)
    i = iota((length, length), 1)
    for l, n in enumerate(LEVELS):
        same = (j // (2 * n)) == (i // (2 * n))
        if n == LEVELS[-1]:
            keep = same & (j <= i)
        else:
            keep = same & ((j % (2 * n)) < n) & ((i % (2 * n)) >= n)
        masks[l] = jnp.where(keep, 1.0, 0.0).astype(bf16)


def prompt_result(r, x_held, b_held, c_held, w_in, w_out, w_skip, masks, out_held):
    width, length = x_held.shape[1], x_held.shape[2]
    group = width // HP
    half = length // 2
    inputs = x_held[r].astype(f32).reshape(group, HP, length)
    scores = dot_nt(b_held[r], c_held[r]).astype(bf16)
    total = inputs * w_skip[r][:, None, :]
    left, right = total[..., :half], total[..., half:]
    for l, n in enumerate(LEVELS):
        if 2 * n == length:
            scaled = (inputs[..., :half] * w_in[l, r][:, None, :half]).astype(bf16).reshape(width, half)
            added = jnp.dot(scaled, scores[:half, half:], preferred_element_type=f32)
            right = right + added.reshape(group, HP, half) * w_out[l, r][:, None, half:]
        else:
            scaled = (inputs * w_in[l, r][:, None, :]).astype(bf16).reshape(width, length)
            added = jnp.dot(scaled, scores * masks[l], preferred_element_type=f32)
            added = added.reshape(group, HP, length) * w_out[l, r][:, None, :]
            left = left + added[..., :half]
            right = right + added[..., half:]
    out_held[r] = jnp.concatenate([left, right], axis=-1).reshape(width, length).astype(bf16)


def state_kernel(
    rate_any,
    skip_any,
    len_any,
    owner_any,
    table_any,
    slot_any,
    dt_any,
    x_any,
    b_any,
    c_any,
    pages_any,
    other_any,
    state_any,
    key_any,
    value_any,
    code_any,
    out_any,
    x_held,
    b_held,
    c_held,
    out_held,
    w_in,
    w_out,
    w_skip,
    masks,
    signs,
    w_tail,
    state_held,
    pages_held,
    key_held,
    value_held,
    code_held,
    rate_ref,
    skip_ref,
    len_ref,
    owner_ref,
    table_ref,
    slot_ref,
    dt_ref,
    x_sem,
    b_sem,
    c_sem,
    out_sem,
    state_sem,
    sems,
):
    group, prompts, length = dt_ref.shape
    smalls = fetches(
        [
            (dt_any, dt_ref),
            (rate_any, rate_ref),
            (skip_any, skip_ref),
            (len_any, len_ref),
            (owner_any, owner_ref),
            (table_any, table_ref),
            (slot_any, slot_ref),
        ],
        sems,
    )
    me = lax.axis_index("heads")
    core = lax.rem(me, 2)
    first = me * group
    column = pl.multiple_of((first // HPG) * NS, NS)

    def x_copy(r):
        return pltpu.make_async_copy(x_any.at[r], x_held.at[r], x_sem.at[r])

    def b_copy(r):
        return pltpu.make_async_copy(b_any.at[r, :, pl.ds(column, NS)], b_held.at[r], b_sem.at[r])

    def c_copy(r):
        return pltpu.make_async_copy(c_any.at[r, :, pl.ds(column, NS)], c_held.at[r], c_sem.at[r])

    def out_copy(r):
        return pltpu.make_async_copy(out_held.at[r], out_any.at[r], out_sem.at[r])

    def state_copy(r):
        return pltpu.make_async_copy(state_held.at[r], state_any.at[r], state_sem.at[r])

    def ask(r):
        x_copy(r).start()
        b_copy(r).start()

    pages = fetches([(pages_any, pages_held.at[core]), (other_any, pages_held.at[1 - core])], sems, len(smalls))
    for r in range(prompts):
        ask(r)
    for r in range(EARLY):
        c_copy(r).start()
    sign_tables(signs, True)
    level_masks(masks)
    for copy in smalls:
        copy.wait()
    head_factors(first, dt_ref, rate_ref, skip_ref, len_ref, signs, w_in, w_out, w_skip, w_tail)

    width = x_held.shape[1]
    for begin in range(0, prompts, prompts // 2):
        some = range(begin, begin + prompts // 2)
        for r in some:
            x_copy(r).wait()
            b_copy(r).wait()
        for r in some:
            inputs = x_held[r].astype(f32).reshape(group, HP, length)
            scaled = (inputs * w_tail[r][:, None, :]).astype(bf16).reshape(width, length)
            state_held[r] = jnp.dot(scaled, b_held[r], preferred_element_type=f32).astype(bf16)
        for r in some:
            state_copy(r).start()
    spread = table_ref.shape[1] // owner_ref.shape[1]
    for copy in pages:
        copy.wait()
    for n in range(2):
        for r in range(prompts):
            for page in range(spread):
                holder = me - core + n
                row = table_ref[r, holder * spread + page] - holder * (prompts * spread)
                block = pages_held[n, row]
                place = pl.ds((n * spread + page) * PAGE, PAGE)
                columns = pl.ds(r % 2 * HD, HD)
                key_held[r // 2, place, columns] = block[:, :HD]
                value_held[r // 2, place, columns] = block[:, HD:]

    owners = owner_ref.shape[1]
    rows_dev = slot_ref.shape[0] // owners
    inner = iota((2 * SUB, LANES), 0)

    order = exchange_order(owners)
    for rank in range(0, owners, 2):
        block = jnp.zeros((2 * SUB, LANES), jnp.int32)
        for n in range(2):
            s = order[rank + n]
            for i in range(rows_dev):
                target = owner_ref[slot_ref[s * rows_dev + i], s]
                code = target * (1 << LENGTH_BITS) + len_ref[target]
                block = jnp.where((inner // SUB == n) & (inner % rows_dev == i), code, block)
        code_held[rank * SUB : (rank + 2) * SUB, :] = block
    marks = fetches([(key_held, key_any), (value_held, value_any), (code_held, code_any)], sems)

    for r in range(EARLY):
        c_copy(r).wait()
    for r in range(EARLY):
        prompt_result(r, x_held, b_held, c_held, w_in, w_out, w_skip, masks, out_held)
    for r in range(EARLY):
        out_copy(r).start()
    for copy in marks:
        copy.wait()
    for r in range(prompts):
        state_copy(r).wait()
    for r in range(EARLY):
        out_copy(r).wait()


def serve_kernel(
    recv_any,
    key_any,
    value_any,
    code_any,
    state_any,
    out_ref,
    recv_ref,
    key_ref,
    value_ref,
    code_ref,
    state_ref,
    query_ref,
    state_sem,
    sems,
):
    rows = recv_ref.shape[0]
    prompts, width = state_ref.shape[0], state_ref.shape[1]
    copies = fetches(
        [(recv_any, recv_ref), (code_any, code_ref), (key_any, key_ref), (value_any, value_ref)], sems
    )
    states = fetches([(state_any.at[r], state_ref.at[r]) for r in range(prompts)], state_sem)
    heads = HALF // HD
    keys = key_ref.shape[1]
    chips = keys // PAGE
    begin = lax.rem(lax.axis_index("heads") // 2 * chips, PAGES) * PAGE
    copies[0].wait()
    copies[1].wait()
    code = code_ref[...]
    target = code >> LENGTH_BITS
    lengths = code & ((1 << LENGTH_BITS) - 1)
    for r in range(prompts):
        for g in range(heads):
            query = recv_ref[:, g * HD : (g + 1) * HD].astype(f32)
            query_ref[r // 2, g * rows : (g + 1) * rows, r % 2 * HD : (r % 2 + 1) * HD] = jnp.where(
                target == r, query, 0.0
            ).astype(bf16)
    copies[2].wait()
    scores = jnp.zeros((heads * rows, keys), f32)
    for pair in range(prompts // 2):
        scores = scores + dot_nt(query_ref[pair], key_ref[pair])
    copies[3].wait()
    for copy in states:
        copy.wait()
    seen = jnp.concatenate([lengths[:, :1]] * heads, axis=0) > iota((heads * rows, keys), 1) + begin
    scores = jnp.where(seen, scores * SCORE, NONE)
    highest = jnp.maximum(jnp.max(scores, axis=1, keepdims=True), FLOOR)
    weight = jnp.exp2(scores - highest)
    total = jnp.sum(weight, axis=1, keepdims=True)
    some = total > 0.0
    safe = jnp.where(some, total, 1.0)
    result = jnp.where(some, highest + jnp.log2(safe), NONE)
    weight = weight.astype(bf16)
    targets = jnp.concatenate([target] * heads, axis=0)
    value = jnp.zeros((heads * rows, HD), f32)
    for pair in range(prompts // 2):
        both = jnp.dot(weight, value_ref[pair], preferred_element_type=f32)
        for n in range(2):
            value = jnp.where(targets == 2 * pair + n, both[:, n * HD : (n + 1) * HD], value)
    value = value / safe
    lane = iota((rows, LANES), 1)
    sums = jnp.zeros((rows, LANES), f32)
    for g in range(heads):
        sums = jnp.where(lane % 4 == g, result[g * rows : (g + 1) * rows], sums)
    high = sums.astype(bf16).astype(f32)
    rest = sums - high
    middle = rest.astype(bf16).astype(f32)
    piece = lane % 16 // 4
    pieces = jnp.where(piece == 0, high, jnp.where(piece == 1, middle, rest - middle))
    pair = iota((rows, LANES), 0) % SUB
    pieces = jnp.where((lane // 16 == pair) & (piece < 3), pieces, 0.0)
    packed = jnp.sum(pieces.reshape(rows // SUB, SUB, LANES), axis=1, keepdims=True)

    given = recv_ref[...].astype(f32).reshape(rows // SUB, SUB, recv_ref.shape[1])
    ending = lift(given, spare(heads + 1, 0))
    readout = jnp.concatenate([given[..., HALF:], ending], axis=-1).reshape(rows, NS)
    target = jnp.concatenate([target, target], axis=-1)
    found = jnp.zeros((rows, width), f32)
    for r in range(prompts):
        picked = jnp.where(target == r, readout, 0.0).astype(bf16)
        found = found + dot_nt(picked, state_ref[r])
    if width < LANES:
        found = jnp.concatenate([found, jnp.zeros((rows, LANES - width), f32)], axis=-1)
    blocks = [value[g * rows : (g + 1) * rows] for g in range(heads)]
    blocks += [found[:, b : b + LANES] for b in range(0, found.shape[1], LANES)]
    blocks = [one.reshape(rows // SUB, SUB, LANES) for one in blocks]
    row = iota((rows // SUB, SUB, LANES), 1)
    last = blocks.pop()
    blocks[0] = jnp.where(row == PAIRS, jnp.broadcast_to(packed, row.shape), blocks[0])
    for n, (at, b) in enumerate(spare(len(blocks), 1)):
        one = jnp.broadcast_to(last[:, n : n + 1, :], row.shape)
        blocks[b] = jnp.where(row == at, one, blocks[b])
    for b, one in enumerate(blocks):
        out_ref[:, b * LANES : (b + 1) * LANES] = one.reshape(rows, LANES).astype(bf16)


def prompt_kernel(
    rate_any,
    skip_any,
    len_any,
    dt_any,
    rates_any,
    skips_any,
    send_any,
    fresh_any,
    sx_any,
    sb_any,
    sc_any,
    sdt_any,
    x_any,
    b_any,
    c_any,
    after_any,
    early_any,
    out_any,
    own_any,
    ownsum_any,
    fade_any,
    local_any,
    x_held,
    b_held,
    c_held,
    out_held,
    w_in,
    w_out,
    w_skip,
    masks,
    signs,
    own_ref,
    ownsum_ref,
    fade_ref,
    local_ref,
    fresh_held,
    c_rows,
    x_rows,
    rate_ref,
    skip_ref,
    len_ref,
    dt_ref,
    rates_ref,
    skips_ref,
    send_ref,
    fresh_ref,
    sx_ref,
    sb_ref,
    sc_ref,
    sdt_ref,
    x_sem,
    b_sem,
    c_sem,
    out_sem,
    sems,
):
    group, prompts, length = dt_ref.shape
    smalls = fetches(
        [
            (dt_any, dt_ref),
            (rate_any, rate_ref),
            (skip_any, skip_ref),
            (len_any, len_ref),
            (rates_any, rates_ref),
            (skips_any, skips_ref),
            (send_any, send_ref),
            (fresh_any, fresh_ref),
            (sx_any, sx_ref),
            (sb_any, sb_ref),
            (sc_any, sc_ref),
            (sdt_any, sdt_ref),
        ],
        sems,
    )
    me = lax.axis_index("heads")
    first = me * group
    column = pl.multiple_of((first // HPG) * NS, NS)

    def x_copy(r):
        return pltpu.make_async_copy(x_any.at[r], x_held.at[r], x_sem.at[r])

    def b_copy(r):
        return pltpu.make_async_copy(b_any.at[r, :, pl.ds(column, NS)], b_held.at[r], b_sem.at[r])

    def c_copy(r):
        return pltpu.make_async_copy(c_any.at[r, :, pl.ds(column, NS)], c_held.at[r], c_sem.at[r])

    def out_copy(r):
        return pltpu.make_async_copy(out_held.at[r], out_any.at[r], out_sem.at[r])

    def ask(r):
        x_copy(r).start()
        b_copy(r).start()
        c_copy(r).start()

    for r in range(EARLY, min(EARLY + AHEAD, prompts)):
        ask(r)
    sign_tables(signs, False)
    level_masks(masks)
    for copy in smalls:
        copy.wait()
    head_factors(first, dt_ref, rate_ref, skip_ref, len_ref, signs, w_in, w_out, w_skip, None)
    own_attention(send_ref, fresh_ref, fresh_held, own_ref, ownsum_ref)
    own_mixer(rates_ref, skips_ref, sx_ref, sb_ref, sc_ref, sdt_ref, c_rows, x_rows, fade_ref, local_ref)
    outs = fetches(
        [(own_ref, own_any), (ownsum_ref, ownsum_any), (fade_ref, fade_any), (local_ref, local_any)], sems
    )

    def some(n, _):
        begin = EARLY + n * AHEAD

        @pl.when(begin + AHEAD < prompts)
        def _():
            for r in range(AHEAD):
                ask(begin + AHEAD + r)

        for r in range(AHEAD):
            x_copy(begin + r).wait()
            b_copy(begin + r).wait()
            c_copy(begin + r).wait()
        for r in range(AHEAD):
            prompt_result(begin + r, x_held, b_held, c_held, w_in, w_out, w_skip, masks, out_held)
        for r in range(AHEAD):
            out_copy(begin + r).start()
        return 0

    lax.fori_loop(0, (prompts - EARLY) // AHEAD, some, 0)
    for copy in outs:
        copy.wait()
    for r in range(EARLY, prompts):
        out_copy(r).wait()


def own_attention(send_ref, fresh_ref, fresh_held, own_ref, ownsum_ref):
    steps, rows = fresh_ref.shape[0], fresh_ref.shape[1]
    owners = send_ref.shape[0]
    order = exchange_order(owners)
    ways = owners // KVH
    stack_rows(fresh_ref, fresh_held)
    count = HALF // HD * 2 * SUB
    pair = iota((count, SUB), 0) % SUB
    key = iota((count, SUB), 1)
    seen = (key % rows == pair % rows) & (key <= pair) & (key < rows * steps)
    seen = seen | ((pair >= rows * steps) & (key == 0))
    for v in range(KVH):
        halves = [send_ref[order.index(v * ways + n), :, :HALF].astype(f32) for n in range(2)]
        parts = [half[:, g * HD : (g + 1) * HD] for g in range(HALF // HD) for half in halves]
        query = jnp.concatenate(parts, axis=0).astype(bf16)
        keys = fresh_held[:, v * HD : (v + 1) * HD].astype(bf16)
        values = fresh_held[:, (KVH + v) * HD : (KVH + v + 1) * HD].astype(bf16)
        scores = jnp.where(seen, dot_nt(query, keys) * SCORE, NONE)
        highest = jnp.max(scores, axis=1, keepdims=True)
        weight = jnp.exp2(scores - highest)
        total = jnp.sum(weight, axis=1, keepdims=True)
        weight = (weight / total).astype(bf16)
        own_ref[v] = jnp.dot(weight, values, preferred_element_type=f32)
        ownsum_ref[v] = jnp.broadcast_to(highest + jnp.log2(total), (count, HD))


def own_mixer(rates_ref, skips_ref, sx_ref, sb_ref, sc_ref, sdt_ref, c_rows, x_rows, fade_ref, local_ref):
    steps, rows, heads = sdt_ref.shape
    stack_rows(sc_ref, c_rows)
    for u in range(steps):
        given = sx_ref[u].astype(f32)
        for k in range(SUB // rows):
            x_rows[u, k * rows : (k + 1) * rows, :] = given
    pair = iota((SUB, heads), 0)
    step = pair // rows
    live = pair < rows * steps
    head = iota((SUB, heads), 1)

    def spread_rows(ref, u):
        given = ref[u].astype(f32)
        return jnp.concatenate([given] * (SUB // rows), axis=0)

    rates = jnp.broadcast_to(rates_ref[...], (SUB, heads)) * LOG2E
    skips = jnp.broadcast_to(skips_ref[...], (SUB, heads))
    moved = [spread_rows(sdt_ref, u) for u in range(steps)]
    kept = [jnp.where(u <= step, moved[u], 0.0) for u in range(steps)]
    parts = [jnp.where(live, jnp.exp2(-(rates * sum(kept))), 0.0)]
    for u in range(steps):
        products = c_rows[...] * spread_rows(sb_ref, u)
        inner = jnp.zeros((SUB, heads), f32)
        for e in range(products.shape[1] // NS):
            found = jnp.sum(products[:, e * NS : (e + 1) * NS], axis=1, keepdims=True)
            inner = jnp.where(head // HPG == e, found, inner)
        gap = jnp.zeros((SUB, heads), f32)
        for t in range(u + 1, steps):
            gap = gap + kept[t]
        weight = jnp.where(u <= step, jnp.exp2(-(rates * gap)) * moved[u] * inner, 0.0)
        weight = weight + jnp.where(u == step, skips, 0.0)
        parts.append(jnp.where(live, weight, 0.0))
    stacked = jnp.concatenate(parts, axis=0)
    high = stacked.astype(bf16)
    low = (stacked - high.astype(f32)).astype(bf16)
    both = jnp.concatenate([high.astype(f32), low.astype(f32)], axis=0)
    count = stacked.shape[0]
    chunk = SUB * HP
    widen = jnp.where(iota((heads, chunk), 0) % SUB == iota((heads, chunk), 1) // HP, 1.0, 0.0).astype(bf16)
    lane = iota(both.shape, 1)
    for d in range(heads // SUB):
        picked = jnp.where(lane // SUB == d, both, 0.0).astype(bf16)
        wide = jnp.dot(picked, widen, preferred_element_type=f32)
        wide = wide[:count] + wide[count:]
        columns = slice(d * chunk, (d + 1) * chunk)
        fade_ref[:, columns] = wide[:SUB]
        value = jnp.zeros((SUB, chunk), f32)
        for u in range(steps):
            value = value + wide[(u + 1) * SUB : (u + 2) * SUB] * x_rows[u, :, columns]
        local_ref[:, columns] = value


def merge_kernel(
    width,
    back_any,
    own_any,
    ownsum_any,
    fade_any,
    local_any,
    mixer_any,
    attention_any,
    back_ref,
    own_ref,
    ownsum_ref,
    fade_ref,
    local_ref,
    mixed,
    attended,
    mixer_ref,
    attention_ref,
    sems,
):
    copies = fetches([(back_any, back_ref), (fade_any, fade_ref), (local_any, local_ref)], sems)
    rest = fetches([(own_any, own_ref), (ownsum_any, ownsum_ref)], sems, len(copies))
    for copy in copies:
        copy.wait()
    owners = back_ref.shape[0]
    ways = owners // KVH
    order = exchange_order(owners)
    steps, rows = mixer_ref.shape[0], mixer_ref.shape[1]
    for d in range(0, owners, 2):
        block = jnp.stack([back_ref[order.index(d + n)].astype(f32) for n in range(2)])
        ending = lift(block, spare(back_ref.shape[2] // LANES, 1))
        if back_ref.shape[2] > HALF:
            ending = jnp.concatenate([block[..., HALF:], ending], axis=-1)
        found = ending[..., :width]
        found = jnp.concatenate([found[0], found[1]], axis=-1)
        columns = slice(d * width, (d + 2) * width)
        mixed[:, columns] = found * fade_ref[:, columns] + local_ref[:, columns]
    for k in range(steps):
        mixer_ref[k] = mixed[k * rows : (k + 1) * rows, :].astype(bf16)
    outs = fetches([(mixer_ref, mixer_any)], sems)
    for copy in rest:
        copy.wait()
    lane = iota((2, SUB, LANES), 2)
    mine = (lane // 16 == iota((2, SUB, LANES), 1)) & (lane % 16 < 12)
    for v in range(KVH):
        blocks, pieces = [], []
        for d in range(v * ways, (v + 1) * ways, 2):
            block = jnp.stack([back_ref[order.index(d + n), :, :HALF].astype(f32) for n in range(2)])
            packed = block[:, PAIRS : PAIRS + 1, :LANES]
            blocks.append(block.reshape(2 * SUB, HALF))
            pieces.append(jnp.where(mine, jnp.broadcast_to(packed, (2, SUB, LANES)), 0.0))
        for g in range(HALF // HD):
            part = slice(g * 2 * SUB, (g + 1) * 2 * SUB)
            own_sum = ownsum_ref[v, part, :]
            wide = []
            for piece in pieces:
                one = jnp.sum(jnp.where(lane % 4 == g, piece, 0.0), axis=-1, keepdims=True)
                wide.append(jnp.broadcast_to(one, (2, SUB, HD)).reshape(2 * SUB, HD))
            highest = functools.reduce(jnp.maximum, wide, own_sum)
            weight = jnp.exp2(own_sum - highest)
            total = weight
            value = weight * own_ref[v, part, :]
            for one, block in zip(wide, blocks):
                weight = jnp.exp2(one - highest)
                total = total + weight
                value = value + weight * block[:, g * HD : (g + 1) * HD]
            value = value / total
            start = v * 2 * HALF + g * HD
            attended[:, start : start + HD] = value[:SUB]
            attended[:, start + HALF : start + HALF + HD] = value[SUB:]
    for k in range(steps):
        attention_ref[k] = attended[k * rows : (k + 1) * rows, :].astype(bf16)
    outs += fetches([(attention_ref, attention_any)], sems, 1)
    for copy in outs:
        copy.wait()


def call(kernel, out_shape, in_spaces, out_spaces, scratch, cost, aliases=None):
    def spec(space):
        return pl.BlockSpec(memory_space=space)

    return pl.pallas_call(
        kernel,
        out_shape=out_shape,
        in_specs=[spec(space) for space in in_spaces],
        out_specs=jax.tree.map(spec, out_spaces),
        scratch_shapes=scratch,
        input_output_aliases=aliases or {},
        compiler_params=pltpu.CompilerParams(vmem_limit_bytes=VMEM_LIMIT),
        cost_estimate=pl.CostEstimate(flops=cost[0], bytes_accessed=cost[1], transcendentals=0),
    )


def on_device(
    prompt_x,
    prompt_b,
    prompt_c,
    prompt_dt,
    decay_rate,
    skip_gain,
    lengths,
    owner_list,
    page_table,
    cache_pages,
    row_slot,
    step_x,
    step_b,
    step_c,
    step_dt,
    queries,
    fresh_cache,
):
    owners = lax.axis_size("heads")
    ways = owners // KVH
    group, prompts, length = prompt_dt.shape
    width = prompt_x.shape[1]
    keys = cache_pages.shape[0] * PAGE
    span = 2 * keys // prompts
    steps = step_x.shape[1]
    all_rows = owners * SUB
    shape = jax.ShapeDtypeStruct
    smem, vmem, hbm = pltpu.SMEM, pltpu.VMEM, pltpu.HBM
    sem = pltpu.SemaphoreType.DMA((prompts,))
    levels = len(LEVELS)
    step_x, step_b, step_c, step_dt, queries, fresh_cache = (
        jnp.swapaxes(one, 0, 1) for one in (step_x, step_b, step_c, step_dt, queries, fresh_cache)
    )
    owner_list = owner_list.T

    def like(space, array):
        return space(array.shape, array.dtype)

    def sems(count):
        return pltpu.SemaphoreType.DMA((count,))

    other_pages = lax.ppermute(cache_pages, "heads", [(d, d + 1 - 2 * (d % 2)) for d in range(owners)])
    send = call(
        functools.partial(pack_kernel, group, ways),
        shape((all_rows, HALF + LANES), bf16),
        [hbm, hbm],
        vmem,
        [
            like(vmem, queries),
            like(vmem, step_c),
            vmem((SUB, queries.shape[2]), f32),
            vmem((SUB, step_c.shape[2]), f32),
            vmem((step_c.shape[2] // NS, SUB, HALF + LANES), f32),
            sems(2),
        ],
        (0, 1 << 19),
    )(queries, step_c)
    order = [exchange_order(owners)]
    recv = lax.all_to_all(
        send, "heads", split_axis=0, concat_axis=0, tiled=True, axis_index_groups=order
    )

    block = [
        vmem((prompts, width, length), bf16),
        vmem((prompts, length, NS), bf16),
        vmem((prompts, length, NS), bf16),
        vmem((prompts, width, length), bf16),
        vmem((levels, prompts, group, length), f32),
        vmem((levels, prompts, group, length), f32),
        vmem((prompts, group, length), f32),
    ]
    tables = [vmem((levels, length, length), bf16), vmem((levels + 1, length, length), bf16)]
    work = 2 * width * length * NS
    states, sorted_keys, sorted_values, codes, early_out = call(
        state_kernel,
        (
            shape((prompts, width, NS), bf16),
            shape((prompts // 2, span, 2 * HD), bf16),
            shape((prompts // 2, span, 2 * HD), bf16),
            shape((all_rows, LANES), jnp.int32),
            shape(prompt_x.shape, bf16),
        ),
        [hbm] * 12,
        (hbm,) * 5,
        block
        + tables
        + [vmem((prompts, group, length), f32), vmem((prompts, width, NS), bf16)]
        + [vmem((2,) + cache_pages.shape, bf16)]
        + [vmem((prompts // 2, span, 2 * HD), bf16)] * 2
        + [vmem((all_rows, LANES), jnp.int32)]
        + [like(smem, one) for one in (decay_rate, skip_gain, lengths, owner_list, page_table, row_slot)]
        + [like(vmem, prompt_dt), sem, sem, sem, sem, sem, sems(9)],
        (work * (prompts + 5 * EARLY), 6 << 20),
    )(
        decay_rate,
        skip_gain,
        lengths,
        owner_list,
        page_table,
        row_slot,
        prompt_dt,
        prompt_x,
        prompt_b,
        prompt_c,
        cache_pages,
        other_pages,
    )

    back = call(
        serve_kernel,
        shape((all_rows, HALF + max(LANES, width) - LANES), bf16),
        [hbm] * 5,
        vmem,
        [like(vmem, one) for one in (recv, sorted_keys, sorted_values, codes, states)]
        + [vmem((prompts // 2, HALF // HD * all_rows, 2 * HD), bf16), sem, sems(4)],
        (8 * all_rows * keys * HD, 4 << 20),
    )(recv, sorted_keys, sorted_values, codes, states)
    returned = lax.all_to_all(
        back, "heads", split_axis=0, concat_axis=0, tiled=True, axis_index_groups=order
    ).reshape(owners, SUB, back.shape[1])

    count = HALF // HD * 2 * SUB
    channels = step_x.shape[2]
    rates, skips = decay_rate.reshape(1, -1), skip_gain.reshape(1, -1)
    prompt_out, own, own_sum, fade, local = call(
        prompt_kernel,
        (
            shape(prompt_x.shape, bf16),
            shape((KVH, count, HD), f32),
            shape((KVH, count, HD), f32),
            shape((SUB, channels), f32),
            shape((SUB, channels), f32),
        ),
        [hbm] * 17,
        (hbm,) * 5,
        block
        + tables
        + [
            vmem((KVH, count, HD), f32),
            vmem((KVH, count, HD), f32),
            vmem((SUB, channels), f32),
            vmem((SUB, channels), f32),
            vmem((SUB, fresh_cache.shape[2]), f32),
            vmem((SUB, step_c.shape[2]), f32),
            vmem((steps, SUB, channels), f32),
            like(smem, decay_rate),
            like(smem, skip_gain),
            like(smem, lengths),
            like(vmem, prompt_dt),
            like(vmem, rates),
            like(vmem, skips),
            vmem((owners, SUB, HALF + LANES), bf16),
            like(vmem, fresh_cache),
            like(vmem, step_x),
            like(vmem, step_b),
            like(vmem, step_c),
            like(vmem, step_dt),
            sem,
            sem,
            sem,
            sem,
            sems(12),
        ],
        (work * 5 * (prompts - EARLY), 8 << 20),
        {16: 0},
    )(
        decay_rate,
        skip_gain,
        lengths,
        prompt_dt,
        rates,
        skips,
        send.reshape(owners, SUB, HALF + LANES),
        fresh_cache,
        step_x,
        step_b,
        step_c,
        step_dt,
        prompt_x,
        prompt_b,
        prompt_c,
        back,
        early_out,
    )

    mixer_out, attention_out = call(
        functools.partial(merge_kernel, width),
        (shape(step_x.shape, bf16), shape(queries.shape, bf16)),
        [hbm] * 5,
        (hbm, hbm),
        [like(vmem, one) for one in (returned, own, own_sum, fade, local)]
        + [vmem((SUB, channels), f32), vmem((SUB, queries.shape[2]), f32)]
        + [like(vmem, step_x), like(vmem, queries), sems(5)],
        (0, 2 << 20),
    )(returned, own, own_sum, fade, local)
    return (prompt_out, jnp.swapaxes(mixer_out, 0, 1), jnp.swapaxes(attention_out, 0, 1))


def solution(mesh):
    in_specs = (
        P("groups", "heads", None),
        P("groups", None, None),
        P("groups", None, None),
        P("heads", "groups", None),
        P(),
        P(),
        P("groups"),
        P("groups", None),
        P("groups", None),
        P(("groups", "heads"), None, None),
        P("groups"),
        P(("groups", "heads"), None, None),
        P(("groups", "heads"), None, None),
        P(("groups", "heads"), None, None),
        P(("groups", "heads"), None, None),
        P(("groups", "heads"), None, None),
        P(("groups", "heads"), None, None),
    )
    out_specs = (
        P("groups", "heads", None),
        P(("groups", "heads"), None, None),
        P(("groups", "heads"), None, None),
    )
    return jax.shard_map(
        on_device, mesh=mesh, in_specs=in_specs, out_specs=out_specs, check_vma=False
    )
```

```python
import functools
import math

import jax
import jax.numpy as jnp
from jax import lax
from jax.experimental import pallas as pl
from jax.experimental.pallas import tpu as pltpu
from jax.sharding import PartitionSpec as P

NS = 256
HP = 64
HPG = 32
KVH = 8
HD = 128
PAGE = 16
PAGES = 16
LANES = 128
SUB = 8
HALF = 512
LEVELS = (128, 64, 32, 16)
LOG2E = math.log2(math.e)
SCORE = LOG2E / math.sqrt(HD)
NONE = -1e30
FLOOR = -1e29
PAIRS = 6
LENGTH_BITS = 10
AHEAD = 2
EARLY = 2
VMEM_LIMIT = 64 * 1024 * 1024

f32 = jnp.float32
bf16 = jnp.bfloat16


def iota(shape, dim):
    return lax.broadcasted_iota(jnp.int32, shape, dim)


def exchange_order(owners):
    first = owners * 5 // 8
    return [first] + [d for d in range(owners) if d != first]


def dot_nt(left, right):
    return lax.dot_general(left, right, (((1,), (1,)), ((), ())), preferred_element_type=f32)


def stack_rows(source, held):
    steps, rows = source.shape[0], source.shape[1]
    held[...] = jnp.zeros_like(held)
    for k in range(steps):
        held[k * rows : (k + 1) * rows, :] = source[k].astype(f32)


def spare(blocks, taken):
    return [(row, b) for row in range(PAIRS, SUB) for b in range(blocks)][taken : taken + PAIRS]


def lift(value, slots):
    row = iota(value.shape[:2] + (LANES,), 1)
    found = jnp.zeros(row.shape, f32)
    for pair, (at, b) in enumerate(slots):
        one = value[:, at : at + 1, b * LANES : (b + 1) * LANES]
        found = jnp.where(row == pair, jnp.broadcast_to(one, row.shape), found)
    return found


def fetches(pairs, sems, first=0):
    copies = [pltpu.make_async_copy(src, dst, sems.at[first + n]) for n, (src, dst) in enumerate(pairs)]
    for copy in copies:
        copy.start()
    return copies


def pack_kernel(group, ways, q_any, c_any, out_ref, q_ref, c_ref, q_held, c_held, rest, sems):
    owners = out_ref.shape[0] // SUB
    for copy in fetches([(q_any, q_ref), (c_any, c_ref)], sems):
        copy.wait()
    stack_rows(q_ref, q_held)
    stack_rows(c_ref, c_held)
    span = 2 * HALF
    slots = spare(HALF // LANES + 1, 0)
    rest[...] = jnp.zeros_like(rest)
    for e in range(c_ref.shape[2] // NS):
        rest[e, :PAIRS, HALF:] = c_held[:PAIRS, e * NS : e * NS + LANES]
        for pair, (row, b) in enumerate(slots):
            rest[e, row : row + 1, b * LANES : (b + 1) * LANES] = c_held[
                pair : pair + 1, e * NS + LANES : (e + 1) * NS
            ]
    real = iota((SUB, HALF), 0) < PAIRS
    order = exchange_order(owners)
    for rank in range(0, owners, 2):
        blocks, ends = [], []
        for d in order[rank : rank + 2]:
            begin, e = d // ways * span + d % 2 * HALF, (d * group) // HPG
            blocks.append(jnp.where(real, q_held[:, begin : begin + HALF], rest[e, :, :HALF]))
            ends.append(rest[e, :, HALF:])
        place = slice(rank * SUB, (rank + 2) * SUB)
        out_ref[place, :HALF] = jnp.concatenate(blocks, axis=0).astype(bf16)
        out_ref[place, HALF:] = jnp.concatenate(ends, axis=0).astype(bf16)


def sign_tables(signs, tail):
    length = signs.shape[-1]
    j = iota((length, length), 0)
    i = iota((length, length), 1)
    for l, n in enumerate(LEVELS):
        middle = (i // (2 * n)) * (2 * n) + (n - 1)
        signs[l] = (jnp.where(j <= i, 1.0, 0.0) - jnp.where(j <= middle, 1.0, 0.0)).astype(bf16)
    if tail:
        signs[len(LEVELS)] = jnp.where(j > i, 1.0, 0.0).astype(bf16)


def head_factors(first, dt_ref, rate_ref, skip_ref, len_ref, signs, w_in, w_out, w_skip, w_tail):
    group, prompts, length = dt_ref.shape
    row = iota((prompts, length), 0)
    lens = jnp.zeros((prompts, length), jnp.int32)
    for r in range(prompts):
        lens = jnp.where(row == r, len_ref[r], lens)
    valid = iota((prompts, length), 1) < lens
    moved = [jnp.where(valid, dt_ref[h].astype(f32), 0.0) for h in range(group)]
    every = jnp.concatenate(moved, axis=0).astype(bf16)
    rates = [rate_ref[first + h] * LOG2E for h in range(group)]
    if w_tail is not None:
        total = jnp.dot(every, signs[len(LEVELS)], preferred_element_type=f32)
        for h in range(group):
            part = total[h * prompts : (h + 1) * prompts]
            w_tail[:, h, :] = jnp.exp2(-(rates[h] * part)) * moved[h]
    for h in range(group):
        w_skip[:, h, :] = jnp.where(valid, skip_ref[first + h], 0.0)
    for l, n in enumerate(LEVELS):
        total = jnp.dot(every, signs[l], preferred_element_type=f32)
        for h in range(group):
            gap = rates[h] * total[h * prompts : (h + 1) * prompts]
            if n == LEVELS[-1]:
                up, down = jnp.exp2(gap), jnp.exp2(-gap)
            else:
                up, down = jnp.exp2(jnp.minimum(gap, 0.0)), jnp.exp2(-jnp.maximum(gap, 0.0))
            w_in[l, :, h, :] = up * moved[h]
            w_out[l, :, h, :] = jnp.where(valid, down, 0.0)


def level_masks(masks):
    length = masks.shape[-1]
    j = iota((length, length), 0)
    i = iota((length, length), 1)
    for l, n in enumerate(LEVELS):
        same = (j // (2 * n)) == (i // (2 * n))
        if n == LEVELS[-1]:
            keep = same & (j <= i)
        else:
            keep = same & ((j % (2 * n)) < n) & ((i % (2 * n)) >= n)
        masks[l] = jnp.where(keep, 1.0, 0.0).astype(bf16)


def prompt_result(r, x_held, b_held, c_held, w_in, w_out, w_skip, masks, out_held):
    width, length = x_held.shape[1], x_held.shape[2]
    group = width // HP
    half = length // 2
    inputs = x_held[r].astype(f32).reshape(group, HP, length)
    scores = dot_nt(b_held[r], c_held[r]).astype(bf16)
    total = inputs * w_skip[r][:, None, :]
    left, right = total[..., :half], total[..., half:]
    for l, n in enumerate(LEVELS):
        if 2 * n == length:
            scaled = (inputs[..., :half] * w_in[l, r][:, None, :half]).astype(bf16).reshape(width, half)
            added = jnp.dot(scaled, scores[:half, half:], preferred_element_type=f32)
            right = right + added.reshape(group, HP, half) * w_out[l, r][:, None, half:]
        else:
            scaled = (inputs * w_in[l, r][:, None, :]).astype(bf16).reshape(width, length)
            added = jnp.dot(scaled, scores * masks[l], preferred_element_type=f32)
            added = added.reshape(group, HP, length) * w_out[l, r][:, None, :]
            left = left + added[..., :half]
            right = right + added[..., half:]
    out_held[r] = jnp.concatenate([left, right], axis=-1).reshape(width, length).astype(bf16)


def state_kernel(
    rate_any,
    skip_any,
    len_any,
    owner_any,
    table_any,
    slot_any,
    dt_any,
    x_any,
    b_any,
    c_any,
    pages_any,
    other_any,
    state_any,
    key_any,
    value_any,
    code_any,
    out_any,
    x_held,
    b_held,
    c_held,
    out_held,
    w_in,
    w_out,
    w_skip,
    masks,
    signs,
    w_tail,
    state_held,
    pages_held,
    key_held,
    value_held,
    code_held,
    rate_ref,
    skip_ref,
    len_ref,
    owner_ref,
    table_ref,
    slot_ref,
    dt_ref,
    x_sem,
    b_sem,
    c_sem,
    out_sem,
    state_sem,
    sems,
):
    group, prompts, length = dt_ref.shape
    smalls = fetches(
        [
            (dt_any, dt_ref),
            (rate_any, rate_ref),
            (skip_any, skip_ref),
            (len_any, len_ref),
            (owner_any, owner_ref),
            (table_any, table_ref),
            (slot_any, slot_ref),
        ],
        sems,
    )
    me = lax.axis_index("heads")
    core = lax.rem(me, 2)
    first = me * group
    column = pl.multiple_of((first // HPG) * NS, NS)

    def x_copy(r):
        return pltpu.make_async_copy(x_any.at[r], x_held.at[r], x_sem.at[r])

    def b_copy(r):
        return pltpu.make_async_copy(b_any.at[r, :, pl.ds(column, NS)], b_held.at[r], b_sem.at[r])

    def c_copy(r):
        return pltpu.make_async_copy(c_any.at[r, :, pl.ds(column, NS)], c_held.at[r], c_sem.at[r])

    def out_copy(r):
        return pltpu.make_async_copy(out_held.at[r], out_any.at[r], out_sem.at[r])

    def state_copy(r):
        return pltpu.make_async_copy(state_held.at[r], state_any.at[r], state_sem.at[r])

    def ask(r):
        x_copy(r).start()
        b_copy(r).start()

    pages = fetches([(pages_any, pages_held.at[core]), (other_any, pages_held.at[1 - core])], sems, len(smalls))
    for r in range(prompts):
        ask(r)
    for r in range(EARLY):
        c_copy(r).start()
    sign_tables(signs, True)
    level_masks(masks)
    for copy in smalls:
        copy.wait()
    head_factors(first, dt_ref, rate_ref, skip_ref, len_ref, signs, w_in, w_out, w_skip, w_tail)

    width = x_held.shape[1]
    for begin in range(0, prompts, prompts // 2):
        some = range(begin, begin + prompts // 2)
        for r in some:
            x_copy(r).wait()
            b_copy(r).wait()
        for r in some:
            inputs = x_held[r].astype(f32).reshape(group, HP, length)
            scaled = (inputs * w_tail[r][:, None, :]).astype(bf16).reshape(width, length)
            state_held[r] = jnp.dot(scaled, b_held[r], preferred_element_type=f32).astype(bf16)
        for r in some:
            state_copy(r).start()
    spread = table_ref.shape[1] // owner_ref.shape[1]
    for copy in pages:
        copy.wait()
    for n in range(2):
        for r in range(prompts):
            for page in range(spread):
                holder = me - core + n
                row = table_ref[r, holder * spread + page] - holder * (prompts * spread)
                block = pages_held[n, row]
                place = pl.ds((n * spread + page) * PAGE, PAGE)
                columns = pl.ds(r % 2 * HD, HD)
                key_held[r // 2, place, columns] = block[:, :HD]
                value_held[r // 2, place, columns] = block[:, HD:]

    owners = owner_ref.shape[1]
    rows_dev = slot_ref.shape[0] // owners
    inner = iota((2 * SUB, LANES), 0)

    order = exchange_order(owners)
    for rank in range(0, owners, 2):
        block = jnp.zeros((2 * SUB, LANES), jnp.int32)
        for n in range(2):
            s = order[rank + n]
            for i in range(rows_dev):
                target = owner_ref[slot_ref[s * rows_dev + i], s]
                code = target * (1 << LENGTH_BITS) + len_ref[target]
                block = jnp.where((inner // SUB == n) & (inner % rows_dev == i), code, block)
        code_held[rank * SUB : (rank + 2) * SUB, :] = block
    marks = fetches([(key_held, key_any), (value_held, value_any), (code_held, code_any)], sems)

    for r in range(EARLY):
        c_copy(r).wait()
    for r in range(EARLY):
        prompt_result(r, x_held, b_held, c_held, w_in, w_out, w_skip, masks, out_held)
    for r in range(EARLY):
        out_copy(r).start()
    for copy in marks:
        copy.wait()
    for r in range(prompts):
        state_copy(r).wait()
    for r in range(EARLY):
        out_copy(r).wait()


def serve_kernel(
    recv_any,
    key_any,
    value_any,
    code_any,
    state_any,
    out_ref,
    recv_ref,
    key_ref,
    value_ref,
    code_ref,
    state_ref,
    query_ref,
    state_sem,
    sems,
):
    rows = recv_ref.shape[0]
    prompts, width = state_ref.shape[0], state_ref.shape[1]
    copies = fetches(
        [(recv_any, recv_ref), (code_any, code_ref), (key_any, key_ref), (value_any, value_ref)], sems
    )
    states = fetches([(state_any.at[r], state_ref.at[r]) for r in range(prompts)], state_sem)
    heads = HALF // HD
    keys = key_ref.shape[1]
    chips = keys // PAGE
    begin = lax.rem(lax.axis_index("heads") // 2 * chips, PAGES) * PAGE
    copies[0].wait()
    copies[1].wait()
    code = code_ref[...]
    target = code >> LENGTH_BITS
    lengths = code & ((1 << LENGTH_BITS) - 1)
    for r in range(prompts):
        for g in range(heads):
            query = recv_ref[:, g * HD : (g + 1) * HD].astype(f32)
            query_ref[r // 2, g * rows : (g + 1) * rows, r % 2 * HD : (r % 2 + 1) * HD] = jnp.where(
                target == r, query, 0.0
            ).astype(bf16)
    copies[2].wait()
    scores = jnp.zeros((heads * rows, keys), f32)
    for pair in range(prompts // 2):
        scores = scores + dot_nt(query_ref[pair], key_ref[pair])
    copies[3].wait()
    for copy in states:
        copy.wait()
    seen = jnp.concatenate([lengths[:, :1]] * heads, axis=0) > iota((heads * rows, keys), 1) + begin
    scores = jnp.where(seen, scores * SCORE, NONE)
    highest = jnp.maximum(jnp.max(scores, axis=1, keepdims=True), FLOOR)
    weight = jnp.exp2(scores - highest)
    total = jnp.sum(weight, axis=1, keepdims=True)
    some = total > 0.0
    safe = jnp.where(some, total, 1.0)
    result = jnp.where(some, highest + jnp.log2(safe), NONE)
    weight = weight.astype(bf16)
    targets = jnp.concatenate([target] * heads, axis=0)
    value = jnp.zeros((heads * rows, HD), f32)
    for pair in range(prompts // 2):
        both = jnp.dot(weight, value_ref[pair], preferred_element_type=f32)
        for n in range(2):
            value = jnp.where(targets == 2 * pair + n, both[:, n * HD : (n + 1) * HD], value)
    value = value / safe
    lane = iota((rows, LANES), 1)
    sums = jnp.zeros((rows, LANES), f32)
    for g in range(heads):
        sums = jnp.where(lane % 4 == g, result[g * rows : (g + 1) * rows], sums)
    high = sums.astype(bf16).astype(f32)
    rest = sums - high
    middle = rest.astype(bf16).astype(f32)
    piece = lane % 16 // 4
    pieces = jnp.where(piece == 0, high, jnp.where(piece == 1, middle, rest - middle))
    pair = iota((rows, LANES), 0) % SUB
    pieces = jnp.where((lane // 16 == pair) & (piece < 3), pieces, 0.0)
    packed = jnp.sum(pieces.reshape(rows // SUB, SUB, LANES), axis=1, keepdims=True)

    given = recv_ref[...].astype(f32).reshape(rows // SUB, SUB, recv_ref.shape[1])
    ending = lift(given, spare(heads + 1, 0))
    readout = jnp.concatenate([given[..., HALF:], ending], axis=-1).reshape(rows, NS)
    target = jnp.concatenate([target, target], axis=-1)
    found = jnp.zeros((rows, width), f32)
    for r in range(prompts):
        picked = jnp.where(target == r, readout, 0.0).astype(bf16)
        found = found + dot_nt(picked, state_ref[r])
    if width < LANES:
        found = jnp.concatenate([found, jnp.zeros((rows, LANES - width), f32)], axis=-1)
    blocks = [value[g * rows : (g + 1) * rows] for g in range(heads)]
    blocks += [found[:, b : b + LANES] for b in range(0, found.shape[1], LANES)]
    blocks = [one.reshape(rows // SUB, SUB, LANES) for one in blocks]
    row = iota((rows // SUB, SUB, LANES), 1)
    last = blocks.pop()
    blocks[0] = jnp.where(row == PAIRS, jnp.broadcast_to(packed, row.shape), blocks[0])
    for n, (at, b) in enumerate(spare(len(blocks), 1)):
        one = jnp.broadcast_to(last[:, n : n + 1, :], row.shape)
        blocks[b] = jnp.where(row == at, one, blocks[b])
    for b, one in enumerate(blocks):
        out_ref[:, b * LANES : (b + 1) * LANES] = one.reshape(rows, LANES).astype(bf16)


def prompt_kernel(
    rate_any,
    skip_any,
    len_any,
    dt_any,
    rates_any,
    skips_any,
    send_any,
    fresh_any,
    sx_any,
    sb_any,
    sc_any,
    sdt_any,
    x_any,
    b_any,
    c_any,
    after_any,
    early_any,
    out_any,
    own_any,
    ownsum_any,
    fade_any,
    local_any,
    x_held,
    b_held,
    c_held,
    out_held,
    w_in,
    w_out,
    w_skip,
    masks,
    signs,
    own_ref,
    ownsum_ref,
    fade_ref,
    local_ref,
    fresh_held,
    c_rows,
    x_rows,
    rate_ref,
    skip_ref,
    len_ref,
    dt_ref,
    rates_ref,
    skips_ref,
    send_ref,
    fresh_ref,
    sx_ref,
    sb_ref,
    sc_ref,
    sdt_ref,
    x_sem,
    b_sem,
    c_sem,
    out_sem,
    sems,
):
    group, prompts, length = dt_ref.shape
    smalls = fetches(
        [
            (dt_any, dt_ref),
            (rate_any, rate_ref),
            (skip_any, skip_ref),
            (len_any, len_ref),
            (rates_any, rates_ref),
            (skips_any, skips_ref),
            (send_any, send_ref),
            (fresh_any, fresh_ref),
            (sx_any, sx_ref),
            (sb_any, sb_ref),
            (sc_any, sc_ref),
            (sdt_any, sdt_ref),
        ],
        sems,
    )
    me = lax.axis_index("heads")
    first = me * group
    column = pl.multiple_of((first // HPG) * NS, NS)

    def x_copy(r):
        return pltpu.make_async_copy(x_any.at[r], x_held.at[r], x_sem.at[r])

    def b_copy(r):
        return pltpu.make_async_copy(b_any.at[r, :, pl.ds(column, NS)], b_held.at[r], b_sem.at[r])

    def c_copy(r):
        return pltpu.make_async_copy(c_any.at[r, :, pl.ds(column, NS)], c_held.at[r], c_sem.at[r])

    def out_copy(r):
        return pltpu.make_async_copy(out_held.at[r], out_any.at[r], out_sem.at[r])

    def ask(r):
        x_copy(r).start()
        b_copy(r).start()
        c_copy(r).start()

    for r in range(EARLY, min(EARLY + AHEAD, prompts)):
        ask(r)
    sign_tables(signs, False)
    level_masks(masks)
    for copy in smalls:
        copy.wait()
    head_factors(first, dt_ref, rate_ref, skip_ref, len_ref, signs, w_in, w_out, w_skip, None)
    own_attention(send_ref, fresh_ref, fresh_held, own_ref, ownsum_ref)
    own_mixer(rates_ref, skips_ref, sx_ref, sb_ref, sc_ref, sdt_ref, c_rows, x_rows, fade_ref, local_ref)
    outs = fetches(
        [(own_ref, own_any), (ownsum_ref, ownsum_any), (fade_ref, fade_any), (local_ref, local_any)], sems
    )

    def some(n, _):
        begin = EARLY + n * AHEAD

        @pl.when(begin + AHEAD < prompts)
        def _():
            for r in range(AHEAD):
                ask(begin + AHEAD + r)

        for r in range(AHEAD):
            x_copy(begin + r).wait()
            b_copy(begin + r).wait()
            c_copy(begin + r).wait()
        for r in range(AHEAD):
            prompt_result(begin + r, x_held, b_held, c_held, w_in, w_out, w_skip, masks, out_held)
        for r in range(AHEAD):
            out_copy(begin + r).start()
        return 0

    lax.fori_loop(0, (prompts - EARLY) // AHEAD, some, 0)
    for copy in outs:
        copy.wait()
    for r in range(EARLY, prompts):
        out_copy(r).wait()


def own_attention(send_ref, fresh_ref, fresh_held, own_ref, ownsum_ref):
    steps, rows = fresh_ref.shape[0], fresh_ref.shape[1]
    owners = send_ref.shape[0]
    order = exchange_order(owners)
    ways = owners // KVH
    stack_rows(fresh_ref, fresh_held)
    count = HALF // HD * 2 * SUB
    pair = iota((count, SUB), 0) % SUB
    key = iota((count, SUB), 1)
    seen = (key % rows == pair % rows) & (key <= pair) & (key < rows * steps)
    seen = seen | ((pair >= rows * steps) & (key == 0))
    lane = iota((count, LANES), 1)
    sums = jnp.zeros((count, LANES), f32)
    for v in range(KVH):
        halves = [send_ref[order.index(v * ways + n), :, :HALF].astype(f32) for n in range(2)]
        parts = [half[:, g * HD : (g + 1) * HD] for g in range(HALF // HD) for half in halves]
        query = jnp.concatenate(parts, axis=0).astype(bf16)
        keys = fresh_held[:, v * HD : (v + 1) * HD].astype(bf16)
        values = fresh_held[:, (KVH + v) * HD : (KVH + v + 1) * HD].astype(bf16)
        scores = jnp.where(seen, dot_nt(query, keys) * SCORE, NONE)
        highest = jnp.max(scores, axis=1, keepdims=True)
        weight = jnp.exp2(scores - highest)
        total = jnp.sum(weight, axis=1, keepdims=True)
        weight = (weight / total).astype(bf16)
        own_ref[v] = jnp.dot(weight, values, preferred_element_type=f32).astype(bf16)
        sums = jnp.where(lane == v, highest + jnp.log2(total), sums)
    ownsum_ref[...] = sums


def own_mixer(rates_ref, skips_ref, sx_ref, sb_ref, sc_ref, sdt_ref, c_rows, x_rows, fade_ref, local_ref):
    steps, rows, heads = sdt_ref.shape
    stack_rows(sc_ref, c_rows)
    for u in range(steps):
        given = sx_ref[u].astype(f32)
        for k in range(SUB // rows):
            x_rows[u, k * rows : (k + 1) * rows, :] = given
    pair = iota((SUB, heads), 0)
    step = pair // rows
    live = pair < rows * steps
    head = iota((SUB, heads), 1)

    def spread_rows(ref, u):
        given = ref[u].astype(f32)
        return jnp.concatenate([given] * (SUB // rows), axis=0)

    rates = jnp.broadcast_to(rates_ref[...], (SUB, heads)) * LOG2E
    skips = jnp.broadcast_to(skips_ref[...], (SUB, heads))
    moved = [spread_rows(sdt_ref, u) for u in range(steps)]
    kept = [jnp.where(u <= step, moved[u], 0.0) for u in range(steps)]
    parts = [jnp.where(live, jnp.exp2(-(rates * sum(kept))), 0.0)]
    for u in range(steps):
        products = c_rows[...] * spread_rows(sb_ref, u)
        inner = jnp.zeros((SUB, heads), f32)
        for e in range(products.shape[1] // NS):
            found = jnp.sum(products[:, e * NS : (e + 1) * NS], axis=1, keepdims=True)
            inner = jnp.where(head // HPG == e, found, inner)
        gap = jnp.zeros((SUB, heads), f32)
        for t in range(u + 1, steps):
            gap = gap + kept[t]
        weight = jnp.where(u <= step, jnp.exp2(-(rates * gap)) * moved[u] * inner, 0.0)
        weight = weight + jnp.where(u == step, skips, 0.0)
        parts.append(jnp.where(live, weight, 0.0))
    stacked = jnp.concatenate(parts, axis=0)
    high = stacked.astype(bf16)
    low = (stacked - high.astype(f32)).astype(bf16)
    both = jnp.concatenate([high.astype(f32), low.astype(f32)], axis=0)
    count = stacked.shape[0]
    chunk = SUB * HP
    widen = jnp.where(iota((heads, chunk), 0) % SUB == iota((heads, chunk), 1) // HP, 1.0, 0.0).astype(bf16)
    lane = iota(both.shape, 1)
    for d in range(heads // SUB):
        picked = jnp.where(lane // SUB == d, both, 0.0).astype(bf16)
        wide = jnp.dot(picked, widen, preferred_element_type=f32)
        wide = wide[:count] + wide[count:]
        columns = slice(d * chunk, (d + 1) * chunk)
        fade_ref[:, columns] = wide[:SUB]
        value = jnp.zeros((SUB, chunk), f32)
        for u in range(steps):
            value = value + wide[(u + 1) * SUB : (u + 2) * SUB] * x_rows[u, :, columns]
        local_ref[:, columns] = value


def merge_kernel(
    width,
    back_any,
    own_any,
    ownsum_any,
    fade_any,
    local_any,
    mixer_any,
    attention_any,
    back_ref,
    own_ref,
    ownsum_ref,
    fade_ref,
    local_ref,
    mixed,
    attended,
    mixer_ref,
    attention_ref,
    sems,
):
    copies = fetches([(back_any, back_ref), (fade_any, fade_ref), (local_any, local_ref)], sems)
    copies += fetches([(own_any, own_ref), (ownsum_any, ownsum_ref)], sems, len(copies))
    for copy in copies:
        copy.wait()
    owners = back_ref.shape[0]
    ways = owners // KVH
    order = exchange_order(owners)
    steps, rows = mixer_ref.shape[0], mixer_ref.shape[1]
    for d in range(0, owners, 2):
        block = jnp.stack([back_ref[order.index(d + n)].astype(f32) for n in range(2)])
        ending = lift(block, spare(back_ref.shape[2] // LANES, 1))
        if back_ref.shape[2] > HALF:
            ending = jnp.concatenate([block[..., HALF:], ending], axis=-1)
        found = ending[..., :width]
        found = jnp.concatenate([found[0], found[1]], axis=-1)
        columns = slice(d * width, (d + 2) * width)
        mixed[:, columns] = found * fade_ref[:, columns] + local_ref[:, columns]
    for k in range(steps):
        mixer_ref[k] = mixed[k * rows : (k + 1) * rows, :].astype(bf16)
    lane = iota((2, SUB, LANES), 2)
    mine = (lane // 16 == iota((2, SUB, LANES), 1)) & (lane % 16 < 12)
    for v in range(KVH):
        blocks, pieces = [], []
        for d in range(v * ways, (v + 1) * ways, 2):
            block = jnp.stack([back_ref[order.index(d + n), :, :HALF].astype(f32) for n in range(2)])
            packed = block[:, PAIRS : PAIRS + 1, :LANES]
            blocks.append(block.reshape(2 * SUB, HALF))
            pieces.append(jnp.where(mine, jnp.broadcast_to(packed, (2, SUB, LANES)), 0.0))
        for g in range(HALF // HD):
            part = slice(g * 2 * SUB, (g + 1) * 2 * SUB)
            own_sum = jnp.broadcast_to(ownsum_ref[part, v : v + 1], (2 * SUB, HD))
            wide = []
            for piece in pieces:
                one = jnp.sum(jnp.where(lane % 4 == g, piece, 0.0), axis=-1, keepdims=True)
                wide.append(jnp.broadcast_to(one, (2, SUB, HD)).reshape(2 * SUB, HD))
            highest = functools.reduce(jnp.maximum, wide, own_sum)
            weight = jnp.exp2(own_sum - highest)
            total = weight
            value = weight * own_ref[v, part, :].astype(f32)
            for one, block in zip(wide, blocks):
                weight = jnp.exp2(one - highest)
                total = total + weight
                value = value + weight * block[:, g * HD : (g + 1) * HD]
            value = value / total
            start = v * 2 * HALF + g * HD
            attended[:, start : start + HD] = value[:SUB]
            attended[:, start + HALF : start + HALF + HD] = value[SUB:]
    for k in range(steps):
        attention_ref[k] = attended[k * rows : (k + 1) * rows, :].astype(bf16)
    for copy in fetches([(mixer_ref, mixer_any), (attention_ref, attention_any)], sems):
        copy.wait()


def call(kernel, out_shape, in_spaces, out_spaces, scratch, cost, aliases=None):
    def spec(space):
        return pl.BlockSpec(memory_space=space)

    return pl.pallas_call(
        kernel,
        out_shape=out_shape,
        in_specs=[spec(space) for space in in_spaces],
        out_specs=jax.tree.map(spec, out_spaces),
        scratch_shapes=scratch,
        input_output_aliases=aliases or {},
        compiler_params=pltpu.CompilerParams(vmem_limit_bytes=VMEM_LIMIT),
        cost_estimate=pl.CostEstimate(flops=cost[0], bytes_accessed=cost[1], transcendentals=0),
    )


def on_device(
    prompt_x,
    prompt_b,
    prompt_c,
    prompt_dt,
    decay_rate,
    skip_gain,
    lengths,
    owner_list,
    page_table,
    cache_pages,
    row_slot,
    step_x,
    step_b,
    step_c,
    step_dt,
    queries,
    fresh_cache,
):
    owners = lax.axis_size("heads")
    ways = owners // KVH
    group, prompts, length = prompt_dt.shape
    width = prompt_x.shape[1]
    keys = cache_pages.shape[0] * PAGE
    span = 2 * keys // prompts
    steps = step_x.shape[1]
    all_rows = owners * SUB
    shape = jax.ShapeDtypeStruct
    smem, vmem, hbm = pltpu.SMEM, pltpu.VMEM, pltpu.HBM
    sem = pltpu.SemaphoreType.DMA((prompts,))
    levels = len(LEVELS)
    step_x, step_b, step_c, step_dt, queries, fresh_cache = (
        jnp.swapaxes(one, 0, 1) for one in (step_x, step_b, step_c, step_dt, queries, fresh_cache)
    )
    owner_list = owner_list.T

    def like(space, array):
        return space(array.shape, array.dtype)

    def sems(count):
        return pltpu.SemaphoreType.DMA((count,))

    other_pages = lax.ppermute(cache_pages, "heads", [(d, d + 1 - 2 * (d % 2)) for d in range(owners)])
    send = call(
        functools.partial(pack_kernel, group, ways),
        shape((all_rows, HALF + LANES), bf16),
        [hbm, hbm],
        vmem,
        [
            like(vmem, queries),
            like(vmem, step_c),
            vmem((SUB, queries.shape[2]), f32),
            vmem((SUB, step_c.shape[2]), f32),
            vmem((step_c.shape[2] // NS, SUB, HALF + LANES), f32),
            sems(2),
        ],
        (0, 1 << 19),
    )(queries, step_c)
    order = [exchange_order(owners)]
    recv = lax.all_to_all(
        send, "heads", split_axis=0, concat_axis=0, tiled=True, axis_index_groups=order
    )

    block = [
        vmem((prompts, width, length), bf16),
        vmem((prompts, length, NS), bf16),
        vmem((prompts, length, NS), bf16),
        vmem((prompts, width, length), bf16),
        vmem((levels, prompts, group, length), f32),
        vmem((levels, prompts, group, length), f32),
        vmem((prompts, group, length), f32),
    ]
    tables = [vmem((levels, length, length), bf16), vmem((levels + 1, length, length), bf16)]
    work = 2 * width * length * NS
    states, sorted_keys, sorted_values, codes, early_out = call(
        state_kernel,
        (
            shape((prompts, width, NS), bf16),
            shape((prompts // 2, span, 2 * HD), bf16),
            shape((prompts // 2, span, 2 * HD), bf16),
            shape((all_rows, LANES), jnp.int32),
            shape(prompt_x.shape, bf16),
        ),
        [hbm] * 12,
        (hbm,) * 5,
        block
        + tables
        + [vmem((prompts, group, length), f32), vmem((prompts, width, NS), bf16)]
        + [vmem((2,) + cache_pages.shape, bf16)]
        + [vmem((prompts // 2, span, 2 * HD), bf16)] * 2
        + [vmem((all_rows, LANES), jnp.int32)]
        + [like(smem, one) for one in (decay_rate, skip_gain, lengths, owner_list, page_table, row_slot)]
        + [like(vmem, prompt_dt), sem, sem, sem, sem, sem, sems(9)],
        (work * (prompts + 5 * EARLY), 6 << 20),
    )(
        decay_rate,
        skip_gain,
        lengths,
        owner_list,
        page_table,
        row_slot,
        prompt_dt,
        prompt_x,
        prompt_b,
        prompt_c,
        cache_pages,
        other_pages,
    )

    back = call(
        serve_kernel,
        shape((all_rows, HALF + max(LANES, width) - LANES), bf16),
        [hbm] * 5,
        vmem,
        [like(vmem, one) for one in (recv, sorted_keys, sorted_values, codes, states)]
        + [vmem((prompts // 2, HALF // HD * all_rows, 2 * HD), bf16), sem, sems(4)],
        (8 * all_rows * keys * HD, 4 << 20),
    )(recv, sorted_keys, sorted_values, codes, states)
    returned = lax.all_to_all(
        back, "heads", split_axis=0, concat_axis=0, tiled=True, axis_index_groups=order
    ).reshape(owners, SUB, back.shape[1])

    count = HALF // HD * 2 * SUB
    channels = step_x.shape[2]
    rates, skips = decay_rate.reshape(1, -1), skip_gain.reshape(1, -1)
    prompt_out, own, own_sum, fade, local = call(
        prompt_kernel,
        (
            shape(prompt_x.shape, bf16),
            shape((KVH, count, HD), bf16),
            shape((count, LANES), f32),
            shape((SUB, channels), f32),
            shape((SUB, channels), f32),
        ),
        [hbm] * 17,
        (hbm,) * 5,
        block
        + tables
        + [
            vmem((KVH, count, HD), bf16),
            vmem((count, LANES), f32),
            vmem((SUB, channels), f32),
            vmem((SUB, channels), f32),
            vmem((SUB, fresh_cache.shape[2]), f32),
            vmem((SUB, step_c.shape[2]), f32),
            vmem((steps, SUB, channels), f32),
            like(smem, decay_rate),
            like(smem, skip_gain),
            like(smem, lengths),
            like(vmem, prompt_dt),
            like(vmem, rates),
            like(vmem, skips),
            vmem((owners, SUB, HALF + LANES), bf16),
            like(vmem, fresh_cache),
            like(vmem, step_x),
            like(vmem, step_b),
            like(vmem, step_c),
            like(vmem, step_dt),
            sem,
            sem,
            sem,
            sem,
            sems(12),
        ],
        (work * 5 * (prompts - EARLY), 8 << 20),
        {16: 0},
    )(
        decay_rate,
        skip_gain,
        lengths,
        prompt_dt,
        rates,
        skips,
        send.reshape(owners, SUB, HALF + LANES),
        fresh_cache,
        step_x,
        step_b,
        step_c,
        step_dt,
        prompt_x,
        prompt_b,
        prompt_c,
        back,
        early_out,
    )

    mixer_out, attention_out = call(
        functools.partial(merge_kernel, width),
        (shape(step_x.shape, bf16), shape(queries.shape, bf16)),
        [hbm] * 5,
        (hbm, hbm),
        [like(vmem, one) for one in (returned, own, own_sum, fade, local)]
        + [vmem((SUB, channels), f32), vmem((SUB, queries.shape[2]), f32)]
        + [like(vmem, step_x), like(vmem, queries), sems(5)],
        (0, 2 << 20),
    )(returned, own, own_sum, fade, local)
    return (prompt_out, jnp.swapaxes(mixer_out, 0, 1), jnp.swapaxes(attention_out, 0, 1))


def solution(mesh):
    in_specs = (
        P("groups", "heads", None),
        P("groups", None, None),
        P("groups", None, None),
        P("heads", "groups", None),
        P(),
        P(),
        P("groups"),
        P("groups", None),
        P("groups", None),
        P(("groups", "heads"), None, None),
        P("groups"),
        P(("groups", "heads"), None, None),
        P(("groups", "heads"), None, None),
        P(("groups", "heads"), None, None),
        P(("groups", "heads"), None, None),
        P(("groups", "heads"), None, None),
        P(("groups", "heads"), None, None),
    )
    out_specs = (
        P("groups", "heads", None),
        P(("groups", "heads"), None, None),
        P(("groups", "heads"), None, None),
    )
    return jax.shard_map(
        on_device, mesh=mesh, in_specs=in_specs, out_specs=out_specs, check_vma=False
    )
```

```python
import functools
import math

import jax
import jax.numpy as jnp
from jax import lax
from jax.experimental import pallas as pl
from jax.experimental.pallas import tpu as pltpu
from jax.sharding import PartitionSpec as P

NS = 256
HP = 64
HPG = 32
KVH = 8
HD = 128
PAGE = 16
PAGES = 16
LANES = 128
ROWS16 = 16
SUB = 8
HALF = 512
LEVELS = (128, 64, 32, 16)
LOG2E = math.log2(math.e)
SCORE = LOG2E / math.sqrt(HD)
NONE = -1e30
FLOOR = -1e29
PAIRS = 6
LENGTH_BITS = 10
AHEAD = 2
EARLY = 2
VMEM_LIMIT = 64 * 1024 * 1024

f32 = jnp.float32
bf16 = jnp.bfloat16


def iota(shape, dim):
    return lax.broadcasted_iota(jnp.int32, shape, dim)


def exchange_order(owners):
    first = owners * 5 // 8
    return [first] + [d for d in range(owners) if d != first]


def dot_nt(left, right):
    return lax.dot_general(left, right, (((1,), (1,)), ((), ())), preferred_element_type=f32)


def stack_rows(source, held):
    steps, rows = source.shape[0], source.shape[1]
    held[...] = jnp.zeros_like(held)
    for k in range(steps):
        held[k * rows : (k + 1) * rows, :] = source[k].astype(f32)


def spare(blocks, taken):
    return [(row, b) for row in range(PAIRS, SUB) for b in range(blocks)][taken : taken + PAIRS]


def lift(value, slots):
    row = iota(value.shape[:2] + (LANES,), 1)
    found = jnp.zeros(row.shape, f32)
    for pair, (at, b) in enumerate(slots):
        one = value[:, at : at + 1, b * LANES : (b + 1) * LANES]
        found = jnp.where(row == pair, jnp.broadcast_to(one, row.shape), found)
    return found


def fetches(pairs, sems, first=0):
    copies = [pltpu.make_async_copy(src, dst, sems.at[first + n]) for n, (src, dst) in enumerate(pairs)]
    for copy in copies:
        copy.start()
    return copies


def pack_kernel(group, ways, q_any, c_any, out_ref, q_ref, c_ref, q_held, c_held, rest, sems):
    owners = out_ref.shape[0] // SUB
    for copy in fetches([(q_any, q_ref), (c_any, c_ref)], sems):
        copy.wait()
    stack_rows(q_ref, q_held)
    stack_rows(c_ref, c_held)
    span = 2 * HALF
    slots = spare(HALF // LANES + 1, 0)
    rest[...] = jnp.zeros_like(rest)
    for e in range(c_ref.shape[2] // NS):
        rest[e, :PAIRS, HALF:] = c_held[:PAIRS, e * NS : e * NS + LANES]
        for pair, (row, b) in enumerate(slots):
            rest[e, row : row + 1, b * LANES : (b + 1) * LANES] = c_held[
                pair : pair + 1, e * NS + LANES : (e + 1) * NS
            ]
    real = iota((SUB, HALF), 0) < PAIRS
    order = exchange_order(owners)
    for rank in range(0, owners, 2):
        blocks, ends = [], []
        for d in order[rank : rank + 2]:
            begin, e = d // ways * span + d % 2 * HALF, (d * group) // HPG
            blocks.append(jnp.where(real, q_held[:, begin : begin + HALF], rest[e, :, :HALF]))
            ends.append(rest[e, :, HALF:])
        place = slice(rank * SUB, (rank + 2) * SUB)
        out_ref[place, :HALF] = jnp.concatenate(blocks, axis=0).astype(bf16)
        out_ref[place, HALF:] = jnp.concatenate(ends, axis=0).astype(bf16)


def sign_tables(signs, tail):
    length = signs.shape[-1]
    j = iota((length, length), 0)
    i = iota((length, length), 1)
    for l, n in enumerate(LEVELS):
        middle = (i // (2 * n)) * (2 * n) + (n - 1)
        signs[l] = (jnp.where(j <= i, 1.0, 0.0) - jnp.where(j <= middle, 1.0, 0.0)).astype(bf16)
    if tail:
        signs[len(LEVELS)] = jnp.where(j > i, 1.0, 0.0).astype(bf16)


def head_factors(first, some, dt_ref, rate_ref, skip_ref, len_ref, signs, w_in, w_out, w_skip, w_tail):
    group, prompts, length = dt_ref.shape
    row = iota((prompts, length), 0)
    lens = jnp.zeros((prompts, length), jnp.int32)
    for r in range(prompts):
        lens = jnp.where(row == r, len_ref[r], lens)
    valid = iota((prompts, length), 1) < lens
    moved = [jnp.where(valid, dt_ref[h].astype(f32), 0.0) for h in range(group)]
    every = jnp.concatenate(moved, axis=0).astype(bf16)
    rates = [rate_ref[first + h] * LOG2E for h in range(group)]
    if w_tail is not None:
        total = jnp.dot(every, signs[len(LEVELS)], preferred_element_type=f32)
        for h in range(group):
            part = total[h * prompts : (h + 1) * prompts]
            w_tail[:, h, :] = jnp.exp2(-(rates[h] * part)) * moved[h]
    for h in range(group):
        w_skip[:, h, :] = jnp.where(valid, skip_ref[first + h], 0.0)
    for l, n in enumerate(LEVELS):
        total = jnp.dot(every, signs[l], preferred_element_type=f32)
        for h in range(group):
            gap = rates[h] * total[h * prompts : (h + 1) * prompts]
            if n == LEVELS[-1]:
                up, down = jnp.exp2(gap), jnp.exp2(-gap)
            else:
                up, down = jnp.exp2(jnp.minimum(gap, 0.0)), jnp.exp2(-jnp.maximum(gap, 0.0))
            enter = up * moved[h]
            for r in some:
                w_in[l, r, h] = jnp.broadcast_to(enter[r : r + 1], w_in.shape[3:]).astype(bf16)
            w_out[l, :, h, :] = jnp.where(valid, down, 0.0)


def level_masks(masks):
    length = masks.shape[-1]
    j = iota((length, length), 0)
    i = iota((length, length), 1)
    for l, n in enumerate(LEVELS):
        same = (j // (2 * n)) == (i // (2 * n))
        if n == LEVELS[-1]:
            keep = same & (j <= i)
        else:
            keep = same & ((j % (2 * n)) < n) & ((i % (2 * n)) >= n)
        masks[l] = jnp.where(keep, 1.0, 0.0).astype(bf16)


def prompt_result(r, x_held, b_held, c_held, w_in, w_out, w_skip, masks, out_held):
    width, length = x_held.shape[1], x_held.shape[2]
    group = width // HP
    half = length // 2
    given = x_held[r]
    inputs = given.astype(f32).reshape(group, HP, length)
    given = given.reshape(group, HP // ROWS16, ROWS16, length)
    scores = dot_nt(b_held[r], c_held[r]).astype(bf16)
    total = inputs * w_skip[r][:, None, :]
    left, right = total[..., :half], total[..., half:]
    for l, n in enumerate(LEVELS):
        if 2 * n == length:
            scaled = (given[..., :half] * w_in[l, r][:, None, :, :half]).reshape(width, half)
            added = jnp.dot(scaled, scores[:half, half:], preferred_element_type=f32)
            right = right + added.reshape(group, HP, half) * w_out[l, r][:, None, half:]
        else:
            scaled = (given * w_in[l, r][:, None]).reshape(width, length)
            added = jnp.dot(scaled, scores * masks[l], preferred_element_type=f32)
            added = added.reshape(group, HP, length) * w_out[l, r][:, None, :]
            left = left + added[..., :half]
            right = right + added[..., half:]
    out_held[r] = jnp.concatenate([left, right], axis=-1).reshape(width, length).astype(bf16)


def state_kernel(
    rate_any,
    skip_any,
    len_any,
    owner_any,
    table_any,
    slot_any,
    dt_any,
    x_any,
    b_any,
    c_any,
    pages_any,
    other_any,
    state_any,
    key_any,
    value_any,
    code_any,
    out_any,
    x_held,
    b_held,
    c_held,
    out_held,
    w_in,
    w_out,
    w_skip,
    masks,
    signs,
    w_tail,
    state_held,
    pages_held,
    key_held,
    value_held,
    code_held,
    rate_ref,
    skip_ref,
    len_ref,
    owner_ref,
    table_ref,
    slot_ref,
    dt_ref,
    x_sem,
    b_sem,
    c_sem,
    out_sem,
    state_sem,
    sems,
):
    group, prompts, length = dt_ref.shape
    smalls = fetches(
        [
            (dt_any, dt_ref),
            (rate_any, rate_ref),
            (skip_any, skip_ref),
            (len_any, len_ref),
            (owner_any, owner_ref),
            (table_any, table_ref),
            (slot_any, slot_ref),
        ],
        sems,
    )
    me = lax.axis_index("heads")
    core = lax.rem(me, 2)
    first = me * group
    column = pl.multiple_of((first // HPG) * NS, NS)

    def x_copy(r):
        return pltpu.make_async_copy(x_any.at[r], x_held.at[r], x_sem.at[r])

    def b_copy(r):
        return pltpu.make_async_copy(b_any.at[r, :, pl.ds(column, NS)], b_held.at[r], b_sem.at[r])

    def c_copy(r):
        return pltpu.make_async_copy(c_any.at[r, :, pl.ds(column, NS)], c_held.at[r], c_sem.at[r])

    def out_copy(r):
        return pltpu.make_async_copy(out_held.at[r], out_any.at[r], out_sem.at[r])

    def state_copy(r):
        return pltpu.make_async_copy(state_held.at[r], state_any.at[r], state_sem.at[r])

    def ask(r):
        x_copy(r).start()
        b_copy(r).start()

    pages = fetches([(pages_any, pages_held.at[core]), (other_any, pages_held.at[1 - core])], sems, len(smalls))
    for r in range(prompts):
        ask(r)
    for r in range(EARLY):
        c_copy(r).start()
    sign_tables(signs, True)
    level_masks(masks)
    for copy in smalls:
        copy.wait()
    head_factors(
        first, range(EARLY), dt_ref, rate_ref, skip_ref, len_ref, signs, w_in, w_out, w_skip, w_tail
    )

    width = x_held.shape[1]
    for begin in range(0, prompts, prompts // 2):
        some = range(begin, begin + prompts // 2)
        for r in some:
            x_copy(r).wait()
            b_copy(r).wait()
        for r in some:
            inputs = x_held[r].astype(f32).reshape(group, HP, length)
            scaled = (inputs * w_tail[r][:, None, :]).astype(bf16).reshape(width, length)
            state_held[r] = jnp.dot(scaled, b_held[r], preferred_element_type=f32).astype(bf16)
        for r in some:
            state_copy(r).start()
    spread = table_ref.shape[1] // owner_ref.shape[1]
    for copy in pages:
        copy.wait()
    for n in range(2):
        for r in range(prompts):
            for page in range(spread):
                holder = me - core + n
                row = table_ref[r, holder * spread + page] - holder * (prompts * spread)
                block = pages_held[n, row]
                place = pl.ds((n * spread + page) * PAGE, PAGE)
                columns = pl.ds(r % 2 * HD, HD)
                key_held[r // 2, place, columns] = block[:, :HD]
                value_held[r // 2, place, columns] = block[:, HD:]

    owners = owner_ref.shape[1]
    rows_dev = slot_ref.shape[0] // owners
    inner = iota((2 * SUB, LANES), 0)

    order = exchange_order(owners)
    for rank in range(0, owners, 2):
        block = jnp.zeros((2 * SUB, LANES), jnp.int32)
        for n in range(2):
            s = order[rank + n]
            for i in range(rows_dev):
                target = owner_ref[slot_ref[s * rows_dev + i], s]
                code = target * (1 << LENGTH_BITS) + len_ref[target]
                block = jnp.where((inner // SUB == n) & (inner % rows_dev == i), code, block)
        code_held[rank * SUB : (rank + 2) * SUB, :] = block
    marks = fetches([(key_held, key_any), (value_held, value_any), (code_held, code_any)], sems)

    for r in range(EARLY):
        c_copy(r).wait()
    for r in range(EARLY):
        prompt_result(r, x_held, b_held, c_held, w_in, w_out, w_skip, masks, out_held)
    for r in range(EARLY):
        out_copy(r).start()
    for copy in marks:
        copy.wait()
    for r in range(prompts):
        state_copy(r).wait()
    for r in range(EARLY):
        out_copy(r).wait()


def serve_kernel(
    recv_any,
    key_any,
    value_any,
    code_any,
    state_any,
    out_ref,
    recv_ref,
    key_ref,
    value_ref,
    code_ref,
    state_ref,
    query_ref,
    state_sem,
    sems,
):
    rows = recv_ref.shape[0]
    prompts, width = state_ref.shape[0], state_ref.shape[1]
    copies = fetches(
        [(recv_any, recv_ref), (code_any, code_ref), (key_any, key_ref), (value_any, value_ref)], sems
    )
    states = fetches([(state_any.at[r], state_ref.at[r]) for r in range(prompts)], state_sem)
    heads = HALF // HD
    keys = key_ref.shape[1]
    chips = keys // PAGE
    begin = lax.rem(lax.axis_index("heads") // 2 * chips, PAGES) * PAGE
    copies[0].wait()
    copies[1].wait()
    code = code_ref[...]
    target = code >> LENGTH_BITS
    lengths = code & ((1 << LENGTH_BITS) - 1)
    for r in range(prompts):
        for g in range(heads):
            query = recv_ref[:, g * HD : (g + 1) * HD].astype(f32)
            query_ref[r // 2, g * rows : (g + 1) * rows, r % 2 * HD : (r % 2 + 1) * HD] = jnp.where(
                target == r, query, 0.0
            ).astype(bf16)
    copies[2].wait()
    scores = jnp.zeros((heads * rows, keys), f32)
    for pair in range(prompts // 2):
        scores = scores + dot_nt(query_ref[pair], key_ref[pair])
    copies[3].wait()
    for copy in states:
        copy.wait()
    seen = jnp.concatenate([lengths[:, :1]] * heads, axis=0) > iota((heads * rows, keys), 1) + begin
    scores = jnp.where(seen, scores * SCORE, NONE)
    highest = jnp.maximum(jnp.max(scores, axis=1, keepdims=True), FLOOR)
    weight = jnp.exp2(scores - highest)
    total = jnp.sum(weight, axis=1, keepdims=True)
    some = total > 0.0
    safe = jnp.where(some, total, 1.0)
    result = jnp.where(some, highest + jnp.log2(safe), NONE)
    weight = weight.astype(bf16)
    targets = jnp.concatenate([target] * heads, axis=0)
    value = jnp.zeros((heads * rows, HD), f32)
    for pair in range(prompts // 2):
        both = jnp.dot(weight, value_ref[pair], preferred_element_type=f32)
        for n in range(2):
            value = jnp.where(targets == 2 * pair + n, both[:, n * HD : (n + 1) * HD], value)
    value = value / safe
    lane = iota((rows, LANES), 1)
    sums = jnp.zeros((rows, LANES), f32)
    for g in range(heads):
        sums = jnp.where(lane % 4 == g, result[g * rows : (g + 1) * rows], sums)
    high = sums.astype(bf16).astype(f32)
    rest = sums - high
    middle = rest.astype(bf16).astype(f32)
    piece = lane % 16 // 4
    pieces = jnp.where(piece == 0, high, jnp.where(piece == 1, middle, rest - middle))
    pair = iota((rows, LANES), 0) % SUB
    pieces = jnp.where((lane // 16 == pair) & (piece < 3), pieces, 0.0)
    packed = jnp.sum(pieces.reshape(rows // SUB, SUB, LANES), axis=1, keepdims=True)

    given = recv_ref[...].astype(f32).reshape(rows // SUB, SUB, recv_ref.shape[1])
    ending = lift(given, spare(heads + 1, 0))
    readout = jnp.concatenate([given[..., HALF:], ending], axis=-1).reshape(rows, NS)
    target = jnp.concatenate([target, target], axis=-1)
    found = jnp.zeros((rows, width), f32)
    for r in range(prompts):
        picked = jnp.where(target == r, readout, 0.0).astype(bf16)
        found = found + dot_nt(picked, state_ref[r])
    if width < LANES:
        found = jnp.concatenate([found, jnp.zeros((rows, LANES - width), f32)], axis=-1)
    blocks = [value[g * rows : (g + 1) * rows] for g in range(heads)]
    blocks += [found[:, b : b + LANES] for b in range(0, found.shape[1], LANES)]
    blocks = [one.reshape(rows // SUB, SUB, LANES) for one in blocks]
    row = iota((rows // SUB, SUB, LANES), 1)
    last = blocks.pop()
    blocks[0] = jnp.where(row == PAIRS, jnp.broadcast_to(packed, row.shape), blocks[0])
    for n, (at, b) in enumerate(spare(len(blocks), 1)):
        one = jnp.broadcast_to(last[:, n : n + 1, :], row.shape)
        blocks[b] = jnp.where(row == at, one, blocks[b])
    for b, one in enumerate(blocks):
        out_ref[:, b * LANES : (b + 1) * LANES] = one.reshape(rows, LANES).astype(bf16)


def prompt_kernel(
    rate_any,
    skip_any,
    len_any,
    dt_any,
    rates_any,
    skips_any,
    send_any,
    fresh_any,
    sx_any,
    sb_any,
    sc_any,
    sdt_any,
    x_any,
    b_any,
    c_any,
    after_any,
    early_any,
    out_any,
    own_any,
    ownsum_any,
    fade_any,
    local_any,
    x_held,
    b_held,
    c_held,
    out_held,
    w_in,
    w_out,
    w_skip,
    masks,
    signs,
    own_ref,
    ownsum_ref,
    fade_ref,
    local_ref,
    fresh_held,
    c_rows,
    x_rows,
    rate_ref,
    skip_ref,
    len_ref,
    dt_ref,
    rates_ref,
    skips_ref,
    send_ref,
    fresh_ref,
    sx_ref,
    sb_ref,
    sc_ref,
    sdt_ref,
    x_sem,
    b_sem,
    c_sem,
    out_sem,
    sems,
):
    group, prompts, length = dt_ref.shape
    smalls = fetches(
        [
            (dt_any, dt_ref),
            (rate_any, rate_ref),
            (skip_any, skip_ref),
            (len_any, len_ref),
            (rates_any, rates_ref),
            (skips_any, skips_ref),
            (send_any, send_ref),
            (fresh_any, fresh_ref),
            (sx_any, sx_ref),
            (sb_any, sb_ref),
            (sc_any, sc_ref),
            (sdt_any, sdt_ref),
        ],
        sems,
    )
    me = lax.axis_index("heads")
    first = me * group
    column = pl.multiple_of((first // HPG) * NS, NS)

    def x_copy(r):
        return pltpu.make_async_copy(x_any.at[r], x_held.at[r], x_sem.at[r])

    def b_copy(r):
        return pltpu.make_async_copy(b_any.at[r, :, pl.ds(column, NS)], b_held.at[r], b_sem.at[r])

    def c_copy(r):
        return pltpu.make_async_copy(c_any.at[r, :, pl.ds(column, NS)], c_held.at[r], c_sem.at[r])

    def out_copy(r):
        return pltpu.make_async_copy(out_held.at[r], out_any.at[r], out_sem.at[r])

    def ask(r):
        x_copy(r).start()
        b_copy(r).start()
        c_copy(r).start()

    for r in range(EARLY, min(EARLY + AHEAD, prompts)):
        ask(r)
    sign_tables(signs, False)
    level_masks(masks)
    for copy in smalls:
        copy.wait()
    head_factors(
        first, range(EARLY, prompts), dt_ref, rate_ref, skip_ref, len_ref, signs, w_in, w_out, w_skip, None
    )
    own_attention(send_ref, fresh_ref, fresh_held, own_ref, ownsum_ref)
    own_mixer(rates_ref, skips_ref, sx_ref, sb_ref, sc_ref, sdt_ref, c_rows, x_rows, fade_ref, local_ref)
    outs = fetches(
        [(own_ref, own_any), (ownsum_ref, ownsum_any), (fade_ref, fade_any), (local_ref, local_any)], sems
    )

    def some(n, _):
        begin = EARLY + n * AHEAD

        @pl.when(begin + AHEAD < prompts)
        def _():
            for r in range(AHEAD):
                ask(begin + AHEAD + r)

        for r in range(AHEAD):
            x_copy(begin + r).wait()
            b_copy(begin + r).wait()
            c_copy(begin + r).wait()
        for r in range(AHEAD):
            prompt_result(begin + r, x_held, b_held, c_held, w_in, w_out, w_skip, masks, out_held)
        for r in range(AHEAD):
            out_copy(begin + r).start()
        return 0

    lax.fori_loop(0, (prompts - EARLY) // AHEAD, some, 0)
    for copy in outs:
        copy.wait()
    for r in range(EARLY, prompts):
        out_copy(r).wait()


def own_attention(send_ref, fresh_ref, fresh_held, own_ref, ownsum_ref):
    steps, rows = fresh_ref.shape[0], fresh_ref.shape[1]
    owners = send_ref.shape[0]
    order = exchange_order(owners)
    ways = owners // KVH
    stack_rows(fresh_ref, fresh_held)
    count = HALF // HD * 2 * SUB
    pair = iota((count, SUB), 0) % SUB
    key = iota((count, SUB), 1)
    seen = (key % rows == pair % rows) & (key <= pair) & (key < rows * steps)
    seen = seen | ((pair >= rows * steps) & (key == 0))
    lane = iota((count, LANES), 1)
    sums = jnp.zeros((count, LANES), f32)
    for v in range(KVH):
        halves = [send_ref[order.index(v * ways + n), :, :HALF].astype(f32) for n in range(2)]
        parts = [half[:, g * HD : (g + 1) * HD] for g in range(HALF // HD) for half in halves]
        query = jnp.concatenate(parts, axis=0).astype(bf16)
        keys = fresh_held[:, v * HD : (v + 1) * HD].astype(bf16)
        values = fresh_held[:, (KVH + v) * HD : (KVH + v + 1) * HD].astype(bf16)
        scores = jnp.where(seen, dot_nt(query, keys) * SCORE, NONE)
        highest = jnp.max(scores, axis=1, keepdims=True)
        weight = jnp.exp2(scores - highest)
        total = jnp.sum(weight, axis=1, keepdims=True)
        weight = (weight / total).astype(bf16)
        own_ref[v] = jnp.dot(weight, values, preferred_element_type=f32).astype(bf16)
        sums = jnp.where(lane == v, highest + jnp.log2(total), sums)
    ownsum_ref[...] = sums


def own_mixer(rates_ref, skips_ref, sx_ref, sb_ref, sc_ref, sdt_ref, c_rows, x_rows, fade_ref, local_ref):
    steps, rows, heads = sdt_ref.shape
    stack_rows(sc_ref, c_rows)
    for u in range(steps):
        given = sx_ref[u].astype(f32)
        for k in range(SUB // rows):
            x_rows[u, k * rows : (k + 1) * rows, :] = given
    pair = iota((SUB, heads), 0)
    step = pair // rows
    live = pair < rows * steps
    head = iota((SUB, heads), 1)

    def spread_rows(ref, u):
        given = ref[u].astype(f32)
        return jnp.concatenate([given] * (SUB // rows), axis=0)

    rates = jnp.broadcast_to(rates_ref[...], (SUB, heads)) * LOG2E
    skips = jnp.broadcast_to(skips_ref[...], (SUB, heads))
    moved = [spread_rows(sdt_ref, u) for u in range(steps)]
    kept = [jnp.where(u <= step, moved[u], 0.0) for u in range(steps)]
    parts = [jnp.where(live, jnp.exp2(-(rates * sum(kept))), 0.0)]
    for u in range(steps):
        products = c_rows[...] * spread_rows(sb_ref, u)
        inner = jnp.zeros((SUB, heads), f32)
        for e in range(products.shape[1] // NS):
            found = jnp.sum(products[:, e * NS : (e + 1) * NS], axis=1, keepdims=True)
            inner = jnp.where(head // HPG == e, found, inner)
        gap = jnp.zeros((SUB, heads), f32)
        for t in range(u + 1, steps):
            gap = gap + kept[t]
        weight = jnp.where(u <= step, jnp.exp2(-(rates * gap)) * moved[u] * inner, 0.0)
        weight = weight + jnp.where(u == step, skips, 0.0)
        parts.append(jnp.where(live, weight, 0.0))
    stacked = jnp.concatenate(parts, axis=0)
    high = stacked.astype(bf16)
    low = (stacked - high.astype(f32)).astype(bf16)
    both = jnp.concatenate([high.astype(f32), low.astype(f32)], axis=0)
    count = stacked.shape[0]
    chunk = SUB * HP
    widen = jnp.where(iota((heads, chunk), 0) % SUB == iota((heads, chunk), 1) // HP, 1.0, 0.0).astype(bf16)
    lane = iota(both.shape, 1)
    for d in range(heads // SUB):
        picked = jnp.where(lane // SUB == d, both, 0.0).astype(bf16)
        wide = jnp.dot(picked, widen, preferred_element_type=f32)
        wide = wide[:count] + wide[count:]
        columns = slice(d * chunk, (d + 1) * chunk)
        fade_ref[:, columns] = wide[:SUB]
        value = jnp.zeros((SUB, chunk), f32)
        for u in range(steps):
            value = value + wide[(u + 1) * SUB : (u + 2) * SUB] * x_rows[u, :, columns]
        local_ref[:, columns] = value


def merge_kernel(
    width,
    back_any,
    own_any,
    ownsum_any,
    fade_any,
    local_any,
    mixer_any,
    attention_any,
    back_ref,
    own_ref,
    ownsum_ref,
    fade_ref,
    local_ref,
    mixed,
    attended,
    mixer_ref,
    attention_ref,
    sems,
):
    copies = fetches([(back_any, back_ref), (fade_any, fade_ref), (local_any, local_ref)], sems)
    rest = fetches([(own_any, own_ref), (ownsum_any, ownsum_ref)], sems, len(copies))
    for copy in copies:
        copy.wait()
    owners = back_ref.shape[0]
    ways = owners // KVH
    order = exchange_order(owners)
    steps, rows = mixer_ref.shape[0], mixer_ref.shape[1]
    for d in range(0, owners, 2):
        block = jnp.stack([back_ref[order.index(d + n)].astype(f32) for n in range(2)])
        ending = lift(block, spare(back_ref.shape[2] // LANES, 1))
        if back_ref.shape[2] > HALF:
            ending = jnp.concatenate([block[..., HALF:], ending], axis=-1)
        found = ending[..., :width]
        found = jnp.concatenate([found[0], found[1]], axis=-1)
        columns = slice(d * width, (d + 2) * width)
        mixed[:, columns] = found * fade_ref[:, columns] + local_ref[:, columns]
    for k in range(steps):
        mixer_ref[k] = mixed[k * rows : (k + 1) * rows, :].astype(bf16)
    outs = fetches([(mixer_ref, mixer_any)], sems)
    for copy in rest:
        copy.wait()
    lane = iota((2, SUB, LANES), 2)
    mine = (lane // 16 == iota((2, SUB, LANES), 1)) & (lane % 16 < 12)
    for v in range(KVH):
        blocks, pieces = [], []
        for d in range(v * ways, (v + 1) * ways, 2):
            block = jnp.stack([back_ref[order.index(d + n), :, :HALF].astype(f32) for n in range(2)])
            packed = block[:, PAIRS : PAIRS + 1, :LANES]
            blocks.append(block.reshape(2 * SUB, HALF))
            pieces.append(jnp.where(mine, jnp.broadcast_to(packed, (2, SUB, LANES)), 0.0))
        for g in range(HALF // HD):
            part = slice(g * 2 * SUB, (g + 1) * 2 * SUB)
            own_sum = jnp.broadcast_to(ownsum_ref[part, v : v + 1], (2 * SUB, HD))
            wide = []
            for piece in pieces:
                one = jnp.sum(jnp.where(lane % 4 == g, piece, 0.0), axis=-1, keepdims=True)
                wide.append(jnp.broadcast_to(one, (2, SUB, HD)).reshape(2 * SUB, HD))
            highest = functools.reduce(jnp.maximum, wide, own_sum)
            weight = jnp.exp2(own_sum - highest)
            total = weight
            value = weight * own_ref[v, part, :].astype(f32)
            for one, block in zip(wide, blocks):
                weight = jnp.exp2(one - highest)
                total = total + weight
                value = value + weight * block[:, g * HD : (g + 1) * HD]
            value = value / total
            start = v * 2 * HALF + g * HD
            attended[:, start : start + HD] = value[:SUB]
            attended[:, start + HALF : start + HALF + HD] = value[SUB:]
    for k in range(steps):
        attention_ref[k] = attended[k * rows : (k + 1) * rows, :].astype(bf16)
    outs += fetches([(attention_ref, attention_any)], sems, 1)
    for copy in outs:
        copy.wait()


def call(kernel, out_shape, in_spaces, out_spaces, scratch, cost, aliases=None):
    def spec(space):
        return pl.BlockSpec(memory_space=space)

    return pl.pallas_call(
        kernel,
        out_shape=out_shape,
        in_specs=[spec(space) for space in in_spaces],
        out_specs=jax.tree.map(spec, out_spaces),
        scratch_shapes=scratch,
        input_output_aliases=aliases or {},
        compiler_params=pltpu.CompilerParams(vmem_limit_bytes=VMEM_LIMIT),
        cost_estimate=pl.CostEstimate(flops=cost[0], bytes_accessed=cost[1], transcendentals=0),
    )


def on_device(
    prompt_x,
    prompt_b,
    prompt_c,
    prompt_dt,
    decay_rate,
    skip_gain,
    lengths,
    owner_list,
    page_table,
    cache_pages,
    row_slot,
    step_x,
    step_b,
    step_c,
    step_dt,
    queries,
    fresh_cache,
):
    owners = lax.axis_size("heads")
    ways = owners // KVH
    group, prompts, length = prompt_dt.shape
    width = prompt_x.shape[1]
    keys = cache_pages.shape[0] * PAGE
    span = 2 * keys // prompts
    steps = step_x.shape[1]
    all_rows = owners * SUB
    shape = jax.ShapeDtypeStruct
    smem, vmem, hbm = pltpu.SMEM, pltpu.VMEM, pltpu.HBM
    sem = pltpu.SemaphoreType.DMA((prompts,))
    levels = len(LEVELS)
    step_x, step_b, step_c, step_dt, queries, fresh_cache = (
        jnp.swapaxes(one, 0, 1) for one in (step_x, step_b, step_c, step_dt, queries, fresh_cache)
    )
    owner_list = owner_list.T

    def like(space, array):
        return space(array.shape, array.dtype)

    def sems(count):
        return pltpu.SemaphoreType.DMA((count,))

    other_pages = lax.ppermute(cache_pages, "heads", [(d, d + 1 - 2 * (d % 2)) for d in range(owners)])
    send = call(
        functools.partial(pack_kernel, group, ways),
        shape((all_rows, HALF + LANES), bf16),
        [hbm, hbm],
        vmem,
        [
            like(vmem, queries),
            like(vmem, step_c),
            vmem((SUB, queries.shape[2]), f32),
            vmem((SUB, step_c.shape[2]), f32),
            vmem((step_c.shape[2] // NS, SUB, HALF + LANES), f32),
            sems(2),
        ],
        (0, 1 << 19),
    )(queries, step_c)
    order = [exchange_order(owners)]
    recv = lax.all_to_all(
        send, "heads", split_axis=0, concat_axis=0, tiled=True, axis_index_groups=order
    )

    block = [
        vmem((prompts, width, length), bf16),
        vmem((prompts, length, NS), bf16),
        vmem((prompts, length, NS), bf16),
        vmem((prompts, width, length), bf16),
        vmem((levels, prompts, group, ROWS16, length), bf16),
        vmem((levels, prompts, group, length), f32),
        vmem((prompts, group, length), f32),
    ]
    tables = [vmem((levels, length, length), bf16), vmem((levels + 1, length, length), bf16)]
    work = 2 * width * length * NS
    states, sorted_keys, sorted_values, codes, early_out = call(
        state_kernel,
        (
            shape((prompts, width, NS), bf16),
            shape((prompts // 2, span, 2 * HD), bf16),
            shape((prompts // 2, span, 2 * HD), bf16),
            shape((all_rows, LANES), jnp.int32),
            shape(prompt_x.shape, bf16),
        ),
        [hbm] * 12,
        (hbm,) * 5,
        block
        + tables
        + [vmem((prompts, group, length), f32), vmem((prompts, width, NS), bf16)]
        + [vmem((2,) + cache_pages.shape, bf16)]
        + [vmem((prompts // 2, span, 2 * HD), bf16)] * 2
        + [vmem((all_rows, LANES), jnp.int32)]
        + [like(smem, one) for one in (decay_rate, skip_gain, lengths, owner_list, page_table, row_slot)]
        + [like(vmem, prompt_dt), sem, sem, sem, sem, sem, sems(9)],
        (work * (prompts + 5 * EARLY), 6 << 20),
    )(
        decay_rate,
        skip_gain,
        lengths,
        owner_list,
        page_table,
        row_slot,
        prompt_dt,
        prompt_x,
        prompt_b,
        prompt_c,
        cache_pages,
        other_pages,
    )

    back = call(
        serve_kernel,
        shape((all_rows, HALF + max(LANES, width) - LANES), bf16),
        [hbm] * 5,
        vmem,
        [like(vmem, one) for one in (recv, sorted_keys, sorted_values, codes, states)]
        + [vmem((prompts // 2, HALF // HD * all_rows, 2 * HD), bf16), sem, sems(4)],
        (8 * all_rows * keys * HD, 4 << 20),
    )(recv, sorted_keys, sorted_values, codes, states)
    returned = lax.all_to_all(
        back, "heads", split_axis=0, concat_axis=0, tiled=True, axis_index_groups=order
    ).reshape(owners, SUB, back.shape[1])

    count = HALF // HD * 2 * SUB
    channels = step_x.shape[2]
    rates, skips = decay_rate.reshape(1, -1), skip_gain.reshape(1, -1)
    prompt_out, own, own_sum, fade, local = call(
        prompt_kernel,
        (
            shape(prompt_x.shape, bf16),
            shape((KVH, count, HD), bf16),
            shape((count, LANES), f32),
            shape((SUB, channels), f32),
            shape((SUB, channels), f32),
        ),
        [hbm] * 17,
        (hbm,) * 5,
        block
        + tables
        + [
            vmem((KVH, count, HD), bf16),
            vmem((count, LANES), f32),
            vmem((SUB, channels), f32),
            vmem((SUB, channels), f32),
            vmem((SUB, fresh_cache.shape[2]), f32),
            vmem((SUB, step_c.shape[2]), f32),
            vmem((steps, SUB, channels), f32),
            like(smem, decay_rate),
            like(smem, skip_gain),
            like(smem, lengths),
            like(vmem, prompt_dt),
            like(vmem, rates),
            like(vmem, skips),
            vmem((owners, SUB, HALF + LANES), bf16),
            like(vmem, fresh_cache),
            like(vmem, step_x),
            like(vmem, step_b),
            like(vmem, step_c),
            like(vmem, step_dt),
            sem,
            sem,
            sem,
            sem,
            sems(12),
        ],
        (work * 5 * (prompts - EARLY), 8 << 20),
        {16: 0},
    )(
        decay_rate,
        skip_gain,
        lengths,
        prompt_dt,
        rates,
        skips,
        send.reshape(owners, SUB, HALF + LANES),
        fresh_cache,
        step_x,
        step_b,
        step_c,
        step_dt,
        prompt_x,
        prompt_b,
        prompt_c,
        back,
        early_out,
    )

    mixer_out, attention_out = call(
        functools.partial(merge_kernel, width),
        (shape(step_x.shape, bf16), shape(queries.shape, bf16)),
        [hbm] * 5,
        (hbm, hbm),
        [like(vmem, one) for one in (returned, own, own_sum, fade, local)]
        + [vmem((SUB, channels), f32), vmem((SUB, queries.shape[2]), f32)]
        + [like(vmem, step_x), like(vmem, queries), sems(5)],
        (0, 2 << 20),
    )(returned, own, own_sum, fade, local)
    return (prompt_out, jnp.swapaxes(mixer_out, 0, 1), jnp.swapaxes(attention_out, 0, 1))


def solution(mesh):
    in_specs = (
        P("groups", "heads", None),
        P("groups", None, None),
        P("groups", None, None),
        P("heads", "groups", None),
        P(),
        P(),
        P("groups"),
        P("groups", None),
        P("groups", None),
        P(("groups", "heads"), None, None),
        P("groups"),
        P(("groups", "heads"), None, None),
        P(("groups", "heads"), None, None),
        P(("groups", "heads"), None, None),
        P(("groups", "heads"), None, None),
        P(("groups", "heads"), None, None),
        P(("groups", "heads"), None, None),
    )
    out_specs = (
        P("groups", "heads", None),
        P(("groups", "heads"), None, None),
        P(("groups", "heads"), None, None),
    )
    return jax.shard_map(
        on_device, mesh=mesh, in_specs=in_specs, out_specs=out_specs, check_vma=False
    )
```

```python
import functools
import math

import jax
import jax.numpy as jnp
from jax import lax
from jax.experimental import pallas as pl
from jax.experimental.pallas import tpu as pltpu
from jax.sharding import PartitionSpec as P

NS = 256
HP = 64
HPG = 32
KVH = 8
HD = 128
PAGE = 16
PAGES = 16
LANES = 128
SUB = 8
HALF = 512
LEVELS = (128, 64, 32, 16)
LOG2E = math.log2(math.e)
SCORE = LOG2E / math.sqrt(HD)
NONE = -1e30
FLOOR = -1e29
PAIRS = 6
LENGTH_BITS = 10
AHEAD = 2
EARLY = 2
VMEM_LIMIT = 64 * 1024 * 1024

f32 = jnp.float32
bf16 = jnp.bfloat16


def iota(shape, dim):
    return lax.broadcasted_iota(jnp.int32, shape, dim)


def exchange_order(owners):
    first = owners // 2
    return [first] + [d for d in range(owners) if d != first]


def dot_nt(left, right):
    return lax.dot_general(left, right, (((1,), (1,)), ((), ())), preferred_element_type=f32)


def stack_rows(source, held):
    steps, rows = source.shape[0], source.shape[1]
    held[...] = jnp.zeros_like(held)
    for k in range(steps):
        held[k * rows : (k + 1) * rows, :] = source[k].astype(f32)


def spare(blocks, taken):
    return [(row, b) for row in range(PAIRS, SUB) for b in range(blocks)][taken : taken + PAIRS]


def lift(value, slots):
    row = iota(value.shape[:2] + (LANES,), 1)
    found = jnp.zeros(row.shape, f32)
    for pair, (at, b) in enumerate(slots):
        one = value[:, at : at + 1, b * LANES : (b + 1) * LANES]
        found = jnp.where(row == pair, jnp.broadcast_to(one, row.shape), found)
    return found


def fetches(pairs, sems, first=0):
    copies = [pltpu.make_async_copy(src, dst, sems.at[first + n]) for n, (src, dst) in enumerate(pairs)]
    for copy in copies:
        copy.start()
    return copies


def pack_kernel(group, ways, q_any, c_any, out_ref, q_ref, c_ref, q_held, c_held, rest, sems):
    owners = out_ref.shape[0] // SUB
    for copy in fetches([(q_any, q_ref), (c_any, c_ref)], sems):
        copy.wait()
    stack_rows(q_ref, q_held)
    stack_rows(c_ref, c_held)
    span = 2 * HALF
    slots = spare(HALF // LANES + 1, 0)
    rest[...] = jnp.zeros_like(rest)
    for e in range(c_ref.shape[2] // NS):
        rest[e, :PAIRS, HALF:] = c_held[:PAIRS, e * NS : e * NS + LANES]
        for pair, (row, b) in enumerate(slots):
            rest[e, row : row + 1, b * LANES : (b + 1) * LANES] = c_held[
                pair : pair + 1, e * NS + LANES : (e + 1) * NS
            ]
    real = iota((SUB, HALF), 0) < PAIRS
    order = exchange_order(owners)
    for rank in range(0, owners, 2):
        blocks, ends = [], []
        for d in order[rank : rank + 2]:
            begin, e = d // ways * span + d % 2 * HALF, (d * group) // HPG
            blocks.append(jnp.where(real, q_held[:, begin : begin + HALF], rest[e, :, :HALF]))
            ends.append(rest[e, :, HALF:])
        place = slice(rank * SUB, (rank + 2) * SUB)
        out_ref[place, :HALF] = jnp.concatenate(blocks, axis=0).astype(bf16)
        out_ref[place, HALF:] = jnp.concatenate(ends, axis=0).astype(bf16)


def sign_tables(signs, tail):
    length = signs.shape[-1]
    j = iota((length, length), 0)
    i = iota((length, length), 1)
    for l, n in enumerate(LEVELS):
        middle = (i // (2 * n)) * (2 * n) + (n - 1)
        signs[l] = (jnp.where(j <= i, 1.0, 0.0) - jnp.where(j <= middle, 1.0, 0.0)).astype(bf16)
    if tail:
        signs[len(LEVELS)] = jnp.where(j > i, 1.0, 0.0).astype(bf16)


def head_factors(first, dt_ref, rate_ref, skip_ref, len_ref, signs, w_in, w_out, w_skip, w_tail):
    group, prompts, length = dt_ref.shape
    row = iota((prompts, length), 0)
    lens = jnp.zeros((prompts, length), jnp.int32)
    for r in range(prompts):
        lens = jnp.where(row == r, len_ref[r], lens)
    valid = iota((prompts, length), 1) < lens
    moved = [jnp.where(valid, dt_ref[h].astype(f32), 0.0) for h in range(group)]
    every = jnp.concatenate(moved, axis=0).astype(bf16)
    rates = [rate_ref[first + h] * LOG2E for h in range(group)]
    if w_tail is not None:
        total = jnp.dot(every, signs[len(LEVELS)], preferred_element_type=f32)
        for h in range(group):
            part = total[h * prompts : (h + 1) * prompts]
            w_tail[:, h, :] = jnp.exp2(-(rates[h] * part)) * moved[h]
    for h in range(group):
        w_skip[:, h, :] = jnp.where(valid, skip_ref[first + h], 0.0)
    for l, n in enumerate(LEVELS):
        total = jnp.dot(every, signs[l], preferred_element_type=f32)
        for h in range(group):
            gap = rates[h] * total[h * prompts : (h + 1) * prompts]
            if n == LEVELS[-1]:
                up, down = jnp.exp2(gap), jnp.exp2(-gap)
            else:
                up, down = jnp.exp2(jnp.minimum(gap, 0.0)), jnp.exp2(-jnp.maximum(gap, 0.0))
            w_in[l, :, h, :] = up * moved[h]
            w_out[l, :, h, :] = jnp.where(valid, down, 0.0)


def level_masks(masks):
    length = masks.shape[-1]
    j = iota((length, length), 0)
    i = iota((length, length), 1)
    for l, n in enumerate(LEVELS):
        same = (j // (2 * n)) == (i // (2 * n))
        if n == LEVELS[-1]:
            keep = same & (j <= i)
        else:
            keep = same & ((j % (2 * n)) < n) & ((i % (2 * n)) >= n)
        masks[l] = jnp.where(keep, 1.0, 0.0).astype(bf16)


def prompt_result(r, x_held, b_held, c_held, w_in, w_out, w_skip, masks, out_held):
    width, length = x_held.shape[1], x_held.shape[2]
    group = width // HP
    half = length // 2
    inputs = x_held[r].astype(f32).reshape(group, HP, length)
    scores = dot_nt(b_held[r], c_held[r]).astype(bf16)
    total = inputs * w_skip[r][:, None, :]
    left, right = total[..., :half], total[..., half:]
    for l, n in enumerate(LEVELS):
        if 2 * n == length:
            scaled = (inputs[..., :half] * w_in[l, r][:, None, :half]).astype(bf16).reshape(width, half)
            added = jnp.dot(scaled, scores[:half, half:], preferred_element_type=f32)
            right = right + added.reshape(group, HP, half) * w_out[l, r][:, None, half:]
        else:
            scaled = (inputs * w_in[l, r][:, None, :]).astype(bf16).reshape(width, length)
            added = jnp.dot(scaled, scores * masks[l], preferred_element_type=f32)
            added = added.reshape(group, HP, length) * w_out[l, r][:, None, :]
            left = left + added[..., :half]
            right = right + added[..., half:]
    out_held[r] = jnp.concatenate([left, right], axis=-1).reshape(width, length).astype(bf16)


def state_kernel(
    rate_any,
    skip_any,
    len_any,
    owner_any,
    table_any,
    slot_any,
    dt_any,
    x_any,
    b_any,
    c_any,
    pages_any,
    other_any,
    state_any,
    key_any,
    value_any,
    code_any,
    out_any,
    x_held,
    b_held,
    c_held,
    out_held,
    w_in,
    w_out,
    w_skip,
    masks,
    signs,
    w_tail,
    state_held,
    pages_held,
    key_held,
    value_held,
    code_held,
    rate_ref,
    skip_ref,
    len_ref,
    owner_ref,
    table_ref,
    slot_ref,
    dt_ref,
    x_sem,
    b_sem,
    c_sem,
    out_sem,
    state_sem,
    sems,
):
    group, prompts, length = dt_ref.shape
    smalls = fetches(
        [
            (dt_any, dt_ref),
            (rate_any, rate_ref),
            (skip_any, skip_ref),
            (len_any, len_ref),
            (owner_any, owner_ref),
            (table_any, table_ref),
            (slot_any, slot_ref),
        ],
        sems,
    )
    me = lax.axis_index("heads")
    core = lax.rem(me, 2)
    first = me * group
    column = pl.multiple_of((first // HPG) * NS, NS)

    def x_copy(r):
        return pltpu.make_async_copy(x_any.at[r], x_held.at[r], x_sem.at[r])

    def b_copy(r):
        return pltpu.make_async_copy(b_any.at[r, :, pl.ds(column, NS)], b_held.at[r], b_sem.at[r])

    def c_copy(r):
        return pltpu.make_async_copy(c_any.at[r, :, pl.ds(column, NS)], c_held.at[r], c_sem.at[r])

    def out_copy(r):
        return pltpu.make_async_copy(out_held.at[r], out_any.at[r], out_sem.at[r])

    def state_copy(r):
        return pltpu.make_async_copy(state_held.at[r], state_any.at[r], state_sem.at[r])

    def ask(r):
        x_copy(r).start()
        b_copy(r).start()

    pages = fetches([(pages_any, pages_held.at[core]), (other_any, pages_held.at[1 - core])], sems, len(smalls))
    for r in range(prompts):
        ask(r)
    for r in range(EARLY):
        c_copy(r).start()
    sign_tables(signs, True)
    level_masks(masks)
    for copy in smalls:
        copy.wait()
    head_factors(first, dt_ref, rate_ref, skip_ref, len_ref, signs, w_in, w_out, w_skip, w_tail)

    width = x_held.shape[1]
    for begin in range(0, prompts, prompts // 2):
        some = range(begin, begin + prompts // 2)
        for r in some:
            x_copy(r).wait()
            b_copy(r).wait()
        for r in some:
            inputs = x_held[r].astype(f32).reshape(group, HP, length)
            scaled = (inputs * w_tail[r][:, None, :]).astype(bf16).reshape(width, length)
            state_held[r] = jnp.dot(scaled, b_held[r], preferred_element_type=f32).astype(bf16)
        for r in some:
            state_copy(r).start()
    spread = table_ref.shape[1] // owner_ref.shape[1]
    for copy in pages:
        copy.wait()
    for n in range(2):
        for r in range(prompts):
            for page in range(spread):
                holder = me - core + n
                row = table_ref[r, holder * spread + page] - holder * (prompts * spread)
                block = pages_held[n, row]
                place = pl.ds((n * spread + page) * PAGE, PAGE)
                columns = pl.ds(r % 2 * HD, HD)
                key_held[r // 2, place, columns] = block[:, :HD]
                value_held[r // 2, place, columns] = block[:, HD:]

    owners = owner_ref.shape[1]
    rows_dev = slot_ref.shape[0] // owners
    inner = iota((2 * SUB, LANES), 0)

    order = exchange_order(owners)
    for rank in range(0, owners, 2):
        block = jnp.zeros((2 * SUB, LANES), jnp.int32)
        for n in range(2):
            s = order[rank + n]
            for i in range(rows_dev):
                target = owner_ref[slot_ref[s * rows_dev + i], s]
                code = target * (1 << LENGTH_BITS) + len_ref[target]
                block = jnp.where((inner // SUB == n) & (inner % rows_dev == i), code, block)
        code_held[rank * SUB : (rank + 2) * SUB, :] = block
    marks = fetches([(key_held, key_any), (value_held, value_any), (code_held, code_any)], sems)

    for r in range(EARLY):
        c_copy(r).wait()
    for r in range(EARLY):
        prompt_result(r, x_held, b_held, c_held, w_in, w_out, w_skip, masks, out_held)
    for r in range(EARLY):
        out_copy(r).start()
    for copy in marks:
        copy.wait()
    for r in range(prompts):
        state_copy(r).wait()
    for r in range(EARLY):
        out_copy(r).wait()


def serve_kernel(
    recv_any,
    key_any,
    value_any,
    code_any,
    state_any,
    out_ref,
    recv_ref,
    key_ref,
    value_ref,
    code_ref,
    state_ref,
    query_ref,
    state_sem,
    sems,
):
    rows = recv_ref.shape[0]
    prompts, width = state_ref.shape[0], state_ref.shape[1]
    copies = fetches(
        [(recv_any, recv_ref), (code_any, code_ref), (key_any, key_ref), (value_any, value_ref)], sems
    )
    states = fetches([(state_any.at[r], state_ref.at[r]) for r in range(prompts)], state_sem)
    heads = HALF // HD
    keys = key_ref.shape[1]
    chips = keys // PAGE
    begin = lax.rem(lax.axis_index("heads") // 2 * chips, PAGES) * PAGE
    copies[0].wait()
    copies[1].wait()
    code = code_ref[...]
    target = code >> LENGTH_BITS
    lengths = code & ((1 << LENGTH_BITS) - 1)
    for r in range(prompts):
        for g in range(heads):
            query = recv_ref[:, g * HD : (g + 1) * HD].astype(f32)
            query_ref[r // 2, g * rows : (g + 1) * rows, r % 2 * HD : (r % 2 + 1) * HD] = jnp.where(
                target == r, query, 0.0
            ).astype(bf16)
    copies[2].wait()
    scores = jnp.zeros((heads * rows, keys), f32)
    for pair in range(prompts // 2):
        scores = scores + dot_nt(query_ref[pair], key_ref[pair])
    copies[3].wait()
    for copy in states:
        copy.wait()
    seen = jnp.concatenate([lengths[:, :1]] * heads, axis=0) > iota((heads * rows, keys), 1) + begin
    scores = jnp.where(seen, scores * SCORE, NONE)
    highest = jnp.maximum(jnp.max(scores, axis=1, keepdims=True), FLOOR)
    weight = jnp.exp2(scores - highest)
    total = jnp.sum(weight, axis=1, keepdims=True)
    some = total > 0.0
    safe = jnp.where(some, total, 1.0)
    result = jnp.where(some, highest + jnp.log2(safe), NONE)
    weight = weight.astype(bf16)
    targets = jnp.concatenate([target] * heads, axis=0)
    value = jnp.zeros((heads * rows, HD), f32)
    for pair in range(prompts // 2):
        both = jnp.dot(weight, value_ref[pair], preferred_element_type=f32)
        for n in range(2):
            value = jnp.where(targets == 2 * pair + n, both[:, n * HD : (n + 1) * HD], value)
    value = value / safe
    lane = iota((rows, LANES), 1)
    sums = jnp.zeros((rows, LANES), f32)
    for g in range(heads):
        sums = jnp.where(lane % 4 == g, result[g * rows : (g + 1) * rows], sums)
    high = sums.astype(bf16).astype(f32)
    rest = sums - high
    middle = rest.astype(bf16).astype(f32)
    piece = lane % 16 // 4
    pieces = jnp.where(piece == 0, high, jnp.where(piece == 1, middle, rest - middle))
    pair = iota((rows, LANES), 0) % SUB
    pieces = jnp.where((lane // 16 == pair) & (piece < 3), pieces, 0.0)
    packed = jnp.sum(pieces.reshape(rows // SUB, SUB, LANES), axis=1, keepdims=True)

    given = recv_ref[...].astype(f32).reshape(rows // SUB, SUB, recv_ref.shape[1])
    ending = lift(given, spare(heads + 1, 0))
    readout = jnp.concatenate([given[..., HALF:], ending], axis=-1).reshape(rows, NS)
    target = jnp.concatenate([target, target], axis=-1)
    found = jnp.zeros((rows, width), f32)
    for r in range(prompts):
        picked = jnp.where(target == r, readout, 0.0).astype(bf16)
        found = found + dot_nt(picked, state_ref[r])
    if width < LANES:
        found = jnp.concatenate([found, jnp.zeros((rows, LANES - width), f32)], axis=-1)
    blocks = [value[g * rows : (g + 1) * rows] for g in range(heads)]
    blocks += [found[:, b : b + LANES] for b in range(0, found.shape[1], LANES)]
    blocks = [one.reshape(rows // SUB, SUB, LANES) for one in blocks]
    row = iota((rows // SUB, SUB, LANES), 1)
    last = blocks.pop()
    blocks[0] = jnp.where(row == PAIRS, jnp.broadcast_to(packed, row.shape), blocks[0])
    for n, (at, b) in enumerate(spare(len(blocks), 1)):
        one = jnp.broadcast_to(last[:, n : n + 1, :], row.shape)
        blocks[b] = jnp.where(row == at, one, blocks[b])
    for b, one in enumerate(blocks):
        out_ref[:, b * LANES : (b + 1) * LANES] = one.reshape(rows, LANES).astype(bf16)


def prompt_kernel(
    rate_any,
    skip_any,
    len_any,
    dt_any,
    rates_any,
    skips_any,
    send_any,
    fresh_any,
    sx_any,
    sb_any,
    sc_any,
    sdt_any,
    x_any,
    b_any,
    c_any,
    after_any,
    early_any,
    out_any,
    own_any,
    ownsum_any,
    fade_any,
    local_any,
    x_held,
    b_held,
    c_held,
    out_held,
    w_in,
    w_out,
    w_skip,
    masks,
    signs,
    own_ref,
    ownsum_ref,
    fade_ref,
    local_ref,
    fresh_held,
    c_rows,
    x_rows,
    rate_ref,
    skip_ref,
    len_ref,
    dt_ref,
    rates_ref,
    skips_ref,
    send_ref,
    fresh_ref,
    sx_ref,
    sb_ref,
    sc_ref,
    sdt_ref,
    x_sem,
    b_sem,
    c_sem,
    out_sem,
    sems,
):
    group, prompts, length = dt_ref.shape
    smalls = fetches(
        [
            (dt_any, dt_ref),
            (rate_any, rate_ref),
            (skip_any, skip_ref),
            (len_any, len_ref),
            (rates_any, rates_ref),
            (skips_any, skips_ref),
            (send_any, send_ref),
            (fresh_any, fresh_ref),
            (sx_any, sx_ref),
            (sb_any, sb_ref),
            (sc_any, sc_ref),
            (sdt_any, sdt_ref),
        ],
        sems,
    )
    me = lax.axis_index("heads")
    first = me * group
    column = pl.multiple_of((first // HPG) * NS, NS)

    def x_copy(r):
        return pltpu.make_async_copy(x_any.at[r], x_held.at[r], x_sem.at[r])

    def b_copy(r):
        return pltpu.make_async_copy(b_any.at[r, :, pl.ds(column, NS)], b_held.at[r], b_sem.at[r])

    def c_copy(r):
        return pltpu.make_async_copy(c_any.at[r, :, pl.ds(column, NS)], c_held.at[r], c_sem.at[r])

    def out_copy(r):
        return pltpu.make_async_copy(out_held.at[r], out_any.at[r], out_sem.at[r])

    def ask(r):
        x_copy(r).start()
        b_copy(r).start()
        c_copy(r).start()

    for r in range(EARLY, min(EARLY + AHEAD, prompts)):
        ask(r)
    sign_tables(signs, False)
    level_masks(masks)
    for copy in smalls:
        copy.wait()
    head_factors(first, dt_ref, rate_ref, skip_ref, len_ref, signs, w_in, w_out, w_skip, None)
    own_attention(send_ref, fresh_ref, fresh_held, own_ref, ownsum_ref)
    own_mixer(rates_ref, skips_ref, sx_ref, sb_ref, sc_ref, sdt_ref, c_rows, x_rows, fade_ref, local_ref)
    outs = fetches(
        [(own_ref, own_any), (ownsum_ref, ownsum_any), (fade_ref, fade_any), (local_ref, local_any)], sems
    )

    def some(n, _):
        begin = EARLY + n * AHEAD

        @pl.when(begin + AHEAD < prompts)
        def _():
            for r in range(AHEAD):
                ask(begin + AHEAD + r)

        for r in range(AHEAD):
            x_copy(begin + r).wait()
            b_copy(begin + r).wait()
            c_copy(begin + r).wait()
        for r in range(AHEAD):
            prompt_result(begin + r, x_held, b_held, c_held, w_in, w_out, w_skip, masks, out_held)
        for r in range(AHEAD):
            out_copy(begin + r).start()
        return 0

    lax.fori_loop(0, (prompts - EARLY) // AHEAD, some, 0)
    for copy in outs:
        copy.wait()
    for r in range(EARLY, prompts):
        out_copy(r).wait()


def own_attention(send_ref, fresh_ref, fresh_held, own_ref, ownsum_ref):
    steps, rows = fresh_ref.shape[0], fresh_ref.shape[1]
    owners = send_ref.shape[0]
    order = exchange_order(owners)
    ways = owners // KVH
    stack_rows(fresh_ref, fresh_held)
    count = HALF // HD * 2 * SUB
    pair = iota((count, SUB), 0) % SUB
    key = iota((count, SUB), 1)
    seen = (key % rows == pair % rows) & (key <= pair) & (key < rows * steps)
    seen = seen | ((pair >= rows * steps) & (key == 0))
    for v in range(KVH):
        halves = [send_ref[order.index(v * ways + n), :, :HALF].astype(f32) for n in range(2)]
        parts = [half[:, g * HD : (g + 1) * HD] for g in range(HALF // HD) for half in halves]
        query = jnp.concatenate(parts, axis=0).astype(bf16)
        keys = fresh_held[:, v * HD : (v + 1) * HD].astype(bf16)
        values = fresh_held[:, (KVH + v) * HD : (KVH + v + 1) * HD].astype(bf16)
        scores = jnp.where(seen, dot_nt(query, keys) * SCORE, NONE)
        highest = jnp.max(scores, axis=1, keepdims=True)
        weight = jnp.exp2(scores - highest)
        total = jnp.sum(weight, axis=1, keepdims=True)
        weight = (weight / total).astype(bf16)
        own_ref[v] = jnp.dot(weight, values, preferred_element_type=f32)
        ownsum_ref[v] = jnp.broadcast_to(highest + jnp.log2(total), (count, HD))


def own_mixer(rates_ref, skips_ref, sx_ref, sb_ref, sc_ref, sdt_ref, c_rows, x_rows, fade_ref, local_ref):
    steps, rows, heads = sdt_ref.shape
    stack_rows(sc_ref, c_rows)
    for u in range(steps):
        given = sx_ref[u].astype(f32)
        for k in range(SUB // rows):
            x_rows[u, k * rows : (k + 1) * rows, :] = given
    pair = iota((SUB, heads), 0)
    step = pair // rows
    live = pair < rows * steps
    head = iota((SUB, heads), 1)

    def spread_rows(ref, u):
        given = ref[u].astype(f32)
        return jnp.concatenate([given] * (SUB // rows), axis=0)

    rates = jnp.broadcast_to(rates_ref[...], (SUB, heads)) * LOG2E
    skips = jnp.broadcast_to(skips_ref[...], (SUB, heads))
    moved = [spread_rows(sdt_ref, u) for u in range(steps)]
    kept = [jnp.where(u <= step, moved[u], 0.0) for u in range(steps)]
    parts = [jnp.where(live, jnp.exp2(-(rates * sum(kept))), 0.0)]
    for u in range(steps):
        products = c_rows[...] * spread_rows(sb_ref, u)
        inner = jnp.zeros((SUB, heads), f32)
        for e in range(products.shape[1] // NS):
            found = jnp.sum(products[:, e * NS : (e + 1) * NS], axis=1, keepdims=True)
            inner = jnp.where(head // HPG == e, found, inner)
        gap = jnp.zeros((SUB, heads), f32)
        for t in range(u + 1, steps):
            gap = gap + kept[t]
        weight = jnp.where(u <= step, jnp.exp2(-(rates * gap)) * moved[u] * inner, 0.0)
        weight = weight + jnp.where(u == step, skips, 0.0)
        parts.append(jnp.where(live, weight, 0.0))
    stacked = jnp.concatenate(parts, axis=0)
    high = stacked.astype(bf16)
    low = (stacked - high.astype(f32)).astype(bf16)
    both = jnp.concatenate([high.astype(f32), low.astype(f32)], axis=0)
    count = stacked.shape[0]
    chunk = SUB * HP
    widen = jnp.where(iota((heads, chunk), 0) % SUB == iota((heads, chunk), 1) // HP, 1.0, 0.0).astype(bf16)
    lane = iota(both.shape, 1)
    for d in range(heads // SUB):
        picked = jnp.where(lane // SUB == d, both, 0.0).astype(bf16)
        wide = jnp.dot(picked, widen, preferred_element_type=f32)
        wide = wide[:count] + wide[count:]
        columns = slice(d * chunk, (d + 1) * chunk)
        fade_ref[:, columns] = wide[:SUB]
        value = jnp.zeros((SUB, chunk), f32)
        for u in range(steps):
            value = value + wide[(u + 1) * SUB : (u + 2) * SUB] * x_rows[u, :, columns]
        local_ref[:, columns] = value


def merge_kernel(
    width,
    back_any,
    own_any,
    ownsum_any,
    fade_any,
    local_any,
    mixer_any,
    attention_any,
    back_ref,
    own_ref,
    ownsum_ref,
    fade_ref,
    local_ref,
    mixed,
    attended,
    mixer_ref,
    attention_ref,
    sems,
):
    copies = fetches([(back_any, back_ref), (fade_any, fade_ref), (local_any, local_ref)], sems)
    rest = fetches([(own_any, own_ref), (ownsum_any, ownsum_ref)], sems, len(copies))
    for copy in copies:
        copy.wait()
    owners = back_ref.shape[0]
    ways = owners // KVH
    order = exchange_order(owners)
    steps, rows = mixer_ref.shape[0], mixer_ref.shape[1]
    for d in range(0, owners, 2):
        block = jnp.stack([back_ref[order.index(d + n)].astype(f32) for n in range(2)])
        ending = lift(block, spare(back_ref.shape[2] // LANES, 1))
        if back_ref.shape[2] > HALF:
            ending = jnp.concatenate([block[..., HALF:], ending], axis=-1)
        found = ending[..., :width]
        found = jnp.concatenate([found[0], found[1]], axis=-1)
        columns = slice(d * width, (d + 2) * width)
        mixed[:, columns] = found * fade_ref[:, columns] + local_ref[:, columns]
    for k in range(steps):
        mixer_ref[k] = mixed[k * rows : (k + 1) * rows, :].astype(bf16)
    outs = fetches([(mixer_ref, mixer_any)], sems)
    for copy in rest:
        copy.wait()
    lane = iota((2, SUB, LANES), 2)
    mine = (lane // 16 == iota((2, SUB, LANES), 1)) & (lane % 16 < 12)
    for v in range(KVH):
        blocks, pieces = [], []
        for d in range(v * ways, (v + 1) * ways, 2):
            block = jnp.stack([back_ref[order.index(d + n), :, :HALF].astype(f32) for n in range(2)])
            packed = block[:, PAIRS : PAIRS + 1, :LANES]
            blocks.append(block.reshape(2 * SUB, HALF))
            pieces.append(jnp.where(mine, jnp.broadcast_to(packed, (2, SUB, LANES)), 0.0))
        for g in range(HALF // HD):
            part = slice(g * 2 * SUB, (g + 1) * 2 * SUB)
            own_sum = ownsum_ref[v, part, :]
            wide = []
            for piece in pieces:
                one = jnp.sum(jnp.where(lane % 4 == g, piece, 0.0), axis=-1, keepdims=True)
                wide.append(jnp.broadcast_to(one, (2, SUB, HD)).reshape(2 * SUB, HD))
            highest = functools.reduce(jnp.maximum, wide, own_sum)
            weight = jnp.exp2(own_sum - highest)
            total = weight
            value = weight * own_ref[v, part, :]
            for one, block in zip(wide, blocks):
                weight = jnp.exp2(one - highest)
                total = total + weight
                value = value + weight * block[:, g * HD : (g + 1) * HD]
            value = value / total
            start = v * 2 * HALF + g * HD
            attended[:, start : start + HD] = value[:SUB]
            attended[:, start + HALF : start + HALF + HD] = value[SUB:]
    for k in range(steps):
        attention_ref[k] = attended[k * rows : (k + 1) * rows, :].astype(bf16)
    outs += fetches([(attention_ref, attention_any)], sems, 1)
    for copy in outs:
        copy.wait()


def call(kernel, out_shape, in_spaces, out_spaces, scratch, cost, aliases=None):
    def spec(space):
        return pl.BlockSpec(memory_space=space)

    return pl.pallas_call(
        kernel,
        out_shape=out_shape,
        in_specs=[spec(space) for space in in_spaces],
        out_specs=jax.tree.map(spec, out_spaces),
        scratch_shapes=scratch,
        input_output_aliases=aliases or {},
        compiler_params=pltpu.CompilerParams(vmem_limit_bytes=VMEM_LIMIT),
        cost_estimate=pl.CostEstimate(flops=cost[0], bytes_accessed=cost[1], transcendentals=0),
    )


def on_device(
    prompt_x,
    prompt_b,
    prompt_c,
    prompt_dt,
    decay_rate,
    skip_gain,
    lengths,
    owner_list,
    page_table,
    cache_pages,
    row_slot,
    step_x,
    step_b,
    step_c,
    step_dt,
    queries,
    fresh_cache,
):
    owners = lax.axis_size("heads")
    ways = owners // KVH
    group, prompts, length = prompt_dt.shape
    width = prompt_x.shape[1]
    keys = cache_pages.shape[0] * PAGE
    span = 2 * keys // prompts
    steps = step_x.shape[1]
    all_rows = owners * SUB
    shape = jax.ShapeDtypeStruct
    smem, vmem, hbm = pltpu.SMEM, pltpu.VMEM, pltpu.HBM
    sem = pltpu.SemaphoreType.DMA((prompts,))
    levels = len(LEVELS)
    step_x, step_b, step_c, step_dt, queries, fresh_cache = (
        jnp.swapaxes(one, 0, 1) for one in (step_x, step_b, step_c, step_dt, queries, fresh_cache)
    )
    owner_list = owner_list.T

    def like(space, array):
        return space(array.shape, array.dtype)

    def sems(count):
        return pltpu.SemaphoreType.DMA((count,))

    other_pages = lax.ppermute(cache_pages, "heads", [(d, d + 1 - 2 * (d % 2)) for d in range(owners)])
    send = call(
        functools.partial(pack_kernel, group, ways),
        shape((all_rows, HALF + LANES), bf16),
        [hbm, hbm],
        vmem,
        [
            like(vmem, queries),
            like(vmem, step_c),
            vmem((SUB, queries.shape[2]), f32),
            vmem((SUB, step_c.shape[2]), f32),
            vmem((step_c.shape[2] // NS, SUB, HALF + LANES), f32),
            sems(2),
        ],
        (0, 1 << 19),
    )(queries, step_c)
    order = [exchange_order(owners)]
    recv = lax.all_to_all(
        send, "heads", split_axis=0, concat_axis=0, tiled=True, axis_index_groups=order
    )

    block = [
        vmem((prompts, width, length), bf16),
        vmem((prompts, length, NS), bf16),
        vmem((prompts, length, NS), bf16),
        vmem((prompts, width, length), bf16),
        vmem((levels, prompts, group, length), f32),
        vmem((levels, prompts, group, length), f32),
        vmem((prompts, group, length), f32),
    ]
    tables = [vmem((levels, length, length), bf16), vmem((levels + 1, length, length), bf16)]
    work = 2 * width * length * NS
    states, sorted_keys, sorted_values, codes, early_out = call(
        state_kernel,
        (
            shape((prompts, width, NS), bf16),
            shape((prompts // 2, span, 2 * HD), bf16),
            shape((prompts // 2, span, 2 * HD), bf16),
            shape((all_rows, LANES), jnp.int32),
            shape(prompt_x.shape, bf16),
        ),
        [hbm] * 12,
        (hbm,) * 5,
        block
        + tables
        + [vmem((prompts, group, length), f32), vmem((prompts, width, NS), bf16)]
        + [vmem((2,) + cache_pages.shape, bf16)]
        + [vmem((prompts // 2, span, 2 * HD), bf16)] * 2
        + [vmem((all_rows, LANES), jnp.int32)]
        + [like(smem, one) for one in (decay_rate, skip_gain, lengths, owner_list, page_table, row_slot)]
        + [like(vmem, prompt_dt), sem, sem, sem, sem, sem, sems(9)],
        (work * (prompts + 5 * EARLY), 6 << 20),
    )(
        decay_rate,
        skip_gain,
        lengths,
        owner_list,
        page_table,
        row_slot,
        prompt_dt,
        prompt_x,
        prompt_b,
        prompt_c,
        cache_pages,
        other_pages,
    )

    back = call(
        serve_kernel,
        shape((all_rows, HALF + max(LANES, width) - LANES), bf16),
        [hbm] * 5,
        vmem,
        [like(vmem, one) for one in (recv, sorted_keys, sorted_values, codes, states)]
        + [vmem((prompts // 2, HALF // HD * all_rows, 2 * HD), bf16), sem, sems(4)],
        (8 * all_rows * keys * HD, 4 << 20),
    )(recv, sorted_keys, sorted_values, codes, states)
    returned = lax.all_to_all(
        back, "heads", split_axis=0, concat_axis=0, tiled=True, axis_index_groups=order
    ).reshape(owners, SUB, back.shape[1])

    count = HALF // HD * 2 * SUB
    channels = step_x.shape[2]
    rates, skips = decay_rate.reshape(1, -1), skip_gain.reshape(1, -1)
    prompt_out, own, own_sum, fade, local = call(
        prompt_kernel,
        (
            shape(prompt_x.shape, bf16),
            shape((KVH, count, HD), f32),
            shape((KVH, count, HD), f32),
            shape((SUB, channels), f32),
            shape((SUB, channels), f32),
        ),
        [hbm] * 17,
        (hbm,) * 5,
        block
        + tables
        + [
            vmem((KVH, count, HD), f32),
            vmem((KVH, count, HD), f32),
            vmem((SUB, channels), f32),
            vmem((SUB, channels), f32),
            vmem((SUB, fresh_cache.shape[2]), f32),
            vmem((SUB, step_c.shape[2]), f32),
            vmem((steps, SUB, channels), f32),
            like(smem, decay_rate),
            like(smem, skip_gain),
            like(smem, lengths),
            like(vmem, prompt_dt),
            like(vmem, rates),
            like(vmem, skips),
            vmem((owners, SUB, HALF + LANES), bf16),
            like(vmem, fresh_cache),
            like(vmem, step_x),
            like(vmem, step_b),
            like(vmem, step_c),
            like(vmem, step_dt),
            sem,
            sem,
            sem,
            sem,
            sems(12),
        ],
        (work * 5 * (prompts - EARLY), 8 << 20),
        {16: 0},
    )(
        decay_rate,
        skip_gain,
        lengths,
        prompt_dt,
        rates,
        skips,
        send.reshape(owners, SUB, HALF + LANES),
        fresh_cache,
        step_x,
        step_b,
        step_c,
        step_dt,
        prompt_x,
        prompt_b,
        prompt_c,
        back,
        early_out,
    )

    mixer_out, attention_out = call(
        functools.partial(merge_kernel, width),
        (shape(step_x.shape, bf16), shape(queries.shape, bf16)),
        [hbm] * 5,
        (hbm, hbm),
        [like(vmem, one) for one in (returned, own, own_sum, fade, local)]
        + [vmem((SUB, channels), f32), vmem((SUB, queries.shape[2]), f32)]
        + [like(vmem, step_x), like(vmem, queries), sems(5)],
        (0, 2 << 20),
    )(returned, own, own_sum, fade, local)
    return (prompt_out, jnp.swapaxes(mixer_out, 0, 1), jnp.swapaxes(attention_out, 0, 1))


def solution(mesh):
    in_specs = (
        P("groups", "heads", None),
        P("groups", None, None),
        P("groups", None, None),
        P("heads", "groups", None),
        P(),
        P(),
        P("groups"),
        P("groups", None),
        P("groups", None),
        P(("groups", "heads"), None, None),
        P("groups"),
        P(("groups", "heads"), None, None),
        P(("groups", "heads"), None, None),
        P(("groups", "heads"), None, None),
        P(("groups", "heads"), None, None),
        P(("groups", "heads"), None, None),
        P(("groups", "heads"), None, None),
    )
    out_specs = (
        P("groups", "heads", None),
        P(("groups", "heads"), None, None),
        P(("groups", "heads"), None, None),
    )
    return jax.shard_map(
        on_device, mesh=mesh, in_specs=in_specs, out_specs=out_specs, check_vma=False
    )
```

```python
import functools
import math

import jax
import jax.numpy as jnp
from jax import lax
from jax.experimental import pallas as pl
from jax.experimental.pallas import tpu as pltpu
from jax.sharding import PartitionSpec as P

NS = 256
HP = 64
HPG = 32
KVH = 8
HD = 128
PAGE = 16
PAGES = 16
LANES = 128
SUB = 8
HALF = 512
LEVELS = (128, 64, 32, 16)
LOG2E = math.log2(math.e)
SCORE = LOG2E / math.sqrt(HD)
NONE = -1e30
FLOOR = -1e29
PAIRS = 6
LENGTH_BITS = 10
AHEAD = 2
EARLY = 2
VMEM_LIMIT = 64 * 1024 * 1024

f32 = jnp.float32
bf16 = jnp.bfloat16


def iota(shape, dim):
    return lax.broadcasted_iota(jnp.int32, shape, dim)


def exchange_order(owners):
    first = owners // 2
    return [first] + [d for d in range(owners) if d != first]


def dot_nt(left, right):
    return lax.dot_general(left, right, (((1,), (1,)), ((), ())), preferred_element_type=f32)


def stack_rows(source, held):
    steps, rows = source.shape[0], source.shape[1]
    held[...] = jnp.zeros_like(held)
    for k in range(steps):
        held[k * rows : (k + 1) * rows, :] = source[k].astype(f32)


def spare(blocks, taken):
    return [(row, b) for row in range(PAIRS, SUB) for b in range(blocks)][taken : taken + PAIRS]


def lift(value, slots):
    row = iota(value.shape[:2] + (LANES,), 1)
    found = jnp.zeros(row.shape, f32)
    for pair, (at, b) in enumerate(slots):
        one = value[:, at : at + 1, b * LANES : (b + 1) * LANES]
        found = jnp.where(row == pair, jnp.broadcast_to(one, row.shape), found)
    return found


def fetches(pairs, sems, first=0):
    copies = [pltpu.make_async_copy(src, dst, sems.at[first + n]) for n, (src, dst) in enumerate(pairs)]
    for copy in copies:
        copy.start()
    return copies


def pack_kernel(group, ways, q_any, c_any, out_ref, q_ref, c_ref, q_held, c_held, rest, sems):
    owners = out_ref.shape[0] // SUB
    c_copy, q_copy = fetches([(c_any, c_ref), (q_any, q_ref)], sems)
    c_copy.wait()
    stack_rows(c_ref, c_held)
    span = 2 * HALF
    slots = spare(HALF // LANES + 1, 0)
    rest[...] = jnp.zeros_like(rest)
    for e in range(c_ref.shape[2] // NS):
        rest[e, :PAIRS, HALF:] = c_held[:PAIRS, e * NS : e * NS + LANES]
        for pair, (row, b) in enumerate(slots):
            rest[e, row : row + 1, b * LANES : (b + 1) * LANES] = c_held[
                pair : pair + 1, e * NS + LANES : (e + 1) * NS
            ]
    q_copy.wait()
    stack_rows(q_ref, q_held)
    real = iota((SUB, HALF), 0) < PAIRS
    order = exchange_order(owners)
    for rank in range(0, owners, 2):
        blocks, ends = [], []
        for d in order[rank : rank + 2]:
            begin, e = d // ways * span + d % 2 * HALF, (d * group) // HPG
            blocks.append(jnp.where(real, q_held[:, begin : begin + HALF], rest[e, :, :HALF]))
            ends.append(rest[e, :, HALF:])
        place = slice(rank * SUB, (rank + 2) * SUB)
        out_ref[place, :HALF] = jnp.concatenate(blocks, axis=0).astype(bf16)
        out_ref[place, HALF:] = jnp.concatenate(ends, axis=0).astype(bf16)


def sign_tables(signs, tail):
    length = signs.shape[-1]
    j = iota((length, length), 0)
    i = iota((length, length), 1)
    for l, n in enumerate(LEVELS):
        middle = (i // (2 * n)) * (2 * n) + (n - 1)
        signs[l] = (jnp.where(j <= i, 1.0, 0.0) - jnp.where(j <= middle, 1.0, 0.0)).astype(bf16)
    if tail:
        signs[len(LEVELS)] = jnp.where(j > i, 1.0, 0.0).astype(bf16)


def head_factors(first, dt_ref, rate_ref, skip_ref, len_ref, signs, w_in, w_out, w_skip, w_tail):
    group, prompts, length = dt_ref.shape
    row = iota((prompts, length), 0)
    lens = jnp.zeros((prompts, length), jnp.int32)
    for r in range(prompts):
        lens = jnp.where(row == r, len_ref[r], lens)
    valid = iota((prompts, length), 1) < lens
    moved = [jnp.where(valid, dt_ref[h].astype(f32), 0.0) for h in range(group)]
    every = jnp.concatenate(moved, axis=0).astype(bf16)
    rates = [rate_ref[first + h] * LOG2E for h in range(group)]
    if w_tail is not None:
        total = jnp.dot(every, signs[len(LEVELS)], preferred_element_type=f32)
        for h in range(group):
            part = total[h * prompts : (h + 1) * prompts]
            w_tail[:, h, :] = jnp.exp2(-(rates[h] * part)) * moved[h]
    for h in range(group):
        w_skip[:, h, :] = jnp.where(valid, skip_ref[first + h], 0.0)
    for l, n in enumerate(LEVELS):
        total = jnp.dot(every, signs[l], preferred_element_type=f32)
        for h in range(group):
            gap = rates[h] * total[h * prompts : (h + 1) * prompts]
            if n == LEVELS[-1]:
                up, down = jnp.exp2(gap), jnp.exp2(-gap)
            else:
                up, down = jnp.exp2(jnp.minimum(gap, 0.0)), jnp.exp2(-jnp.maximum(gap, 0.0))
            w_in[l, :, h, :] = up * moved[h]
            w_out[l, :, h, :] = jnp.where(valid, down, 0.0)


def level_masks(masks):
    length = masks.shape[-1]
    j = iota((length, length), 0)
    i = iota((length, length), 1)
    for l, n in enumerate(LEVELS):
        same = (j // (2 * n)) == (i // (2 * n))
        if n == LEVELS[-1]:
            keep = same & (j <= i)
        else:
            keep = same & ((j % (2 * n)) < n) & ((i % (2 * n)) >= n)
        masks[l] = jnp.where(keep, 1.0, 0.0).astype(bf16)


def prompt_result(r, x_held, b_held, c_held, w_in, w_out, w_skip, masks, out_held):
    width, length = x_held.shape[1], x_held.shape[2]
    group = width // HP
    half = length // 2
    inputs = x_held[r].astype(f32).reshape(group, HP, length)
    scores = dot_nt(b_held[r], c_held[r]).astype(bf16)
    total = inputs * w_skip[r][:, None, :]
    left, right = total[..., :half], total[..., half:]
    for l, n in enumerate(LEVELS):
        if 2 * n == length:
            scaled = (inputs[..., :half] * w_in[l, r][:, None, :half]).astype(bf16).reshape(width, half)
            added = jnp.dot(scaled, scores[:half, half:], preferred_element_type=f32)
            right = right + added.reshape(group, HP, half) * w_out[l, r][:, None, half:]
        else:
            scaled = (inputs * w_in[l, r][:, None, :]).astype(bf16).reshape(width, length)
            added = jnp.dot(scaled, scores * masks[l], preferred_element_type=f32)
            added = added.reshape(group, HP, length) * w_out[l, r][:, None, :]
            left = left + added[..., :half]
            right = right + added[..., half:]
    out_held[r] = jnp.concatenate([left, right], axis=-1).reshape(width, length).astype(bf16)


def state_kernel(
    rate_any,
    skip_any,
    len_any,
    owner_any,
    table_any,
    slot_any,
    dt_any,
    x_any,
    b_any,
    c_any,
    pages_any,
    other_any,
    state_any,
    key_any,
    value_any,
    code_any,
    out_any,
    x_held,
    b_held,
    c_held,
    out_held,
    w_in,
    w_out,
    w_skip,
    masks,
    signs,
    w_tail,
    state_held,
    pages_held,
    key_held,
    value_held,
    code_held,
    rate_ref,
    skip_ref,
    len_ref,
    owner_ref,
    table_ref,
    slot_ref,
    dt_ref,
    x_sem,
    b_sem,
    c_sem,
    out_sem,
    state_sem,
    sems,
):
    group, prompts, length = dt_ref.shape
    smalls = fetches(
        [
            (dt_any, dt_ref),
            (rate_any, rate_ref),
            (skip_any, skip_ref),
            (len_any, len_ref),
            (owner_any, owner_ref),
            (table_any, table_ref),
            (slot_any, slot_ref),
        ],
        sems,
    )
    me = lax.axis_index("heads")
    core = lax.rem(me, 2)
    first = me * group
    column = pl.multiple_of((first // HPG) * NS, NS)

    def x_copy(r):
        return pltpu.make_async_copy(x_any.at[r], x_held.at[r], x_sem.at[r])

    def b_copy(r):
        return pltpu.make_async_copy(b_any.at[r, :, pl.ds(column, NS)], b_held.at[r], b_sem.at[r])

    def c_copy(r):
        return pltpu.make_async_copy(c_any.at[r, :, pl.ds(column, NS)], c_held.at[r], c_sem.at[r])

    def out_copy(r):
        return pltpu.make_async_copy(out_held.at[r], out_any.at[r], out_sem.at[r])

    def state_copy(r):
        return pltpu.make_async_copy(state_held.at[r], state_any.at[r], state_sem.at[r])

    def ask(r):
        x_copy(r).start()
        b_copy(r).start()

    pages = fetches([(pages_any, pages_held.at[core]), (other_any, pages_held.at[1 - core])], sems, len(smalls))
    for r in range(prompts):
        ask(r)
    for r in range(EARLY):
        c_copy(r).start()
    sign_tables(signs, True)
    level_masks(masks)
    for copy in smalls:
        copy.wait()
    head_factors(first, dt_ref, rate_ref, skip_ref, len_ref, signs, w_in, w_out, w_skip, w_tail)

    width = x_held.shape[1]
    for begin in range(0, prompts, prompts // 2):
        some = range(begin, begin + prompts // 2)
        for r in some:
            x_copy(r).wait()
            b_copy(r).wait()
        for r in some:
            inputs = x_held[r].astype(f32).reshape(group, HP, length)
            scaled = (inputs * w_tail[r][:, None, :]).astype(bf16).reshape(width, length)
            state_held[r] = jnp.dot(scaled, b_held[r], preferred_element_type=f32).astype(bf16)
        for r in some:
            state_copy(r).start()
    spread = table_ref.shape[1] // owner_ref.shape[1]
    for copy in pages:
        copy.wait()
    for n in range(2):
        for r in range(prompts):
            for page in range(spread):
                holder = me - core + n
                row = table_ref[r, holder * spread + page] - holder * (prompts * spread)
                block = pages_held[n, row]
                place = pl.ds((n * spread + page) * PAGE, PAGE)
                columns = pl.ds(r % 2 * HD, HD)
                key_held[r // 2, place, columns] = block[:, :HD]
                value_held[r // 2, place, columns] = block[:, HD:]

    owners = owner_ref.shape[1]
    rows_dev = slot_ref.shape[0] // owners
    inner = iota((2 * SUB, LANES), 0)

    order = exchange_order(owners)
    for rank in range(0, owners, 2):
        block = jnp.zeros((2 * SUB, LANES), jnp.int32)
        for n in range(2):
            s = order[rank + n]
            for i in range(rows_dev):
                target = owner_ref[slot_ref[s * rows_dev + i], s]
                code = target * (1 << LENGTH_BITS) + len_ref[target]
                block = jnp.where((inner // SUB == n) & (inner % rows_dev == i), code, block)
        code_held[rank * SUB : (rank + 2) * SUB, :] = block
    marks = fetches([(key_held, key_any), (value_held, value_any), (code_held, code_any)], sems)

    for r in range(EARLY):
        c_copy(r).wait()
    for r in range(EARLY):
        prompt_result(r, x_held, b_held, c_held, w_in, w_out, w_skip, masks, out_held)
    for r in range(EARLY):
        out_copy(r).start()
    for copy in marks:
        copy.wait()
    for r in range(prompts):
        state_copy(r).wait()
    for r in range(EARLY):
        out_copy(r).wait()


def serve_kernel(
    recv_any,
    key_any,
    value_any,
    code_any,
    state_any,
    out_ref,
    recv_ref,
    key_ref,
    value_ref,
    code_ref,
    state_ref,
    query_ref,
    state_sem,
    sems,
):
    rows = recv_ref.shape[0]
    prompts, width = state_ref.shape[0], state_ref.shape[1]
    copies = fetches(
        [(recv_any, recv_ref), (code_any, code_ref), (key_any, key_ref), (value_any, value_ref)], sems
    )
    states = fetches([(state_any.at[r], state_ref.at[r]) for r in range(prompts)], state_sem)
    heads = HALF // HD
    keys = key_ref.shape[1]
    chips = keys // PAGE
    begin = lax.rem(lax.axis_index("heads") // 2 * chips, PAGES) * PAGE
    copies[0].wait()
    copies[1].wait()
    code = code_ref[...]
    target = code >> LENGTH_BITS
    lengths = code & ((1 << LENGTH_BITS) - 1)
    for r in range(prompts):
        for g in range(heads):
            query = recv_ref[:, g * HD : (g + 1) * HD].astype(f32)
            query_ref[r // 2, g * rows : (g + 1) * rows, r % 2 * HD : (r % 2 + 1) * HD] = jnp.where(
                target == r, query, 0.0
            ).astype(bf16)
    copies[2].wait()
    scores = jnp.zeros((heads * rows, keys), f32)
    for pair in range(prompts // 2):
        scores = scores + dot_nt(query_ref[pair], key_ref[pair])
    copies[3].wait()
    for copy in states:
        copy.wait()
    seen = jnp.concatenate([lengths[:, :1]] * heads, axis=0) > iota((heads * rows, keys), 1) + begin
    scores = jnp.where(seen, scores * SCORE, NONE)
    highest = jnp.maximum(jnp.max(scores, axis=1, keepdims=True), FLOOR)
    weight = jnp.exp2(scores - highest)
    total = jnp.sum(weight, axis=1, keepdims=True)
    some = total > 0.0
    safe = jnp.where(some, total, 1.0)
    result = jnp.where(some, highest + jnp.log2(safe), NONE)
    weight = weight.astype(bf16)
    targets = jnp.concatenate([target] * heads, axis=0)
    value = jnp.zeros((heads * rows, HD), f32)
    for pair in range(prompts // 2):
        both = jnp.dot(weight, value_ref[pair], preferred_element_type=f32)
        for n in range(2):
            value = jnp.where(targets == 2 * pair + n, both[:, n * HD : (n + 1) * HD], value)
    value = value / safe
    lane = iota((rows, LANES), 1)
    sums = jnp.zeros((rows, LANES), f32)
    for g in range(heads):
        sums = jnp.where(lane % 4 == g, result[g * rows : (g + 1) * rows], sums)
    high = sums.astype(bf16).astype(f32)
    rest = sums - high
    middle = rest.astype(bf16).astype(f32)
    piece = lane % 16 // 4
    pieces = jnp.where(piece == 0, high, jnp.where(piece == 1, middle, rest - middle))
    pair = iota((rows, LANES), 0) % SUB
    pieces = jnp.where((lane // 16 == pair) & (piece < 3), pieces, 0.0)
    packed = jnp.sum(pieces.reshape(rows // SUB, SUB, LANES), axis=1, keepdims=True)

    given = recv_ref[...].astype(f32).reshape(rows // SUB, SUB, recv_ref.shape[1])
    ending = lift(given, spare(heads + 1, 0))
    readout = jnp.concatenate([given[..., HALF:], ending], axis=-1).reshape(rows, NS)
    target = jnp.concatenate([target, target], axis=-1)
    found = jnp.zeros((rows, width), f32)
    for r in range(prompts):
        picked = jnp.where(target == r, readout, 0.0).astype(bf16)
        found = found + dot_nt(picked, state_ref[r])
    if width < LANES:
        found = jnp.concatenate([found, jnp.zeros((rows, LANES - width), f32)], axis=-1)
    blocks = [value[g * rows : (g + 1) * rows] for g in range(heads)]
    blocks += [found[:, b : b + LANES] for b in range(0, found.shape[1], LANES)]
    blocks = [one.reshape(rows // SUB, SUB, LANES) for one in blocks]
    row = iota((rows // SUB, SUB, LANES), 1)
    last = blocks.pop()
    blocks[0] = jnp.where(row == PAIRS, jnp.broadcast_to(packed, row.shape), blocks[0])
    for n, (at, b) in enumerate(spare(len(blocks), 1)):
        one = jnp.broadcast_to(last[:, n : n + 1, :], row.shape)
        blocks[b] = jnp.where(row == at, one, blocks[b])
    for b, one in enumerate(blocks):
        out_ref[:, b * LANES : (b + 1) * LANES] = one.reshape(rows, LANES).astype(bf16)


def prompt_kernel(
    rate_any,
    skip_any,
    len_any,
    dt_any,
    rates_any,
    skips_any,
    send_any,
    fresh_any,
    sx_any,
    sb_any,
    sc_any,
    sdt_any,
    x_any,
    b_any,
    c_any,
    after_any,
    early_any,
    out_any,
    own_any,
    ownsum_any,
    fade_any,
    local_any,
    x_held,
    b_held,
    c_held,
    out_held,
    w_in,
    w_out,
    w_skip,
    masks,
    signs,
    own_ref,
    ownsum_ref,
    fade_ref,
    local_ref,
    fresh_held,
    c_rows,
    x_rows,
    rate_ref,
    skip_ref,
    len_ref,
    dt_ref,
    rates_ref,
    skips_ref,
    send_ref,
    fresh_ref,
    sx_ref,
    sb_ref,
    sc_ref,
    sdt_ref,
    x_sem,
    b_sem,
    c_sem,
    out_sem,
    sems,
):
    group, prompts, length = dt_ref.shape
    smalls = fetches(
        [
            (dt_any, dt_ref),
            (rate_any, rate_ref),
            (skip_any, skip_ref),
            (len_any, len_ref),
            (rates_any, rates_ref),
            (skips_any, skips_ref),
            (send_any, send_ref),
            (fresh_any, fresh_ref),
            (sx_any, sx_ref),
            (sb_any, sb_ref),
            (sc_any, sc_ref),
            (sdt_any, sdt_ref),
        ],
        sems,
    )
    me = lax.axis_index("heads")
    first = me * group
    column = pl.multiple_of((first // HPG) * NS, NS)

    def x_copy(r):
        return pltpu.make_async_copy(x_any.at[r], x_held.at[r], x_sem.at[r])

    def b_copy(r):
        return pltpu.make_async_copy(b_any.at[r, :, pl.ds(column, NS)], b_held.at[r], b_sem.at[r])

    def c_copy(r):
        return pltpu.make_async_copy(c_any.at[r, :, pl.ds(column, NS)], c_held.at[r], c_sem.at[r])

    def out_copy(r):
        return pltpu.make_async_copy(out_held.at[r], out_any.at[r], out_sem.at[r])

    def ask(r):
        x_copy(r).start()
        b_copy(r).start()
        c_copy(r).start()

    for r in range(EARLY, min(EARLY + AHEAD, prompts)):
        ask(r)
    sign_tables(signs, False)
    level_masks(masks)
    for copy in smalls:
        copy.wait()
    head_factors(first, dt_ref, rate_ref, skip_ref, len_ref, signs, w_in, w_out, w_skip, None)
    own_attention(send_ref, fresh_ref, fresh_held, own_ref, ownsum_ref)
    own_mixer(rates_ref, skips_ref, sx_ref, sb_ref, sc_ref, sdt_ref, c_rows, x_rows, fade_ref, local_ref)
    outs = fetches(
        [(own_ref, own_any), (ownsum_ref, ownsum_any), (fade_ref, fade_any), (local_ref, local_any)], sems
    )

    def some(n, _):
        begin = EARLY + n * AHEAD

        @pl.when(begin + AHEAD < prompts)
        def _():
            for r in range(AHEAD):
                ask(begin + AHEAD + r)

        for r in range(AHEAD):
            x_copy(begin + r).wait()
            b_copy(begin + r).wait()
            c_copy(begin + r).wait()
        for r in range(AHEAD):
            prompt_result(begin + r, x_held, b_held, c_held, w_in, w_out, w_skip, masks, out_held)
        for r in range(AHEAD):
            out_copy(begin + r).start()
        return 0

    lax.fori_loop(0, (prompts - EARLY) // AHEAD, some, 0)
    for copy in outs:
        copy.wait()
    for r in range(EARLY, prompts):
        out_copy(r).wait()


def own_attention(send_ref, fresh_ref, fresh_held, own_ref, ownsum_ref):
    steps, rows = fresh_ref.shape[0], fresh_ref.shape[1]
    owners = send_ref.shape[0]
    order = exchange_order(owners)
    ways = owners // KVH
    stack_rows(fresh_ref, fresh_held)
    count = HALF // HD * 2 * SUB
    pair = iota((count, SUB), 0) % SUB
    key = iota((count, SUB), 1)
    seen = (key % rows == pair % rows) & (key <= pair) & (key < rows * steps)
    seen = seen | ((pair >= rows * steps) & (key == 0))
    for v in range(KVH):
        halves = [send_ref[order.index(v * ways + n), :, :HALF].astype(f32) for n in range(2)]
        parts = [half[:, g * HD : (g + 1) * HD] for g in range(HALF // HD) for half in halves]
        query = jnp.concatenate(parts, axis=0).astype(bf16)
        keys = fresh_held[:, v * HD : (v + 1) * HD].astype(bf16)
        values = fresh_held[:, (KVH + v) * HD : (KVH + v + 1) * HD].astype(bf16)
        scores = jnp.where(seen, dot_nt(query, keys) * SCORE, NONE)
        highest = jnp.max(scores, axis=1, keepdims=True)
        weight = jnp.exp2(scores - highest)
        total = jnp.sum(weight, axis=1, keepdims=True)
        weight = (weight / total).astype(bf16)
        own_ref[v] = jnp.dot(weight, values, preferred_element_type=f32)
        ownsum_ref[v] = jnp.broadcast_to(highest + jnp.log2(total), (count, HD))


def own_mixer(rates_ref, skips_ref, sx_ref, sb_ref, sc_ref, sdt_ref, c_rows, x_rows, fade_ref, local_ref):
    steps, rows, heads = sdt_ref.shape
    stack_rows(sc_ref, c_rows)
    for u in range(steps):
        given = sx_ref[u].astype(f32)
        for k in range(SUB // rows):
            x_rows[u, k * rows : (k + 1) * rows, :] = given
    pair = iota((SUB, heads), 0)
    step = pair // rows
    live = pair < rows * steps
    head = iota((SUB, heads), 1)

    def spread_rows(ref, u):
        given = ref[u].astype(f32)
        return jnp.concatenate([given] * (SUB // rows), axis=0)

    rates = jnp.broadcast_to(rates_ref[...], (SUB, heads)) * LOG2E
    skips = jnp.broadcast_to(skips_ref[...], (SUB, heads))
    moved = [spread_rows(sdt_ref, u) for u in range(steps)]
    kept = [jnp.where(u <= step, moved[u], 0.0) for u in range(steps)]
    parts = [jnp.where(live, jnp.exp2(-(rates * sum(kept))), 0.0)]
    for u in range(steps):
        products = c_rows[...] * spread_rows(sb_ref, u)
        inner = jnp.zeros((SUB, heads), f32)
        for e in range(products.shape[1] // NS):
            found = jnp.sum(products[:, e * NS : (e + 1) * NS], axis=1, keepdims=True)
            inner = jnp.where(head // HPG == e, found, inner)
        gap = jnp.zeros((SUB, heads), f32)
        for t in range(u + 1, steps):
            gap = gap + kept[t]
        weight = jnp.where(u <= step, jnp.exp2(-(rates * gap)) * moved[u] * inner, 0.0)
        weight = weight + jnp.where(u == step, skips, 0.0)
        parts.append(jnp.where(live, weight, 0.0))
    stacked = jnp.concatenate(parts, axis=0)
    high = stacked.astype(bf16)
    low = (stacked - high.astype(f32)).astype(bf16)
    both = jnp.concatenate([high.astype(f32), low.astype(f32)], axis=0)
    count = stacked.shape[0]
    chunk = SUB * HP
    widen = jnp.where(iota((heads, chunk), 0) % SUB == iota((heads, chunk), 1) // HP, 1.0, 0.0).astype(bf16)
    lane = iota(both.shape, 1)
    for d in range(heads // SUB):
        picked = jnp.where(lane // SUB == d, both, 0.0).astype(bf16)
        wide = jnp.dot(picked, widen, preferred_element_type=f32)
        wide = wide[:count] + wide[count:]
        columns = slice(d * chunk, (d + 1) * chunk)
        fade_ref[:, columns] = wide[:SUB]
        value = jnp.zeros((SUB, chunk), f32)
        for u in range(steps):
            value = value + wide[(u + 1) * SUB : (u + 2) * SUB] * x_rows[u, :, columns]
        local_ref[:, columns] = value


def merge_kernel(
    width,
    back_any,
    own_any,
    ownsum_any,
    fade_any,
    local_any,
    mixer_any,
    attention_any,
    back_ref,
    own_ref,
    ownsum_ref,
    fade_ref,
    local_ref,
    mixed,
    attended,
    mixer_ref,
    attention_ref,
    sems,
):
    copies = fetches([(back_any, back_ref), (fade_any, fade_ref), (local_any, local_ref)], sems)
    rest = fetches([(own_any, own_ref), (ownsum_any, ownsum_ref)], sems, len(copies))
    for copy in copies:
        copy.wait()
    owners = back_ref.shape[0]
    ways = owners // KVH
    order = exchange_order(owners)
    steps, rows = mixer_ref.shape[0], mixer_ref.shape[1]
    for d in range(0, owners, 2):
        block = jnp.stack([back_ref[order.index(d + n)].astype(f32) for n in range(2)])
        ending = lift(block, spare(back_ref.shape[2] // LANES, 1))
        if back_ref.shape[2] > HALF:
            ending = jnp.concatenate([block[..., HALF:], ending], axis=-1)
        found = ending[..., :width]
        found = jnp.concatenate([found[0], found[1]], axis=-1)
        columns = slice(d * width, (d + 2) * width)
        mixed[:, columns] = found * fade_ref[:, columns] + local_ref[:, columns]
    for k in range(steps):
        mixer_ref[k] = mixed[k * rows : (k + 1) * rows, :].astype(bf16)
    outs = fetches([(mixer_ref, mixer_any)], sems)
    for copy in rest:
        copy.wait()
    lane = iota((2, SUB, LANES), 2)
    mine = (lane // 16 == iota((2, SUB, LANES), 1)) & (lane % 16 < 12)
    for v in range(KVH):
        blocks, pieces = [], []
        for d in range(v * ways, (v + 1) * ways, 2):
            block = jnp.stack([back_ref[order.index(d + n), :, :HALF].astype(f32) for n in range(2)])
            packed = block[:, PAIRS : PAIRS + 1, :LANES]
            blocks.append(block.reshape(2 * SUB, HALF))
            pieces.append(jnp.where(mine, jnp.broadcast_to(packed, (2, SUB, LANES)), 0.0))
        for g in range(HALF // HD):
            part = slice(g * 2 * SUB, (g + 1) * 2 * SUB)
            own_sum = ownsum_ref[v, part, :]
            wide = []
            for piece in pieces:
                one = jnp.sum(jnp.where(lane % 4 == g, piece, 0.0), axis=-1, keepdims=True)
                wide.append(jnp.broadcast_to(one, (2, SUB, HD)).reshape(2 * SUB, HD))
            highest = functools.reduce(jnp.maximum, wide, own_sum)
            weight = jnp.exp2(own_sum - highest)
            total = weight
            value = weight * own_ref[v, part, :]
            for one, block in zip(wide, blocks):
                weight = jnp.exp2(one - highest)
                total = total + weight
                value = value + weight * block[:, g * HD : (g + 1) * HD]
            value = value / total
            start = v * 2 * HALF + g * HD
            attended[:, start : start + HD] = value[:SUB]
            attended[:, start + HALF : start + HALF + HD] = value[SUB:]
    for k in range(steps):
        attention_ref[k] = attended[k * rows : (k + 1) * rows, :].astype(bf16)
    outs += fetches([(attention_ref, attention_any)], sems, 1)
    for copy in outs:
        copy.wait()


def call(kernel, out_shape, in_spaces, out_spaces, scratch, cost, aliases=None):
    def spec(space):
        return pl.BlockSpec(memory_space=space)

    return pl.pallas_call(
        kernel,
        out_shape=out_shape,
        in_specs=[spec(space) for space in in_spaces],
        out_specs=jax.tree.map(spec, out_spaces),
        scratch_shapes=scratch,
        input_output_aliases=aliases or {},
        compiler_params=pltpu.CompilerParams(vmem_limit_bytes=VMEM_LIMIT),
        cost_estimate=pl.CostEstimate(flops=cost[0], bytes_accessed=cost[1], transcendentals=0),
    )


def on_device(
    prompt_x,
    prompt_b,
    prompt_c,
    prompt_dt,
    decay_rate,
    skip_gain,
    lengths,
    owner_list,
    page_table,
    cache_pages,
    row_slot,
    step_x,
    step_b,
    step_c,
    step_dt,
    queries,
    fresh_cache,
):
    owners = lax.axis_size("heads")
    ways = owners // KVH
    group, prompts, length = prompt_dt.shape
    width = prompt_x.shape[1]
    keys = cache_pages.shape[0] * PAGE
    span = 2 * keys // prompts
    steps = step_x.shape[1]
    all_rows = owners * SUB
    shape = jax.ShapeDtypeStruct
    smem, vmem, hbm = pltpu.SMEM, pltpu.VMEM, pltpu.HBM
    sem = pltpu.SemaphoreType.DMA((prompts,))
    levels = len(LEVELS)
    step_x, step_b, step_c, step_dt, queries, fresh_cache = (
        jnp.swapaxes(one, 0, 1) for one in (step_x, step_b, step_c, step_dt, queries, fresh_cache)
    )
    owner_list = owner_list.T

    def like(space, array):
        return space(array.shape, array.dtype)

    def sems(count):
        return pltpu.SemaphoreType.DMA((count,))

    other_pages = lax.ppermute(cache_pages, "heads", [(d, d + 1 - 2 * (d % 2)) for d in range(owners)])
    send = call(
        functools.partial(pack_kernel, group, ways),
        shape((all_rows, HALF + LANES), bf16),
        [hbm, hbm],
        vmem,
        [
            like(vmem, queries),
            like(vmem, step_c),
            vmem((SUB, queries.shape[2]), f32),
            vmem((SUB, step_c.shape[2]), f32),
            vmem((step_c.shape[2] // NS, SUB, HALF + LANES), f32),
            sems(2),
        ],
        (0, 1 << 19),
    )(queries, step_c)
    order = [exchange_order(owners)]
    recv = lax.all_to_all(
        send, "heads", split_axis=0, concat_axis=0, tiled=True, axis_index_groups=order
    )

    block = [
        vmem((prompts, width, length), bf16),
        vmem((prompts, length, NS), bf16),
        vmem((prompts, length, NS), bf16),
        vmem((prompts, width, length), bf16),
        vmem((levels, prompts, group, length), f32),
        vmem((levels, prompts, group, length), f32),
        vmem((prompts, group, length), f32),
    ]
    tables = [vmem((levels, length, length), bf16), vmem((levels + 1, length, length), bf16)]
    work = 2 * width * length * NS
    states, sorted_keys, sorted_values, codes, early_out = call(
        state_kernel,
        (
            shape((prompts, width, NS), bf16),
            shape((prompts // 2, span, 2 * HD), bf16),
            shape((prompts // 2, span, 2 * HD), bf16),
            shape((all_rows, LANES), jnp.int32),
            shape(prompt_x.shape, bf16),
        ),
        [hbm] * 12,
        (hbm,) * 5,
        block
        + tables
        + [vmem((prompts, group, length), f32), vmem((prompts, width, NS), bf16)]
        + [vmem((2,) + cache_pages.shape, bf16)]
        + [vmem((prompts // 2, span, 2 * HD), bf16)] * 2
        + [vmem((all_rows, LANES), jnp.int32)]
        + [like(smem, one) for one in (decay_rate, skip_gain, lengths, owner_list, page_table, row_slot)]
        + [like(vmem, prompt_dt), sem, sem, sem, sem, sem, sems(9)],
        (work * (prompts + 5 * EARLY), 6 << 20),
    )(
        decay_rate,
        skip_gain,
        lengths,
        owner_list,
        page_table,
        row_slot,
        prompt_dt,
        prompt_x,
        prompt_b,
        prompt_c,
        cache_pages,
        other_pages,
    )

    back = call(
        serve_kernel,
        shape((all_rows, HALF + max(LANES, width) - LANES), bf16),
        [hbm] * 5,
        vmem,
        [like(vmem, one) for one in (recv, sorted_keys, sorted_values, codes, states)]
        + [vmem((prompts // 2, HALF // HD * all_rows, 2 * HD), bf16), sem, sems(4)],
        (8 * all_rows * keys * HD, 4 << 20),
    )(recv, sorted_keys, sorted_values, codes, states)
    returned = lax.all_to_all(
        back, "heads", split_axis=0, concat_axis=0, tiled=True, axis_index_groups=order
    ).reshape(owners, SUB, back.shape[1])

    count = HALF // HD * 2 * SUB
    channels = step_x.shape[2]
    rates, skips = decay_rate.reshape(1, -1), skip_gain.reshape(1, -1)
    prompt_out, own, own_sum, fade, local = call(
        prompt_kernel,
        (
            shape(prompt_x.shape, bf16),
            shape((KVH, count, HD), f32),
            shape((KVH, count, HD), f32),
            shape((SUB, channels), f32),
            shape((SUB, channels), f32),
        ),
        [hbm] * 17,
        (hbm,) * 5,
        block
        + tables
        + [
            vmem((KVH, count, HD), f32),
            vmem((KVH, count, HD), f32),
            vmem((SUB, channels), f32),
            vmem((SUB, channels), f32),
            vmem((SUB, fresh_cache.shape[2]), f32),
            vmem((SUB, step_c.shape[2]), f32),
            vmem((steps, SUB, channels), f32),
            like(smem, decay_rate),
            like(smem, skip_gain),
            like(smem, lengths),
            like(vmem, prompt_dt),
            like(vmem, rates),
            like(vmem, skips),
            vmem((owners, SUB, HALF + LANES), bf16),
            like(vmem, fresh_cache),
            like(vmem, step_x),
            like(vmem, step_b),
            like(vmem, step_c),
            like(vmem, step_dt),
            sem,
            sem,
            sem,
            sem,
            sems(12),
        ],
        (work * 5 * (prompts - EARLY), 8 << 20),
        {16: 0},
    )(
        decay_rate,
        skip_gain,
        lengths,
        prompt_dt,
        rates,
        skips,
        send.reshape(owners, SUB, HALF + LANES),
        fresh_cache,
        step_x,
        step_b,
        step_c,
        step_dt,
        prompt_x,
        prompt_b,
        prompt_c,
        back,
        early_out,
    )

    mixer_out, attention_out = call(
        functools.partial(merge_kernel, width),
        (shape(step_x.shape, bf16), shape(queries.shape, bf16)),
        [hbm] * 5,
        (hbm, hbm),
        [like(vmem, one) for one in (returned, own, own_sum, fade, local)]
        + [vmem((SUB, channels), f32), vmem((SUB, queries.shape[2]), f32)]
        + [like(vmem, step_x), like(vmem, queries), sems(5)],
        (0, 2 << 20),
    )(returned, own, own_sum, fade, local)
    return (prompt_out, jnp.swapaxes(mixer_out, 0, 1), jnp.swapaxes(attention_out, 0, 1))


def solution(mesh):
    in_specs = (
        P("groups", "heads", None),
        P("groups", None, None),
        P("groups", None, None),
        P("heads", "groups", None),
        P(),
        P(),
        P("groups"),
        P("groups", None),
        P("groups", None),
        P(("groups", "heads"), None, None),
        P("groups"),
        P(("groups", "heads"), None, None),
        P(("groups", "heads"), None, None),
        P(("groups", "heads"), None, None),
        P(("groups", "heads"), None, None),
        P(("groups", "heads"), None, None),
        P(("groups", "heads"), None, None),
    )
    out_specs = (
        P("groups", "heads", None),
        P(("groups", "heads"), None, None),
        P(("groups", "heads"), None, None),
    )
    return jax.shard_map(
        on_device, mesh=mesh, in_specs=in_specs, out_specs=out_specs, check_vma=False
    )
```

```python
import functools
import math

import jax
import jax.numpy as jnp
from jax import lax
from jax.experimental import pallas as pl
from jax.experimental.pallas import tpu as pltpu
from jax.sharding import PartitionSpec as P

NS = 256
HP = 64
HPG = 32
KVH = 8
HD = 128
PAGE = 16
PAGES = 16
LANES = 128
SUB = 8
HALF = 512
LEVELS = (128, 64, 32, 16)
LOG2E = math.log2(math.e)
SCORE = LOG2E / math.sqrt(HD)
NONE = -1e30
FLOOR = -1e29
PAIRS = 6
LENGTH_BITS = 10
AHEAD = 2
EARLY = 2
VMEM_LIMIT = 64 * 1024 * 1024

f32 = jnp.float32
bf16 = jnp.bfloat16


def iota(shape, dim):
    return lax.broadcasted_iota(jnp.int32, shape, dim)


def exchange_order(owners):
    first = owners // 2
    return [first] + [d for d in range(owners) if d != first]


def dot_nt(left, right):
    return lax.dot_general(left, right, (((1,), (1,)), ((), ())), preferred_element_type=f32)


def stack_rows(source, held):
    steps, rows = source.shape[0], source.shape[1]
    held[...] = jnp.zeros_like(held)
    for k in range(steps):
        held[k * rows : (k + 1) * rows, :] = source[k].astype(f32)


def spare(blocks, taken):
    return [(row, b) for row in range(PAIRS, SUB) for b in range(blocks)][taken : taken + PAIRS]


def lift(value, slots):
    row = iota(value.shape[:2] + (LANES,), 1)
    found = jnp.zeros(row.shape, f32)
    for pair, (at, b) in enumerate(slots):
        one = value[:, at : at + 1, b * LANES : (b + 1) * LANES]
        found = jnp.where(row == pair, jnp.broadcast_to(one, row.shape), found)
    return found


def fetches(pairs, sems, first=0):
    copies = [pltpu.make_async_copy(src, dst, sems.at[first + n]) for n, (src, dst) in enumerate(pairs)]
    for copy in copies:
        copy.start()
    return copies


def pack_kernel(group, ways, q_any, c_any, out_ref, q_ref, c_ref, q_held, c_held, rest, sems):
    owners = out_ref.shape[0] // SUB
    c_copy, q_copy = fetches([(c_any, c_ref), (q_any, q_ref)], sems)
    c_copy.wait()
    stack_rows(c_ref, c_held)
    span = 2 * HALF
    slots = spare(HALF // LANES + 1, 0)
    rest[...] = jnp.zeros_like(rest)
    for e in range(c_ref.shape[2] // NS):
        rest[e, :PAIRS, HALF:] = c_held[:PAIRS, e * NS : e * NS + LANES]
        for pair, (row, b) in enumerate(slots):
            rest[e, row : row + 1, b * LANES : (b + 1) * LANES] = c_held[
                pair : pair + 1, e * NS + LANES : (e + 1) * NS
            ]
    q_copy.wait()
    stack_rows(q_ref, q_held)
    real = iota((SUB, HALF), 0) < PAIRS
    order = exchange_order(owners)
    for rank in range(0, owners, 2):
        blocks, ends = [], []
        for d in order[rank : rank + 2]:
            begin, e = d // ways * span + d % 2 * HALF, (d * group) // HPG
            blocks.append(jnp.where(real, q_held[:, begin : begin + HALF], rest[e, :, :HALF]))
            ends.append(rest[e, :, HALF:])
        place = slice(rank * SUB, (rank + 2) * SUB)
        out_ref[place, :HALF] = jnp.concatenate(blocks, axis=0).astype(bf16)
        out_ref[place, HALF:] = jnp.concatenate(ends, axis=0).astype(bf16)


def sign_tables(signs, tail):
    length = signs.shape[-1]
    j = iota((length, length), 0)
    i = iota((length, length), 1)
    for l, n in enumerate(LEVELS):
        middle = (i // (2 * n)) * (2 * n) + (n - 1)
        signs[l] = (jnp.where(j <= i, 1.0, 0.0) - jnp.where(j <= middle, 1.0, 0.0)).astype(bf16)
    if tail:
        signs[len(LEVELS)] = jnp.where(j > i, 1.0, 0.0).astype(bf16)


def head_factors(first, dt_ref, rate_ref, skip_ref, len_ref, signs, w_in, w_out, w_skip, w_tail):
    group, prompts, length = dt_ref.shape
    row = iota((prompts, length), 0)
    lens = jnp.zeros((prompts, length), jnp.int32)
    for r in range(prompts):
        lens = jnp.where(row == r, len_ref[r], lens)
    valid = iota((prompts, length), 1) < lens
    moved = [jnp.where(valid, dt_ref[h].astype(f32), 0.0) for h in range(group)]
    every = jnp.concatenate(moved, axis=0).astype(bf16)
    rates = [rate_ref[first + h] * LOG2E for h in range(group)]
    if w_tail is not None:
        total = jnp.dot(every, signs[len(LEVELS)], preferred_element_type=f32)
        for h in range(group):
            part = total[h * prompts : (h + 1) * prompts]
            w_tail[:, h, :] = jnp.exp2(-(rates[h] * part)) * moved[h]
    for h in range(group):
        w_skip[:, h, :] = jnp.where(valid, skip_ref[first + h], 0.0)
    for l, n in enumerate(LEVELS):
        total = jnp.dot(every, signs[l], preferred_element_type=f32)
        for h in range(group):
            gap = rates[h] * total[h * prompts : (h + 1) * prompts]
            if n == LEVELS[-1]:
                up, down = jnp.exp2(gap), jnp.exp2(-gap)
            else:
                up, down = jnp.exp2(jnp.minimum(gap, 0.0)), jnp.exp2(-jnp.maximum(gap, 0.0))
            w_in[l, :, h, :] = up * moved[h]
            w_out[l, :, h, :] = jnp.where(valid, down, 0.0)


def level_masks(masks):
    length = masks.shape[-1]
    j = iota((length, length), 0)
    i = iota((length, length), 1)
    for l, n in enumerate(LEVELS):
        same = (j // (2 * n)) == (i // (2 * n))
        if n == LEVELS[-1]:
            keep = same & (j <= i)
        else:
            keep = same & ((j % (2 * n)) < n) & ((i % (2 * n)) >= n)
        masks[l] = jnp.where(keep, 1.0, 0.0).astype(bf16)


def prompt_result(r, x_held, b_held, c_held, w_in, w_out, w_skip, masks, out_held):
    width, length = x_held.shape[1], x_held.shape[2]
    group = width // HP
    half = length // 2
    inputs = x_held[r].astype(f32).reshape(group, HP, length)
    scores = dot_nt(b_held[r], c_held[r]).astype(bf16)
    total = inputs * w_skip[r][:, None, :]
    left, right = total[..., :half], total[..., half:]
    for l, n in enumerate(LEVELS):
        if 2 * n == length:
            scaled = (inputs[..., :half] * w_in[l, r][:, None, :half]).astype(bf16).reshape(width, half)
            added = jnp.dot(scaled, scores[:half, half:], preferred_element_type=f32)
            right = right + added.reshape(group, HP, half) * w_out[l, r][:, None, half:]
        else:
            scaled = (inputs * w_in[l, r][:, None, :]).astype(bf16).reshape(width, length)
            added = jnp.dot(scaled, scores * masks[l], preferred_element_type=f32)
            added = added.reshape(group, HP, length) * w_out[l, r][:, None, :]
            left = left + added[..., :half]
            right = right + added[..., half:]
    out_held[r] = jnp.concatenate([left, right], axis=-1).reshape(width, length).astype(bf16)


def state_kernel(
    rate_any,
    skip_any,
    len_any,
    owner_any,
    table_any,
    slot_any,
    dt_any,
    x_any,
    b_any,
    c_any,
    pages_any,
    other_any,
    state_any,
    key_any,
    value_any,
    code_any,
    out_any,
    x_held,
    b_held,
    c_held,
    out_held,
    w_in,
    w_out,
    w_skip,
    masks,
    signs,
    w_tail,
    state_held,
    pages_held,
    key_held,
    value_held,
    code_held,
    rate_ref,
    skip_ref,
    len_ref,
    owner_ref,
    table_ref,
    slot_ref,
    dt_ref,
    x_sem,
    b_sem,
    c_sem,
    out_sem,
    state_sem,
    sems,
):
    group, prompts, length = dt_ref.shape
    smalls = fetches(
        [
            (dt_any, dt_ref),
            (rate_any, rate_ref),
            (skip_any, skip_ref),
            (len_any, len_ref),
            (owner_any, owner_ref),
            (table_any, table_ref),
            (slot_any, slot_ref),
        ],
        sems,
    )
    me = lax.axis_index("heads")
    core = lax.rem(me, 2)
    first = me * group
    column = pl.multiple_of((first // HPG) * NS, NS)

    def x_copy(r):
        return pltpu.make_async_copy(x_any.at[r], x_held.at[r], x_sem.at[r])

    def b_copy(r):
        return pltpu.make_async_copy(b_any.at[r, :, pl.ds(column, NS)], b_held.at[r], b_sem.at[r])

    def c_copy(r):
        return pltpu.make_async_copy(c_any.at[r, :, pl.ds(column, NS)], c_held.at[r], c_sem.at[r])

    def out_copy(r):
        return pltpu.make_async_copy(out_held.at[r], out_any.at[r], out_sem.at[r])

    def state_copy(r):
        return pltpu.make_async_copy(state_held.at[r], state_any.at[r], state_sem.at[r])

    def ask(r):
        x_copy(r).start()
        b_copy(r).start()

    pages = fetches([(pages_any, pages_held.at[core]), (other_any, pages_held.at[1 - core])], sems, len(smalls))
    for r in range(prompts):
        ask(r)
    for r in range(EARLY):
        c_copy(r).start()
    sign_tables(signs, True)
    level_masks(masks)
    for copy in smalls:
        copy.wait()
    head_factors(first, dt_ref, rate_ref, skip_ref, len_ref, signs, w_in, w_out, w_skip, w_tail)

    width = x_held.shape[1]
    for begin in range(0, prompts, prompts // 2):
        some = range(begin, begin + prompts // 2)
        for r in some:
            x_copy(r).wait()
            b_copy(r).wait()
        for r in some:
            inputs = x_held[r].astype(f32).reshape(group, HP, length)
            scaled = (inputs * w_tail[r][:, None, :]).astype(bf16).reshape(width, length)
            state_held[r] = jnp.dot(scaled, b_held[r], preferred_element_type=f32).astype(bf16)
        for r in some:
            state_copy(r).start()
    spread = table_ref.shape[1] // owner_ref.shape[1]
    for copy in pages:
        copy.wait()
    for n in range(2):
        for r in range(prompts):
            for page in range(spread):
                holder = me - core + n
                row = table_ref[r, holder * spread + page] - holder * (prompts * spread)
                block = pages_held[n, row]
                place = pl.ds((n * spread + page) * PAGE, PAGE)
                columns = pl.ds(r % 2 * HD, HD)
                key_held[r // 2, place, columns] = block[:, :HD]
                value_held[r // 2, place, columns] = block[:, HD:]

    owners = owner_ref.shape[1]
    rows_dev = slot_ref.shape[0] // owners
    inner = iota((2 * SUB, LANES), 0)

    order = exchange_order(owners)
    for rank in range(0, owners, 2):
        block = jnp.zeros((2 * SUB, LANES), jnp.int32)
        for n in range(2):
            s = order[rank + n]
            for i in range(rows_dev):
                target = owner_ref[slot_ref[s * rows_dev + i], s]
                code = target * (1 << LENGTH_BITS) + len_ref[target]
                block = jnp.where((inner // SUB == n) & (inner % rows_dev == i), code, block)
        code_held[rank * SUB : (rank + 2) * SUB, :] = block
    marks = fetches([(key_held, key_any), (value_held, value_any), (code_held, code_any)], sems)

    for r in range(EARLY):
        c_copy(r).wait()
    for r in range(EARLY):
        prompt_result(r, x_held, b_held, c_held, w_in, w_out, w_skip, masks, out_held)
    for r in range(EARLY):
        out_copy(r).start()
    for copy in marks:
        copy.wait()
    for r in range(prompts):
        state_copy(r).wait()
    for r in range(EARLY):
        out_copy(r).wait()


def serve_kernel(
    recv_any,
    key_any,
    value_any,
    code_any,
    state_any,
    out_ref,
    recv_ref,
    key_ref,
    value_ref,
    code_ref,
    state_ref,
    query_ref,
    state_sem,
    sems,
):
    rows = recv_ref.shape[0]
    prompts, width = state_ref.shape[0], state_ref.shape[1]
    copies = fetches(
        [(recv_any, recv_ref), (code_any, code_ref), (key_any, key_ref), (value_any, value_ref)], sems
    )
    states = fetches([(state_any.at[r], state_ref.at[r]) for r in range(prompts)], state_sem)
    heads = HALF // HD
    keys = key_ref.shape[1]
    chips = keys // PAGE
    begin = lax.rem(lax.axis_index("heads") // 2 * chips, PAGES) * PAGE
    copies[0].wait()
    copies[1].wait()
    code = code_ref[...]
    target = code >> LENGTH_BITS
    lengths = code & ((1 << LENGTH_BITS) - 1)
    for r in range(prompts):
        for g in range(heads):
            query = recv_ref[:, g * HD : (g + 1) * HD].astype(f32)
            query_ref[r // 2, g * rows : (g + 1) * rows, r % 2 * HD : (r % 2 + 1) * HD] = jnp.where(
                target == r, query, 0.0
            ).astype(bf16)
    copies[2].wait()
    scores = jnp.zeros((heads * rows, keys), f32)
    for pair in range(prompts // 2):
        scores = scores + dot_nt(query_ref[pair], key_ref[pair])
    copies[3].wait()
    for copy in states[: prompts // 2]:
        copy.wait()
    seen = jnp.concatenate([lengths[:, :1]] * heads, axis=0) > iota((heads * rows, keys), 1) + begin
    scores = jnp.where(seen, scores * SCORE, NONE)
    highest = jnp.maximum(jnp.max(scores, axis=1, keepdims=True), FLOOR)
    weight = jnp.exp2(scores - highest)
    total = jnp.sum(weight, axis=1, keepdims=True)
    some = total > 0.0
    safe = jnp.where(some, total, 1.0)
    result = jnp.where(some, highest + jnp.log2(safe), NONE)
    weight = weight.astype(bf16)
    targets = jnp.concatenate([target] * heads, axis=0)
    value = jnp.zeros((heads * rows, HD), f32)
    for pair in range(prompts // 2):
        both = jnp.dot(weight, value_ref[pair], preferred_element_type=f32)
        for n in range(2):
            value = jnp.where(targets == 2 * pair + n, both[:, n * HD : (n + 1) * HD], value)
    value = value / safe
    lane = iota((rows, LANES), 1)
    sums = jnp.zeros((rows, LANES), f32)
    for g in range(heads):
        sums = jnp.where(lane % 4 == g, result[g * rows : (g + 1) * rows], sums)
    high = sums.astype(bf16).astype(f32)
    rest = sums - high
    middle = rest.astype(bf16).astype(f32)
    piece = lane % 16 // 4
    pieces = jnp.where(piece == 0, high, jnp.where(piece == 1, middle, rest - middle))
    pair = iota((rows, LANES), 0) % SUB
    pieces = jnp.where((lane // 16 == pair) & (piece < 3), pieces, 0.0)
    packed = jnp.sum(pieces.reshape(rows // SUB, SUB, LANES), axis=1, keepdims=True)

    given = recv_ref[...].astype(f32).reshape(rows // SUB, SUB, recv_ref.shape[1])
    ending = lift(given, spare(heads + 1, 0))
    readout = jnp.concatenate([given[..., HALF:], ending], axis=-1).reshape(rows, NS)
    target = jnp.concatenate([target, target], axis=-1)
    found = jnp.zeros((rows, width), f32)
    for r in range(prompts):
        if r >= prompts // 2:
            states[r].wait()
        picked = jnp.where(target == r, readout, 0.0).astype(bf16)
        found = found + dot_nt(picked, state_ref[r])
    if width < LANES:
        found = jnp.concatenate([found, jnp.zeros((rows, LANES - width), f32)], axis=-1)
    blocks = [value[g * rows : (g + 1) * rows] for g in range(heads)]
    blocks += [found[:, b : b + LANES] for b in range(0, found.shape[1], LANES)]
    blocks = [one.reshape(rows // SUB, SUB, LANES) for one in blocks]
    row = iota((rows // SUB, SUB, LANES), 1)
    last = blocks.pop()
    blocks[0] = jnp.where(row == PAIRS, jnp.broadcast_to(packed, row.shape), blocks[0])
    for n, (at, b) in enumerate(spare(len(blocks), 1)):
        one = jnp.broadcast_to(last[:, n : n + 1, :], row.shape)
        blocks[b] = jnp.where(row == at, one, blocks[b])
    for b, one in enumerate(blocks):
        out_ref[:, b * LANES : (b + 1) * LANES] = one.reshape(rows, LANES).astype(bf16)


def prompt_kernel(
    rate_any,
    skip_any,
    len_any,
    dt_any,
    rates_any,
    skips_any,
    send_any,
    fresh_any,
    sx_any,
    sb_any,
    sc_any,
    sdt_any,
    x_any,
    b_any,
    c_any,
    after_any,
    early_any,
    out_any,
    own_any,
    ownsum_any,
    fade_any,
    local_any,
    x_held,
    b_held,
    c_held,
    out_held,
    w_in,
    w_out,
    w_skip,
    masks,
    signs,
    own_ref,
    ownsum_ref,
    fade_ref,
    local_ref,
    fresh_held,
    c_rows,
    x_rows,
    rate_ref,
    skip_ref,
    len_ref,
    dt_ref,
    rates_ref,
    skips_ref,
    send_ref,
    fresh_ref,
    sx_ref,
    sb_ref,
    sc_ref,
    sdt_ref,
    x_sem,
    b_sem,
    c_sem,
    out_sem,
    sems,
):
    group, prompts, length = dt_ref.shape
    smalls = fetches(
        [
            (dt_any, dt_ref),
            (rate_any, rate_ref),
            (skip_any, skip_ref),
            (len_any, len_ref),
            (rates_any, rates_ref),
            (skips_any, skips_ref),
            (send_any, send_ref),
            (fresh_any, fresh_ref),
            (sx_any, sx_ref),
            (sb_any, sb_ref),
            (sc_any, sc_ref),
            (sdt_any, sdt_ref),
        ],
        sems,
    )
    me = lax.axis_index("heads")
    first = me * group
    column = pl.multiple_of((first // HPG) * NS, NS)

    def x_copy(r):
        return pltpu.make_async_copy(x_any.at[r], x_held.at[r], x_sem.at[r])

    def b_copy(r):
        return pltpu.make_async_copy(b_any.at[r, :, pl.ds(column, NS)], b_held.at[r], b_sem.at[r])

    def c_copy(r):
        return pltpu.make_async_copy(c_any.at[r, :, pl.ds(column, NS)], c_held.at[r], c_sem.at[r])

    def out_copy(r):
        return pltpu.make_async_copy(out_held.at[r], out_any.at[r], out_sem.at[r])

    def ask(r):
        x_copy(r).start()
        b_copy(r).start()
        c_copy(r).start()

    for r in range(EARLY, min(EARLY + AHEAD, prompts)):
        ask(r)
    sign_tables(signs, False)
    level_masks(masks)
    for copy in smalls:
        copy.wait()
    head_factors(first, dt_ref, rate_ref, skip_ref, len_ref, signs, w_in, w_out, w_skip, None)
    own_attention(send_ref, fresh_ref, fresh_held, own_ref, ownsum_ref)
    own_mixer(rates_ref, skips_ref, sx_ref, sb_ref, sc_ref, sdt_ref, c_rows, x_rows, fade_ref, local_ref)
    outs = fetches(
        [(own_ref, own_any), (ownsum_ref, ownsum_any), (fade_ref, fade_any), (local_ref, local_any)], sems
    )

    def some(n, _):
        begin = EARLY + n * AHEAD

        @pl.when(begin + AHEAD < prompts)
        def _():
            for r in range(AHEAD):
                ask(begin + AHEAD + r)

        for r in range(AHEAD):
            x_copy(begin + r).wait()
            b_copy(begin + r).wait()
            c_copy(begin + r).wait()
        for r in range(AHEAD):
            prompt_result(begin + r, x_held, b_held, c_held, w_in, w_out, w_skip, masks, out_held)
        for r in range(AHEAD):
            out_copy(begin + r).start()
        return 0

    lax.fori_loop(0, (prompts - EARLY) // AHEAD, some, 0)
    for copy in outs:
        copy.wait()
    for r in range(EARLY, prompts):
        out_copy(r).wait()


def own_attention(send_ref, fresh_ref, fresh_held, own_ref, ownsum_ref):
    steps, rows = fresh_ref.shape[0], fresh_ref.shape[1]
    owners = send_ref.shape[0]
    order = exchange_order(owners)
    ways = owners // KVH
    stack_rows(fresh_ref, fresh_held)
    count = HALF // HD * 2 * SUB
    pair = iota((count, SUB), 0) % SUB
    key = iota((count, SUB), 1)
    seen = (key % rows == pair % rows) & (key <= pair) & (key < rows * steps)
    seen = seen | ((pair >= rows * steps) & (key == 0))
    for v in range(KVH):
        halves = [send_ref[order.index(v * ways + n), :, :HALF].astype(f32) for n in range(2)]
        parts = [half[:, g * HD : (g + 1) * HD] for g in range(HALF // HD) for half in halves]
        query = jnp.concatenate(parts, axis=0).astype(bf16)
        keys = fresh_held[:, v * HD : (v + 1) * HD].astype(bf16)
        values = fresh_held[:, (KVH + v) * HD : (KVH + v + 1) * HD].astype(bf16)
        scores = jnp.where(seen, dot_nt(query, keys) * SCORE, NONE)
        highest = jnp.max(scores, axis=1, keepdims=True)
        weight = jnp.exp2(scores - highest)
        total = jnp.sum(weight, axis=1, keepdims=True)
        weight = (weight / total).astype(bf16)
        own_ref[v] = jnp.dot(weight, values, preferred_element_type=f32)
        ownsum_ref[v] = jnp.broadcast_to(highest + jnp.log2(total), (count, HD))


def own_mixer(rates_ref, skips_ref, sx_ref, sb_ref, sc_ref, sdt_ref, c_rows, x_rows, fade_ref, local_ref):
    steps, rows, heads = sdt_ref.shape
    stack_rows(sc_ref, c_rows)
    for u in range(steps):
        given = sx_ref[u].astype(f32)
        for k in range(SUB // rows):
            x_rows[u, k * rows : (k + 1) * rows, :] = given
    pair = iota((SUB, heads), 0)
    step = pair // rows
    live = pair < rows * steps
    head = iota((SUB, heads), 1)

    def spread_rows(ref, u):
        given = ref[u].astype(f32)
        return jnp.concatenate([given] * (SUB // rows), axis=0)

    rates = jnp.broadcast_to(rates_ref[...], (SUB, heads)) * LOG2E
    skips = jnp.broadcast_to(skips_ref[...], (SUB, heads))
    moved = [spread_rows(sdt_ref, u) for u in range(steps)]
    kept = [jnp.where(u <= step, moved[u], 0.0) for u in range(steps)]
    parts = [jnp.where(live, jnp.exp2(-(rates * sum(kept))), 0.0)]
    for u in range(steps):
        products = c_rows[...] * spread_rows(sb_ref, u)
        inner = jnp.zeros((SUB, heads), f32)
        for e in range(products.shape[1] // NS):
            found = jnp.sum(products[:, e * NS : (e + 1) * NS], axis=1, keepdims=True)
            inner = jnp.where(head // HPG == e, found, inner)
        gap = jnp.zeros((SUB, heads), f32)
        for t in range(u + 1, steps):
            gap = gap + kept[t]
        weight = jnp.where(u <= step, jnp.exp2(-(rates * gap)) * moved[u] * inner, 0.0)
        weight = weight + jnp.where(u == step, skips, 0.0)
        parts.append(jnp.where(live, weight, 0.0))
    stacked = jnp.concatenate(parts, axis=0)
    high = stacked.astype(bf16)
    low = (stacked - high.astype(f32)).astype(bf16)
    both = jnp.concatenate([high.astype(f32), low.astype(f32)], axis=0)
    count = stacked.shape[0]
    chunk = SUB * HP
    widen = jnp.where(iota((heads, chunk), 0) % SUB == iota((heads, chunk), 1) // HP, 1.0, 0.0).astype(bf16)
    lane = iota(both.shape, 1)
    for d in range(heads // SUB):
        picked = jnp.where(lane // SUB == d, both, 0.0).astype(bf16)
        wide = jnp.dot(picked, widen, preferred_element_type=f32)
        wide = wide[:count] + wide[count:]
        columns = slice(d * chunk, (d + 1) * chunk)
        fade_ref[:, columns] = wide[:SUB]
        value = jnp.zeros((SUB, chunk), f32)
        for u in range(steps):
            value = value + wide[(u + 1) * SUB : (u + 2) * SUB] * x_rows[u, :, columns]
        local_ref[:, columns] = value


def merge_kernel(
    width,
    back_any,
    own_any,
    ownsum_any,
    fade_any,
    local_any,
    mixer_any,
    attention_any,
    back_ref,
    own_ref,
    ownsum_ref,
    fade_ref,
    local_ref,
    mixed,
    attended,
    mixer_ref,
    attention_ref,
    sems,
):
    copies = fetches([(back_any, back_ref), (fade_any, fade_ref), (local_any, local_ref)], sems)
    rest = fetches([(own_any, own_ref), (ownsum_any, ownsum_ref)], sems, len(copies))
    for copy in copies:
        copy.wait()
    owners = back_ref.shape[0]
    ways = owners // KVH
    order = exchange_order(owners)
    steps, rows = mixer_ref.shape[0], mixer_ref.shape[1]
    for d in range(0, owners, 2):
        block = jnp.stack([back_ref[order.index(d + n)].astype(f32) for n in range(2)])
        ending = lift(block, spare(back_ref.shape[2] // LANES, 1))
        if back_ref.shape[2] > HALF:
            ending = jnp.concatenate([block[..., HALF:], ending], axis=-1)
        found = ending[..., :width]
        found = jnp.concatenate([found[0], found[1]], axis=-1)
        columns = slice(d * width, (d + 2) * width)
        mixed[:, columns] = found * fade_ref[:, columns] + local_ref[:, columns]
    for k in range(steps):
        mixer_ref[k] = mixed[k * rows : (k + 1) * rows, :].astype(bf16)
    outs = fetches([(mixer_ref, mixer_any)], sems)
    for copy in rest:
        copy.wait()
    lane = iota((2, SUB, LANES), 2)
    mine = (lane // 16 == iota((2, SUB, LANES), 1)) & (lane % 16 < 12)
    for v in range(KVH):
        blocks, pieces = [], []
        for d in range(v * ways, (v + 1) * ways, 2):
            block = jnp.stack([back_ref[order.index(d + n), :, :HALF].astype(f32) for n in range(2)])
            packed = block[:, PAIRS : PAIRS + 1, :LANES]
            blocks.append(block.reshape(2 * SUB, HALF))
            pieces.append(jnp.where(mine, jnp.broadcast_to(packed, (2, SUB, LANES)), 0.0))
        for g in range(HALF // HD):
            part = slice(g * 2 * SUB, (g + 1) * 2 * SUB)
            own_sum = ownsum_ref[v, part, :]
            wide = []
            for piece in pieces:
                one = jnp.sum(jnp.where(lane % 4 == g, piece, 0.0), axis=-1, keepdims=True)
                wide.append(jnp.broadcast_to(one, (2, SUB, HD)).reshape(2 * SUB, HD))
            highest = functools.reduce(jnp.maximum, wide, own_sum)
            weight = jnp.exp2(own_sum - highest)
            total = weight
            value = weight * own_ref[v, part, :]
            for one, block in zip(wide, blocks):
                weight = jnp.exp2(one - highest)
                total = total + weight
                value = value + weight * block[:, g * HD : (g + 1) * HD]
            value = value / total
            start = v * 2 * HALF + g * HD
            attended[:, start : start + HD] = value[:SUB]
            attended[:, start + HALF : start + HALF + HD] = value[SUB:]
    for k in range(steps):
        attention_ref[k] = attended[k * rows : (k + 1) * rows, :].astype(bf16)
    outs += fetches([(attention_ref, attention_any)], sems, 1)
    for copy in outs:
        copy.wait()


def call(kernel, out_shape, in_spaces, out_spaces, scratch, cost, aliases=None):
    def spec(space):
        return pl.BlockSpec(memory_space=space)

    return pl.pallas_call(
        kernel,
        out_shape=out_shape,
        in_specs=[spec(space) for space in in_spaces],
        out_specs=jax.tree.map(spec, out_spaces),
        scratch_shapes=scratch,
        input_output_aliases=aliases or {},
        compiler_params=pltpu.CompilerParams(vmem_limit_bytes=VMEM_LIMIT),
        cost_estimate=pl.CostEstimate(flops=cost[0], bytes_accessed=cost[1], transcendentals=0),
    )


def on_device(
    prompt_x,
    prompt_b,
    prompt_c,
    prompt_dt,
    decay_rate,
    skip_gain,
    lengths,
    owner_list,
    page_table,
    cache_pages,
    row_slot,
    step_x,
    step_b,
    step_c,
    step_dt,
    queries,
    fresh_cache,
):
    owners = lax.axis_size("heads")
    ways = owners // KVH
    group, prompts, length = prompt_dt.shape
    width = prompt_x.shape[1]
    keys = cache_pages.shape[0] * PAGE
    span = 2 * keys // prompts
    steps = step_x.shape[1]
    all_rows = owners * SUB
    shape = jax.ShapeDtypeStruct
    smem, vmem, hbm = pltpu.SMEM, pltpu.VMEM, pltpu.HBM
    sem = pltpu.SemaphoreType.DMA((prompts,))
    levels = len(LEVELS)
    step_x, step_b, step_c, step_dt, queries, fresh_cache = (
        jnp.swapaxes(one, 0, 1) for one in (step_x, step_b, step_c, step_dt, queries, fresh_cache)
    )
    owner_list = owner_list.T

    def like(space, array):
        return space(array.shape, array.dtype)

    def sems(count):
        return pltpu.SemaphoreType.DMA((count,))

    other_pages = lax.ppermute(cache_pages, "heads", [(d, d + 1 - 2 * (d % 2)) for d in range(owners)])
    send = call(
        functools.partial(pack_kernel, group, ways),
        shape((all_rows, HALF + LANES), bf16),
        [hbm, hbm],
        vmem,
        [
            like(vmem, queries),
            like(vmem, step_c),
            vmem((SUB, queries.shape[2]), f32),
            vmem((SUB, step_c.shape[2]), f32),
            vmem((step_c.shape[2] // NS, SUB, HALF + LANES), f32),
            sems(2),
        ],
        (0, 1 << 19),
    )(queries, step_c)
    order = [exchange_order(owners)]
    recv = lax.all_to_all(
        send, "heads", split_axis=0, concat_axis=0, tiled=True, axis_index_groups=order
    )

    block = [
        vmem((prompts, width, length), bf16),
        vmem((prompts, length, NS), bf16),
        vmem((prompts, length, NS), bf16),
        vmem((prompts, width, length), bf16),
        vmem((levels, prompts, group, length), f32),
        vmem((levels, prompts, group, length), f32),
        vmem((prompts, group, length), f32),
    ]
    tables = [vmem((levels, length, length), bf16), vmem((levels + 1, length, length), bf16)]
    work = 2 * width * length * NS
    states, sorted_keys, sorted_values, codes, early_out = call(
        state_kernel,
        (
            shape((prompts, width, NS), bf16),
            shape((prompts // 2, span, 2 * HD), bf16),
            shape((prompts // 2, span, 2 * HD), bf16),
            shape((all_rows, LANES), jnp.int32),
            shape(prompt_x.shape, bf16),
        ),
        [hbm] * 12,
        (hbm,) * 5,
        block
        + tables
        + [vmem((prompts, group, length), f32), vmem((prompts, width, NS), bf16)]
        + [vmem((2,) + cache_pages.shape, bf16)]
        + [vmem((prompts // 2, span, 2 * HD), bf16)] * 2
        + [vmem((all_rows, LANES), jnp.int32)]
        + [like(smem, one) for one in (decay_rate, skip_gain, lengths, owner_list, page_table, row_slot)]
        + [like(vmem, prompt_dt), sem, sem, sem, sem, sem, sems(9)],
        (work * (prompts + 5 * EARLY), 6 << 20),
    )(
        decay_rate,
        skip_gain,
        lengths,
        owner_list,
        page_table,
        row_slot,
        prompt_dt,
        prompt_x,
        prompt_b,
        prompt_c,
        cache_pages,
        other_pages,
    )

    back = call(
        serve_kernel,
        shape((all_rows, HALF + max(LANES, width) - LANES), bf16),
        [hbm] * 5,
        vmem,
        [like(vmem, one) for one in (recv, sorted_keys, sorted_values, codes, states)]
        + [vmem((prompts // 2, HALF // HD * all_rows, 2 * HD), bf16), sem, sems(4)],
        (8 * all_rows * keys * HD, 4 << 20),
    )(recv, sorted_keys, sorted_values, codes, states)
    returned = lax.all_to_all(
        back, "heads", split_axis=0, concat_axis=0, tiled=True, axis_index_groups=order
    ).reshape(owners, SUB, back.shape[1])

    count = HALF // HD * 2 * SUB
    channels = step_x.shape[2]
    rates, skips = decay_rate.reshape(1, -1), skip_gain.reshape(1, -1)
    prompt_out, own, own_sum, fade, local = call(
        prompt_kernel,
        (
            shape(prompt_x.shape, bf16),
            shape((KVH, count, HD), f32),
            shape((KVH, count, HD), f32),
            shape((SUB, channels), f32),
            shape((SUB, channels), f32),
        ),
        [hbm] * 17,
        (hbm,) * 5,
        block
        + tables
        + [
            vmem((KVH, count, HD), f32),
            vmem((KVH, count, HD), f32),
            vmem((SUB, channels), f32),
            vmem((SUB, channels), f32),
            vmem((SUB, fresh_cache.shape[2]), f32),
            vmem((SUB, step_c.shape[2]), f32),
            vmem((steps, SUB, channels), f32),
            like(smem, decay_rate),
            like(smem, skip_gain),
            like(smem, lengths),
            like(vmem, prompt_dt),
            like(vmem, rates),
            like(vmem, skips),
            vmem((owners, SUB, HALF + LANES), bf16),
            like(vmem, fresh_cache),
            like(vmem, step_x),
            like(vmem, step_b),
            like(vmem, step_c),
            like(vmem, step_dt),
            sem,
            sem,
            sem,
            sem,
            sems(12),
        ],
        (work * 5 * (prompts - EARLY), 8 << 20),
        {16: 0},
    )(
        decay_rate,
        skip_gain,
        lengths,
        prompt_dt,
        rates,
        skips,
        send.reshape(owners, SUB, HALF + LANES),
        fresh_cache,
        step_x,
        step_b,
        step_c,
        step_dt,
        prompt_x,
        prompt_b,
        prompt_c,
        back,
        early_out,
    )

    mixer_out, attention_out = call(
        functools.partial(merge_kernel, width),
        (shape(step_x.shape, bf16), shape(queries.shape, bf16)),
        [hbm] * 5,
        (hbm, hbm),
        [like(vmem, one) for one in (returned, own, own_sum, fade, local)]
        + [vmem((SUB, channels), f32), vmem((SUB, queries.shape[2]), f32)]
        + [like(vmem, step_x), like(vmem, queries), sems(5)],
        (0, 2 << 20),
    )(returned, own, own_sum, fade, local)
    return (prompt_out, jnp.swapaxes(mixer_out, 0, 1), jnp.swapaxes(attention_out, 0, 1))


def solution(mesh):
    in_specs = (
        P("groups", "heads", None),
        P("groups", None, None),
        P("groups", None, None),
        P("heads", "groups", None),
        P(),
        P(),
        P("groups"),
        P("groups", None),
        P("groups", None),
        P(("groups", "heads"), None, None),
        P("groups"),
        P(("groups", "heads"), None, None),
        P(("groups", "heads"), None, None),
        P(("groups", "heads"), None, None),
        P(("groups", "heads"), None, None),
        P(("groups", "heads"), None, None),
        P(("groups", "heads"), None, None),
    )
    out_specs = (
        P("groups", "heads", None),
        P(("groups", "heads"), None, None),
        P(("groups", "heads"), None, None),
    )
    return jax.shard_map(
        on_device, mesh=mesh, in_specs=in_specs, out_specs=out_specs, check_vma=False
    )
```
